512 devices in a mesh: gx: 16 (over x, y_hi), gy: 8 (over z), gz: 4 (over y_lo, core).
Axes of the slice: x: 4, y: 8 (y_hi: 4, y_lo: 2; y = y_hi * 2 + y_lo), z: 8, core: 2. Of those that a mesh axis runs over, the one named last changes fastest.
Arguments:
- displacement: float32 [3, 128, 128, 512], P(None, 'gx', 'gy', 'gz'), may hold values from -6 to 6
- previous: float32 [3, 128, 128, 512], P(None, 'gx', 'gy', 'gz'), may hold values from -6 to 6
- courant: float32 [128, 128, 512], P('gx', 'gy', 'gz'), may hold values from 0.02 to 0.2
- damping: float32 [128, 128, 512], P('gx', 'gy', 'gz'), may hold values from 0 to 0.3
- send_cells: int32 [256, 8, 128], P('gx', 'gy'), may hold values from 0 to 127
- building_slot: int32 [524288], P(('gx', 'gy', 'gz')), may hold values from 0 to 2047
- building_class: int32 [524288], P(('gx', 'gy', 'gz')), may hold values from 0 to 7
- city: int32 [524288], P(('gx', 'gy', 'gz')), may hold values from 0 to 15
- mode_count: int32 [8], replicated, may hold values from 1 to 8
- modal_filter: bfloat16 [64, 24], replicated, may hold values from -1.25 to 1.25
- amplify: float32 [16], replicated, may hold values from 0.5 to 3
- median: float32 [16, 8], replicated, may hold values from 0 to 1.5
- spread: float32 [16, 8], replicated, may hold values from 0.2 to 0.8
Outputs:
- final_field: float32 [3, 128, 128, 512], P(None, 'gx', 'gy', 'gz')
- probability: float32 [16, 524288], P(None, ('gx', 'gy', 'gz'))
The draws below stay inside these ranges and needn't reach their ends.
All inputs are finite; a program needn't handle non-finite values.
Results may differ from the reference program's by a relative error of at most 0.00079.
Values may be sent and summed in bfloat16 or wider, within the bound.
No kernel may reach another device: no remote copies, remote signals or barrier semaphores. Data moves between devices by JAX's collectives and lax.ppermute only.
A program may use at most 64 MiB of HBM per device.

```python
import math
import jax
import jax.numpy as jnp
import numpy as np
from jax import lax

CX = 8
CY = 16
STEPS = 8
CAP = 128
B_DEV = 1024
CLASSES = 8
MODES = 8
CITIES = 16
BATCHES = 16
NX = 128
NY = 128
NZ = 512
BUILDINGS = 524288
N_GX = 16
N_GY = 8
N_GZ = 4


def with_ends(entries, stream_key, low, largest):
    shape = entries.shape
    index_at = [jax.random.randint(jax.random.fold_in(stream_key, axis), (), 0, shape[axis]) for axis in range(len(shape))]
    entries = entries.at[tuple(index_at)].set(low)
    longest = shape.index(max(shape))
    index_at[longest] = (index_at[longest] + 1) % shape[longest]
    return entries.at[tuple(index_at)].set(largest)


def level_of(own_key, shape, split, smallest, largest):
    def one(axis_at, blocks):
        draws = jax.random.uniform(jax.random.fold_in(jax.random.fold_in(own_key, 6), axis_at), (blocks,), jnp.float32, smallest / len(split), largest / len(split))
        return jnp.repeat(jnp.exp(draws), shape[axis_at] // blocks).reshape((-1,) + (1,) * (len(shape) - axis_at - 1))

    factor_of = one(*split[0])
    for cut in split[1:]:
        factor_of = factor_of * one(*cut)
    return factor_of


def cumulative_ranks(amount, lean):
    loads = [(1 << 20) // math.isqrt(rank ** lean) + 1 for rank in range(1, amount + 1)]
    deviation = 1 + sum(loads) // (1 << 30)
    return np.cumsum(np.array([max(1, weight // deviation) for weight in loads]))


def ranked_ids(own_key, extent, number_of, lean):
    grid = cumulative_ranks(number_of, lean)
    pick = jax.random.randint(jax.random.fold_in(own_key, 1), extent, 0, int(grid[number_of - 1]))
    grade = jnp.searchsorted(jnp.asarray(grid, jnp.int32), pick, side="right")
    return jax.random.permutation(jax.random.fold_in(own_key, 2), number_of)[grade].astype(jnp.int32)


def centred(stream_key, shape, scale, most, pieces=(), dtype=jnp.bfloat16):
    result = jax.random.normal(stream_key, shape, jnp.float32) * scale
    if len(pieces) > 0:
        result = level_of(stream_key, shape, pieces, -0.22, 0.18) * result
    return jnp.clip(result, min=-most, max=most).astype(dtype)


def setup_inputs(seed: int = 0) -> dict:
    key_of = jax.random.split(jax.random.key(seed), 14)
    return {
        "displacement": centred(key_of[0], (3, NX, NY, NZ), 1.0, 6.0, ((1, 16), (2, 8), (3, 4)), jnp.float32),
        "previous": centred(key_of[1], (3, NX, NY, NZ), 1.0, 6.0, ((1, 16), (2, 8), (3, 4)), jnp.float32),
        "courant": jnp.clip(jnp.exp(math.log(0.2) - 2.3025851 * jax.random.uniform(key_of[2], (NX, NY, NZ), jnp.float32) ** level_of(key_of[2], (NX, NY, NZ), ((0, 16), (1, 8), (2, 4)), -0.2, 0.2)), 0.02, 0.2),
        "damping": jnp.clip(0.3 * jax.random.uniform(key_of[3], (NX, NY, NZ), jnp.float32) ** level_of(key_of[3], (NX, NY, NZ), ((0, 16), (1, 8), (2, 4)), -0.2, 0.2), 0.0, 0.3),
        "send_cells": with_ends(jax.random.randint(key_of[4], (N_GX * N_GX, N_GY, CAP), 0, CX * CY), jax.random.fold_in(key_of[4], 1), 0, (CX * CY) - 1).astype(jnp.int32),
        "building_slot": with_ends(jax.random.randint(key_of[5], (BUILDINGS,), 0, N_GX * CAP), jax.random.fold_in(key_of[5], 1), 0, (N_GX * CAP) - 1).astype(jnp.int32),
        "building_class": with_ends(jax.random.randint(key_of[6], (BUILDINGS,), 0, CLASSES), jax.random.fold_in(key_of[6], 1), 0, CLASSES - 1).astype(jnp.int32),
        "city": with_ends(ranked_ids(key_of[7], (BUILDINGS,), CITIES, 2), jax.random.fold_in(key_of[7], 3), 0, CITIES - 1).astype(jnp.int32),
        "mode_count": with_ends(jax.random.randint(key_of[8], (CLASSES,), 1, MODES + 1), jax.random.fold_in(key_of[8], 1), 1, MODES).astype(jnp.int32),
        "modal_filter": centred(key_of[9], (CLASSES * MODES, 3 * STEPS), (3 * STEPS) ** -0.5, 1.25),
        "amplify": jnp.clip(jnp.exp(jax.random.uniform(key_of[10], (CITIES,), jnp.float32, math.log(0.5), math.log(3.0))), 0.5, 3.0),
        "median": jnp.clip(jax.random.uniform(key_of[11], (BATCHES, CLASSES), jnp.float32, 0.0, 1.5), 0.0, 1.5),
        "spread": jnp.clip(jnp.exp(jax.random.uniform(key_of[12], (BATCHES, CLASSES), jnp.float32, math.log(0.2), math.log(0.8))), 0.2, 0.8),
    }


def window(extended, axis_dim, offset):
    starts = [0, 2, 2, 2]
    limits = [extended.shape[0], extended.shape[1] - 2, extended.shape[2] - 2, extended.shape[3] - 2]
    starts[axis_dim] = starts[axis_dim] + offset
    limits[axis_dim] = limits[axis_dim] + offset
    return lax.slice(extended, starts, limits)


def advance(extended, prev_core, rate_core, damp_core):
    core = extended[:, 2:-2, 2:-2, 2:-2]
    laplace = -7.5 * core
    for axis_dim in (1, 2, 3):
        for offset, weight in ((-2, -1.0 / 12.0), (-1, 4.0 / 3.0), (1, 4.0 / 3.0), (2, -1.0 / 12.0)):
            laplace = laplace + weight * window(extended, axis_dim, offset)
    return (2.0 * core - (1.0 - damp_core) * prev_core + rate_core * laplace) / (1.0 + damp_core)


def reference(displacement, previous, courant, damping, send_cells, building_slot, building_class, city, mode_count, modal_filter, amplify, median, spread):
    field = displacement
    earlier = previous
    records = []
    for step_index in range(STEPS):
        extended = jnp.pad(field, ((0, 0), (2, 2), (2, 2), (2, 2)))
        fresh = advance(extended, earlier, courant, damping)
        records.append(fresh[:, :, :, 0])
        earlier = field
        field = fresh
    record = jnp.stack(records).reshape(3 * STEPS, NX, NY).astype(jnp.bfloat16)
    number = jnp.arange(BUILDINGS).astype(jnp.int32)
    device = number // B_DEV
    owner = device // (N_GY * N_GZ)
    row_index = (device // N_GZ) % N_GY
    source = building_slot // CAP
    column = building_slot % CAP
    cell = send_cells[source * N_GX + owner, row_index, column]
    xpos = source * CX + cell // CY
    ypos = row_index * CY + cell % CY
    motion = record[:, xpos, ypos]
    modal = jnp.dot(modal_filter, motion, preferred_element_type=jnp.float32)
    squared = (modal * modal).reshape(CLASSES, MODES, BUILDINGS)
    mode_mask = (jnp.arange(MODES)[None, :] < mode_count[:, None]).astype(jnp.float32)
    per_class = jnp.sum(squared * mode_mask[:, :, None], axis=1)
    onehot = (building_class[None, :] == jnp.arange(CLASSES)[:, None]).astype(jnp.float32)
    energy = jnp.sum(onehot * per_class, axis=0)
    city_hot = (city[None, :] == jnp.arange(CITIES)[:, None]).astype(jnp.float32)
    amp_each = jnp.sum(city_hot * amplify[:, None], axis=0)
    logdemand = jnp.log(amp_each) + 0.5 * jnp.log1p(energy)
    med_each = jnp.dot(median, onehot, precision=lax.Precision.HIGHEST)
    spread_each = jnp.dot(spread, onehot, precision=lax.Precision.HIGHEST)
    probability = jax.nn.sigmoid((logdemand[None, :] - med_each) / spread_each)
    return field, probability
```

```python
import functools

import jax
import jax.numpy as jnp
from jax import lax
from jax.experimental import pallas as pl
from jax.experimental.pallas import tpu as pltpu
from jax.sharding import PartitionSpec as P

STEPS = 8
HALF = 4
DEEP = 2 * HALF
CLASSES = 8
MODES = 8
F32 = jnp.float32
VMEM_LIMIT = 48 * 1024 * 1024

XU, XP, XH = 8, 6, 7
YU, YP, YH = 22, 18, 20


def lane_of():
    return lax.broadcasted_iota(jnp.int32, (8, 128), 1)


def pack_faces(values, lane):
    packed = pltpu.roll(values[0], 8, 1)
    for at in range(1, len(values)):
        packed = jnp.where(lane // 16 == at, pltpu.roll(values[at], (16 * at + 8) % 128, 1), packed)
    return packed


def pack_kernel(u_ref, p_ref, c_ref, d_ref, out_ref):
    lane = lane_of()

    def plane(x, carry):
        for row in (0, 8):
            rows = pl.ds(row, 8)
            values = [u_ref[k, x, rows, :] for k in range(3)] + [p_ref[k, x, rows, :] for k in range(3)]
            values += [c_ref[x, rows, :], d_ref[x, rows, :]]
            out_ref[x, rows, :] = pack_faces(values, lane)
        return carry

    lax.fori_loop(0, 8, plane, 0)


def x_message_kernel(coefficients, *refs):
    if coefficients:
        low_ref, high_ref, u_ref, p_ref, c_ref, d_ref, halo_ref, up_ref, down_ref = refs
    else:
        low_ref, high_ref, u_ref, p_ref, halo_ref, up_ref, down_ref = refs
    lane = lax.broadcasted_iota(jnp.int32, (8, 16, 128), 2)
    halo = jnp.where(lane % 16 < 8, low_ref[...], high_ref[...])
    halo_ref[...] = halo
    at = 0
    for k in range(3):
        up_ref[at : at + 8] = u_ref[k]
        down_ref[at : at + 8] = u_ref[k]
        at += XU
    parts = [p_ref.at[k] for k in range(3)] + ([c_ref, d_ref] if coefficients else [])
    for part in parts:
        up_ref[at : at + XP] = part[8 - XP : 8]
        down_ref[at : at + XP] = part[0:XP]
        at += XP
    up_ref[at : at + XH] = halo[8 - XH : 8]
    down_ref[at : at + XH] = halo[0:XH]


def y_message_kernel(coefficients, *refs):
    if coefficients:
        u_ref, p_ref, c_ref, d_ref, halo_ref, low_ref, high_ref, up_ref, down_ref = refs
    else:
        u_ref, p_ref, halo_ref, low_ref, high_ref, up_ref, down_ref = refs
    parts = [(u_ref.at[k], XU, YU) for k in range(3)] + [(p_ref.at[k], XP, YP) for k in range(3)]
    if coefficients:
        parts += [(c_ref, XP, YP), (d_ref, XP, YP)]
    parts += [(halo_ref, XH, YH)]
    x_at = y_at = 0
    for own, x_planes, y_planes in parts:
        side = (y_planes - 8) // 2
        for out_ref, rows in ((up_ref, slice(8, 16)), (down_ref, slice(0, 8))):
            out_ref[y_at : y_at + side] = low_ref[x_at + x_planes - side : x_at + x_planes, rows, :]
            out_ref[y_at + side : y_at + side + 8] = own[:, rows, :]
            out_ref[y_at + side + 8 : y_at + y_planes] = high_ref[x_at : x_at + side, rows, :]
        x_at += x_planes
        y_at += y_planes


def fill(target, own, x_low, x_high, y_low, y_high, x_at, x_planes, y_at, y_planes):
    target[8 - x_planes : 8, 16:32, :] = x_low[x_at : x_at + x_planes]
    target[8:16, 16:32, :] = own[...]
    target[16 : 16 + x_planes, 16:32, :] = x_high[x_at : x_at + x_planes]
    side = (y_planes - 8) // 2
    target[8 - side : 16 + side, 8:16, :] = y_low[y_at : y_at + y_planes]
    target[8 - side : 16 + side, 32:40, :] = y_high[y_at : y_at + y_planes]


def steps_kernel(first, *refs):
    if first:
        (u_in, p_in, c_in, d_in, halo_in, x_low, x_high, y_low, y_high) = refs[:9]
        (u_out, p_out, face_out, seen_out, a_out, e_out, ha_out, he_out) = refs[9:17]
        u_ref, p_ref, hu_ref, hp_ref, c_ref, d_ref = refs[17:]
        a_ref, e_ref, ha_ref, he_ref = a_out, e_out, ha_out, he_out
    else:
        (u_in, p_in, halo_in, x_low, x_high, y_low, y_high, seen_in, a_ref, e_ref, ha_ref, he_ref) = refs[:12]
        (cells_in, filter_in, count_in) = refs[12:15]
        (u_out, table_out) = refs[15:17]
        u_ref, p_ref, hu_ref, hp_ref, seen_out = refs[17:]
    lane = lane_of()
    low1, low2 = lane == 0, lane < 2
    high1, high2 = lane == 127, lane >= 126
    inner = lane % 16
    up1, up2 = inner == 8, (inner == 8) | (inner == 9)
    down1, down2 = inner == 7, (inner == 7) | (inner == 6)

    x_at = y_at = 0
    for k in range(3):
        fill(u_ref.at[k], u_in.at[k], x_low, x_high, y_low, y_high, x_at, XU, y_at, YU)
        x_at, y_at = x_at + XU, y_at + YU
    for k in range(3):
        fill(p_ref.at[k], p_in.at[k], x_low, x_high, y_low, y_high, x_at, XP, y_at, YP)
        x_at, y_at = x_at + XP, y_at + YP
    if first:
        for target, own in ((c_ref, c_in), (d_ref, d_in)):
            fill(target, own, x_low, x_high, y_low, y_high, x_at, XP, y_at, YP)
            x_at, y_at = x_at + XP, y_at + YP
    fill(hu_ref, halo_in, x_low, x_high, y_low, y_high, x_at, XH, y_at, YH)

    def prepare(x, carry):
        for tile in range(4):
            rows = pl.ds(8 + 8 * tile, 8)
            held = pl.ds(8 * tile, 8)
            halo = hu_ref[x, rows, :]
            hp_ref[x, rows, :] = pltpu.roll(halo, 128 - 48, 1)
            if first:
                share = 1.0 / (1.0 + d_ref[x, rows, :])
                a_ref[x, held, :] = 2.0 * share
                e_ref[x, held, :] = c_ref[x, rows, :] * share * (1.0 / 12.0)
                share = 1.0 / (1.0 + pltpu.roll(halo, 128 - 16, 1))
                for target, value in ((ha_ref, 2.0 * share), (he_ref, halo * share * (1.0 / 12.0))):
                    spread = jnp.where(lane < 16, pltpu.roll(value, 32, 1), pltpu.roll(value, 48, 1))
                    target[x, held, :] = jnp.where(lane < 32, spread, pltpu.roll(value, 64, 1))
        return carry

    lax.fori_loop(2, 22, prepare, 0)

    def update(src, dst, hsrc, hdst, x, tile, with_halo):
        row = 8 + 8 * tile
        rows = pl.ds(row, 8)
        halo = hsrc[x, rows, :]
        a_each = a_ref[x, pl.ds(8 * tile, 8), :]
        e_each = e_ref[x, pl.ds(8 * tile, 8), :]
        centres, fresh = [], []
        for k in range(3):
            v = src[k, x, rows, :]
            beyond = pltpu.roll(halo, (128 - 16 * k - 8) % 128, 1)
            near = pltpu.roll(jnp.where(low1, beyond, v), 127, 1) + pltpu.roll(jnp.where(high1, beyond, v), 1, 1)
            far = pltpu.roll(jnp.where(low2, beyond, v), 126, 1) + pltpu.roll(jnp.where(high2, beyond, v), 2, 1)
            near += (src[k, x - 1, rows, :] + src[k, x + 1, rows, :]) + (
                src[k, x, pl.ds(row - 1, 8), :] + src[k, x, pl.ds(row + 1, 8), :]
            )
            far += (src[k, x - 2, rows, :] + src[k, x + 2, rows, :]) + (
                src[k, x, pl.ds(row - 2, 8), :] + src[k, x, pl.ds(row + 2, 8), :]
            )
            laplace = 16.0 * near - far - 90.0 * v
            old = dst[k, x, rows, :]
            new = old + a_each * (v - old) + e_each * laplace
            dst[k, x, rows, :] = new
            centres.append(v)
            fresh.append(new)
        if with_halo:
            edge = pack_faces(centres, lane)
            near = pltpu.roll(jnp.where(up1, edge, halo), 127, 1) + pltpu.roll(jnp.where(down1, edge, halo), 1, 1)
            far = pltpu.roll(jnp.where(up2, edge, halo), 126, 1) + pltpu.roll(jnp.where(down2, edge, halo), 2, 1)
            near += (hsrc[x - 1, rows, :] + hsrc[x + 1, rows, :]) + (
                hsrc[x, pl.ds(row - 1, 8), :] + hsrc[x, pl.ds(row + 1, 8), :]
            )
            far += (hsrc[x - 2, rows, :] + hsrc[x + 2, rows, :]) + (
                hsrc[x, pl.ds(row - 2, 8), :] + hsrc[x, pl.ds(row + 2, 8), :]
            )
            laplace = 16.0 * near - far - 90.0 * halo
            old = hdst[x, rows, :]
            held = pl.ds(8 * tile, 8)
            hdst[x, rows, :] = old + ha_ref[x, held, :] * (halo - old) + he_ref[x, held, :] * laplace
        return fresh

    def see(x, tile, fresh, step):
        rows = pl.ds(8 * (tile - 1), 8)
        seen = seen_out[x - 8, rows, :]
        for k in range(3):
            seen = jnp.where(lane == 3 * step + k, jnp.broadcast_to(fresh[k][:, 0:1], (8, 128)), seen)
        seen_out[x - 8, rows, :] = seen

    if first:
        seen_out[...] = jnp.zeros((8, 16, 128), F32)
    else:
        seen_out[...] = seen_in[...]
    begin = 0 if first else HALF
    buffers = [(u_ref, hu_ref), (p_ref, hp_ref)]
    for step in range(HALF - 1):
        (src, hsrc), (dst, hdst) = buffers[step % 2], buffers[(step + 1) % 2]

        def outer(x, carry, src=src, dst=dst, hsrc=hsrc, hdst=hdst):
            for tile in range(4):
                update(src, dst, hsrc, hdst, x, tile, True)
            return carry

        def own(x, carry, src=src, dst=dst, hsrc=hsrc, hdst=hdst, step=step):
            for tile in range(4):
                fresh = update(src, dst, hsrc, hdst, x, tile, True)
                if tile in (1, 2):
                    see(x, tile, fresh, begin + step)
            return carry

        lax.fori_loop(2 * step + 2, 8, outer, 0)
        lax.fori_loop(8, 16, own, 0)
        lax.fori_loop(16, 22 - 2 * step, outer, 0)

    (src, hsrc), (dst, hdst) = buffers[1], buffers[0]

    def last(x, carry):
        for tile in (1, 2):
            fresh = update(src, dst, hsrc, hdst, x, tile, False)
            see(x, tile, fresh, begin + HALF - 1)
            rows = pl.ds(8 * (tile - 1), 8)
            for k in range(3):
                u_out[k, x - 8, rows, :] = fresh[k]
            if first:
                before = [src[k, x, pl.ds(8 + 8 * tile, 8), :] for k in range(3)]
                for k in range(3):
                    p_out[k, x - 8, rows, :] = before[k]
                face_out[x - 8, rows, :] = pack_faces(fresh + before, lane)
        return carry

    lax.fori_loop(8, 16, last, 0)

    if not first:
        motion = seen_out[...].reshape(128, 128).astype(jnp.bfloat16)
        modal = lax.dot_general(filter_in[...], motion, (((1,), (1,)), ((), ())), preferred_element_type=F32)
        modes = lax.broadcasted_iota(jnp.int32, (MODES, 128), 0)
        energies = []
        for kind in range(CLASSES):
            part = modal[MODES * kind : MODES * (kind + 1), :]
            part = jnp.where(modes < count_in[kind], part * part, 0.0)
            energies.append(jnp.sum(part, axis=0, keepdims=True))
        demand = 0.5 * jnp.log1p(jnp.concatenate(energies, axis=0))
        for owner in range(table_out.shape[0]):
            cells = jnp.broadcast_to(cells_in[owner : owner + 1, :], (CLASSES, 128))
            chosen = jnp.take_along_axis(demand, cells, axis=1)
            for level in range(table_out.shape[1]):
                table_out[owner, level] = chosen


def fragility_kernel(table_ref, slot_ref, kind_ref, city_ref, amplify_ref, median_ref, spread_ref, out_ref):
    sources = table_ref.shape[0]
    slot, kind, city = slot_ref[...], kind_ref[...], city_ref[...]
    column = slot % 128
    key = (slot // 128) * CLASSES + kind
    demand = jnp.zeros((8, 128), F32)
    for source in range(sources):
        for each in range(CLASSES):
            row = jnp.broadcast_to(table_ref[source, each : each + 1, :], (8, 128))
            found = jnp.take_along_axis(row, column, axis=1)
            demand = jnp.where(key == source * CLASSES + each, found, demand)
    gain = jnp.log(jnp.broadcast_to(amplify_ref[...], (8, 128)))
    demand = demand + jnp.take_along_axis(gain, city, axis=1)
    for group in range(8):
        level = jnp.broadcast_to(demand[group : group + 1, :], (8, 128))
        index = jnp.broadcast_to(kind[group : group + 1, :], (8, 128))
        for half in (0, 8):
            middle = jnp.take_along_axis(median_ref[half : half + 8, :], index, axis=1)
            width = jnp.take_along_axis(spread_ref[half : half + 8, :], index, axis=1)
            out_ref[half : half + 8, 128 * group : 128 * group + 128] = jax.nn.sigmoid((level - middle) / width)


VM = pl.BlockSpec(memory_space=pltpu.VMEM)
SM = pl.BlockSpec(memory_space=pltpu.SMEM)


def call(kernel, name, shapes, args, specs=None, scratch=()):
    out = [jax.ShapeDtypeStruct(s, F32) for s in shapes]
    return pl.pallas_call(
        kernel,
        out_shape=out,
        in_specs=specs or [VM] * len(args),
        out_specs=[VM] * len(out),
        scratch_shapes=list(scratch),
        compiler_params=pltpu.CompilerParams(vmem_limit_bytes=VMEM_LIMIT),
        name=name,
    )(*args)


def both_ways(to_up, to_down, axis):
    count = lax.axis_size(axis)
    forward = [(i, i + 1) for i in range(count - 1)]
    backward = [(i + 1, i) for i in range(count - 1)]
    return lax.ppermute(to_up, axis, forward), lax.ppermute(to_down, axis, backward)


def exchange(u, p, faces, coefficients):
    extra = list(coefficients)
    has = bool(extra)
    z_low, z_high = both_ways(faces, faces, "gz")
    planes = 3 * XU + (3 + len(extra)) * XP + XH
    halo, up, down = call(
        functools.partial(x_message_kernel, has),
        "x_message",
        [(8, 16, 128), (planes, 16, 128), (planes, 16, 128)],
        [z_low, z_high, u, p] + extra,
    )
    x_low, x_high = both_ways(up, down, "gx")
    planes = 3 * YU + (3 + len(extra)) * YP + YH
    up, down = call(
        functools.partial(y_message_kernel, has),
        "y_message",
        [(planes, 8, 128), (planes, 8, 128)],
        [u, p] + extra + [halo, x_low, x_high],
    )
    y_low, y_high = both_ways(up, down, "gy")
    return halo, x_low, x_high, y_low, y_high


def body(
    displacement,
    previous,
    courant,
    damping,
    send_cells,
    building_slot,
    building_class,
    city,
    mode_count,
    modal_filter,
    amplify,
    median,
    spread,
):
    own = (3, 8, 16, 128)
    plane = (8, 16, 128)
    wide = [pltpu.VMEM((3, 24, 48, 128), F32)] * 2 + [pltpu.VMEM((24, 48, 128), F32)] * 2

    (faces,) = call(pack_kernel, "faces", [plane], [displacement, previous, courant, damping])
    received = exchange(displacement, previous, faces, (courant, damping))
    u, p, faces, seen, *coefficients = call(
        functools.partial(steps_kernel, True),
        "steps_first",
        [own, own, plane, plane] + [(24, 32, 128)] * 4,
        [displacement, previous, courant, damping, *received],
        scratch=wide + [pltpu.VMEM((24, 48, 128), F32)] * 2,
    )
    received = exchange(u, p, faces, ())
    owners, levels = lax.axis_size("gx"), lax.axis_size("gz")
    filters = jnp.pad(modal_filter, ((0, 0), (0, 128 - 3 * STEPS)))
    args = [u, p, *received, seen, *coefficients, send_cells.reshape(owners, 128), filters, mode_count]
    field, table = call(
        functools.partial(steps_kernel, False),
        "steps_second",
        [own, (owners, levels, CLASSES, 128)],
        args,
        specs=[VM] * (len(args) - 1) + [SM],
        scratch=wide + [pltpu.VMEM(plane, F32)],
    )
    table = table.reshape(owners * levels, CLASSES, 128)
    table = lax.all_to_all(table, ("gx", "gz"), split_axis=0, concat_axis=0, tiled=True)
    table = table.reshape(owners, levels, CLASSES, 128)[:, 0]
    (probability,) = call(
        fragility_kernel,
        "fragility",
        [(16, 1024)],
        [
            table,
            building_slot.reshape(8, 128),
            building_class.reshape(8, 128),
            city.reshape(8, 128),
            jnp.pad(amplify, (0, 112), constant_values=1.0).reshape(1, 128),
            jnp.pad(median, ((0, 0), (0, 120))),
            jnp.pad(spread, ((0, 0), (0, 120)), constant_values=1.0),
        ],
    )
    return (field, probability)


def solution(mesh):
    placed = (
        P(None, "gx", "gy", "gz"),
        P(None, "gx", "gy", "gz"),
        P("gx", "gy", "gz"),
        P("gx", "gy", "gz"),
        P("gx", "gy", None),
        P(("gx", "gy", "gz")),
        P(("gx", "gy", "gz")),
        P(("gx", "gy", "gz")),
        P(),
        P(),
        P(),
        P(),
        P(),
    )
    return jax.shard_map(
        body,
        mesh=mesh,
        in_specs=placed,
        out_specs=(P(None, "gx", "gy", "gz"), P(None, ("gx", "gy", "gz"))),
        check_vma=False,
    )
```

```python
import functools

import jax
import jax.numpy as jnp
from jax import lax
from jax.experimental import pallas as pl
from jax.experimental.pallas import tpu as pltpu
from jax.sharding import PartitionSpec as P

STEPS = 8
HALF = 4
DEEP = 2 * HALF
CLASSES = 8
MODES = 8
F32 = jnp.float32
VMEM_LIMIT = 24 * 1024 * 1024

XU, XP, XH = 8, 6, 7
YU, YP, YH = 22, 18, 20


def lane_of():
    return lax.broadcasted_iota(jnp.int32, (8, 128), 1)


def pack_faces(values, lane):
    packed = pltpu.roll(values[0], 8, 1)
    for at in range(1, len(values)):
        packed = jnp.where(lane // 16 == at, pltpu.roll(values[at], (16 * at + 8) % 128, 1), packed)
    return packed


def start_kernel(u_in, p_in, c_in, d_in, u_ref, p_ref, a_ref, e_ref, face_ref, c_ref, d_ref, sems):
    copies = [pltpu.make_async_copy(c_in, c_ref, sems.at[0]), pltpu.make_async_copy(d_in, d_ref, sems.at[1])]
    for k in range(3):
        copies.append(pltpu.make_async_copy(u_in.at[k], u_ref.at[k], sems.at[2 + k]))
        copies.append(pltpu.make_async_copy(p_in.at[k], p_ref.at[k], sems.at[5 + k]))
    for copy in copies:
        copy.start()
    for copy in copies:
        copy.wait()
    lane = lane_of()

    def plane(x, carry):
        for row in (0, 8):
            rows = pl.ds(row, 8)
            share = 1.0 / (1.0 + d_ref[x, rows, :])
            values = [u_ref[k, x, rows, :] for k in range(3)] + [p_ref[k, x, rows, :] for k in range(3)]
            values += [2.0 * share, c_ref[x, rows, :] * share * (1.0 / 12.0)]
            a_ref[x, rows, :] = values[6]
            e_ref[x, rows, :] = values[7]
            face_ref[x, rows, :] = pack_faces(values, lane)
        return carry

    lax.fori_loop(0, 8, plane, 0)


def x_message_kernel(coefficients, *refs):
    if coefficients:
        low_ref, high_ref, u_ref, p_ref, c_ref, d_ref, halo_ref, up_ref, down_ref = refs
    else:
        low_ref, high_ref, u_ref, p_ref, halo_ref, up_ref, down_ref = refs
    lane = lax.broadcasted_iota(jnp.int32, (8, 16, 128), 2)
    halo = jnp.where(lane % 16 < 8, low_ref[...], high_ref[...])
    halo_ref[...] = halo
    at = 0
    for k in range(3):
        up_ref[at : at + 8] = u_ref[k]
        down_ref[at : at + 8] = u_ref[k]
        at += XU
    parts = [p_ref.at[k] for k in range(3)] + ([c_ref, d_ref] if coefficients else [])
    for part in parts:
        up_ref[at : at + XP] = part[8 - XP : 8]
        down_ref[at : at + XP] = part[0:XP]
        at += XP
    up_ref[at : at + XH] = halo[8 - XH : 8]
    down_ref[at : at + XH] = halo[0:XH]


def y_message_kernel(coefficients, *refs):
    if coefficients:
        u_ref, p_ref, c_ref, d_ref, halo_ref, low_ref, high_ref, up_ref, down_ref = refs
    else:
        u_ref, p_ref, halo_ref, low_ref, high_ref, up_ref, down_ref = refs
    parts = [(u_ref.at[k], XU, YU) for k in range(3)] + [(p_ref.at[k], XP, YP) for k in range(3)]
    if coefficients:
        parts += [(c_ref, XP, YP), (d_ref, XP, YP)]
    parts += [(halo_ref, XH, YH)]
    x_at = y_at = 0
    for own, x_planes, y_planes in parts:
        side = (y_planes - 8) // 2
        for out_ref, rows in ((up_ref, slice(8, 16)), (down_ref, slice(0, 8))):
            out_ref[y_at : y_at + side] = low_ref[x_at + x_planes - side : x_at + x_planes, rows, :]
            out_ref[y_at + side : y_at + side + 8] = own[:, rows, :]
            out_ref[y_at + side + 8 : y_at + y_planes] = high_ref[x_at : x_at + side, rows, :]
        x_at += x_planes
        y_at += y_planes


def fill(parts, x_low, x_high, y_low, y_high, x_at, x_planes, y_at, y_planes):
    count = len(parts)

    def own(i, carry):
        for (target, row), block in parts:
            target[8 + i, row + 8 : row + 24, :] = block[i]
        return carry

    def x_side(i, carry):
        for at, ((target, row), _) in enumerate(parts):
            target[8 - x_planes + i, row + 8 : row + 24, :] = x_low[x_at + at * x_planes + i]
            target[16 + i, row + 8 : row + 24, :] = x_high[x_at + at * x_planes + i]
        return carry

    def y_side(i, carry):
        side = (y_planes - 8) // 2
        for at, ((target, row), _) in enumerate(parts):
            target[8 - side + i, row : row + 8, :] = y_low[y_at + at * y_planes + i]
            target[8 - side + i, row + 24 : row + 32, :] = y_high[y_at + at * y_planes + i]
        return carry

    lax.fori_loop(0, 8, own, 0)
    lax.fori_loop(0, x_planes, x_side, 0)
    lax.fori_loop(0, y_planes, y_side, 0)
    return x_at + count * x_planes, y_at + count * y_planes


def steps_kernel(first, *refs):
    if first:
        (u_in, p_in, a_in, e_in, halo_in, x_low, x_high, y_low, y_high) = refs[:9]
        (u_out, p_out, face_out, seen_out, a_ref, e_ref, ha_ref, he_ref) = refs[9:17]
        state_ref, edge_ref = refs[17:]
    else:
        (u_in, p_in, halo_in, x_low, x_high, y_low, y_high, seen_in, a_ref, e_ref, ha_ref, he_ref) = refs[:12]
        (cells_in, filter_in, count_in) = refs[12:15]
        (u_out, table_out) = refs[15:17]
        state_ref, edge_ref, seen_out = refs[17:]
    lane = lane_of()
    low1, low2 = lane == 0, lane < 2
    high1, high2 = lane == 127, lane >= 126
    inner = lane % 16
    up1, up2 = inner == 8, (inner == 8) | (inner == 9)
    down1, down2 = inner == 7, (inner == 7) | (inner == 6)

    sides = (x_low, x_high, y_low, y_high)
    x_at, y_at = fill([((state_ref.at[0, k], 8), u_in.at[k]) for k in range(3)], *sides, 0, XU, 0, YU)
    parts = [((state_ref.at[1, k], 8), p_in.at[k]) for k in range(3)]
    if first:
        parts += [((a_ref, 0), a_in), ((e_ref, 0), e_in)]
    x_at, y_at = fill(parts, *sides, x_at, XP, y_at, YP)
    fill([((state_ref.at[0, 3], 8), halo_in)], *sides, x_at, XH, y_at, YH)

    def prepare(x, carry):
        for tile in range(4):
            rows = pl.ds(8 + 8 * tile, 8)
            held = pl.ds(8 * tile, 8)
            halo = state_ref[0, 3, x, rows, :]
            state_ref[1, 3, x, rows, :] = pltpu.roll(halo, 128 - 48, 1)
            if first:
                for target, at in ((ha_ref, 96), (he_ref, 112)):
                    spread = jnp.where(lane < 16, pltpu.roll(halo, 128 - at, 1), pltpu.roll(halo, 144 - at, 1))
                    target[x, held, :] = jnp.where(lane < 32, spread, pltpu.roll(halo, 160 - at, 1))
        return carry

    lax.fori_loop(2, 22, prepare, 0)

    def update(src, dst, x, tile):
        row = 8 + 8 * tile
        rows = pl.ds(row, 8)
        held = pl.ds(8 * tile, 8)
        halo = src[3, 2, rows, :]
        a_each = a_ref[x, held, :]
        e_each = e_ref[x, held, :]
        centres, fresh = [], []

        def around(k, near, far):
            near += (src[k, 1, rows, :] + src[k, 3, rows, :]) + (
                src[k, 2, pl.ds(row - 1, 8), :] + src[k, 2, pl.ds(row + 1, 8), :]
            )
            far += (src[k, 0, rows, :] + src[k, 4, rows, :]) + (
                src[k, 2, pl.ds(row - 2, 8), :] + src[k, 2, pl.ds(row + 2, 8), :]
            )
            return 16.0 * near - far

        for k in range(3):
            v = src[k, 2, rows, :]
            beyond = pltpu.roll(halo, (128 - 16 * k - 8) % 128, 1)
            near = pltpu.roll(jnp.where(low1, beyond, v), 127, 1) + pltpu.roll(jnp.where(high1, beyond, v), 1, 1)
            far = pltpu.roll(jnp.where(low2, beyond, v), 126, 1) + pltpu.roll(jnp.where(high2, beyond, v), 2, 1)
            laplace = around(k, near, far) - 90.0 * v
            old = dst[k, x, rows, :]
            fresh.append(old + a_each * (v - old) + e_each * laplace)
            centres.append(v)
        edge = pack_faces(centres, lane)
        near = pltpu.roll(jnp.where(up1, edge, halo), 127, 1) + pltpu.roll(jnp.where(down1, edge, halo), 1, 1)
        far = pltpu.roll(jnp.where(up2, edge, halo), 126, 1) + pltpu.roll(jnp.where(down2, edge, halo), 2, 1)
        laplace = around(3, near, far) - 90.0 * halo
        old = dst[3, x, rows, :]
        fresh.append(old + ha_ref[x, held, :] * (halo - old) + he_ref[x, held, :] * laplace)
        return fresh, edge

    def one_step(step, carry):
        dst = state_ref.at[(step + 1) % 2]

        def plane(x, inside):
            src = state_ref.at[step % 2, :, pl.ds(x - 2, 5)]
            results = [update(src, dst, x, tile) for tile in range(4)]
            for tile, (fresh, edge) in enumerate(results):
                for k in range(4):
                    dst[k, x, 8 + 8 * tile : 16 + 8 * tile, :] = fresh[k]
                if tile in (1, 2):
                    edge_ref[step, x, 8 * (tile - 1) : 8 * tile, :] = edge
            return inside

        lax.fori_loop(2 * step + 2, 22 - 2 * step, plane, 0)
        return carry

    lax.fori_loop(0, HALF, one_step, 0)

    begin = 0 if first else HALF
    block = pl.ds(16, 16)

    def finish(x, carry):
        for k in range(3):
            u_out[k, x, :, :] = state_ref[0, k, 8 + x, block, :]
            if first:
                p_out[k, x, :, :] = state_ref[1, k, 8 + x, block, :]
        for row in (0, 8):
            rows = pl.ds(row, 8)
            last = pack_faces([state_ref[0, k, 8 + x, pl.ds(16 + row, 8), :] for k in range(3)], lane)
            if first:
                after = pack_faces([state_ref[1, k, 8 + x, pl.ds(16 + row, 8), :] for k in range(3)], lane)
                face_out[x, rows, :] = jnp.where(lane < 48, last, pltpu.roll(after, 48, 1))
                seen = jnp.zeros((8, 128), F32)
            else:
                seen = seen_in[x, rows, :]
            for step in range(HALF):
                edge = last if step == HALF - 1 else edge_ref[step + 1, 8 + x, rows, :]
                at = begin + step
                seen = jnp.where((inner == 8 + at) & (lane < 48), pltpu.roll(edge, at, 1), seen)
            seen_out[x, rows, :] = seen
        return carry

    lax.fori_loop(0, 8, finish, 0)

    if not first:
        motion = seen_out[...].reshape(128, 128).astype(jnp.bfloat16)
        modal = lax.dot_general(filter_in[...], motion, (((1,), (1,)), ((), ())), preferred_element_type=F32)
        modes = lax.broadcasted_iota(jnp.int32, (MODES, 128), 0)
        energies = []
        for kind in range(CLASSES):
            part = modal[MODES * kind : MODES * (kind + 1), :]
            part = jnp.where(modes < count_in[kind], part * part, 0.0)
            energies.append(jnp.sum(part, axis=0, keepdims=True))
        demand = 0.5 * jnp.log1p(jnp.concatenate(energies, axis=0))
        for owner in range(table_out.shape[0]):
            cells = jnp.broadcast_to(cells_in[owner : owner + 1, :], (CLASSES, 128))
            chosen = jnp.take_along_axis(demand, cells, axis=1)
            for level in range(table_out.shape[1]):
                table_out[owner, level] = chosen


def fragility_kernel(table_ref, slot_ref, kind_ref, city_ref, amplify_ref, median_ref, spread_ref, out_ref):
    sources = table_ref.shape[0]
    slot, kind, city = slot_ref[...], kind_ref[...], city_ref[...]
    column = slot % 128
    key = (slot // 128) * CLASSES + kind
    demand = jnp.zeros((8, 128), F32)
    for source in range(sources):
        for each in range(CLASSES):
            row = jnp.broadcast_to(table_ref[source, each : each + 1, :], (8, 128))
            found = jnp.take_along_axis(row, column, axis=1)
            demand = jnp.where(key == source * CLASSES + each, found, demand)
    gain = jnp.log(jnp.broadcast_to(amplify_ref[...], (8, 128)))
    demand = demand + jnp.take_along_axis(gain, city, axis=1)
    for group in range(8):
        level = jnp.broadcast_to(demand[group : group + 1, :], (8, 128))
        index = jnp.broadcast_to(kind[group : group + 1, :], (8, 128))
        for half in (0, 8):
            middle = jnp.take_along_axis(median_ref[half : half + 8, :], index, axis=1)
            width = jnp.take_along_axis(spread_ref[half : half + 8, :], index, axis=1)
            out_ref[half : half + 8, 128 * group : 128 * group + 128] = jax.nn.sigmoid((level - middle) / width)


VM = pl.BlockSpec(memory_space=pltpu.VMEM)
SM = pl.BlockSpec(memory_space=pltpu.SMEM)


def call(kernel, name, shapes, args, specs=None, scratch=()):
    out = [jax.ShapeDtypeStruct(s, F32) for s in shapes]
    return pl.pallas_call(
        kernel,
        out_shape=out,
        in_specs=specs or [VM] * len(args),
        out_specs=[VM] * len(out),
        scratch_shapes=list(scratch),
        compiler_params=pltpu.CompilerParams(vmem_limit_bytes=VMEM_LIMIT),
        name=name,
    )(*args)


def both_ways(to_up, to_down, axis):
    count = lax.axis_size(axis)
    forward = [(i, i + 1) for i in range(count - 1)]
    backward = [(i + 1, i) for i in range(count - 1)]
    return lax.ppermute(to_up, axis, forward), lax.ppermute(to_down, axis, backward)


def exchange(u, p, faces, coefficients):
    extra = list(coefficients)
    has = bool(extra)
    z_low, z_high = both_ways(faces, faces, "gz")
    planes = 3 * XU + (3 + len(extra)) * XP + XH
    halo, up, down = call(
        functools.partial(x_message_kernel, has),
        "x_message",
        [(8, 16, 128), (planes, 16, 128), (planes, 16, 128)],
        [z_low, z_high, u, p] + extra,
    )
    x_low, x_high = both_ways(up, down, "gx")
    planes = 3 * YU + (3 + len(extra)) * YP + YH
    up, down = call(
        functools.partial(y_message_kernel, has),
        "y_message",
        [(planes, 8, 128), (planes, 8, 128)],
        [u, p] + extra + [halo, x_low, x_high],
    )
    y_low, y_high = both_ways(up, down, "gy")
    return halo, x_low, x_high, y_low, y_high


def body(
    displacement,
    previous,
    courant,
    damping,
    send_cells,
    building_slot,
    building_class,
    city,
    mode_count,
    modal_filter,
    amplify,
    median,
    spread,
):
    own = (3, 8, 16, 128)
    plane = (8, 16, 128)
    wide = [pltpu.VMEM((2, 4, 24, 48, 128), F32), pltpu.VMEM((HALF, 24, 16, 128), F32)]

    u, p, a, e, faces = call(
        start_kernel,
        "start",
        [own, own, plane, plane, plane],
        [displacement, previous, courant, damping],
        specs=[pl.BlockSpec(memory_space=pltpu.HBM)] * 4,
        scratch=[pltpu.VMEM(plane, F32)] * 2 + [pltpu.SemaphoreType.DMA((8,))],
    )
    received = exchange(u, p, faces, (a, e))
    u, p, faces, seen, *coefficients = call(
        functools.partial(steps_kernel, True),
        "steps_first",
        [own, own, plane, plane] + [(24, 32, 128)] * 4,
        [u, p, a, e, *received],
        scratch=wide,
    )
    received = exchange(u, p, faces, ())
    owners, levels = lax.axis_size("gx"), lax.axis_size("gz")
    filters = jnp.swapaxes(modal_filter.reshape(CLASSES * MODES, STEPS, 3), 1, 2)
    filters = jnp.pad(filters, ((0, 0), (0, 5), (16 - STEPS, 0))).reshape(CLASSES * MODES, 128)
    args = [u, p, *received, seen, *coefficients, send_cells.reshape(owners, 128), filters, mode_count]
    field, table = call(
        functools.partial(steps_kernel, False),
        "steps_second",
        [own, (owners, levels, CLASSES, 128)],
        args,
        specs=[VM] * (len(args) - 1) + [SM],
        scratch=wide + [pltpu.VMEM(plane, F32)],
    )
    table = table.reshape(owners * levels, CLASSES, 128)
    table = lax.all_to_all(table, ("gx", "gz"), split_axis=0, concat_axis=0, tiled=True)
    table = table.reshape(owners, levels, CLASSES, 128)[:, 0]
    (probability,) = call(
        fragility_kernel,
        "fragility",
        [(16, 1024)],
        [
            table,
            building_slot.reshape(8, 128),
            building_class.reshape(8, 128),
            city.reshape(8, 128),
            jnp.pad(amplify, (0, 112), constant_values=1.0).reshape(1, 128),
            jnp.pad(median, ((0, 0), (0, 120))),
            jnp.pad(spread, ((0, 0), (0, 120)), constant_values=1.0),
        ],
    )
    return (field, probability)


def solution(mesh):
    placed = (
        P(None, "gx", "gy", "gz"),
        P(None, "gx", "gy", "gz"),
        P("gx", "gy", "gz"),
        P("gx", "gy", "gz"),
        P("gx", "gy", None),
        P(("gx", "gy", "gz")),
        P(("gx", "gy", "gz")),
        P(("gx", "gy", "gz")),
        P(),
        P(),
        P(),
        P(),
        P(),
    )
    return jax.shard_map(
        body,
        mesh=mesh,
        in_specs=placed,
        out_specs=(P(None, "gx", "gy", "gz"), P(None, ("gx", "gy", "gz"))),
        check_vma=False,
    )
```

```python
import functools

import jax
import jax.numpy as jnp
from jax import lax
from jax.experimental import pallas as pl
from jax.experimental.pallas import tpu as pltpu
from jax.sharding import PartitionSpec as P

STEPS = 8
HALF = 4
DEEP = 2 * HALF
CLASSES = 8
MODES = 8
F32 = jnp.float32
VMEM_LIMIT = 24 * 1024 * 1024

XU, XP, XH = 8, 6, 7
YU, YP, YH = 24, 20, 20

FULL = 32000.0
BIAS = 200
UNIT_A = 2.0 / FULL
UNIT_E = 0.2 / 12.0 / FULL


def lane_of():
    return lax.broadcasted_iota(jnp.int32, (8, 128), 1)


def pack_faces(values, lane):
    packed = pltpu.roll(values[0], 8, 1)
    for at in range(1, len(values)):
        packed = jnp.where(lane // 16 == at, pltpu.roll(values[at], (16 * at + 8) % 128, 1), packed)
    return packed


def start_kernel(u_in, p_in, c_in, d_in, u_ref, p_ref, a_ref, e_ref, face_ref, c_ref, d_ref, sems):
    copies = [pltpu.make_async_copy(c_in, c_ref, sems.at[0]), pltpu.make_async_copy(d_in, d_ref, sems.at[1])]
    for k in range(3):
        copies.append(pltpu.make_async_copy(u_in.at[k], u_ref.at[k], sems.at[2 + k]))
        copies.append(pltpu.make_async_copy(p_in.at[k], p_ref.at[k], sems.at[5 + k]))
    for copy in copies:
        copy.start()
    for copy in copies:
        copy.wait()
    lane = lane_of()

    def plane(x, carry):
        for row in (0, 8):
            rows = pl.ds(row, 8)
            share = 1.0 / (1.0 + d_ref[x, rows, :])
            values = [u_ref[k, x, rows, :] for k in range(3)] + [p_ref[k, x, rows, :] for k in range(3)]
            values += [2.0 * share, c_ref[x, rows, :] * share * (1.0 / 12.0)]
            a_ref[x, rows, :] = values[6]
            e_ref[x, rows, :] = values[7]
            face_ref[x, rows, :] = pack_faces(values, lane)
        return carry

    lax.fori_loop(0, 8, plane, 0)


def exponent_of(peak):
    peak = jnp.maximum(jnp.max(peak, axis=0, keepdims=True), 1e-30)
    return jnp.broadcast_to(jnp.ceil(jnp.log2(peak)), (8, 128))


def coded(values):
    return jnp.round(values).astype(jnp.int32).astype(jnp.int16)


def decoded(values):
    return values.astype(jnp.int32).astype(F32)


def twice(rows):
    return jnp.concatenate([rows, rows], axis=0)


def sent_exponents(message):
    both = decoded(message[message.shape[0] - 1]) - BIAS
    return both[0:8], both[8:16]


def x_message_kernel(coefficients, *refs):
    if coefficients:
        low_ref, high_ref, u_ref, p_ref, a_ref, e_ref, halo_ref, up_ref, down_ref, power_ref = refs
    else:
        low_ref, high_ref, u_ref, p_ref, halo_ref, up_ref, down_ref, power_ref = refs
    inner = lax.broadcasted_iota(jnp.int32, (16, 128), 1) % 16

    def largest(x, carry):
        field, face = carry
        for k in range(3):
            both = jnp.maximum(jnp.abs(u_ref[k, x]), jnp.abs(p_ref[k, x]))
            field = jnp.maximum(field, jnp.maximum(both[0:8], both[8:16]))
        halo = jnp.where(inner < 8, low_ref[x], high_ref[x])
        halo_ref[x] = halo
        halo = jnp.abs(halo)
        return field, jnp.maximum(face, jnp.maximum(halo[0:8], halo[8:16]))

    zero = jnp.zeros((8, 128), F32)
    field, face = lax.fori_loop(0, 8, largest, (zero, zero))
    powers = jnp.concatenate([exponent_of(field), exponent_of(face)], axis=0)
    power_ref[...] = powers
    up_ref[up_ref.shape[0] - 1] = coded(powers + BIAS)
    down_ref[down_ref.shape[0] - 1] = coded(powers + BIAS)
    scale = FULL * jnp.exp2(-powers)
    field, face = twice(scale[0:8]), twice(scale[8:16])

    def whole(x, carry):
        for k in range(3):
            code = coded(u_ref[k, x] * field)
            up_ref[XU * k + x] = code
            down_ref[XU * k + x] = code
        return carry

    def part(i, carry):
        parts = [(p_ref.at[k], field) for k in range(3)]
        if coefficients:
            parts += [(a_ref, 1.0 / UNIT_A), (e_ref, 1.0 / UNIT_E)]
        for at, (source, unit) in enumerate(parts):
            up_ref[3 * XU + XP * at + i] = coded(source[8 - XP + i] * unit)
            down_ref[3 * XU + XP * at + i] = coded(source[i] * unit)
        return carry

    at = 3 * XU + (5 if coefficients else 3) * XP

    def side(i, carry):
        up_ref[at + i] = coded(halo_ref[8 - XH + i] * face)
        down_ref[at + i] = coded(halo_ref[i] * face)
        return carry

    lax.fori_loop(0, 8, whole, 0)
    lax.fori_loop(0, XP, part, 0)
    lax.fori_loop(0, XH, side, 0)


def y_message_kernel(coefficients, *refs):
    if coefficients:
        u_ref, p_ref, a_ref, e_ref, halo_ref, power_ref, low_ref, high_ref, up_ref, down_ref = refs
    else:
        u_ref, p_ref, halo_ref, power_ref, low_ref, high_ref, up_ref, down_ref = refs
    powers = power_ref[...]
    low_powers = jnp.concatenate(sent_exponents(low_ref), axis=0)
    high_powers = jnp.concatenate(sent_exponents(high_ref), axis=0)
    most = jnp.maximum(powers, jnp.maximum(low_powers, high_powers))
    for out_ref in (up_ref, down_ref):
        out_ref[out_ref.shape[0] - 1] = coded(most + BIAS)
    own_scale = FULL * jnp.exp2(-most)
    low_scale = jnp.exp2(low_powers - most)
    high_scale = jnp.exp2(high_powers - most)
    field = [twice(scale[0:8]) for scale in (own_scale, low_scale, high_scale)]
    face = [twice(scale[8:16]) for scale in (own_scale, low_scale, high_scale)]

    def put(at, pair):
        up_ref[at] = coded(jnp.concatenate([pair[0][8:16], pair[1][8:16]], axis=0))
        down_ref[at] = coded(jnp.concatenate([pair[0][0:8], pair[1][0:8]], axis=0))

    def group(parts, x_planes, y_planes, x_at, y_at):
        side = (y_planes - 8) // 4

        def own(i, carry):
            for at, (source, units) in enumerate(parts):
                put(y_at + at * y_planes // 2 + side + i, [source[2 * i + j] * units[0] for j in (0, 1)])
            return carry

        def sides(i, carry):
            for at, (_, units) in enumerate(parts):
                start = x_at + at * x_planes
                first = start + x_planes - 2 * side + 2 * i
                put(y_at + at * y_planes // 2 + i, [decoded(low_ref[first + j]) * units[1] for j in (0, 1)])
                first = start + 2 * i
                pair = [decoded(high_ref[first + j]) * units[2] for j in (0, 1)]
                put(y_at + at * y_planes // 2 + side + 4 + i, pair)
            return carry

        lax.fori_loop(0, 4, own, 0)
        lax.fori_loop(0, side, sides, 0)
        return x_at + len(parts) * x_planes, y_at + len(parts) * y_planes // 2

    x_at, y_at = group([(u_ref.at[k], field) for k in range(3)], XU, YU, 0, 0)
    parts = [(p_ref.at[k], field) for k in range(3)]
    if coefficients:
        parts += [(a_ref, (1.0 / UNIT_A, 1.0, 1.0)), (e_ref, (1.0 / UNIT_E, 1.0, 1.0))]
    x_at, y_at = group(parts, XP, YP, x_at, y_at)
    group([(halo_ref, face)], XH, YH, x_at, y_at)


def fill(parts, x_low, x_high, y_low, y_high, x_at, x_planes, y_at, y_planes):
    count = len(parts)
    side = (y_planes - 8) // 2

    def own(i, carry):
        for target, row, block, _ in parts:
            target[8 + i, row + 8 : row + 24, :] = block[i]
        return carry

    def x_side(i, carry):
        for at, (target, row, _, units) in enumerate(parts):
            here = x_at + at * x_planes + i
            target[8 - x_planes + i, row + 8 : row + 24, :] = decoded(x_low[here]) * units[0]
            target[16 + i, row + 8 : row + 24, :] = decoded(x_high[here]) * units[1]
        return carry

    def y_side(i, carry):
        for at, (target, row, _, units) in enumerate(parts):
            here = y_at + at * y_planes // 2 + i
            low = decoded(y_low[here]) * units[2]
            high = decoded(y_high[here]) * units[3]
            for j in (0, 1):
                target[8 - side + 2 * i + j, row : row + 8, :] = low[8 * j : 8 * j + 8]
                target[8 - side + 2 * i + j, row + 24 : row + 32, :] = high[8 * j : 8 * j + 8]
        return carry

    lax.fori_loop(0, 8, own, 0)
    lax.fori_loop(0, x_planes, x_side, 0)
    lax.fori_loop(0, y_planes // 2, y_side, 0)
    return x_at + count * x_planes, y_at + count * y_planes // 2


def steps_kernel(first, *refs):
    if first:
        (u_in, p_in, a_in, e_in, halo_in, x_low, x_high, y_low, y_high) = refs[:9]
        (u_out, p_out, face_out, seen_out, rate_ref) = refs[9:14]
        state_ref, edge_ref = refs[14:]
    else:
        (u_in, p_in, halo_in, x_low, x_high, y_low, y_high, seen_in, rate_ref) = refs[:9]
        (cells_in, filter_in) = refs[9:11]
        (u_out, table_out) = refs[11:13]
        state_ref, edge_ref, seen_out = refs[13:]
    a_ref, e_ref, ha_ref, he_ref = (rate_ref.at[at] for at in range(4))
    lane = lane_of()
    low1, low2 = lane == 0, lane < 2
    high1, high2 = lane == 127, lane >= 126
    inner = lane % 16
    up1, up2 = inner == 8, (inner == 8) | (inner == 9)
    down1, down2 = inner == 7, (inner == 7) | (inner == 6)

    sides = (x_low, x_high, y_low, y_high)
    powers = [sent_exponents(message) for message in sides]
    field = [twice(jnp.exp2(power[0]) * (1.0 / FULL)) for power in powers]
    face = [twice(jnp.exp2(power[1]) * (1.0 / FULL)) for power in powers]
    x_at, y_at = fill([(state_ref.at[0, k], 8, u_in.at[k], field) for k in range(3)], *sides, 0, XU, 0, YU)
    parts = [(state_ref.at[1, k], 8, p_in.at[k], field) for k in range(3)]
    if first:
        parts += [(a_ref, 0, a_in, (UNIT_A,) * 4), (e_ref, 0, e_in, (UNIT_E,) * 4)]
    x_at, y_at = fill(parts, *sides, x_at, XP, y_at, YP)
    fill([(state_ref.at[0, 3], 8, halo_in, face)], *sides, x_at, XH, y_at, YH)

    def prepare(x, carry):
        for tile in range(4):
            rows = pl.ds(8 + 8 * tile, 8)
            held = pl.ds(8 * tile, 8)
            halo = state_ref[0, 3, x, rows, :]
            state_ref[1, 3, x, rows, :] = pltpu.roll(halo, 128 - 48, 1)
            if first:
                for target, at in ((ha_ref, 96), (he_ref, 112)):
                    spread = jnp.where(lane < 16, pltpu.roll(halo, 128 - at, 1), pltpu.roll(halo, 144 - at, 1))
                    target[x, held, :] = jnp.where(lane < 32, spread, pltpu.roll(halo, 160 - at, 1))
        return carry

    lax.fori_loop(2, 22, prepare, 0)

    def update(src, dst, x, tile):
        row = 8 + 8 * tile
        rows = pl.ds(row, 8)
        held = pl.ds(8 * tile, 8)
        halo = src[3, 2, rows, :]
        a_each = a_ref[x, held, :]
        e_each = e_ref[x, held, :]
        centres, fresh = [], []

        def around(k, near, far):
            near += (src[k, 1, rows, :] + src[k, 3, rows, :]) + (
                src[k, 2, pl.ds(row - 1, 8), :] + src[k, 2, pl.ds(row + 1, 8), :]
            )
            far += (src[k, 0, rows, :] + src[k, 4, rows, :]) + (
                src[k, 2, pl.ds(row - 2, 8), :] + src[k, 2, pl.ds(row + 2, 8), :]
            )
            return 16.0 * near - far

        for k in range(3):
            v = src[k, 2, rows, :]
            beyond = pltpu.roll(halo, (128 - 16 * k - 8) % 128, 1)
            near = pltpu.roll(jnp.where(low1, beyond, v), 127, 1) + pltpu.roll(jnp.where(high1, beyond, v), 1, 1)
            far = pltpu.roll(jnp.where(low2, beyond, v), 126, 1) + pltpu.roll(jnp.where(high2, beyond, v), 2, 1)
            laplace = around(k, near, far) - 90.0 * v
            old = dst[k, x, rows, :]
            fresh.append(old + a_each * (v - old) + e_each * laplace)
            centres.append(v)
        edge = pack_faces(centres, lane)
        near = pltpu.roll(jnp.where(up1, edge, halo), 127, 1) + pltpu.roll(jnp.where(down1, edge, halo), 1, 1)
        far = pltpu.roll(jnp.where(up2, edge, halo), 126, 1) + pltpu.roll(jnp.where(down2, edge, halo), 2, 1)
        laplace = around(3, near, far) - 90.0 * halo
        old = dst[3, x, rows, :]
        fresh.append(old + ha_ref[x, held, :] * (halo - old) + he_ref[x, held, :] * laplace)
        return fresh, edge

    def one_step(step, carry):
        dst = state_ref.at[(step + 1) % 2]

        def plane(x, inside):
            src = state_ref.at[step % 2, :, pl.ds(x - 2, 5)]
            results = [update(src, dst, x, tile) for tile in range(4)]
            for tile, (fresh, edge) in enumerate(results):
                for k in range(4):
                    dst[k, x, 8 + 8 * tile : 16 + 8 * tile, :] = fresh[k]
                if tile in (1, 2):
                    edge_ref[step, x, 8 * (tile - 1) : 8 * tile, :] = edge
            return inside

        lax.fori_loop(2 * step + 2, 22 - 2 * step, plane, 0)
        return carry

    lax.fori_loop(0, HALF, one_step, 0)

    begin = 0 if first else HALF
    block = pl.ds(16, 16)

    def finish(x, carry):
        for k in range(3):
            u_out[k, x, :, :] = state_ref[0, k, 8 + x, block, :]
            if first:
                p_out[k, x, :, :] = state_ref[1, k, 8 + x, block, :]
        for row in (0, 8):
            rows = pl.ds(row, 8)
            last = pack_faces([state_ref[0, k, 8 + x, pl.ds(16 + row, 8), :] for k in range(3)], lane)
            if first:
                after = pack_faces([state_ref[1, k, 8 + x, pl.ds(16 + row, 8), :] for k in range(3)], lane)
                face_out[x, rows, :] = jnp.where(lane < 48, last, pltpu.roll(after, 48, 1))
                seen = jnp.zeros((8, 128), F32)
            else:
                seen = seen_in[x, rows, :]
            for step in range(HALF):
                edge = last if step == HALF - 1 else edge_ref[step + 1, 8 + x, rows, :]
                at = begin + step
                seen = jnp.where((inner == 8 + at) & (lane < 48), pltpu.roll(edge, at, 1), seen)
            seen_out[x, rows, :] = seen
        return carry

    lax.fori_loop(0, 8, finish, 0)

    if not first:
        motion = seen_out[...].reshape(128, 128).astype(jnp.bfloat16)
        modal = lax.dot_general(filter_in[...], motion, (((1,), (1,)), ((), ())), preferred_element_type=F32)
        energies = []
        for kind in range(CLASSES):
            part = modal[MODES * kind : MODES * (kind + 1), :]
            energies.append(jnp.sum(part * part, axis=0, keepdims=True))
        demand = 0.5 * jnp.log1p(jnp.concatenate(energies, axis=0))
        for owner in range(table_out.shape[0]):
            cells = jnp.broadcast_to(cells_in[owner : owner + 1, :], (CLASSES, 128))
            chosen = jnp.take_along_axis(demand, cells, axis=1)
            for level in range(table_out.shape[1]):
                table_out[owner, level] = chosen


def fragility_kernel(table_ref, slot_ref, kind_ref, city_ref, amplify_ref, median_ref, spread_ref, out_ref):
    sources = table_ref.shape[0]
    slot, kind, city = slot_ref[...], kind_ref[...], city_ref[...]
    column = slot % 128
    key = (slot // 128) * CLASSES + kind
    demand = jnp.zeros((8, 128), F32)
    for source in range(sources):
        for each in range(CLASSES):
            row = jnp.broadcast_to(table_ref[source, each : each + 1, :], (8, 128))
            found = jnp.take_along_axis(row, column, axis=1)
            demand = jnp.where(key == source * CLASSES + each, found, demand)
    gain = jnp.log(jnp.broadcast_to(amplify_ref[...], (8, 128)))
    demand = demand + jnp.take_along_axis(gain, city, axis=1)
    for group in range(8):
        level = jnp.broadcast_to(demand[group : group + 1, :], (8, 128))
        index = jnp.broadcast_to(kind[group : group + 1, :], (8, 128))
        for half in (0, 8):
            middle = jnp.take_along_axis(median_ref[half : half + 8, :], index, axis=1)
            width = jnp.take_along_axis(spread_ref[half : half + 8, :], index, axis=1)
            out_ref[half : half + 8, 128 * group : 128 * group + 128] = jax.nn.sigmoid((level - middle) / width)


VM = pl.BlockSpec(memory_space=pltpu.VMEM)


def call(kernel, name, shapes, args, specs=None, scratch=()):
    out = [s if isinstance(s, jax.ShapeDtypeStruct) else jax.ShapeDtypeStruct(s, F32) for s in shapes]
    return pl.pallas_call(
        kernel,
        out_shape=out,
        in_specs=specs or [VM] * len(args),
        out_specs=[VM] * len(out),
        scratch_shapes=list(scratch),
        compiler_params=pltpu.CompilerParams(vmem_limit_bytes=VMEM_LIMIT),
        name=name,
    )(*args)


def both_ways(to_up, to_down, axis):
    count = lax.axis_size(axis)
    forward = [(i, i + 1) for i in range(count - 1)]
    backward = [(i + 1, i) for i in range(count - 1)]
    return lax.ppermute(to_up, axis, forward), lax.ppermute(to_down, axis, backward)


def exchange(u, p, faces, coefficients):
    extra = list(coefficients)
    has = bool(extra)
    z_low, z_high = both_ways(faces, faces, "gz")
    planes = 3 * XU + (3 + len(extra)) * XP + XH + 1
    message = jax.ShapeDtypeStruct((planes, 16, 128), jnp.int16)
    halo, up, down, powers = call(
        functools.partial(x_message_kernel, has),
        "x_message",
        [(8, 16, 128), message, message, (16, 128)],
        [z_low, z_high, u, p] + extra,
    )
    x_low, x_high = both_ways(up, down, "gx")
    planes = (3 * YU + (3 + len(extra)) * YP + YH) // 2 + 1
    message = jax.ShapeDtypeStruct((planes, 16, 128), jnp.int16)
    up, down = call(
        functools.partial(y_message_kernel, has),
        "y_message",
        [message, message],
        [u, p] + extra + [halo, powers, x_low, x_high],
    )
    y_low, y_high = both_ways(up, down, "gy")
    return halo, x_low, x_high, y_low, y_high


def body(
    displacement,
    previous,
    courant,
    damping,
    send_cells,
    building_slot,
    building_class,
    city,
    mode_count,
    modal_filter,
    amplify,
    median,
    spread,
):
    own = (3, 8, 16, 128)
    plane = (8, 16, 128)
    wide = [pltpu.VMEM((2, 4, 24, 48, 128), F32), pltpu.VMEM((HALF, 24, 16, 128), F32)]

    u, p, a, e, faces = call(
        start_kernel,
        "start",
        [own, own, plane, plane, plane],
        [displacement, previous, courant, damping],
        specs=[pl.BlockSpec(memory_space=pltpu.HBM)] * 4,
        scratch=[pltpu.VMEM(plane, F32)] * 2 + [pltpu.SemaphoreType.DMA((8,))],
    )
    received = exchange(u, p, faces, (a, e))
    u, p, faces, seen, rates = call(
        functools.partial(steps_kernel, True),
        "steps_first",
        [own, own, plane, plane, (4, 24, 32, 128)],
        [u, p, a, e, *received],
        scratch=wide,
    )
    received = exchange(u, p, faces, ())
    owners, levels = lax.axis_size("gx"), lax.axis_size("gz")
    used = jnp.arange(MODES)[None, :] < mode_count[:, None]
    filters = jnp.where(used.reshape(CLASSES * MODES, 1), modal_filter, 0).astype(modal_filter.dtype)
    filters = jnp.swapaxes(filters.reshape(CLASSES * MODES, STEPS, 3), 1, 2)
    filters = jnp.pad(filters, ((0, 0), (0, 5), (16 - STEPS, 0))).reshape(CLASSES * MODES, 128)
    args = [u, p, *received, seen, rates, send_cells.reshape(owners, 128), filters]
    field, table = call(
        functools.partial(steps_kernel, False),
        "steps_second",
        [own, (owners, levels, CLASSES, 128)],
        args,
        scratch=wide + [pltpu.VMEM(plane, F32)],
    )
    table = table.reshape(owners * levels, CLASSES, 128)
    table = lax.all_to_all(table, ("gx", "gz"), split_axis=0, concat_axis=0, tiled=True)
    table = table.reshape(owners, levels, CLASSES, 128)[:, 0]
    (probability,) = call(
        fragility_kernel,
        "fragility",
        [(16, 1024)],
        [
            table,
            building_slot.reshape(8, 128),
            building_class.reshape(8, 128),
            city.reshape(8, 128),
            jnp.pad(amplify, (0, 112), constant_values=1.0).reshape(1, 128),
            jnp.pad(median, ((0, 0), (0, 120))),
            jnp.pad(spread, ((0, 0), (0, 120)), constant_values=1.0),
        ],
    )
    return (field, probability)


def solution(mesh):
    placed = (
        P(None, "gx", "gy", "gz"),
        P(None, "gx", "gy", "gz"),
        P("gx", "gy", "gz"),
        P("gx", "gy", "gz"),
        P("gx", "gy", None),
        P(("gx", "gy", "gz")),
        P(("gx", "gy", "gz")),
        P(("gx", "gy", "gz")),
        P(),
        P(),
        P(),
        P(),
        P(),
    )
    return jax.shard_map(
        body,
        mesh=mesh,
        in_specs=placed,
        out_specs=(P(None, "gx", "gy", "gz"), P(None, ("gx", "gy", "gz"))),
        check_vma=False,
    )
```

```python
import functools

import jax
import jax.numpy as jnp
import numpy as np
from jax import lax
from jax.experimental import pallas as pl
from jax.experimental.pallas import tpu as pltpu
from jax.sharding import PartitionSpec as P

STEPS = 8
HALF = 4
DEEP = 2 * HALF
CLASSES = 8
MODES = 8
F32 = jnp.float32
VMEM_LIMIT = 24 * 1024 * 1024

XU, XP, XH = 8, 6, 7
YU, YP, YH = 24, 20, 20

FULL = 32000.0
BIAS = 200
UNIT_A = 2.0 / FULL
UNIT_E = 0.2 / 12.0 / FULL


PLANES = 4


def depth_weights():
    lanes = np.arange(256)
    result = np.zeros((3, 256, 256), np.float32)
    for k in range(3):
        at = lanes - 128 - 16 * k
        depth = np.where(lanes < 128, lanes, np.where(at < 8, at - 8, at + 120))
        used = (lanes < 128) | ((at >= 0) & (at < 16))
        apart = np.abs(depth[:, None] - depth[None, :])
        band = np.where(apart == 0, -90.0, np.where(apart == 1, 16.0, np.where(apart == 2, -1.0, 0.0)))
        result[k] = np.where(used[:, None] & used[None, :], band, 0.0)
        result[k, 0, 128 + 64 + 16 * k + 8] = 1.0
    return result


def lane_of():
    return lax.broadcasted_iota(jnp.int32, (8, 128), 1)


def pack_faces(values, lane):
    packed = pltpu.roll(values[0], 8, 1)
    for at in range(1, len(values)):
        packed = jnp.where(lane // 16 == at, pltpu.roll(values[at], (16 * at + 8) % 128, 1), packed)
    return packed


def start_kernel(u_in, p_in, c_in, d_in, u_ref, p_ref, a_ref, e_ref, face_ref, c_ref, d_ref, sems):
    copies = [pltpu.make_async_copy(c_in, c_ref, sems.at[0]), pltpu.make_async_copy(d_in, d_ref, sems.at[1])]
    for k in range(3):
        copies.append(pltpu.make_async_copy(u_in.at[k], u_ref.at[k], sems.at[2 + k]))
        copies.append(pltpu.make_async_copy(p_in.at[k], p_ref.at[k], sems.at[5 + k]))
    for copy in copies:
        copy.start()
    for copy in copies:
        copy.wait()
    lane = lane_of()

    def plane(x, carry):
        for row in (0, 8):
            rows = pl.ds(row, 8)
            share = 1.0 / (1.0 + d_ref[x, rows, :])
            values = [u_ref[k, x, rows, :] for k in range(3)] + [p_ref[k, x, rows, :] for k in range(3)]
            values += [2.0 * share, c_ref[x, rows, :] * share * (1.0 / 12.0)]
            a_ref[x, rows, :] = values[6]
            e_ref[x, rows, :] = values[7]
            face_ref[x, rows, :] = pack_faces(values, lane)
        return carry

    lax.fori_loop(0, 8, plane, 0)


def exponent_of(peak):
    peak = jnp.maximum(jnp.max(peak, axis=0, keepdims=True), 1e-30)
    return jnp.broadcast_to(jnp.ceil(jnp.log2(peak)), (8, 128))


def coded(values):
    return jnp.round(values).astype(jnp.int32).astype(jnp.int16)


def decoded(values):
    return values.astype(jnp.int32).astype(F32)


def twice(rows):
    return jnp.concatenate([rows, rows], axis=0)


def sent_exponents(message):
    both = decoded(message[message.shape[0] - 1]) - BIAS
    return both[0:8], both[8:16]


def x_message_kernel(coefficients, *refs):
    if coefficients:
        low_ref, high_ref, u_ref, p_ref, a_ref, e_ref, halo_ref, up_ref, down_ref, power_ref = refs
    else:
        low_ref, high_ref, u_ref, p_ref, halo_ref, up_ref, down_ref, power_ref = refs
    inner = lax.broadcasted_iota(jnp.int32, (16, 128), 1) % 16

    def largest(x, carry):
        field, face = carry
        for k in range(3):
            both = jnp.maximum(jnp.abs(u_ref[k, x]), jnp.abs(p_ref[k, x]))
            field = jnp.maximum(field, jnp.maximum(both[0:8], both[8:16]))
        halo = jnp.where(inner < 8, low_ref[x], high_ref[x])
        halo_ref[x] = halo
        halo = jnp.abs(halo)
        return field, jnp.maximum(face, jnp.maximum(halo[0:8], halo[8:16]))

    zero = jnp.zeros((8, 128), F32)
    field, face = lax.fori_loop(0, 8, largest, (zero, zero))
    powers = jnp.concatenate([exponent_of(field), exponent_of(face)], axis=0)
    power_ref[...] = powers
    up_ref[up_ref.shape[0] - 1] = coded(powers + BIAS)
    down_ref[down_ref.shape[0] - 1] = coded(powers + BIAS)
    scale = FULL * jnp.exp2(-powers)
    field, face = twice(scale[0:8]), twice(scale[8:16])

    def whole(x, carry):
        for k in range(3):
            code = coded(u_ref[k, x] * field)
            up_ref[XU * k + x] = code
            down_ref[XU * k + x] = code
        return carry

    def part(i, carry):
        parts = [(p_ref.at[k], field) for k in range(3)]
        if coefficients:
            parts += [(a_ref, 1.0 / UNIT_A), (e_ref, 1.0 / UNIT_E)]
        for at, (source, unit) in enumerate(parts):
            up_ref[3 * XU + XP * at + i] = coded(source[8 - XP + i] * unit)
            down_ref[3 * XU + XP * at + i] = coded(source[i] * unit)
        return carry

    at = 3 * XU + (5 if coefficients else 3) * XP

    def side(i, carry):
        up_ref[at + i] = coded(halo_ref[8 - XH + i] * face)
        down_ref[at + i] = coded(halo_ref[i] * face)
        return carry

    lax.fori_loop(0, 8, whole, 0)
    lax.fori_loop(0, XP, part, 0)
    lax.fori_loop(0, XH, side, 0)


def y_message_kernel(coefficients, *refs):
    if coefficients:
        u_ref, p_ref, a_ref, e_ref, halo_ref, power_ref, low_ref, high_ref, up_ref, down_ref = refs
    else:
        u_ref, p_ref, halo_ref, power_ref, low_ref, high_ref, up_ref, down_ref = refs
    powers = power_ref[...]
    low_powers = jnp.concatenate(sent_exponents(low_ref), axis=0)
    high_powers = jnp.concatenate(sent_exponents(high_ref), axis=0)
    most = jnp.maximum(powers, jnp.maximum(low_powers, high_powers))
    for out_ref in (up_ref, down_ref):
        out_ref[out_ref.shape[0] - 1] = coded(most + BIAS)
    own_scale = FULL * jnp.exp2(-most)
    low_scale = jnp.exp2(low_powers - most)
    high_scale = jnp.exp2(high_powers - most)
    field = [twice(scale[0:8]) for scale in (own_scale, low_scale, high_scale)]
    face = [twice(scale[8:16]) for scale in (own_scale, low_scale, high_scale)]

    def put(at, pair):
        up_ref[at] = coded(jnp.concatenate([pair[0][8:16], pair[1][8:16]], axis=0))
        down_ref[at] = coded(jnp.concatenate([pair[0][0:8], pair[1][0:8]], axis=0))

    def group(parts, x_planes, y_planes, x_at, y_at):
        side = (y_planes - 8) // 4

        def own(i, carry):
            for at, (source, units) in enumerate(parts):
                put(y_at + at * y_planes // 2 + side + i, [source[2 * i + j] * units[0] for j in (0, 1)])
            return carry

        def sides(i, carry):
            for at, (_, units) in enumerate(parts):
                start = x_at + at * x_planes
                first = start + x_planes - 2 * side + 2 * i
                put(y_at + at * y_planes // 2 + i, [decoded(low_ref[first + j]) * units[1] for j in (0, 1)])
                first = start + 2 * i
                pair = [decoded(high_ref[first + j]) * units[2] for j in (0, 1)]
                put(y_at + at * y_planes // 2 + side + 4 + i, pair)
            return carry

        lax.fori_loop(0, 4, own, 0)
        lax.fori_loop(0, side, sides, 0)
        return x_at + len(parts) * x_planes, y_at + len(parts) * y_planes // 2

    x_at, y_at = group([(u_ref.at[k], field) for k in range(3)], XU, YU, 0, 0)
    parts = [(p_ref.at[k], field) for k in range(3)]
    if coefficients:
        parts += [(a_ref, (1.0 / UNIT_A, 1.0, 1.0)), (e_ref, (1.0 / UNIT_E, 1.0, 1.0))]
    x_at, y_at = group(parts, XP, YP, x_at, y_at)
    group([(halo_ref, face)], XH, YH, x_at, y_at)


def fill(parts, x_low, x_high, y_low, y_high, x_at, x_planes, y_at, y_planes):
    count = len(parts)
    side = (y_planes - 8) // 2

    def own(i, carry):
        for target, row, block, _ in parts:
            target[8 + i, row + 8 : row + 24, :] = block[i]
        return carry

    def x_side(i, carry):
        for at, (target, row, _, units) in enumerate(parts):
            here = x_at + at * x_planes + i
            target[8 - x_planes + i, row + 8 : row + 24, :] = decoded(x_low[here]) * units[0]
            target[16 + i, row + 8 : row + 24, :] = decoded(x_high[here]) * units[1]
        return carry

    def y_side(i, carry):
        for at, (target, row, _, units) in enumerate(parts):
            here = y_at + at * y_planes // 2 + i
            low = decoded(y_low[here]) * units[2]
            high = decoded(y_high[here]) * units[3]
            for j in (0, 1):
                target[8 - side + 2 * i + j, row : row + 8, :] = low[8 * j : 8 * j + 8]
                target[8 - side + 2 * i + j, row + 24 : row + 32, :] = high[8 * j : 8 * j + 8]
        return carry

    lax.fori_loop(0, 8, own, 0, unroll=2)
    lax.fori_loop(0, x_planes, x_side, 0)
    lax.fori_loop(0, y_planes // 2, y_side, 0, unroll=2)
    return x_at + count * x_planes, y_at + count * y_planes // 2


def steps_kernel(first, *refs):
    if first:
        (u_in, p_in, a_in, e_in, halo_in, x_low, x_high, y_low, y_high, weight_in) = refs[:10]
        (u_out, p_out, face_out, seen_out, rate_ref) = refs[10:15]
        state_ref, edge_ref = refs[15:]
    else:
        (u_in, p_in, halo_in, x_low, x_high, y_low, y_high, weight_in, seen_in, rate_ref) = refs[:10]
        (cells_in, filter_in) = refs[10:12]
        (u_out, table_out) = refs[12:14]
        state_ref, edge_ref, seen_out = refs[14:]
    a_ref, e_ref, ha_ref, he_ref = (rate_ref.at[at] for at in range(4))
    lane = lane_of()
    inner = lane % 16

    sides = (x_low, x_high, y_low, y_high)
    powers = [sent_exponents(message) for message in sides]
    field = [twice(jnp.exp2(power[0]) * (1.0 / FULL)) for power in powers]
    face = [twice(jnp.exp2(power[1]) * (1.0 / FULL)) for power in powers]
    x_at, y_at = fill([(state_ref.at[0, k], 8, u_in.at[k], field) for k in range(3)], *sides, 0, XU, 0, YU)
    parts = [(state_ref.at[1, k], 8, p_in.at[k], field) for k in range(3)]
    if first:
        parts += [(a_ref, 0, a_in, (UNIT_A,) * 4), (e_ref, 0, e_in, (UNIT_E,) * 4)]
    x_at, y_at = fill(parts, *sides, x_at, XP, y_at, YP)
    fill([(state_ref.at[0, 3], 8, halo_in, face)], *sides, x_at, XH, y_at, YH)

    def prepare(x, carry):
        for tile in range(4):
            rows = pl.ds(8 + 8 * tile, 8)
            held = pl.ds(8 * tile, 8)
            halo = state_ref[0, 3, x, rows, :]
            state_ref[0, 3, x, rows, :] = jnp.where(lane < 48, halo, 0.0)
            state_ref[1, 3, x, rows, :] = jnp.where(lane < 48, pltpu.roll(halo, 128 - 48, 1), 0.0)
            if first:
                for target, at in ((ha_ref, 96), (he_ref, 112)):
                    spread = jnp.where(lane < 16, pltpu.roll(halo, 128 - at, 1), pltpu.roll(halo, 144 - at, 1))
                    spread = jnp.where(lane < 32, spread, pltpu.roll(halo, 160 - at, 1))
                    target[x, held, :] = jnp.where(lane < 48, spread, 0.0)
        return carry

    lax.fori_loop(2, 22, prepare, 0, unroll=4)

    def split(v):
        high = v.astype(jnp.bfloat16)
        return high, (v - high.astype(F32)).astype(jnp.bfloat16)

    def advance(src, dst, x):
        rows = pl.ds(8, 32)
        fields = [[src[k, 2 + j, rows, :] for j in range(PLANES)] for k in range(4)]
        parts = [[split(v) for v in field] for field in fields]
        depth = []
        for k in range(3):
            pieces = [jnp.concatenate([parts[k][j][part], parts[3][j][part]], axis=1) for part in (0, 1) for j in range(PLANES)]
            both = jnp.dot(jnp.concatenate(pieces, axis=0), weight_in[k], preferred_element_type=F32)
            depth.append(both[0 : 32 * PLANES] + both[32 * PLANES :])
        side = depth[0][:, 128:] + depth[1][:, 128:] + depth[2][:, 128:]
        fresh = []
        for j in range(PLANES):
            for k in range(4):
                v = fields[k][j]
                near = (src[k, 1 + j, rows, :] + src[k, 3 + j, rows, :]) + (
                    src[k, 2 + j, pl.ds(7, 32), :] + src[k, 2 + j, pl.ds(9, 32), :]
                )
                far = (src[k, j, rows, :] + src[k, 4 + j, rows, :]) + (
                    src[k, 2 + j, pl.ds(6, 32), :] + src[k, 2 + j, pl.ds(10, 32), :]
                )
                along = side if k == 3 else depth[k][:, :128]
                laplace = along[32 * j : 32 * j + 32] + (16.0 * near - far)
                old = dst[k, x + j, rows, :]
                a_each, e_each = (ha_ref, he_ref) if k == 3 else (a_ref, e_ref)
                fresh.append((k, j, old + a_each[x + j] * (v - old) + e_each[x + j] * laplace))
        return fresh, side

    def one_step(step, carry):
        dst = state_ref.at[(step + 1) % 2]

        def planes(at, inside):
            x = 2 * step + 2 + PLANES * at
            fresh, side = advance(state_ref.at[step % 2, :, pl.ds(x - 2, 4 + PLANES)], dst, x)
            for k, j, value in fresh:
                dst[k, x + j, 8:40, :] = value
            for j in range(PLANES):
                edge_ref[step, x + j, :, :] = side[32 * j + 8 : 32 * j + 24]
            return inside

        lax.fori_loop(0, (20 - 4 * step) // PLANES, planes, 0)
        return carry

    lax.fori_loop(0, HALF, one_step, 0)

    begin = 0 if first else HALF
    block = pl.ds(16, 16)

    def finish(x, carry):
        for k in range(3):
            u_out[k, x, :, :] = state_ref[0, k, 8 + x, block, :]
            if first:
                p_out[k, x, :, :] = state_ref[1, k, 8 + x, block, :]
        for row in (0, 8):
            rows = pl.ds(row, 8)
            last = pack_faces([state_ref[0, k, 8 + x, pl.ds(16 + row, 8), :] for k in range(3)], lane)
            if first:
                after = pack_faces([state_ref[1, k, 8 + x, pl.ds(16 + row, 8), :] for k in range(3)], lane)
                face_out[x, rows, :] = jnp.where(lane < 48, last, pltpu.roll(after, 48, 1))
                seen = jnp.zeros((8, 128), F32)
            else:
                seen = seen_in[x, rows, :]
            for step in range(HALF):
                edge = pltpu.roll(last, 64, 1) if step == HALF - 1 else edge_ref[step + 1, 8 + x, rows, :]
                at = begin + step
                seen = jnp.where((inner == 8 + at) & (lane >= 64) & (lane < 112), pltpu.roll(edge, at, 1), seen)
            seen_out[x, rows, :] = seen
        return carry

    lax.fori_loop(0, 8, finish, 0, unroll=4)

    if not first:
        motion = seen_out[...].reshape(128, 128).astype(jnp.bfloat16)
        modal = lax.dot_general(filter_in[...], motion, (((1,), (1,)), ((), ())), preferred_element_type=F32)
        energies = []
        for kind in range(CLASSES):
            part = modal[MODES * kind : MODES * (kind + 1), :]
            energies.append(jnp.sum(part * part, axis=0, keepdims=True))
        demand = 0.5 * jnp.log1p(jnp.concatenate(energies, axis=0))
        for owner in range(table_out.shape[0]):
            cells = jnp.broadcast_to(cells_in[owner : owner + 1, :], (CLASSES, 128))
            chosen = jnp.take_along_axis(demand, cells, axis=1)
            for level in range(table_out.shape[1]):
                table_out[owner, level] = chosen


def fragility_kernel(table_ref, slot_ref, kind_ref, city_ref, amplify_ref, median_ref, spread_ref, out_ref):
    sources = table_ref.shape[0]
    slot, kind, city = slot_ref[...], kind_ref[...], city_ref[...]
    column = slot % 128
    key = (slot // 128) * CLASSES + kind
    demand = jnp.zeros((8, 128), F32)
    for source in range(sources):
        for each in range(CLASSES):
            row = jnp.broadcast_to(table_ref[source, each : each + 1, :], (8, 128))
            found = jnp.take_along_axis(row, column, axis=1)
            demand = jnp.where(key == source * CLASSES + each, found, demand)
    gain = jnp.log(jnp.broadcast_to(amplify_ref[...], (8, 128)))
    demand = demand + jnp.take_along_axis(gain, city, axis=1)
    for group in range(8):
        level = jnp.broadcast_to(demand[group : group + 1, :], (8, 128))
        index = jnp.broadcast_to(kind[group : group + 1, :], (8, 128))
        for half in (0, 8):
            middle = jnp.take_along_axis(median_ref[half : half + 8, :], index, axis=1)
            width = jnp.take_along_axis(spread_ref[half : half + 8, :], index, axis=1)
            out_ref[half : half + 8, 128 * group : 128 * group + 128] = jax.nn.sigmoid((level - middle) / width)


VM = pl.BlockSpec(memory_space=pltpu.VMEM)


def call(kernel, name, shapes, args, specs=None, scratch=()):
    out = [s if isinstance(s, jax.ShapeDtypeStruct) else jax.ShapeDtypeStruct(s, F32) for s in shapes]
    return pl.pallas_call(
        kernel,
        out_shape=out,
        in_specs=specs or [VM] * len(args),
        out_specs=[VM] * len(out),
        scratch_shapes=list(scratch),
        compiler_params=pltpu.CompilerParams(vmem_limit_bytes=VMEM_LIMIT),
        name=name,
    )(*args)


def both_ways(to_up, to_down, axis):
    count = lax.axis_size(axis)
    forward = [(i, i + 1) for i in range(count - 1)]
    backward = [(i + 1, i) for i in range(count - 1)]
    return lax.ppermute(to_up, axis, forward), lax.ppermute(to_down, axis, backward)


def exchange(u, p, faces, coefficients):
    extra = list(coefficients)
    has = bool(extra)
    z_low, z_high = both_ways(faces, faces, "gz")
    planes = 3 * XU + (3 + len(extra)) * XP + XH + 1
    message = jax.ShapeDtypeStruct((planes, 16, 128), jnp.int16)
    halo, up, down, powers = call(
        functools.partial(x_message_kernel, has),
        "x_message",
        [(8, 16, 128), message, message, (16, 128)],
        [z_low, z_high, u, p] + extra,
    )
    x_low, x_high = both_ways(up, down, "gx")
    planes = (3 * YU + (3 + len(extra)) * YP + YH) // 2 + 1
    message = jax.ShapeDtypeStruct((planes, 16, 128), jnp.int16)
    up, down = call(
        functools.partial(y_message_kernel, has),
        "y_message",
        [message, message],
        [u, p] + extra + [halo, powers, x_low, x_high],
    )
    y_low, y_high = both_ways(up, down, "gy")
    return halo, x_low, x_high, y_low, y_high


def body(
    displacement,
    previous,
    courant,
    damping,
    send_cells,
    building_slot,
    building_class,
    city,
    mode_count,
    modal_filter,
    amplify,
    median,
    spread,
):
    own = (3, 8, 16, 128)
    plane = (8, 16, 128)
    wide = [pltpu.VMEM((2, 4, 24, 48, 128), F32), pltpu.VMEM((HALF, 24, 16, 128), F32)]

    u, p, a, e, faces = call(
        start_kernel,
        "start",
        [own, own, plane, plane, plane],
        [displacement, previous, courant, damping],
        specs=[pl.BlockSpec(memory_space=pltpu.HBM)] * 4,
        scratch=[pltpu.VMEM(plane, F32)] * 2 + [pltpu.SemaphoreType.DMA((8,))],
    )
    received = exchange(u, p, faces, (a, e))
    weights = jnp.asarray(depth_weights(), jnp.bfloat16)
    u, p, faces, seen, rates = call(
        functools.partial(steps_kernel, True),
        "steps_first",
        [own, own, plane, plane, (4, 24, 32, 128)],
        [u, p, a, e, *received, weights],
        scratch=wide,
    )
    received = exchange(u, p, faces, ())
    owners, levels = lax.axis_size("gx"), lax.axis_size("gz")
    used = jnp.arange(MODES)[None, :] < mode_count[:, None]
    filters = jnp.where(used.reshape(CLASSES * MODES, 1), modal_filter, 0).astype(modal_filter.dtype)
    filters = jnp.swapaxes(filters.reshape(CLASSES * MODES, STEPS, 3), 1, 2)
    filters = jnp.pad(filters, ((0, 0), (4, 1), (16 - STEPS, 0))).reshape(CLASSES * MODES, 128)
    args = [u, p, *received, weights, seen, rates, send_cells.reshape(owners, 128), filters]
    field, table = call(
        functools.partial(steps_kernel, False),
        "steps_second",
        [own, (owners, levels, CLASSES, 128)],
        args,
        scratch=wide + [pltpu.VMEM(plane, F32)],
    )
    table = table.reshape(owners * levels, CLASSES, 128)
    table = lax.all_to_all(table, ("gx", "gz"), split_axis=0, concat_axis=0, tiled=True)
    table = table.reshape(owners, levels, CLASSES, 128)[:, 0]
    (probability,) = call(
        fragility_kernel,
        "fragility",
        [(16, 1024)],
        [
            table,
            building_slot.reshape(8, 128),
            building_class.reshape(8, 128),
            city.reshape(8, 128),
            jnp.pad(amplify, (0, 112), constant_values=1.0).reshape(1, 128),
            jnp.pad(median, ((0, 0), (0, 120))),
            jnp.pad(spread, ((0, 0), (0, 120)), constant_values=1.0),
        ],
    )
    return (field, probability)


def solution(mesh):
    placed = (
        P(None, "gx", "gy", "gz"),
        P(None, "gx", "gy", "gz"),
        P("gx", "gy", "gz"),
        P("gx", "gy", "gz"),
        P("gx", "gy", None),
        P(("gx", "gy", "gz")),
        P(("gx", "gy", "gz")),
        P(("gx", "gy", "gz")),
        P(),
        P(),
        P(),
        P(),
        P(),
    )
    return jax.shard_map(
        body,
        mesh=mesh,
        in_specs=placed,
        out_specs=(P(None, "gx", "gy", "gz"), P(None, ("gx", "gy", "gz"))),
        check_vma=False,
    )
```

```python
import functools

import jax
import jax.numpy as jnp
import numpy as np
from jax import lax
from jax.experimental import pallas as pl
from jax.experimental.pallas import tpu as pltpu
from jax.sharding import PartitionSpec as P

STEPS = 8
HALF = 4
DEEP = 2 * HALF
CLASSES = 8
MODES = 8
CITIES = 16
F32 = jnp.float32
VMEM_LIMIT = 24 * 1024 * 1024

XU, XP, XH = 8, 6, 7
YU, YP, YH = 24, 20, 20

FULL = 32000.0
BIAS = 200
UNIT_A = 2.0 / FULL
UNIT_E = 0.2 / 12.0 / FULL


PLANES = 4


def depth_weights():
    lanes = np.arange(256)
    result = np.zeros((3, 256, 256), np.float32)
    for k in range(3):
        at = lanes - 128 - 16 * k
        depth = np.where(lanes < 128, lanes, np.where(at < 8, at - 8, at + 120))
        used = (lanes < 128) | ((at >= 0) & (at < 16))
        apart = np.abs(depth[:, None] - depth[None, :])
        band = np.where(apart == 0, -90.0, np.where(apart == 1, 16.0, np.where(apart == 2, -1.0, 0.0)))
        result[k] = np.where(used[:, None] & used[None, :], band, 0.0)
        result[k, 0, 128 + 64 + 16 * k + 8] = 1.0
    return result


def lane_of():
    return lax.broadcasted_iota(jnp.int32, (8, 128), 1)


def pack_faces(values, lane):
    packed = pltpu.roll(values[0], 8, 1)
    for at in range(1, len(values)):
        packed = jnp.where(lane // 16 == at, pltpu.roll(values[at], (16 * at + 8) % 128, 1), packed)
    return packed


def start_kernel(u_in, p_in, c_in, d_in, u_ref, p_ref, a_ref, e_ref, face_ref, c_ref, d_ref, sems):
    copies = [pltpu.make_async_copy(c_in, c_ref, sems.at[0]), pltpu.make_async_copy(d_in, d_ref, sems.at[1])]
    for k in range(3):
        copies.append(pltpu.make_async_copy(u_in.at[k], u_ref.at[k], sems.at[2 + k]))
        copies.append(pltpu.make_async_copy(p_in.at[k], p_ref.at[k], sems.at[5 + k]))
    for copy in copies:
        copy.start()
    for copy in copies:
        copy.wait()
    lane = lane_of()

    def plane(x, carry):
        for row in (0, 8):
            rows = pl.ds(row, 8)
            share = 1.0 / (1.0 + d_ref[x, rows, :])
            values = [u_ref[k, x, rows, :] for k in range(3)] + [p_ref[k, x, rows, :] for k in range(3)]
            values += [2.0 * share, c_ref[x, rows, :] * share * (1.0 / 12.0)]
            a_ref[x, rows, :] = values[6]
            e_ref[x, rows, :] = values[7]
            face_ref[x, rows, :] = pack_faces(values, lane)
        return carry

    lax.fori_loop(0, 8, plane, 0)


def exponent_of(peak):
    peak = jnp.maximum(jnp.max(peak, axis=0, keepdims=True), 1e-30)
    return jnp.broadcast_to(jnp.ceil(jnp.log2(peak)), (8, 128))


def coded(values):
    return jnp.round(values).astype(jnp.int32).astype(jnp.int16)


def decoded(values):
    return values.astype(jnp.int32).astype(F32)


def twice(rows):
    return jnp.concatenate([rows, rows], axis=0)


def sent_exponents(message):
    both = decoded(message[message.shape[0] - 1]) - BIAS
    return both[0:8], both[8:16]


def x_message_kernel(coefficients, *refs):
    if coefficients:
        z_low_ref, z_high_ref, u_ref, p_ref, a_ref, e_ref, halo_ref, up_ref, down_ref, power_ref = refs
    else:
        z_low_ref, z_high_ref, u_ref, p_ref, halo_ref, up_ref, down_ref, power_ref = refs
    inner = lax.broadcasted_iota(jnp.int32, (16, 128), 1) % 16

    def largest(x, carry):
        field, face = carry
        for k in range(3):
            both = jnp.maximum(jnp.abs(u_ref[k, x]), jnp.abs(p_ref[k, x]))
            field = jnp.maximum(field, jnp.maximum(both[0:8], both[8:16]))
        halo = jnp.where(inner < 8, z_low_ref[x], z_high_ref[x])
        halo_ref[x] = halo
        halo = jnp.abs(halo)
        return field, jnp.maximum(face, jnp.maximum(halo[0:8], halo[8:16]))

    zero = jnp.zeros((8, 128), F32)
    field, face = lax.fori_loop(0, 8, largest, (zero, zero))
    powers = jnp.concatenate([exponent_of(field), exponent_of(face)], axis=0)
    power_ref[...] = powers
    up_ref[up_ref.shape[0] - 1] = coded(powers + BIAS)
    down_ref[down_ref.shape[0] - 1] = coded(powers + BIAS)
    scale = FULL * jnp.exp2(-powers)
    field, face = twice(scale[0:8]), twice(scale[8:16])

    def whole(x, carry):
        for k in range(3):
            code = coded(u_ref[k, x] * field)
            up_ref[XU * k + x] = code
            down_ref[XU * k + x] = code
        return carry

    def part(i, carry):
        parts = [(p_ref.at[k], field) for k in range(3)]
        if coefficients:
            parts += [(a_ref, 1.0 / UNIT_A), (e_ref, 1.0 / UNIT_E)]
        for at, (source, unit) in enumerate(parts):
            up_ref[3 * XU + XP * at + i] = coded(source[8 - XP + i] * unit)
            down_ref[3 * XU + XP * at + i] = coded(source[i] * unit)
        return carry

    at = 3 * XU + (5 if coefficients else 3) * XP

    def side(i, carry):
        up_ref[at + i] = coded(halo_ref[8 - XH + i] * face)
        down_ref[at + i] = coded(halo_ref[i] * face)
        return carry

    lax.fori_loop(0, 8, whole, 0)
    lax.fori_loop(0, XP, part, 0)
    lax.fori_loop(0, XH, side, 0)


def y_message_kernel(coefficients, *refs):
    if coefficients:
        u_ref, p_ref, a_ref, e_ref, halo_ref, power_ref, low_ref, high_ref, up_ref, down_ref = refs
    else:
        u_ref, p_ref, halo_ref, power_ref, low_ref, high_ref, up_ref, down_ref = refs
    powers = power_ref[...]
    low_powers = jnp.concatenate(sent_exponents(low_ref), axis=0)
    high_powers = jnp.concatenate(sent_exponents(high_ref), axis=0)
    most = jnp.maximum(powers, jnp.maximum(low_powers, high_powers))
    for out_ref in (up_ref, down_ref):
        out_ref[out_ref.shape[0] - 1] = coded(most + BIAS)
    own_scale = FULL * jnp.exp2(-most)
    low_scale = jnp.exp2(low_powers - most)
    high_scale = jnp.exp2(high_powers - most)
    field = [twice(scale[0:8]) for scale in (own_scale, low_scale, high_scale)]
    face = [twice(scale[8:16]) for scale in (own_scale, low_scale, high_scale)]

    def put(at, pair):
        up_ref[at] = coded(jnp.concatenate([pair[0][8:16], pair[1][8:16]], axis=0))
        down_ref[at] = coded(jnp.concatenate([pair[0][0:8], pair[1][0:8]], axis=0))

    def group(parts, x_planes, y_planes, x_at, y_at):
        side = (y_planes - 8) // 4

        def own(i, carry):
            for at, (source, units) in enumerate(parts):
                put(y_at + at * y_planes // 2 + side + i, [source[2 * i + j] * units[0] for j in (0, 1)])
            return carry

        def sides(i, carry):
            for at, (_, units) in enumerate(parts):
                start = x_at + at * x_planes
                first = start + x_planes - 2 * side + 2 * i
                put(y_at + at * y_planes // 2 + i, [decoded(low_ref[first + j]) * units[1] for j in (0, 1)])
                first = start + 2 * i
                pair = [decoded(high_ref[first + j]) * units[2] for j in (0, 1)]
                put(y_at + at * y_planes // 2 + side + 4 + i, pair)
            return carry

        lax.fori_loop(0, 4, own, 0)
        lax.fori_loop(0, side, sides, 0)
        return x_at + len(parts) * x_planes, y_at + len(parts) * y_planes // 2

    x_at, y_at = group([(u_ref.at[k], field) for k in range(3)], XU, YU, 0, 0)
    parts = [(p_ref.at[k], field) for k in range(3)]
    if coefficients:
        parts += [(a_ref, (1.0 / UNIT_A, 1.0, 1.0)), (e_ref, (1.0 / UNIT_E, 1.0, 1.0))]
    x_at, y_at = group(parts, XP, YP, x_at, y_at)
    group([(halo_ref, face)], XH, YH, x_at, y_at)


def fill(parts, x_low, x_high, y_low, y_high, x_at, x_planes, y_at, y_planes):
    count = len(parts)
    side = (y_planes - 8) // 2

    def own(i, carry):
        for target, row, block, _ in parts:
            target[8 + i, row + 8 : row + 24, :] = block[i]
        return carry

    def x_side(i, carry):
        for at, (target, row, _, units) in enumerate(parts):
            here = x_at + at * x_planes + i
            target[8 - x_planes + i, row + 8 : row + 24, :] = decoded(x_low[here]) * units[0]
            target[16 + i, row + 8 : row + 24, :] = decoded(x_high[here]) * units[1]
        return carry

    def y_side(i, carry):
        for at, (target, row, _, units) in enumerate(parts):
            here = y_at + at * y_planes // 2 + i
            low = decoded(y_low[here]) * units[2]
            high = decoded(y_high[here]) * units[3]
            for j in (0, 1):
                target[8 - side + 2 * i + j, row : row + 8, :] = low[8 * j : 8 * j + 8]
                target[8 - side + 2 * i + j, row + 24 : row + 32, :] = high[8 * j : 8 * j + 8]
        return carry

    lax.fori_loop(0, 8, own, 0, unroll=2)
    lax.fori_loop(0, x_planes, x_side, 0)
    lax.fori_loop(0, y_planes // 2, y_side, 0, unroll=2)
    return x_at + count * x_planes, y_at + count * y_planes // 2


def steps_kernel(first, *refs):
    if first:
        (u_in, p_in, a_in, e_in, halo_in, x_low, x_high, y_low, y_high, weight_in) = refs[:10]
        (u_out, p_out, face_out, seen_out, rate_ref) = refs[10:15]
        state_ref, edge_ref = refs[15:]
    else:
        (u_in, p_in, halo_in, x_low, x_high, y_low, y_high, weight_in, seen_in, rate_ref) = refs[:10]
        (cells_in, filter_in, count_in) = refs[10:13]
        (u_out, table_out) = refs[13:15]
        state_ref, edge_ref, seen_out, filter_ref, count_ref = refs[15:]
    a_ref, e_ref, ha_ref, he_ref = (rate_ref.at[at] for at in range(4))
    lane = lane_of()
    inner = lane % 16

    sides = (x_low, x_high, y_low, y_high)
    powers = [sent_exponents(message) for message in sides]
    field = [twice(jnp.exp2(power[0]) * (1.0 / FULL)) for power in powers]
    face = [twice(jnp.exp2(power[1]) * (1.0 / FULL)) for power in powers]
    x_at, y_at = fill([(state_ref.at[0, k], 8, u_in.at[k], field) for k in range(3)], *sides, 0, XU, 0, YU)
    parts = [(state_ref.at[1, k], 8, p_in.at[k], field) for k in range(3)]
    if first:
        parts += [(a_ref, 0, a_in, (UNIT_A,) * 4), (e_ref, 0, e_in, (UNIT_E,) * 4)]
    x_at, y_at = fill(parts, *sides, x_at, XP, y_at, YP)
    fill([(state_ref.at[0, 3], 8, halo_in, face)], *sides, x_at, XH, y_at, YH)

    def prepare(x, carry):
        for tile in range(4):
            rows = pl.ds(8 + 8 * tile, 8)
            held = pl.ds(8 * tile, 8)
            halo = state_ref[0, 3, x, rows, :]
            state_ref[0, 3, x, rows, :] = jnp.where(lane < 48, halo, 0.0)
            state_ref[1, 3, x, rows, :] = jnp.where(lane < 48, pltpu.roll(halo, 128 - 48, 1), 0.0)
            if first:
                for target, at in ((ha_ref, 96), (he_ref, 112)):
                    spread = jnp.where(lane < 16, pltpu.roll(halo, 128 - at, 1), pltpu.roll(halo, 144 - at, 1))
                    spread = jnp.where(lane < 32, spread, pltpu.roll(halo, 160 - at, 1))
                    target[x, held, :] = jnp.where(lane < 48, spread, 0.0)
        return carry

    lax.fori_loop(2, 22, prepare, 0, unroll=4)

    def split(v):
        high = v.astype(jnp.bfloat16)
        return high, (v - high.astype(F32)).astype(jnp.bfloat16)

    def advance(src, dst, x):
        rows = pl.ds(8, 32)
        fields = [[src[k, 2 + j, rows, :] for j in range(PLANES)] for k in range(4)]
        parts = [[split(v) for v in field] for field in fields]
        depth = []
        for k in range(3):
            pieces = [jnp.concatenate([parts[k][j][part], parts[3][j][part]], axis=1) for part in (0, 1) for j in range(PLANES)]
            both = jnp.dot(jnp.concatenate(pieces, axis=0), weight_in[k], preferred_element_type=F32)
            depth.append(both[0 : 32 * PLANES] + both[32 * PLANES :])
        side = depth[0][:, 128:] + depth[1][:, 128:] + depth[2][:, 128:]
        fresh = []
        for j in range(PLANES):
            for k in range(4):
                v = fields[k][j]
                near = (src[k, 1 + j, rows, :] + src[k, 3 + j, rows, :]) + (
                    src[k, 2 + j, pl.ds(7, 32), :] + src[k, 2 + j, pl.ds(9, 32), :]
                )
                far = (src[k, j, rows, :] + src[k, 4 + j, rows, :]) + (
                    src[k, 2 + j, pl.ds(6, 32), :] + src[k, 2 + j, pl.ds(10, 32), :]
                )
                along = side if k == 3 else depth[k][:, :128]
                laplace = along[32 * j : 32 * j + 32] + (16.0 * near - far)
                old = dst[k, x + j, rows, :]
                a_each, e_each = (ha_ref, he_ref) if k == 3 else (a_ref, e_ref)
                fresh.append((k, j, old + a_each[x + j] * (v - old) + e_each[x + j] * laplace))
        return fresh, side

    def one_step(step, carry):
        dst = state_ref.at[(step + 1) % 2]

        def planes(at, inside):
            x = 2 * step + 2 + PLANES * at
            fresh, side = advance(state_ref.at[step % 2, :, pl.ds(x - 2, 4 + PLANES)], dst, x)
            for k, j, value in fresh:
                dst[k, x + j, 8:40, :] = value
            for j in range(PLANES):
                edge_ref[step, x + j, :, :] = side[32 * j + 8 : 32 * j + 24]
            return inside

        lax.fori_loop(0, (20 - 4 * step) // PLANES, planes, 0)
        return carry

    lax.fori_loop(0, HALF, one_step, 0)

    begin = 0 if first else HALF
    block = pl.ds(16, 16)

    def finish(x, carry):
        for k in range(3):
            u_out[k, x, :, :] = state_ref[0, k, 8 + x, block, :]
            if first:
                p_out[k, x, :, :] = state_ref[1, k, 8 + x, block, :]
        for row in (0, 8):
            rows = pl.ds(row, 8)
            last = pack_faces([state_ref[0, k, 8 + x, pl.ds(16 + row, 8), :] for k in range(3)], lane)
            if first:
                after = pack_faces([state_ref[1, k, 8 + x, pl.ds(16 + row, 8), :] for k in range(3)], lane)
                face_out[x, rows, :] = jnp.where(lane < 48, last, pltpu.roll(after, 48, 1))
                seen = jnp.zeros((8, 128), F32)
            else:
                seen = seen_in[x, rows, :]
            for step in range(HALF):
                edge = pltpu.roll(last, 64, 1) if step == HALF - 1 else edge_ref[step + 1, 8 + x, rows, :]
                at = begin + step
                seen = jnp.where((inner == 8 + at) & (lane >= 64) & (lane < 112), pltpu.roll(edge, at, 1), seen)
            seen_out[x, rows, :] = seen
        return carry

    lax.fori_loop(0, 8, finish, 0, unroll=4)

    if not first:
        filter_ref[...] = filter_in[...].astype(F32)
        blank = jnp.zeros((8, CLASSES * MODES), F32)
        blocks = [blank] * 16
        for k in range(3):
            blocks[9 + 2 * k] = filter_ref[pl.ds(k, STEPS, stride=3), :]
        filters = jnp.concatenate(blocks, axis=0).astype(jnp.bfloat16)
        motion = seen_out[...].reshape(128, 128).astype(jnp.bfloat16)
        modal = lax.dot_general(filters, motion, (((0,), (1,)), ((), ())), preferred_element_type=F32)
        modes = lax.broadcasted_iota(jnp.int32, (MODES, 128), 0)
        count_ref[...] = jnp.zeros((8, 128), jnp.int32)
        count_ref[0:1, 0:CLASSES] = count_in[...]
        counts = jnp.where(modes == lane, jnp.broadcast_to(count_ref[0:1, :], (8, 128)), 0)
        counts = jnp.sum(counts, axis=1, keepdims=True)
        energies = []
        for kind in range(CLASSES):
            part = modal[MODES * kind : MODES * (kind + 1), :]
            part = jnp.where(modes < counts[kind : kind + 1, :], part * part, 0.0)
            energies.append(jnp.sum(part, axis=0, keepdims=True))
        demand = 0.5 * jnp.log1p(jnp.concatenate(energies, axis=0))
        for owner in range(table_out.shape[0]):
            cells = jnp.broadcast_to(cells_in[owner : owner + 1, :], (CLASSES, 128))
            chosen = jnp.take_along_axis(demand, cells, axis=1)
            for level in range(table_out.shape[1]):
                table_out[owner, level] = chosen


def fragility_kernel(
    table_ref, slot_ref, kind_ref, city_ref, amplify_ref, median_ref, spread_ref, out_ref, gain_ref, tables_ref
):
    sources = table_ref.shape[0]
    slot, kind, city = slot_ref[...], kind_ref[...], city_ref[...]
    column = slot % 128
    key = (slot // 128) * CLASSES + kind
    demand = jnp.zeros((8, 128), F32)
    for source in range(sources):
        for each in range(CLASSES):
            row = jnp.broadcast_to(table_ref[source, 0, each : each + 1, :], (8, 128))
            found = jnp.take_along_axis(row, column, axis=1)
            demand = jnp.where(key == source * CLASSES + each, found, demand)
    gain_ref[...] = jnp.ones((8, 128), F32)
    gain_ref[0:1, 0:CITIES] = amplify_ref[...]
    gain = jnp.log(jnp.broadcast_to(gain_ref[0:1, :], (8, 128)))
    demand = demand + jnp.take_along_axis(gain, city, axis=1)
    tables_ref[...] = jnp.ones((128, 128), F32)
    batches = median_ref.shape[1]
    tables_ref[0:CLASSES, 0:batches] = median_ref[...]
    medians = tables_ref[...].T
    tables_ref[0:CLASSES, 0:batches] = spread_ref[...]
    spreads = tables_ref[...].T
    for group in range(8):
        level = jnp.broadcast_to(demand[group : group + 1, :], (8, 128))
        index = jnp.broadcast_to(kind[group : group + 1, :], (8, 128))
        for half in range(0, batches, 8):
            middle = jnp.take_along_axis(medians[half : half + 8, :], index, axis=1)
            width = jnp.take_along_axis(spreads[half : half + 8, :], index, axis=1)
            out_ref[half : half + 8, 128 * group : 128 * group + 128] = jax.nn.sigmoid((level - middle) / width)


VM = pl.BlockSpec(memory_space=pltpu.VMEM)


def call(kernel, name, shapes, args, specs=None, scratch=()):
    out = [s if isinstance(s, jax.ShapeDtypeStruct) else jax.ShapeDtypeStruct(s, F32) for s in shapes]
    return pl.pallas_call(
        kernel,
        out_shape=out,
        in_specs=specs or [VM] * len(args),
        out_specs=[VM] * len(out),
        scratch_shapes=list(scratch),
        compiler_params=pltpu.CompilerParams(vmem_limit_bytes=VMEM_LIMIT),
        name=name,
    )(*args)


def both_ways(to_up, to_down, axis):
    count = lax.axis_size(axis)
    forward = [(i, i + 1) for i in range(count - 1)]
    backward = [(i + 1, i) for i in range(count - 1)]
    return lax.ppermute(to_up, axis, forward), lax.ppermute(to_down, axis, backward)


def exchange(u, p, faces, coefficients):
    extra = list(coefficients)
    has = bool(extra)
    z_low, z_high = both_ways(faces, faces, "gz")
    planes = 3 * XU + (3 + len(extra)) * XP + XH + 1
    message = jax.ShapeDtypeStruct((planes, 16, 128), jnp.int16)
    halo, up, down, powers = call(
        functools.partial(x_message_kernel, has),
        "x_message",
        [(8, 16, 128), message, message, (16, 128)],
        [z_low, z_high, u, p] + extra,
    )
    x_low, x_high = both_ways(up, down, "gx")
    planes = (3 * YU + (3 + len(extra)) * YP + YH) // 2 + 1
    message = jax.ShapeDtypeStruct((planes, 16, 128), jnp.int16)
    up, down = call(
        functools.partial(y_message_kernel, has),
        "y_message",
        [message, message],
        [u, p] + extra + [halo, powers, x_low, x_high],
    )
    y_low, y_high = both_ways(up, down, "gy")
    return halo, x_low, x_high, y_low, y_high


def body(
    displacement,
    previous,
    courant,
    damping,
    send_cells,
    building_slot,
    building_class,
    city,
    mode_count,
    modal_filter,
    amplify,
    median,
    spread,
):
    own = (3, 8, 16, 128)
    plane = (8, 16, 128)
    wide = [pltpu.VMEM((2, 4, 24, 48, 128), F32), pltpu.VMEM((HALF, 24, 16, 128), F32)]

    u, p, a, e, faces = call(
        start_kernel,
        "start",
        [own, own, plane, plane, plane],
        [displacement, previous, courant, damping],
        specs=[pl.BlockSpec(memory_space=pltpu.HBM)] * 4,
        scratch=[pltpu.VMEM(plane, F32)] * 2 + [pltpu.SemaphoreType.DMA((8,))],
    )
    received = exchange(u, p, faces, (a, e))
    weights = jnp.asarray(depth_weights(), jnp.bfloat16)
    u, p, faces, seen, rates = call(
        functools.partial(steps_kernel, True),
        "steps_first",
        [own, own, plane, plane, (4, 24, 32, 128)],
        [u, p, a, e, *received, weights],
        scratch=wide,
    )
    received = exchange(u, p, faces, ())
    owners, levels = lax.axis_size("gx"), lax.axis_size("gz")
    args = [u, p, *received, weights, seen, rates, send_cells.reshape(owners, 128), modal_filter.T, mode_count.reshape(1, CLASSES)]
    field, table = call(
        functools.partial(steps_kernel, False),
        "steps_second",
        [own, (owners, levels, CLASSES, 128)],
        args,
        scratch=wide
        + [pltpu.VMEM(plane, F32), pltpu.VMEM((3 * STEPS, CLASSES * MODES), F32), pltpu.VMEM((8, 128), jnp.int32)],
    )
    table = table.reshape(owners * levels, CLASSES, 128)
    table = lax.all_to_all(table, ("gx", "gz"), split_axis=0, concat_axis=0, tiled=True)
    (probability,) = call(
        fragility_kernel,
        "fragility",
        [(16, 1024)],
        [
            table.reshape(owners, levels, CLASSES, 128),
            building_slot.reshape(8, 128),
            building_class.reshape(8, 128),
            city.reshape(8, 128),
            amplify.reshape(1, CITIES),
            median.T,
            spread.T,
        ],
        scratch=[pltpu.VMEM((8, 128), F32), pltpu.VMEM((128, 128), F32)],
    )
    return (field, probability)


def solution(mesh):
    placed = (
        P(None, "gx", "gy", "gz"),
        P(None, "gx", "gy", "gz"),
        P("gx", "gy", "gz"),
        P("gx", "gy", "gz"),
        P("gx", "gy", None),
        P(("gx", "gy", "gz")),
        P(("gx", "gy", "gz")),
        P(("gx", "gy", "gz")),
        P(),
        P(),
        P(),
        P(),
        P(),
    )
    return jax.shard_map(
        body,
        mesh=mesh,
        in_specs=placed,
        out_specs=(P(None, "gx", "gy", "gz"), P(None, ("gx", "gy", "gz"))),
        check_vma=False,
    )
```

```python
import functools

import jax
import jax.numpy as jnp
import numpy as np
from jax import lax
from jax.experimental import pallas as pl
from jax.experimental.pallas import tpu as pltpu
from jax.sharding import PartitionSpec as P

STEPS = 8
HALF = 4
DEEP = 2 * HALF
CLASSES = 8
MODES = 8
CITIES = 16
F32 = jnp.float32
VMEM_LIMIT = 24 * 1024 * 1024

XU, XP, XH = 8, 6, 7
YU, YP, YH = 24, 20, 20

FULL = 32000.0
BIAS = 200
UNIT_A = 2.0 / FULL
UNIT_E = 0.2 / 12.0 / FULL


PLANES = 4


def depth_weights():
    lanes = np.arange(256)
    result = np.zeros((3, 256, 256), np.float32)
    for k in range(3):
        at = lanes - 128 - 16 * k
        depth = np.where(lanes < 128, lanes, np.where(at < 8, at - 8, at + 120))
        used = (lanes < 128) | ((at >= 0) & (at < 16))
        apart = np.abs(depth[:, None] - depth[None, :])
        band = np.where(apart == 0, -90.0, np.where(apart == 1, 16.0, np.where(apart == 2, -1.0, 0.0)))
        result[k] = np.where(used[:, None] & used[None, :], band, 0.0)
        result[k, 0, 128 + 64 + 16 * k + 8] = 1.0
    return result


def slab_weights():
    lanes = np.arange(128)
    apart = np.abs(lanes[:, None] - lanes[None, :])
    band = np.where(apart == 0, -90.0, np.where(apart == 1, 16.0, np.where(apart == 2, -1.0, 0.0)))
    same = (lanes[:, None] // 16 == lanes[None, :] // 16) & (lanes[:, None] < 48)
    band = np.where(same, band, 0.0)
    return np.concatenate([band, band], axis=0)


def split(v):
    high = v.astype(jnp.bfloat16)
    return high, (v - high.astype(F32)).astype(jnp.bfloat16)


def lane_of():
    return lax.broadcasted_iota(jnp.int32, (8, 128), 1)


def pack_faces(values, lane):
    packed = pltpu.roll(values[0], 8, 1)
    for at in range(1, len(values)):
        packed = jnp.where(lane // 16 == at, pltpu.roll(values[at], (16 * at + 8) % 128, 1), packed)
    return packed


def start_kernel(u_in, p_in, c_in, d_in, u_ref, p_ref, a_ref, e_ref, face_ref, c_ref, d_ref, sems):
    copies = [pltpu.make_async_copy(c_in, c_ref, sems.at[0]), pltpu.make_async_copy(d_in, d_ref, sems.at[1])]
    for k in range(3):
        copies.append(pltpu.make_async_copy(u_in.at[k], u_ref.at[k], sems.at[2 + k]))
        copies.append(pltpu.make_async_copy(p_in.at[k], p_ref.at[k], sems.at[5 + k]))
    for copy in copies:
        copy.start()
    for copy in copies:
        copy.wait()
    lane = lane_of()

    def plane(x, carry):
        for row in (0, 8):
            rows = pl.ds(row, 8)
            share = 1.0 / (1.0 + d_ref[x, rows, :])
            values = [u_ref[k, x, rows, :] for k in range(3)] + [p_ref[k, x, rows, :] for k in range(3)]
            values += [2.0 * share, c_ref[x, rows, :] * share * (1.0 / 12.0)]
            a_ref[x, rows, :] = values[6]
            e_ref[x, rows, :] = values[7]
            face_ref[x, rows, :] = pack_faces(values, lane)
        return carry

    lax.fori_loop(0, 8, plane, 0)


def exponent_of(peak):
    peak = jnp.maximum(jnp.max(peak, axis=0, keepdims=True), 1e-30)
    return jnp.broadcast_to(jnp.ceil(jnp.log2(peak)), (8, 128))


def coded(values):
    return jnp.round(values).astype(jnp.int32).astype(jnp.int16)


def decoded(values):
    return values.astype(jnp.int32).astype(F32)


def twice(rows):
    return jnp.concatenate([rows, rows], axis=0)


def sent_exponents(message):
    both = decoded(message[message.shape[0] - 1]) - BIAS
    return both[0:8], both[8:16]


def x_message_kernel(coefficients, *refs):
    if coefficients:
        z_low_ref, z_high_ref, u_ref, p_ref, a_ref, e_ref, halo_ref, up_ref, down_ref, power_ref = refs
    else:
        z_low_ref, z_high_ref, u_ref, p_ref, halo_ref, up_ref, down_ref, power_ref = refs
    inner = lax.broadcasted_iota(jnp.int32, (16, 128), 1) % 16

    def largest(x, carry):
        field, face = carry
        for k in range(3):
            both = jnp.maximum(jnp.abs(u_ref[k, x]), jnp.abs(p_ref[k, x]))
            field = jnp.maximum(field, jnp.maximum(both[0:8], both[8:16]))
        halo = jnp.where(inner < 8, z_low_ref[x], z_high_ref[x])
        halo_ref[x] = halo
        halo = jnp.abs(halo)
        return field, jnp.maximum(face, jnp.maximum(halo[0:8], halo[8:16]))

    zero = jnp.zeros((8, 128), F32)
    field, face = lax.fori_loop(0, 8, largest, (zero, zero))
    powers = jnp.concatenate([exponent_of(field), exponent_of(face)], axis=0)
    power_ref[...] = powers
    up_ref[up_ref.shape[0] - 1] = coded(powers + BIAS)
    down_ref[down_ref.shape[0] - 1] = coded(powers + BIAS)
    scale = FULL * jnp.exp2(-powers)
    field, face = twice(scale[0:8]), twice(scale[8:16])

    def whole(x, carry):
        for k in range(3):
            code = coded(u_ref[k, x] * field)
            up_ref[XU * k + x] = code
            down_ref[XU * k + x] = code
        return carry

    def part(i, carry):
        parts = [(p_ref.at[k], field) for k in range(3)]
        if coefficients:
            parts += [(a_ref, 1.0 / UNIT_A), (e_ref, 1.0 / UNIT_E)]
        for at, (source, unit) in enumerate(parts):
            up_ref[3 * XU + XP * at + i] = coded(source[8 - XP + i] * unit)
            down_ref[3 * XU + XP * at + i] = coded(source[i] * unit)
        return carry

    at = 3 * XU + (5 if coefficients else 3) * XP

    def side(i, carry):
        up_ref[at + i] = coded(halo_ref[8 - XH + i] * face)
        down_ref[at + i] = coded(halo_ref[i] * face)
        return carry

    lax.fori_loop(0, 8, whole, 0)
    lax.fori_loop(0, XP, part, 0)
    lax.fori_loop(0, XH, side, 0)


def y_message_kernel(coefficients, *refs):
    if coefficients:
        u_ref, p_ref, a_ref, e_ref, halo_ref, power_ref, low_ref, high_ref, up_ref, down_ref = refs
    else:
        u_ref, p_ref, halo_ref, power_ref, low_ref, high_ref, up_ref, down_ref = refs
    powers = power_ref[...]
    low_powers = jnp.concatenate(sent_exponents(low_ref), axis=0)
    high_powers = jnp.concatenate(sent_exponents(high_ref), axis=0)
    most = jnp.maximum(powers, jnp.maximum(low_powers, high_powers))
    for out_ref in (up_ref, down_ref):
        out_ref[out_ref.shape[0] - 1] = coded(most + BIAS)
    own_scale = FULL * jnp.exp2(-most)
    low_scale = jnp.exp2(low_powers - most)
    high_scale = jnp.exp2(high_powers - most)
    field = [twice(scale[0:8]) for scale in (own_scale, low_scale, high_scale)]
    face = [twice(scale[8:16]) for scale in (own_scale, low_scale, high_scale)]

    def put(at, pair):
        up_ref[at] = coded(jnp.concatenate([pair[0][8:16], pair[1][8:16]], axis=0))
        down_ref[at] = coded(jnp.concatenate([pair[0][0:8], pair[1][0:8]], axis=0))

    def group(parts, x_planes, y_planes, x_at, y_at):
        side = (y_planes - 8) // 4

        def own(i, carry):
            for at, (source, units) in enumerate(parts):
                put(y_at + at * y_planes // 2 + side + i, [source[2 * i + j] * units[0] for j in (0, 1)])
            return carry

        def sides(i, carry):
            for at, (_, units) in enumerate(parts):
                start = x_at + at * x_planes
                first = start + x_planes - 2 * side + 2 * i
                put(y_at + at * y_planes // 2 + i, [decoded(low_ref[first + j]) * units[1] for j in (0, 1)])
                first = start + 2 * i
                pair = [decoded(high_ref[first + j]) * units[2] for j in (0, 1)]
                put(y_at + at * y_planes // 2 + side + 4 + i, pair)
            return carry

        lax.fori_loop(0, 4, own, 0)
        lax.fori_loop(0, side, sides, 0)
        return x_at + len(parts) * x_planes, y_at + len(parts) * y_planes // 2

    x_at, y_at = group([(u_ref.at[k], field) for k in range(3)], XU, YU, 0, 0)
    parts = [(p_ref.at[k], field) for k in range(3)]
    if coefficients:
        parts += [(a_ref, (1.0 / UNIT_A, 1.0, 1.0)), (e_ref, (1.0 / UNIT_E, 1.0, 1.0))]
    x_at, y_at = group(parts, XP, YP, x_at, y_at)
    group([(halo_ref, face)], XH, YH, x_at, y_at)


def fill(parts, x_low, x_high, y_low, y_high, x_at, x_planes, y_at, y_planes):
    count = len(parts)
    side = (y_planes - 8) // 2

    def own(i, carry):
        for target, row, block, _ in parts:
            target[8 + i, row + 8 : row + 24, :] = block[i]
        return carry

    def x_side(i, carry):
        for at, (target, row, _, units) in enumerate(parts):
            here = x_at + at * x_planes + i
            target[8 - x_planes + i, row + 8 : row + 24, :] = decoded(x_low[here]) * units[0]
            target[16 + i, row + 8 : row + 24, :] = decoded(x_high[here]) * units[1]
        return carry

    def y_side(i, carry):
        for at, (target, row, _, units) in enumerate(parts):
            here = y_at + at * y_planes // 2 + i
            low = decoded(y_low[here]) * units[2]
            high = decoded(y_high[here]) * units[3]
            for j in (0, 1):
                target[8 - side + 2 * i + j, row : row + 8, :] = low[8 * j : 8 * j + 8]
                target[8 - side + 2 * i + j, row + 24 : row + 32, :] = high[8 * j : 8 * j + 8]
        return carry

    lax.fori_loop(0, 8, own, 0, unroll=2)
    lax.fori_loop(0, x_planes, x_side, 0)
    lax.fori_loop(0, y_planes // 2, y_side, 0, unroll=2)
    return x_at + count * x_planes, y_at + count * y_planes // 2


def steps_kernel(first, *refs):
    if first:
        (u_in, p_in, a_in, e_in, halo_in, x_low, x_high, y_low, y_high, weight_in) = refs[:10]
        (u_out, p_out, face_out, slab_out, seen_out, rate_ref) = refs[10:16]
        state_ref, edge_ref = refs[16:]
    else:
        (u_in, p_in, halo_in, x_low, x_high, y_low, y_high, weight_in, rate_ref) = refs[:9]
        u_out, state_ref = refs[9:]
    a_ref, e_ref, ha_ref, he_ref = (rate_ref.at[at] for at in range(4))
    lane = lane_of()
    inner = lane % 16

    sides = (x_low, x_high, y_low, y_high)
    powers = [sent_exponents(message) for message in sides]
    field = [twice(jnp.exp2(power[0]) * (1.0 / FULL)) for power in powers]
    face = [twice(jnp.exp2(power[1]) * (1.0 / FULL)) for power in powers]
    x_at, y_at = fill([(state_ref.at[0, k], 8, u_in.at[k], field) for k in range(3)], *sides, 0, XU, 0, YU)
    parts = [(state_ref.at[1, k], 8, p_in.at[k], field) for k in range(3)]
    if first:
        parts += [(a_ref, 0, a_in, (UNIT_A,) * 4), (e_ref, 0, e_in, (UNIT_E,) * 4)]
    x_at, y_at = fill(parts, *sides, x_at, XP, y_at, YP)
    fill([(state_ref.at[0, 3], 8, halo_in, face)], *sides, x_at, XH, y_at, YH)

    def prepare(x, carry):
        for tile in range(4):
            rows = pl.ds(8 + 8 * tile, 8)
            held = pl.ds(8 * tile, 8)
            halo = state_ref[0, 3, x, rows, :]
            state_ref[0, 3, x, rows, :] = jnp.where(lane < 48, halo, 0.0)
            state_ref[1, 3, x, rows, :] = jnp.where(lane < 48, pltpu.roll(halo, 128 - 48, 1), 0.0)
            if first:
                for target, at in ((ha_ref, 96), (he_ref, 112)):
                    spread = jnp.where(lane < 16, pltpu.roll(halo, 128 - at, 1), pltpu.roll(halo, 144 - at, 1))
                    spread = jnp.where(lane < 32, spread, pltpu.roll(halo, 160 - at, 1))
                    target[x, held, :] = jnp.where(lane < 48, spread, 0.0)
        return carry

    lax.fori_loop(2, 22, prepare, 0, unroll=4)

    def advance(src, dst, x):
        rows = pl.ds(8, 32)
        fields = [[src[k, 2 + j, rows, :] for j in range(PLANES)] for k in range(4)]
        parts = [[split(v) for v in field] for field in fields]
        depth = []
        for k in range(3):
            pieces = [jnp.concatenate([parts[k][j][part], parts[3][j][part]], axis=1) for part in (0, 1) for j in range(PLANES)]
            both = jnp.dot(jnp.concatenate(pieces, axis=0), weight_in[k], preferred_element_type=F32)
            depth.append(both[0 : 32 * PLANES] + both[32 * PLANES :])
        side = depth[0][:, 128:] + depth[1][:, 128:] + depth[2][:, 128:]
        fresh = []
        for j in range(PLANES):
            for k in range(4):
                v = fields[k][j]
                near = (src[k, 1 + j, rows, :] + src[k, 3 + j, rows, :]) + (
                    src[k, 2 + j, pl.ds(7, 32), :] + src[k, 2 + j, pl.ds(9, 32), :]
                )
                far = (src[k, j, rows, :] + src[k, 4 + j, rows, :]) + (
                    src[k, 2 + j, pl.ds(6, 32), :] + src[k, 2 + j, pl.ds(10, 32), :]
                )
                along = side if k == 3 else depth[k][:, :128]
                laplace = along[32 * j : 32 * j + 32] + (16.0 * near - far)
                old = dst[k, x + j, rows, :]
                a_each, e_each = (ha_ref, he_ref) if k == 3 else (a_ref, e_ref)
                fresh.append((k, j, old + a_each[x + j] * (v - old) + e_each[x + j] * laplace))
        return fresh, side

    def one_step(step, carry):
        dst = state_ref.at[(step + 1) % 2]

        def planes(at, inside):
            x = 2 * step + 2 + PLANES * at
            fresh, side = advance(state_ref.at[step % 2, :, pl.ds(x - 2, 4 + PLANES)], dst, x)
            for k, j, value in fresh:
                dst[k, x + j, 8:40, :] = value
            if first:
                for j in range(PLANES):
                    edge_ref[step, x + j, :, :] = side[32 * j + 8 : 32 * j + 24]
            return inside

        lax.fori_loop(0, (20 - 4 * step) // PLANES, planes, 0)
        return carry

    lax.fori_loop(0, HALF, one_step, 0)

    block = pl.ds(16, 16)

    def finish(x, carry):
        for k in range(3):
            u_out[k, x, :, :] = state_ref[0, k, 8 + x, block, :]
            if first:
                p_out[k, x, :, :] = state_ref[1, k, 8 + x, block, :]
        if first:
            for row in (0, 8):
                rows = pl.ds(row, 8)
                values = [state_ref[slot, k, 8 + x, pl.ds(16 + row, 8), :] for slot in (0, 1) for k in range(3)]
                last = pack_faces(values, lane)
                face_out[x, rows, :] = last
                slab = values[0]
                for at in range(1, 6):
                    slab = jnp.where(lane // 16 == at, pltpu.roll(values[at], 16 * at, 1), slab)
                slab_out[x, rows, :] = slab
                seen = jnp.zeros((8, 128), F32)
                for step in range(HALF):
                    if step < HALF - 1:
                        sample = pltpu.roll(edge_ref[step + 1, 8 + x, rows, :], 56 + step, 1)
                    else:
                        sample = pltpu.roll(last, 120 + step, 1)
                    seen = jnp.where((inner == step) & (lane < 48), sample, seen)
                seen_out[x, rows, :] = seen
        return carry

    lax.fori_loop(0, 8, finish, 0, unroll=4)


def slab_message_kernel(own_ref, low_ref, high_ref, up_ref, down_ref):
    def plane(i, carry):
        for at, source in ((0, low_ref), (8, own_ref), (16, high_ref)):
            up_ref[at + i] = source[i, 8:16, :]
            down_ref[at + i] = source[i, 0:8, :]
        return carry

    lax.fori_loop(0, 8, plane, 0, unroll=2)


def surface_kernel(
    own_in, x_low, x_high, y_low, y_high, weight_in, rate_in, seen_in, cells_in, filter_in, count_in,
    table_out, state_ref, rate_ref, sample_ref, seen_ref, filter_ref, count_ref,
):
    lane = lane_of()
    inner = lane % 16

    def near_side(i, carry):
        state_ref[0, i, 16:32, :] = x_low[i]
        state_ref[0, 8 + i, 16:32, :] = own_in[i]
        state_ref[0, 16 + i, 16:32, :] = x_high[i]
        for part in range(3):
            state_ref[0, 8 * part + i, 8:16, :] = y_low[8 * part + i]
            state_ref[0, 8 * part + i, 32:40, :] = y_high[8 * part + i]
        return carry

    lax.fori_loop(0, 8, near_side, 0, unroll=2)

    def prepare(x, carry):
        for tile in range(4):
            rows = pl.ds(8 + 8 * tile, 8)
            held = pl.ds(8 * tile, 8)
            value = state_ref[0, x, rows, :]
            state_ref[0, x, rows, :] = jnp.where(lane < 48, value, 0.0)
            state_ref[1, x, rows, :] = jnp.where(lane < 48, pltpu.roll(value, 128 - 48, 1), 0.0)
            for at in (0, 1):
                rate = rate_in[at, x, held, :]
                spread = jnp.where(lane < 16, rate, jnp.where(lane < 32, pltpu.roll(rate, 16, 1), pltpu.roll(rate, 32, 1)))
                rate_ref[at, x, held, :] = jnp.where(lane < 48, spread, 0.0)
        return carry

    lax.fori_loop(0, 24, prepare, 0, unroll=4)

    def one_step(step, carry):
        dst = state_ref.at[(step + 1) % 2]

        def planes(at, inside):
            x = 2 * step + 2 + PLANES * at
            src = state_ref.at[step % 2, pl.ds(x - 2, 4 + PLANES)]
            rows = pl.ds(8, 32)
            fields = [src[2 + j, rows, :] for j in range(PLANES)]
            halves = jnp.concatenate([jnp.concatenate(split(v), axis=1) for v in fields], axis=0)
            depth = jnp.dot(halves, weight_in[...], preferred_element_type=F32)
            fresh = []
            for j, v in enumerate(fields):
                near = (src[1 + j, rows, :] + src[3 + j, rows, :]) + (src[2 + j, pl.ds(7, 32), :] + src[2 + j, pl.ds(9, 32), :])
                far = (src[j, rows, :] + src[4 + j, rows, :]) + (src[2 + j, pl.ds(6, 32), :] + src[2 + j, pl.ds(10, 32), :])
                laplace = depth[32 * j : 32 * j + 32] + (16.0 * near - far)
                old = dst[x + j, rows, :]
                fresh.append(old + rate_ref[0, x + j] * (v - old) + rate_ref[1, x + j] * laplace)
            for j, value in enumerate(fresh):
                dst[x + j, 8:40, :] = value
                sample_ref[step, x + j, :, :] = value[8:24]
            return inside

        lax.fori_loop(0, (20 - 4 * step) // PLANES, planes, 0)
        return carry

    lax.fori_loop(0, HALF, one_step, 0)

    def finish(x, carry):
        for row in (0, 8):
            rows = pl.ds(row, 8)
            seen = seen_in[x, rows, :]
            for step in range(HALF):
                at = HALF + step
                sample = pltpu.roll(sample_ref[step, 8 + x, rows, :], at, 1)
                seen = jnp.where((inner == at) & (lane < 48), sample, seen)
            seen_ref[x, rows, :] = seen
        return carry

    lax.fori_loop(0, 8, finish, 0, unroll=4)

    filter_ref[...] = filter_in[...].astype(F32)
    blocks = [jnp.zeros((8, CLASSES * MODES), F32)] * 16
    for k in range(3):
        blocks[2 * k] = filter_ref[pl.ds(k, STEPS, stride=3), :]
    filters = jnp.concatenate(blocks, axis=0).astype(jnp.bfloat16)
    motion = seen_ref[...].reshape(128, 128).astype(jnp.bfloat16)
    modal = lax.dot_general(filters, motion, (((0,), (1,)), ((), ())), preferred_element_type=F32)
    modes = lax.broadcasted_iota(jnp.int32, (MODES, 128), 0)
    count_ref[...] = jnp.zeros((8, 128), jnp.int32)
    count_ref[0:1, 0:CLASSES] = count_in[...]
    counts = jnp.where(modes == lane, jnp.broadcast_to(count_ref[0:1, :], (8, 128)), 0)
    counts = jnp.sum(counts, axis=1, keepdims=True)
    energies = []
    for kind in range(CLASSES):
        part = modal[MODES * kind : MODES * (kind + 1), :]
        part = jnp.where(modes < counts[kind : kind + 1, :], part * part, 0.0)
        energies.append(jnp.sum(part, axis=0, keepdims=True))
    demand = 0.5 * jnp.log1p(jnp.concatenate(energies, axis=0))
    for owner in range(table_out.shape[0]):
        cells = jnp.broadcast_to(cells_in[owner : owner + 1, :], (CLASSES, 128))
        chosen = jnp.take_along_axis(demand, cells, axis=1)
        for level in range(table_out.shape[1]):
            table_out[owner, level] = chosen


def fragility_kernel(
    table_ref, slot_ref, kind_ref, city_ref, amplify_ref, median_ref, spread_ref, out_ref, gain_ref, tables_ref
):
    sources = table_ref.shape[0]
    slot, kind, city = slot_ref[...], kind_ref[...], city_ref[...]
    column = slot % 128
    key = (slot // 128) * CLASSES + kind
    demand = jnp.zeros((8, 128), F32)
    for source in range(sources):
        for each in range(CLASSES):
            row = jnp.broadcast_to(table_ref[source, 0, each : each + 1, :], (8, 128))
            found = jnp.take_along_axis(row, column, axis=1)
            demand = jnp.where(key == source * CLASSES + each, found, demand)
    gain_ref[...] = jnp.ones((8, 128), F32)
    gain_ref[0:1, 0:CITIES] = amplify_ref[...]
    gain = jnp.log(jnp.broadcast_to(gain_ref[0:1, :], (8, 128)))
    demand = demand + jnp.take_along_axis(gain, city, axis=1)
    tables_ref[...] = jnp.ones((128, 128), F32)
    batches = median_ref.shape[1]
    tables_ref[0:CLASSES, 0:batches] = median_ref[...]
    medians = tables_ref[...].T
    tables_ref[0:CLASSES, 0:batches] = spread_ref[...]
    spreads = tables_ref[...].T
    for group in range(8):
        level = jnp.broadcast_to(demand[group : group + 1, :], (8, 128))
        index = jnp.broadcast_to(kind[group : group + 1, :], (8, 128))
        for half in range(0, batches, 8):
            middle = jnp.take_along_axis(medians[half : half + 8, :], index, axis=1)
            width = jnp.take_along_axis(spreads[half : half + 8, :], index, axis=1)
            out_ref[half : half + 8, 128 * group : 128 * group + 128] = jax.nn.sigmoid((level - middle) / width)


VM = pl.BlockSpec(memory_space=pltpu.VMEM)


def call(kernel, name, shapes, args, specs=None, scratch=()):
    out = [s if isinstance(s, jax.ShapeDtypeStruct) else jax.ShapeDtypeStruct(s, F32) for s in shapes]
    return pl.pallas_call(
        kernel,
        out_shape=out,
        in_specs=specs or [VM] * len(args),
        out_specs=[VM] * len(out),
        scratch_shapes=list(scratch),
        compiler_params=pltpu.CompilerParams(vmem_limit_bytes=VMEM_LIMIT),
        name=name,
    )(*args)


def both_ways(to_up, to_down, axis):
    count = lax.axis_size(axis)
    forward = [(i, i + 1) for i in range(count - 1)]
    backward = [(i + 1, i) for i in range(count - 1)]
    return lax.ppermute(to_up, axis, forward), lax.ppermute(to_down, axis, backward)


def exchange(u, p, faces, coefficients):
    extra = list(coefficients)
    has = bool(extra)
    z_low, z_high = both_ways(faces, faces, "gz")
    planes = 3 * XU + (3 + len(extra)) * XP + XH + 1
    message = jax.ShapeDtypeStruct((planes, 16, 128), jnp.int16)
    halo, up, down, powers = call(
        functools.partial(x_message_kernel, has),
        "x_message",
        [(8, 16, 128), message, message, (16, 128)],
        [z_low, z_high, u, p] + extra,
    )
    x_low, x_high = both_ways(up, down, "gx")
    planes = (3 * YU + (3 + len(extra)) * YP + YH) // 2 + 1
    message = jax.ShapeDtypeStruct((planes, 16, 128), jnp.int16)
    up, down = call(
        functools.partial(y_message_kernel, has),
        "y_message",
        [message, message],
        [u, p] + extra + [halo, powers, x_low, x_high],
    )
    y_low, y_high = both_ways(up, down, "gy")
    return halo, x_low, x_high, y_low, y_high


def body(
    displacement,
    previous,
    courant,
    damping,
    send_cells,
    building_slot,
    building_class,
    city,
    mode_count,
    modal_filter,
    amplify,
    median,
    spread,
):
    own = (3, 8, 16, 128)
    plane = (8, 16, 128)
    wide = pltpu.VMEM((2, 4, 24, 48, 128), F32)
    samples = pltpu.VMEM((HALF, 24, 16, 128), F32)

    u, p, a, e, faces = call(
        start_kernel,
        "start",
        [own, own, plane, plane, plane],
        [displacement, previous, courant, damping],
        specs=[pl.BlockSpec(memory_space=pltpu.HBM)] * 4,
        scratch=[pltpu.VMEM(plane, F32)] * 2 + [pltpu.SemaphoreType.DMA((8,))],
    )
    received = exchange(u, p, faces, (a, e))
    weights = jnp.asarray(depth_weights(), jnp.bfloat16)
    u, p, faces, slab, seen, rates = call(
        functools.partial(steps_kernel, True),
        "steps_first",
        [own, own, plane, plane, plane, (4, 24, 32, 128)],
        [u, p, a, e, *received, weights],
        scratch=[wide, samples],
    )

    x_low, x_high = both_ways(slab, slab, "gx")
    y_low, y_high = both_ways(*call(slab_message_kernel, "slab_message", [(24, 8, 128)] * 2, [slab, x_low, x_high]), "gy")
    owners, levels = lax.axis_size("gx"), lax.axis_size("gz")
    (table,) = call(
        surface_kernel,
        "surface",
        [(owners, levels, CLASSES, 128)],
        [slab, x_low, x_high, y_low, y_high, jnp.asarray(slab_weights(), jnp.bfloat16), rates, seen]
        + [send_cells.reshape(owners, 128), modal_filter.T, mode_count.reshape(1, CLASSES)],
        scratch=[
            pltpu.VMEM((2, 24, 48, 128), F32),
            pltpu.VMEM((2, 24, 32, 128), F32),
            samples,
            pltpu.VMEM(plane, F32),
            pltpu.VMEM((3 * STEPS, CLASSES * MODES), F32),
            pltpu.VMEM((8, 128), jnp.int32),
        ],
    )
    table = table.reshape(owners * levels, CLASSES, 128)
    table = lax.all_to_all(table, ("gx", "gz"), split_axis=0, concat_axis=0, tiled=True)
    received = exchange(u, p, faces, ())
    (field,) = call(
        functools.partial(steps_kernel, False), "steps_second", [own], [u, p, *received, weights, rates], scratch=[wide]
    )
    (probability,) = call(
        fragility_kernel,
        "fragility",
        [(16, 1024)],
        [
            table.reshape(owners, levels, CLASSES, 128),
            building_slot.reshape(8, 128),
            building_class.reshape(8, 128),
            city.reshape(8, 128),
            amplify.reshape(1, CITIES),
            median.T,
            spread.T,
        ],
        scratch=[pltpu.VMEM((8, 128), F32), pltpu.VMEM((128, 128), F32)],
    )
    return (field, probability)


def solution(mesh):
    placed = (
        P(None, "gx", "gy", "gz"),
        P(None, "gx", "gy", "gz"),
        P("gx", "gy", "gz"),
        P("gx", "gy", "gz"),
        P("gx", "gy", None),
        P(("gx", "gy", "gz")),
        P(("gx", "gy", "gz")),
        P(("gx", "gy", "gz")),
        P(),
        P(),
        P(),
        P(),
        P(),
    )
    return jax.shard_map(
        body,
        mesh=mesh,
        in_specs=placed,
        out_specs=(P(None, "gx", "gy", "gz"), P(None, ("gx", "gy", "gz"))),
        check_vma=False,
    )
```

```python
import functools

import jax
import jax.numpy as jnp
import numpy as np
from jax import lax
from jax.experimental import pallas as pl
from jax.experimental.pallas import tpu as pltpu
from jax.sharding import PartitionSpec as P

STEPS = 8
HALF = 4
DEEP = 2 * HALF
CLASSES = 8
MODES = 8
CITIES = 16
F32 = jnp.float32
VMEM_LIMIT = 24 * 1024 * 1024

XU, XP, XH = 8, 6, 7
YU, YP, YH = 24, 20, 20

FULL = 32000.0
BIAS = 200
UNIT_A = 2.0 / FULL
UNIT_E = 0.2 / 12.0 / FULL


PLANES = 4


def depth_weights():
    lanes = np.arange(256)
    result = np.zeros((3, 256, 256), np.float32)
    for k in range(3):
        at = lanes - 128 - 16 * k
        depth = np.where(lanes < 128, lanes, np.where(at < 8, at - 8, at + 120))
        used = (lanes < 128) | ((at >= 0) & (at < 16))
        apart = np.abs(depth[:, None] - depth[None, :])
        band = np.where(apart == 0, -90.0, np.where(apart == 1, 16.0, np.where(apart == 2, -1.0, 0.0)))
        result[k] = np.where(used[:, None] & used[None, :], band, 0.0)
        result[k, 0, 128 + 64 + 16 * k + 8] = 1.0
    return result


def slab_weights():
    lanes = np.arange(128)
    apart = np.abs(lanes[:, None] - lanes[None, :])
    band = np.where(apart == 0, -90.0, np.where(apart == 1, 16.0, np.where(apart == 2, -1.0, 0.0)))
    same = (lanes[:, None] // 16 == lanes[None, :] // 16) & (lanes[:, None] < 48)
    band = np.where(same, band, 0.0)
    return np.concatenate([band, band], axis=0)


def split(v):
    high = v.astype(jnp.bfloat16)
    return high, (v - high.astype(F32)).astype(jnp.bfloat16)


def lane_of():
    return lax.broadcasted_iota(jnp.int32, (8, 128), 1)


def pack_faces(values, lane):
    packed = pltpu.roll(values[0], 8, 1)
    for at in range(1, len(values)):
        packed = jnp.where(lane // 16 == at, pltpu.roll(values[at], (16 * at + 8) % 128, 1), packed)
    return packed


def start_kernel(u_in, p_in, c_in, d_in, u_ref, p_ref, a_ref, e_ref, face_ref, c_ref, d_ref, sems):
    copies = [pltpu.make_async_copy(c_in, c_ref, sems.at[0]), pltpu.make_async_copy(d_in, d_ref, sems.at[1])]
    for k in range(3):
        copies.append(pltpu.make_async_copy(u_in.at[k], u_ref.at[k], sems.at[2 + k]))
        copies.append(pltpu.make_async_copy(p_in.at[k], p_ref.at[k], sems.at[5 + k]))
    for copy in copies:
        copy.start()
    for copy in copies:
        copy.wait()
    lane = lane_of()

    def plane(x, carry):
        for row in (0, 8):
            rows = pl.ds(row, 8)
            share = 1.0 / (1.0 + d_ref[x, rows, :])
            values = [u_ref[k, x, rows, :] for k in range(3)] + [p_ref[k, x, rows, :] for k in range(3)]
            values += [2.0 * share, c_ref[x, rows, :] * share * (1.0 / 12.0)]
            a_ref[x, rows, :] = values[6]
            e_ref[x, rows, :] = values[7]
            face_ref[x, rows, :] = pack_faces(values, lane)
        return carry

    lax.fori_loop(0, 8, plane, 0)


def exponent_of(peak):
    peak = jnp.maximum(jnp.max(peak, axis=0, keepdims=True), 1e-30)
    return jnp.broadcast_to(jnp.ceil(jnp.log2(peak)), (8, 128))


def coded(values):
    return jnp.round(values).astype(jnp.int32).astype(jnp.int16)


def decoded(values):
    return values.astype(jnp.int32).astype(F32)


def twice(rows):
    return jnp.concatenate([rows, rows], axis=0)


def sent_exponents(message):
    both = decoded(message[message.shape[0] - 1]) - BIAS
    return both[0:8], both[8:16]


def x_message_kernel(coefficients, *refs):
    if coefficients:
        z_low_ref, z_high_ref, u_ref, p_ref, a_ref, e_ref, halo_ref, up_ref, down_ref, power_ref = refs
    else:
        z_low_ref, z_high_ref, u_ref, p_ref, halo_ref, up_ref, down_ref, power_ref = refs
    inner = lax.broadcasted_iota(jnp.int32, (16, 128), 1) % 16

    def largest(x, carry):
        field, face = carry
        for k in range(3):
            both = jnp.maximum(jnp.abs(u_ref[k, x]), jnp.abs(p_ref[k, x]))
            field = jnp.maximum(field, jnp.maximum(both[0:8], both[8:16]))
        halo = jnp.where(inner < 8, z_low_ref[x], z_high_ref[x])
        halo_ref[x] = halo
        halo = jnp.abs(halo)
        return field, jnp.maximum(face, jnp.maximum(halo[0:8], halo[8:16]))

    zero = jnp.zeros((8, 128), F32)
    field, face = lax.fori_loop(0, 8, largest, (zero, zero))
    powers = jnp.concatenate([exponent_of(field), exponent_of(face)], axis=0)
    power_ref[...] = powers
    up_ref[up_ref.shape[0] - 1] = coded(powers + BIAS)
    down_ref[down_ref.shape[0] - 1] = coded(powers + BIAS)
    scale = FULL * jnp.exp2(-powers)
    field, face = twice(scale[0:8]), twice(scale[8:16])

    def whole(x, carry):
        for k in range(3):
            code = coded(u_ref[k, x] * field)
            up_ref[XU * k + x] = code
            down_ref[XU * k + x] = code
        return carry

    def part(i, carry):
        parts = [(p_ref.at[k], field) for k in range(3)]
        if coefficients:
            parts += [(a_ref, 1.0 / UNIT_A), (e_ref, 1.0 / UNIT_E)]
        for at, (source, unit) in enumerate(parts):
            up_ref[3 * XU + XP * at + i] = coded(source[8 - XP + i] * unit)
            down_ref[3 * XU + XP * at + i] = coded(source[i] * unit)
        return carry

    at = 3 * XU + (5 if coefficients else 3) * XP

    def side(i, carry):
        up_ref[at + i] = coded(halo_ref[8 - XH + i] * face)
        down_ref[at + i] = coded(halo_ref[i] * face)
        return carry

    lax.fori_loop(0, 8, whole, 0)
    lax.fori_loop(0, XP, part, 0)
    lax.fori_loop(0, XH, side, 0)


def y_message_kernel(coefficients, *refs):
    if coefficients:
        u_ref, p_ref, a_ref, e_ref, halo_ref, power_ref, low_ref, high_ref, up_ref, down_ref = refs
    else:
        u_ref, p_ref, halo_ref, power_ref, low_ref, high_ref, up_ref, down_ref = refs
    powers = power_ref[...]
    low_powers = jnp.concatenate(sent_exponents(low_ref), axis=0)
    high_powers = jnp.concatenate(sent_exponents(high_ref), axis=0)
    most = jnp.maximum(powers, jnp.maximum(low_powers, high_powers))
    for out_ref in (up_ref, down_ref):
        out_ref[out_ref.shape[0] - 1] = coded(most + BIAS)
    own_scale = FULL * jnp.exp2(-most)
    low_scale = jnp.exp2(low_powers - most)
    high_scale = jnp.exp2(high_powers - most)
    field = [twice(scale[0:8]) for scale in (own_scale, low_scale, high_scale)]
    face = [twice(scale[8:16]) for scale in (own_scale, low_scale, high_scale)]

    def put(at, pair):
        up_ref[at] = coded(jnp.concatenate([pair[0][8:16], pair[1][8:16]], axis=0))
        down_ref[at] = coded(jnp.concatenate([pair[0][0:8], pair[1][0:8]], axis=0))

    def group(parts, x_planes, y_planes, x_at, y_at):
        side = (y_planes - 8) // 4

        def own(i, carry):
            for at, (source, units) in enumerate(parts):
                put(y_at + at * y_planes // 2 + side + i, [source[2 * i + j] * units[0] for j in (0, 1)])
            return carry

        def sides(i, carry):
            for at, (_, units) in enumerate(parts):
                start = x_at + at * x_planes
                first = start + x_planes - 2 * side + 2 * i
                put(y_at + at * y_planes // 2 + i, [decoded(low_ref[first + j]) * units[1] for j in (0, 1)])
                first = start + 2 * i
                pair = [decoded(high_ref[first + j]) * units[2] for j in (0, 1)]
                put(y_at + at * y_planes // 2 + side + 4 + i, pair)
            return carry

        lax.fori_loop(0, 4, own, 0)
        lax.fori_loop(0, side, sides, 0)
        return x_at + len(parts) * x_planes, y_at + len(parts) * y_planes // 2

    x_at, y_at = group([(u_ref.at[k], field) for k in range(3)], XU, YU, 0, 0)
    parts = [(p_ref.at[k], field) for k in range(3)]
    if coefficients:
        parts += [(a_ref, (1.0 / UNIT_A, 1.0, 1.0)), (e_ref, (1.0 / UNIT_E, 1.0, 1.0))]
    x_at, y_at = group(parts, XP, YP, x_at, y_at)
    group([(halo_ref, face)], XH, YH, x_at, y_at)


def fill(parts, x_low, x_high, y_low, y_high, x_at, x_planes, y_at, y_planes):
    count = len(parts)
    side = (y_planes - 8) // 2

    def own(i, carry):
        for target, row, block, _ in parts:
            target[8 + i, row + 8 : row + 24, :] = block[i]
        return carry

    def x_side(i, carry):
        for at, (target, row, _, units) in enumerate(parts):
            here = x_at + at * x_planes + i
            target[8 - x_planes + i, row + 8 : row + 24, :] = decoded(x_low[here]) * units[0]
            target[16 + i, row + 8 : row + 24, :] = decoded(x_high[here]) * units[1]
        return carry

    def y_side(i, carry):
        for at, (target, row, _, units) in enumerate(parts):
            here = y_at + at * y_planes // 2 + i
            low = decoded(y_low[here]) * units[2]
            high = decoded(y_high[here]) * units[3]
            for j in (0, 1):
                target[8 - side + 2 * i + j, row : row + 8, :] = low[8 * j : 8 * j + 8]
                target[8 - side + 2 * i + j, row + 24 : row + 32, :] = high[8 * j : 8 * j + 8]
        return carry

    lax.fori_loop(0, 8, own, 0, unroll=2)
    lax.fori_loop(0, x_planes, x_side, 0)
    lax.fori_loop(0, y_planes // 2, y_side, 0, unroll=2)
    return x_at + count * x_planes, y_at + count * y_planes // 2


def steps_kernel(first, *refs):
    if first:
        (u_in, p_in, a_in, e_in, halo_in, x_low, x_high, y_low, y_high, weight_in) = refs[:10]
        (u_out, p_out, face_out, slab_out, seen_out, rate_ref) = refs[10:16]
        state_ref, edge_ref = refs[16:]
    else:
        (u_in, p_in, halo_in, x_low, x_high, y_low, y_high, weight_in, rate_ref) = refs[:9]
        u_out, state_ref = refs[9:]
    a_ref, e_ref, ha_ref, he_ref = (rate_ref.at[at] for at in range(4))
    lane = lane_of()
    inner = lane % 16

    sides = (x_low, x_high, y_low, y_high)
    powers = [sent_exponents(message) for message in sides]
    field = [twice(jnp.exp2(power[0]) * (1.0 / FULL)) for power in powers]
    face = [twice(jnp.exp2(power[1]) * (1.0 / FULL)) for power in powers]
    x_at, y_at = fill([(state_ref.at[0, k], 8, u_in.at[k], field) for k in range(3)], *sides, 0, XU, 0, YU)
    parts = [(state_ref.at[1, k], 8, p_in.at[k], field) for k in range(3)]
    if first:
        parts += [(a_ref, 0, a_in, (UNIT_A,) * 4), (e_ref, 0, e_in, (UNIT_E,) * 4)]
    x_at, y_at = fill(parts, *sides, x_at, XP, y_at, YP)
    fill([(state_ref.at[0, 3], 8, halo_in, face)], *sides, x_at, XH, y_at, YH)

    def prepare(x, carry):
        for tile in range(4):
            rows = pl.ds(8 + 8 * tile, 8)
            held = pl.ds(8 * tile, 8)
            halo = state_ref[0, 3, x, rows, :]
            state_ref[0, 3, x, rows, :] = jnp.where(lane < 48, halo, 0.0)
            state_ref[1, 3, x, rows, :] = jnp.where(lane < 48, pltpu.roll(halo, 128 - 48, 1), 0.0)
            if first:
                for target, at in ((ha_ref, 96), (he_ref, 112)):
                    spread = jnp.where(lane < 16, pltpu.roll(halo, 128 - at, 1), pltpu.roll(halo, 144 - at, 1))
                    spread = jnp.where(lane < 32, spread, pltpu.roll(halo, 160 - at, 1))
                    target[x, held, :] = jnp.where(lane < 48, spread, 0.0)
        return carry

    lax.fori_loop(2, 22, prepare, 0, unroll=4)

    def advance(src, dst, x):
        rows = pl.ds(8, 32)
        fields = [[src[k, 2 + j, rows, :] for j in range(PLANES)] for k in range(4)]
        parts = [[split(v) for v in field] for field in fields]
        depth = []
        for k in range(3):
            pieces = [jnp.concatenate([parts[k][j][part], parts[3][j][part]], axis=1) for part in (0, 1) for j in range(PLANES)]
            both = jnp.dot(jnp.concatenate(pieces, axis=0), weight_in[k], preferred_element_type=F32)
            depth.append(both[0 : 32 * PLANES] + both[32 * PLANES :])
        side = depth[0][:, 128:] + depth[1][:, 128:] + depth[2][:, 128:]
        fresh = []
        for j in range(PLANES):
            for k in range(4):
                v = fields[k][j]
                near = (src[k, 1 + j, rows, :] + src[k, 3 + j, rows, :]) + (
                    src[k, 2 + j, pl.ds(7, 32), :] + src[k, 2 + j, pl.ds(9, 32), :]
                )
                far = (src[k, j, rows, :] + src[k, 4 + j, rows, :]) + (
                    src[k, 2 + j, pl.ds(6, 32), :] + src[k, 2 + j, pl.ds(10, 32), :]
                )
                along = side if k == 3 else depth[k][:, :128]
                laplace = along[32 * j : 32 * j + 32] + (16.0 * near - far)
                old = dst[k, x + j, rows, :]
                a_each, e_each = (ha_ref, he_ref) if k == 3 else (a_ref, e_ref)
                fresh.append((k, j, old + a_each[x + j] * (v - old) + e_each[x + j] * laplace))
        return fresh, side

    def one_step(step, carry):
        dst = state_ref.at[(step + 1) % 2]

        def planes(at, inside):
            x = 2 * step + 2 + PLANES * at
            fresh, side = advance(state_ref.at[step % 2, :, pl.ds(x - 2, 4 + PLANES)], dst, x)
            for k, j, value in fresh:
                dst[k, x + j, 8:40, :] = value
            if first:
                for j in range(PLANES):
                    edge_ref[step, x + j, :, :] = side[32 * j + 8 : 32 * j + 24]
            return inside

        lax.fori_loop(0, (20 - 4 * step) // PLANES, planes, 0)
        return carry

    lax.fori_loop(0, HALF, one_step, 0)

    block = pl.ds(16, 16)

    def finish(x, carry):
        for k in range(3):
            u_out[k, x, :, :] = state_ref[0, k, 8 + x, block, :]
            if first:
                p_out[k, x, :, :] = state_ref[1, k, 8 + x, block, :]
        if first:
            for row in (0, 8):
                rows = pl.ds(row, 8)
                values = [state_ref[slot, k, 8 + x, pl.ds(16 + row, 8), :] for slot in (0, 1) for k in range(3)]
                last = pack_faces(values, lane)
                face_out[x, rows, :] = last
                slab = values[0]
                for at in range(1, 6):
                    slab = jnp.where(lane // 16 == at, pltpu.roll(values[at], 16 * at, 1), slab)
                slab_out[x, rows, :] = slab
                seen = jnp.zeros((8, 128), F32)
                for step in range(HALF):
                    if step < HALF - 1:
                        sample = pltpu.roll(edge_ref[step + 1, 8 + x, rows, :], 56 + step, 1)
                    else:
                        sample = pltpu.roll(last, 120 + step, 1)
                    seen = jnp.where((inner == step) & (lane < 48), sample, seen)
                seen_out[x, rows, :] = seen
        return carry

    lax.fori_loop(0, 8, finish, 0, unroll=4)


def slab_message_kernel(own_ref, low_ref, high_ref, after_ref, up_ref, down_ref):
    def plane(i, carry):
        for at, source in ((0, low_ref), (8, own_ref), (16, high_ref)):
            up_ref[at + i] = source[i, 8:16, :]
            down_ref[at + i] = source[i, 0:8, :]
        return carry

    lax.fori_loop(0, 8, plane, 0, unroll=2)


def surface_kernel(
    own_in, x_low, x_high, y_low, y_high, weight_in, rate_in, seen_in, cells_in, filter_in, count_in, after_in,
    table_out, state_ref, rate_ref, sample_ref, seen_ref, filter_ref, count_ref,
):
    lane = lane_of()
    inner = lane % 16

    def near_side(i, carry):
        state_ref[0, i, 16:32, :] = x_low[i]
        state_ref[0, 8 + i, 16:32, :] = own_in[i]
        state_ref[0, 16 + i, 16:32, :] = x_high[i]
        for part in range(3):
            state_ref[0, 8 * part + i, 8:16, :] = y_low[8 * part + i]
            state_ref[0, 8 * part + i, 32:40, :] = y_high[8 * part + i]
        return carry

    lax.fori_loop(0, 8, near_side, 0, unroll=2)

    def prepare(x, carry):
        for tile in range(4):
            rows = pl.ds(8 + 8 * tile, 8)
            held = pl.ds(8 * tile, 8)
            value = state_ref[0, x, rows, :]
            state_ref[0, x, rows, :] = jnp.where(lane < 48, value, 0.0)
            state_ref[1, x, rows, :] = jnp.where(lane < 48, pltpu.roll(value, 128 - 48, 1), 0.0)
            for at in (0, 1):
                rate = rate_in[at, x, held, :]
                spread = jnp.where(lane < 16, rate, jnp.where(lane < 32, pltpu.roll(rate, 16, 1), pltpu.roll(rate, 32, 1)))
                rate_ref[at, x, held, :] = jnp.where(lane < 48, spread, 0.0)
        return carry

    lax.fori_loop(0, 24, prepare, 0, unroll=4)

    def one_step(step, carry):
        dst = state_ref.at[(step + 1) % 2]

        def planes(at, inside):
            x = 2 * step + 2 + PLANES * at
            src = state_ref.at[step % 2, pl.ds(x - 2, 4 + PLANES)]
            rows = pl.ds(8, 32)
            fields = [src[2 + j, rows, :] for j in range(PLANES)]
            halves = jnp.concatenate([jnp.concatenate(split(v), axis=1) for v in fields], axis=0)
            depth = jnp.dot(halves, weight_in[...], preferred_element_type=F32)
            fresh = []
            for j, v in enumerate(fields):
                near = (src[1 + j, rows, :] + src[3 + j, rows, :]) + (src[2 + j, pl.ds(7, 32), :] + src[2 + j, pl.ds(9, 32), :])
                far = (src[j, rows, :] + src[4 + j, rows, :]) + (src[2 + j, pl.ds(6, 32), :] + src[2 + j, pl.ds(10, 32), :])
                laplace = depth[32 * j : 32 * j + 32] + (16.0 * near - far)
                old = dst[x + j, rows, :]
                fresh.append(old + rate_ref[0, x + j] * (v - old) + rate_ref[1, x + j] * laplace)
            for j, value in enumerate(fresh):
                dst[x + j, 8:40, :] = value
                sample_ref[step, x + j, :, :] = value[8:24]
            return inside

        lax.fori_loop(0, (20 - 4 * step) // PLANES, planes, 0)
        return carry

    lax.fori_loop(0, HALF, one_step, 0)

    def finish(x, carry):
        for row in (0, 8):
            rows = pl.ds(row, 8)
            seen = seen_in[x, rows, :]
            for step in range(HALF):
                at = HALF + step
                sample = pltpu.roll(sample_ref[step, 8 + x, rows, :], at, 1)
                seen = jnp.where((inner == at) & (lane < 48), sample, seen)
            seen_ref[x, rows, :] = seen
        return carry

    lax.fori_loop(0, 8, finish, 0, unroll=4)

    filter_ref[...] = filter_in[...].astype(F32)
    blocks = [jnp.zeros((8, CLASSES * MODES), F32)] * 16
    for k in range(3):
        blocks[2 * k] = filter_ref[pl.ds(k, STEPS, stride=3), :]
    filters = jnp.concatenate(blocks, axis=0).astype(jnp.bfloat16)
    motion = seen_ref[...].reshape(128, 128).astype(jnp.bfloat16)
    modal = lax.dot_general(filters, motion, (((0,), (1,)), ((), ())), preferred_element_type=F32)
    modes = lax.broadcasted_iota(jnp.int32, (MODES, 128), 0)
    count_ref[...] = jnp.zeros((8, 128), jnp.int32)
    count_ref[0:1, 0:CLASSES] = count_in[...]
    counts = jnp.where(modes == lane, jnp.broadcast_to(count_ref[0:1, :], (8, 128)), 0)
    counts = jnp.sum(counts, axis=1, keepdims=True)
    energies = []
    for kind in range(CLASSES):
        part = modal[MODES * kind : MODES * (kind + 1), :]
        part = jnp.where(modes < counts[kind : kind + 1, :], part * part, 0.0)
        energies.append(jnp.sum(part, axis=0, keepdims=True))
    demand = 0.5 * jnp.log1p(jnp.concatenate(energies, axis=0))
    for owner in range(table_out.shape[0]):
        cells = jnp.broadcast_to(cells_in[owner : owner + 1, :], (CLASSES, 128))
        chosen = jnp.take_along_axis(demand, cells, axis=1)
        for level in range(table_out.shape[1]):
            table_out[owner, level] = chosen


def fragility_kernel(
    table_ref, slot_ref, kind_ref, city_ref, amplify_ref, median_ref, spread_ref, out_ref, gain_ref, tables_ref
):
    sources = table_ref.shape[0]
    slot, kind, city = slot_ref[...], kind_ref[...], city_ref[...]
    column = slot % 128
    key = (slot // 128) * CLASSES + kind
    demand = jnp.zeros((8, 128), F32)
    for source in range(sources):
        for each in range(CLASSES):
            row = jnp.broadcast_to(table_ref[source, 0, each : each + 1, :], (8, 128))
            found = jnp.take_along_axis(row, column, axis=1)
            demand = jnp.where(key == source * CLASSES + each, found, demand)
    gain_ref[...] = jnp.ones((8, 128), F32)
    gain_ref[0:1, 0:CITIES] = amplify_ref[...]
    gain = jnp.log(jnp.broadcast_to(gain_ref[0:1, :], (8, 128)))
    demand = demand + jnp.take_along_axis(gain, city, axis=1)
    tables_ref[...] = jnp.ones((128, 128), F32)
    batches = median_ref.shape[1]
    tables_ref[0:CLASSES, 0:batches] = median_ref[...]
    medians = tables_ref[...].T
    tables_ref[0:CLASSES, 0:batches] = spread_ref[...]
    spreads = tables_ref[...].T
    for group in range(8):
        level = jnp.broadcast_to(demand[group : group + 1, :], (8, 128))
        index = jnp.broadcast_to(kind[group : group + 1, :], (8, 128))
        for half in range(0, batches, 8):
            middle = jnp.take_along_axis(medians[half : half + 8, :], index, axis=1)
            width = jnp.take_along_axis(spreads[half : half + 8, :], index, axis=1)
            out_ref[half : half + 8, 128 * group : 128 * group + 128] = jax.nn.sigmoid((level - middle) / width)


VM = pl.BlockSpec(memory_space=pltpu.VMEM)


TIMES = {"start": 1.4, "steps_first": 6.7, "steps_second": 6.5, "surface": 4.5, "fragility": 1.0}
FLOPS_A_US = 1.15e9


def call(kernel, name, shapes, args, specs=None, scratch=()):
    out = [s if isinstance(s, jax.ShapeDtypeStruct) else jax.ShapeDtypeStruct(s, F32) for s in shapes]
    return pl.pallas_call(
        kernel,
        out_shape=out,
        in_specs=specs or [VM] * len(args),
        out_specs=[VM] * len(out),
        scratch_shapes=list(scratch),
        compiler_params=pltpu.CompilerParams(vmem_limit_bytes=VMEM_LIMIT),
        cost_estimate=pl.CostEstimate(flops=int(TIMES.get(name, 0.3) * FLOPS_A_US), bytes_accessed=0, transcendentals=0),
        name=name,
    )(*args)


def both_ways(to_up, to_down, axis):
    count = lax.axis_size(axis)
    forward = [(i, i + 1) for i in range(count - 1)]
    backward = [(i + 1, i) for i in range(count - 1)]
    return lax.ppermute(to_up, axis, forward), lax.ppermute(to_down, axis, backward)


def exchange_x(u, p, faces, coefficients):
    extra = list(coefficients)
    z_low, z_high = both_ways(faces, faces, "gz")
    planes = 3 * XU + (3 + len(extra)) * XP + XH + 1
    message = jax.ShapeDtypeStruct((planes, 16, 128), jnp.int16)
    halo, up, down, powers = call(
        functools.partial(x_message_kernel, bool(extra)),
        "x_message",
        [(8, 16, 128), message, message, (16, 128)],
        [z_low, z_high, u, p] + extra,
    )
    return halo, powers, *both_ways(up, down, "gx")


def y_messages(u, p, coefficients, halo, powers, x_low, x_high):
    extra = list(coefficients)
    planes = (3 * YU + (3 + len(extra)) * YP + YH) // 2 + 1
    message = jax.ShapeDtypeStruct((planes, 16, 128), jnp.int16)
    return call(
        functools.partial(y_message_kernel, bool(extra)),
        "y_message",
        [message, message],
        [u, p] + extra + [halo, powers, x_low, x_high],
    )


def body(
    displacement,
    previous,
    courant,
    damping,
    send_cells,
    building_slot,
    building_class,
    city,
    mode_count,
    modal_filter,
    amplify,
    median,
    spread,
):
    own = (3, 8, 16, 128)
    plane = (8, 16, 128)
    wide = pltpu.VMEM((2, 4, 24, 48, 128), F32)
    samples = pltpu.VMEM((HALF, 24, 16, 128), F32)

    u, p, a, e, faces = call(
        start_kernel,
        "start",
        [own, own, plane, plane, plane],
        [displacement, previous, courant, damping],
        specs=[pl.BlockSpec(memory_space=pltpu.HBM)] * 4,
        scratch=[pltpu.VMEM(plane, F32)] * 2 + [pltpu.SemaphoreType.DMA((8,))],
    )
    halo, powers, x_low, x_high = exchange_x(u, p, faces, (a, e))
    messages = y_messages(u, p, (a, e), halo, powers, x_low, x_high)
    received = (halo, x_low, x_high, *both_ways(*messages, "gy"))
    weights = jnp.asarray(depth_weights(), jnp.bfloat16)
    u, p, faces, slab, seen, rates = call(
        functools.partial(steps_kernel, True),
        "steps_first",
        [own, own, plane, plane, plane, (4, 24, 32, 128)],
        [u, p, a, e, *received, weights],
        scratch=[wide, samples],
    )

    near_low, near_high = both_ways(slab, slab, "gx")
    halo, powers, x_low, x_high = exchange_x(u, p, faces, ())
    slab_messages = call(slab_message_kernel, "slab_message", [(24, 8, 128)] * 2, [slab, near_low, near_high, powers])
    side_low, side_high = both_ways(*slab_messages, "gy")
    messages = y_messages(u, p, (), halo, powers, x_low, x_high)
    received = (halo, x_low, x_high, *both_ways(*messages, "gy"))
    owners, levels = lax.axis_size("gx"), lax.axis_size("gz")
    (table,) = call(
        surface_kernel,
        "surface",
        [(owners, levels, CLASSES, 128)],
        [slab, near_low, near_high, side_low, side_high, jnp.asarray(slab_weights(), jnp.bfloat16), rates, seen]
        + [send_cells.reshape(owners, 128), modal_filter.T, mode_count.reshape(1, CLASSES), messages[0]],
        specs=[VM] * 11 + [pl.BlockSpec(memory_space=pl.ANY)],
        scratch=[
            pltpu.VMEM((2, 24, 48, 128), F32),
            pltpu.VMEM((2, 24, 32, 128), F32),
            samples,
            pltpu.VMEM(plane, F32),
            pltpu.VMEM((3 * STEPS, CLASSES * MODES), F32),
            pltpu.VMEM((8, 128), jnp.int32),
        ],
    )
    table = table.reshape(owners * levels, CLASSES, 128)
    table = lax.all_to_all(table, ("gx", "gz"), split_axis=0, concat_axis=0, tiled=True)
    (field,) = call(
        functools.partial(steps_kernel, False), "steps_second", [own], [u, p, *received, weights, rates], scratch=[wide]
    )
    (probability,) = call(
        fragility_kernel,
        "fragility",
        [(16, 1024)],
        [
            table.reshape(owners, levels, CLASSES, 128),
            building_slot.reshape(8, 128),
            building_class.reshape(8, 128),
            city.reshape(8, 128),
            amplify.reshape(1, CITIES),
            median.T,
            spread.T,
        ],
        scratch=[pltpu.VMEM((8, 128), F32), pltpu.VMEM((128, 128), F32)],
    )
    return (field, probability)


def solution(mesh):
    placed = (
        P(None, "gx", "gy", "gz"),
        P(None, "gx", "gy", "gz"),
        P("gx", "gy", "gz"),
        P("gx", "gy", "gz"),
        P("gx", "gy", None),
        P(("gx", "gy", "gz")),
        P(("gx", "gy", "gz")),
        P(("gx", "gy", "gz")),
        P(),
        P(),
        P(),
        P(),
        P(),
    )
    return jax.shard_map(
        body,
        mesh=mesh,
        in_specs=placed,
        out_specs=(P(None, "gx", "gy", "gz"), P(None, ("gx", "gy", "gz"))),
        check_vma=False,
    )
```

```python
import functools

import jax
import jax.numpy as jnp
import numpy as np
from jax import lax
from jax.experimental import pallas as pl
from jax.experimental.pallas import tpu as pltpu
from jax.sharding import PartitionSpec as P

STEPS = 8
HALF = 4
DEEP = 2 * HALF
CLASSES = 8
MODES = 8
CITIES = 16
F32 = jnp.float32
VMEM_LIMIT = 24 * 1024 * 1024

XU, XP, XH = 8, 6, 7
YU, YP, YH = 24, 20, 20

FULL = 32000.0
BIAS = 200
UNIT_A = 2.0 / FULL
UNIT_E = 0.2 / 12.0 / FULL


PLANES = 4


def depth_weights():
    lanes = np.arange(256)
    result = np.zeros((3, 256, 256), np.float32)
    for k in range(3):
        at = lanes - 128 - 16 * k
        depth = np.where(lanes < 128, lanes, np.where(at < 8, at - 8, at + 120))
        used = (lanes < 128) | ((at >= 0) & (at < 16))
        apart = np.abs(depth[:, None] - depth[None, :])
        band = np.where(apart == 0, -90.0, np.where(apart == 1, 16.0, np.where(apart == 2, -1.0, 0.0)))
        result[k] = np.where(used[:, None] & used[None, :], band, 0.0)
        result[k, 0, 128 + 64 + 16 * k + 8] = 1.0
    return result


def slab_weights():
    lanes = np.arange(128)
    apart = np.abs(lanes[:, None] - lanes[None, :])
    band = np.where(apart == 0, -90.0, np.where(apart == 1, 16.0, np.where(apart == 2, -1.0, 0.0)))
    same = (lanes[:, None] // 16 == lanes[None, :] // 16) & (lanes[:, None] < 48)
    band = np.where(same, band, 0.0)
    return np.concatenate([band, band], axis=0)


def split(v):
    high = v.astype(jnp.bfloat16)
    return high, (v - high.astype(F32)).astype(jnp.bfloat16)


def lane_of():
    return lax.broadcasted_iota(jnp.int32, (8, 128), 1)


def pack_faces(values, lane):
    packed = pltpu.roll(values[0], 8, 1)
    for at in range(1, len(values)):
        packed = jnp.where(lane // 16 == at, pltpu.roll(values[at], (16 * at + 8) % 128, 1), packed)
    return packed


def start_kernel(u_in, p_in, c_in, d_in, u_ref, p_ref, a_ref, e_ref, face_ref, c_ref, d_ref, sems):
    copies = [pltpu.make_async_copy(c_in, c_ref, sems.at[0]), pltpu.make_async_copy(d_in, d_ref, sems.at[1])]
    for k in range(3):
        copies.append(pltpu.make_async_copy(u_in.at[k], u_ref.at[k], sems.at[2 + k]))
        copies.append(pltpu.make_async_copy(p_in.at[k], p_ref.at[k], sems.at[5 + k]))
    for copy in copies:
        copy.start()
    for copy in copies:
        copy.wait()
    lane = lane_of()

    def plane(x, carry):
        for row in (0, 8):
            rows = pl.ds(row, 8)
            share = 1.0 / (1.0 + d_ref[x, rows, :])
            values = [u_ref[k, x, rows, :] for k in range(3)] + [p_ref[k, x, rows, :] for k in range(3)]
            values += [2.0 * share, c_ref[x, rows, :] * share * (1.0 / 12.0)]
            a_ref[x, rows, :] = values[6]
            e_ref[x, rows, :] = values[7]
            face_ref[x, rows, :] = pack_faces(values, lane)
        return carry

    lax.fori_loop(0, 8, plane, 0)


def exponent_of(peak):
    peak = jnp.maximum(jnp.max(peak, axis=0, keepdims=True), 1e-30)
    return jnp.broadcast_to(jnp.ceil(jnp.log2(peak)), (8, 128))


def coded(values):
    return jnp.round(values).astype(jnp.int32).astype(jnp.int16)


def decoded(values):
    return values.astype(jnp.int32).astype(F32)


def twice(rows):
    return jnp.concatenate([rows, rows], axis=0)


def sent_exponents(message):
    both = decoded(message[message.shape[0] - 1]) - BIAS
    return both[0:8], both[8:16]


def x_message_kernel(coefficients, *refs):
    if coefficients:
        z_low_ref, z_high_ref, u_ref, p_ref, a_ref, e_ref, halo_ref, up_ref, down_ref, power_ref = refs
    else:
        z_low_ref, z_high_ref, u_ref, p_ref, halo_ref, up_ref, down_ref, power_ref = refs
    inner = lax.broadcasted_iota(jnp.int32, (16, 128), 1) % 16

    def largest(x, carry):
        field, face = carry
        for k in range(3):
            both = jnp.maximum(jnp.abs(u_ref[k, x]), jnp.abs(p_ref[k, x]))
            field = jnp.maximum(field, jnp.maximum(both[0:8], both[8:16]))
        halo = jnp.where(inner < 8, z_low_ref[x], z_high_ref[x])
        halo_ref[x] = halo
        halo = jnp.abs(halo)
        return field, jnp.maximum(face, jnp.maximum(halo[0:8], halo[8:16]))

    zero = jnp.zeros((8, 128), F32)
    field, face = lax.fori_loop(0, 8, largest, (zero, zero))
    powers = jnp.concatenate([exponent_of(field), exponent_of(face)], axis=0)
    power_ref[...] = powers
    up_ref[up_ref.shape[0] - 1] = coded(powers + BIAS)
    down_ref[down_ref.shape[0] - 1] = coded(powers + BIAS)
    scale = FULL * jnp.exp2(-powers)
    field, face = twice(scale[0:8]), twice(scale[8:16])

    def whole(x, carry):
        for k in range(3):
            code = coded(u_ref[k, x] * field)
            up_ref[XU * k + x] = code
            down_ref[XU * k + x] = code
        return carry

    def part(i, carry):
        parts = [(p_ref.at[k], field) for k in range(3)]
        if coefficients:
            parts += [(a_ref, 1.0 / UNIT_A), (e_ref, 1.0 / UNIT_E)]
        for at, (source, unit) in enumerate(parts):
            up_ref[3 * XU + XP * at + i] = coded(source[8 - XP + i] * unit)
            down_ref[3 * XU + XP * at + i] = coded(source[i] * unit)
        return carry

    at = 3 * XU + (5 if coefficients else 3) * XP

    def side(i, carry):
        up_ref[at + i] = coded(halo_ref[8 - XH + i] * face)
        down_ref[at + i] = coded(halo_ref[i] * face)
        return carry

    lax.fori_loop(0, 8, whole, 0)
    lax.fori_loop(0, XP, part, 0)
    lax.fori_loop(0, XH, side, 0)


def y_message_kernel(coefficients, *refs):
    if coefficients:
        u_ref, p_ref, a_ref, e_ref, halo_ref, power_ref, low_ref, high_ref, up_ref, down_ref = refs
    else:
        u_ref, p_ref, halo_ref, power_ref, low_ref, high_ref, up_ref, down_ref = refs
    powers = power_ref[...]
    low_powers = jnp.concatenate(sent_exponents(low_ref), axis=0)
    high_powers = jnp.concatenate(sent_exponents(high_ref), axis=0)
    most = jnp.maximum(powers, jnp.maximum(low_powers, high_powers))
    for out_ref in (up_ref, down_ref):
        out_ref[out_ref.shape[0] - 1] = coded(most + BIAS)
    own_scale = FULL * jnp.exp2(-most)
    low_scale = jnp.exp2(low_powers - most)
    high_scale = jnp.exp2(high_powers - most)
    field = [twice(scale[0:8]) for scale in (own_scale, low_scale, high_scale)]
    face = [twice(scale[8:16]) for scale in (own_scale, low_scale, high_scale)]

    def put(at, pair):
        up_ref[at] = coded(jnp.concatenate([pair[0][8:16], pair[1][8:16]], axis=0))
        down_ref[at] = coded(jnp.concatenate([pair[0][0:8], pair[1][0:8]], axis=0))

    def group(parts, x_planes, y_planes, x_at, y_at):
        side = (y_planes - 8) // 4

        def own(i, carry):
            for at, (source, units) in enumerate(parts):
                put(y_at + at * y_planes // 2 + side + i, [source[2 * i + j] * units[0] for j in (0, 1)])
            return carry

        def sides(i, carry):
            for at, (_, units) in enumerate(parts):
                start = x_at + at * x_planes
                first = start + x_planes - 2 * side + 2 * i
                put(y_at + at * y_planes // 2 + i, [decoded(low_ref[first + j]) * units[1] for j in (0, 1)])
                first = start + 2 * i
                pair = [decoded(high_ref[first + j]) * units[2] for j in (0, 1)]
                put(y_at + at * y_planes // 2 + side + 4 + i, pair)
            return carry

        lax.fori_loop(0, 4, own, 0)
        lax.fori_loop(0, side, sides, 0)
        return x_at + len(parts) * x_planes, y_at + len(parts) * y_planes // 2

    x_at, y_at = group([(u_ref.at[k], field) for k in range(3)], XU, YU, 0, 0)
    parts = [(p_ref.at[k], field) for k in range(3)]
    if coefficients:
        parts += [(a_ref, (1.0 / UNIT_A, 1.0, 1.0)), (e_ref, (1.0 / UNIT_E, 1.0, 1.0))]
    x_at, y_at = group(parts, XP, YP, x_at, y_at)
    group([(halo_ref, face)], XH, YH, x_at, y_at)


def fill(parts, x_low, x_high, y_low, y_high, x_at, x_planes, y_at, y_planes):
    count = len(parts)
    side = (y_planes - 8) // 2

    def own(i, carry):
        for target, row, block, _ in parts:
            target[8 + i, row + 8 : row + 24, :] = block[i]
        return carry

    def x_side(i, carry):
        for at, (target, row, _, units) in enumerate(parts):
            here = x_at + at * x_planes + i
            target[8 - x_planes + i, row + 8 : row + 24, :] = decoded(x_low[here]) * units[0]
            target[16 + i, row + 8 : row + 24, :] = decoded(x_high[here]) * units[1]
        return carry

    def y_side(i, carry):
        for at, (target, row, _, units) in enumerate(parts):
            here = y_at + at * y_planes // 2 + i
            low = decoded(y_low[here]) * units[2]
            high = decoded(y_high[here]) * units[3]
            for j in (0, 1):
                target[8 - side + 2 * i + j, row : row + 8, :] = low[8 * j : 8 * j + 8]
                target[8 - side + 2 * i + j, row + 24 : row + 32, :] = high[8 * j : 8 * j + 8]
        return carry

    lax.fori_loop(0, 8, own, 0, unroll=2)
    lax.fori_loop(0, x_planes, x_side, 0)
    lax.fori_loop(0, y_planes // 2, y_side, 0, unroll=2)
    return x_at + count * x_planes, y_at + count * y_planes // 2


def steps_kernel(first, *refs):
    if first:
        (u_in, p_in, a_in, e_in, halo_in, x_low, x_high, y_low, y_high, weight_in) = refs[:10]
        (u_out, p_out, face_out, slab_out, seen_out, rate_ref) = refs[10:16]
        state_ref, edge_ref = refs[16:]
    else:
        (u_in, p_in, halo_in, x_low, x_high, y_low, y_high, weight_in, rate_ref) = refs[:9]
        u_out, state_ref = refs[9:]
    a_ref, e_ref, ha_ref, he_ref = (rate_ref.at[at] for at in range(4))
    lane = lane_of()
    inner = lane % 16

    sides = (x_low, x_high, y_low, y_high)
    powers = [sent_exponents(message) for message in sides]
    field = [twice(jnp.exp2(power[0]) * (1.0 / FULL)) for power in powers]
    face = [twice(jnp.exp2(power[1]) * (1.0 / FULL)) for power in powers]
    x_at, y_at = fill([(state_ref.at[0, k], 8, u_in.at[k], field) for k in range(3)], *sides, 0, XU, 0, YU)
    parts = [(state_ref.at[1, k], 8, p_in.at[k], field) for k in range(3)]
    if first:
        parts += [(a_ref, 0, a_in, (UNIT_A,) * 4), (e_ref, 0, e_in, (UNIT_E,) * 4)]
    x_at, y_at = fill(parts, *sides, x_at, XP, y_at, YP)
    fill([(state_ref.at[0, 3], 8, halo_in, face)], *sides, x_at, XH, y_at, YH)

    def prepare(x, carry):
        for tile in range(4):
            rows = pl.ds(8 + 8 * tile, 8)
            held = pl.ds(8 * tile, 8)
            halo = state_ref[0, 3, x, rows, :]
            state_ref[0, 3, x, rows, :] = jnp.where(lane < 48, halo, 0.0)
            state_ref[1, 3, x, rows, :] = jnp.where(lane < 48, pltpu.roll(halo, 128 - 48, 1), 0.0)
            if first:
                for target, at in ((ha_ref, 96), (he_ref, 112)):
                    spread = jnp.where(lane < 16, pltpu.roll(halo, 128 - at, 1), pltpu.roll(halo, 144 - at, 1))
                    spread = jnp.where(lane < 32, spread, pltpu.roll(halo, 160 - at, 1))
                    target[x, held, :] = jnp.where(lane < 48, spread, 0.0)
        return carry

    lax.fori_loop(2, 22, prepare, 0, unroll=4)

    def advance(src, dst, x):
        rows = pl.ds(8, 32)
        fields = [[src[k, 2 + j, rows, :] for j in range(PLANES)] for k in range(4)]
        parts = [[split(v) for v in field] for field in fields]
        depth = []
        for k in range(3):
            pieces = [jnp.concatenate([parts[k][j][part], parts[3][j][part]], axis=1) for part in (0, 1) for j in range(PLANES)]
            both = jnp.dot(jnp.concatenate(pieces, axis=0), weight_in[k], preferred_element_type=F32)
            depth.append(both[0 : 32 * PLANES] + both[32 * PLANES :])
        side = depth[0][:, 128:] + depth[1][:, 128:] + depth[2][:, 128:]
        fresh = []
        for j in range(PLANES):
            for k in range(4):
                v = fields[k][j]
                near = (src[k, 1 + j, rows, :] + src[k, 3 + j, rows, :]) + (
                    src[k, 2 + j, pl.ds(7, 32), :] + src[k, 2 + j, pl.ds(9, 32), :]
                )
                far = (src[k, j, rows, :] + src[k, 4 + j, rows, :]) + (
                    src[k, 2 + j, pl.ds(6, 32), :] + src[k, 2 + j, pl.ds(10, 32), :]
                )
                along = side if k == 3 else depth[k][:, :128]
                laplace = along[32 * j : 32 * j + 32] + (16.0 * near - far)
                old = dst[k, x + j, rows, :]
                a_each, e_each = (ha_ref, he_ref) if k == 3 else (a_ref, e_ref)
                fresh.append((k, j, old + a_each[x + j] * (v - old) + e_each[x + j] * laplace))
        return fresh, side

    def one_step(step, carry):
        dst = state_ref.at[(step + 1) % 2]

        def planes(at, inside):
            x = 2 * step + 2 + PLANES * at
            fresh, side = advance(state_ref.at[step % 2, :, pl.ds(x - 2, 4 + PLANES)], dst, x)
            for k, j, value in fresh:
                dst[k, x + j, 8:40, :] = value
            if first:
                for j in range(PLANES):
                    edge_ref[step, x + j, :, :] = side[32 * j + 8 : 32 * j + 24]
            return inside

        lax.fori_loop(0, (20 - 4 * step) // PLANES, planes, 0)
        return carry

    lax.fori_loop(0, HALF, one_step, 0)

    block = pl.ds(16, 16)

    def finish(x, carry):
        for k in range(3):
            u_out[k, x, :, :] = state_ref[0, k, 8 + x, block, :]
            if first:
                p_out[k, x, :, :] = state_ref[1, k, 8 + x, block, :]
        if first:
            for row in (0, 8):
                rows = pl.ds(row, 8)
                values = [state_ref[slot, k, 8 + x, pl.ds(16 + row, 8), :] for slot in (0, 1) for k in range(3)]
                last = pack_faces(values, lane)
                face_out[x, rows, :] = last
                slab = values[0]
                for at in range(1, 6):
                    slab = jnp.where(lane // 16 == at, pltpu.roll(values[at], 16 * at, 1), slab)
                slab_out[x, rows, :] = slab
                seen = jnp.zeros((8, 128), F32)
                for step in range(HALF):
                    if step < HALF - 1:
                        sample = pltpu.roll(edge_ref[step + 1, 8 + x, rows, :], 56 + step, 1)
                    else:
                        sample = pltpu.roll(last, 120 + step, 1)
                    seen = jnp.where((inner == step) & (lane < 48), sample, seen)
                seen_out[x, rows, :] = seen
        return carry

    lax.fori_loop(0, 8, finish, 0, unroll=4)


def slab_message_kernel(own_ref, low_ref, high_ref, after_ref, up_ref, down_ref):
    def plane(i, carry):
        for at, source in ((0, low_ref), (8, own_ref), (16, high_ref)):
            up_ref[at + i] = source[i, 8:16, :]
            down_ref[at + i] = source[i, 0:8, :]
        return carry

    lax.fori_loop(0, 8, plane, 0, unroll=2)


def surface_kernel(
    own_in, x_low, x_high, y_low, y_high, weight_in, rate_in, seen_in, cells_in, filter_in, count_in, after_in,
    table_out, state_ref, rate_ref, sample_ref, seen_ref, filter_ref, count_ref,
):
    lane = lane_of()
    inner = lane % 16

    def near_side(i, carry):
        state_ref[0, i, 16:32, :] = x_low[i]
        state_ref[0, 8 + i, 16:32, :] = own_in[i]
        state_ref[0, 16 + i, 16:32, :] = x_high[i]
        for part in range(3):
            state_ref[0, 8 * part + i, 8:16, :] = y_low[8 * part + i]
            state_ref[0, 8 * part + i, 32:40, :] = y_high[8 * part + i]
        return carry

    lax.fori_loop(0, 8, near_side, 0, unroll=2)

    def prepare(x, carry):
        for tile in range(4):
            rows = pl.ds(8 + 8 * tile, 8)
            held = pl.ds(8 * tile, 8)
            value = state_ref[0, x, rows, :]
            state_ref[0, x, rows, :] = jnp.where(lane < 48, value, 0.0)
            state_ref[1, x, rows, :] = jnp.where(lane < 48, pltpu.roll(value, 128 - 48, 1), 0.0)
            for at in (0, 1):
                rate = rate_in[at, x, held, :]
                spread = jnp.where(lane < 16, rate, jnp.where(lane < 32, pltpu.roll(rate, 16, 1), pltpu.roll(rate, 32, 1)))
                rate_ref[at, x, held, :] = jnp.where(lane < 48, spread, 0.0)
        return carry

    lax.fori_loop(0, 24, prepare, 0, unroll=4)

    def one_step(step, carry):
        dst = state_ref.at[(step + 1) % 2]

        def planes(at, inside):
            x = 2 * step + 2 + PLANES * at
            src = state_ref.at[step % 2, pl.ds(x - 2, 4 + PLANES)]
            rows = pl.ds(8, 32)
            fields = [src[2 + j, rows, :] for j in range(PLANES)]
            halves = jnp.concatenate([jnp.concatenate(split(v), axis=1) for v in fields], axis=0)
            depth = jnp.dot(halves, weight_in[...], preferred_element_type=F32)
            fresh = []
            for j, v in enumerate(fields):
                near = (src[1 + j, rows, :] + src[3 + j, rows, :]) + (src[2 + j, pl.ds(7, 32), :] + src[2 + j, pl.ds(9, 32), :])
                far = (src[j, rows, :] + src[4 + j, rows, :]) + (src[2 + j, pl.ds(6, 32), :] + src[2 + j, pl.ds(10, 32), :])
                laplace = depth[32 * j : 32 * j + 32] + (16.0 * near - far)
                old = dst[x + j, rows, :]
                fresh.append(old + rate_ref[0, x + j] * (v - old) + rate_ref[1, x + j] * laplace)
            for j, value in enumerate(fresh):
                dst[x + j, 8:40, :] = value
                sample_ref[step, x + j, :, :] = value[8:24]
            return inside

        lax.fori_loop(0, (20 - 4 * step) // PLANES, planes, 0)
        return carry

    lax.fori_loop(0, HALF, one_step, 0)

    def finish(x, carry):
        for row in (0, 8):
            rows = pl.ds(row, 8)
            seen = seen_in[x, rows, :]
            for step in range(HALF):
                at = HALF + step
                sample = pltpu.roll(sample_ref[step, 8 + x, rows, :], at, 1)
                seen = jnp.where((inner == at) & (lane < 48), sample, seen)
            seen_ref[x, rows, :] = seen
        return carry

    lax.fori_loop(0, 8, finish, 0, unroll=4)

    filter_ref[...] = filter_in[...].astype(F32)
    blocks = [jnp.zeros((8, CLASSES * MODES), F32)] * 16
    for k in range(3):
        blocks[2 * k] = filter_ref[pl.ds(k, STEPS, stride=3), :]
    filters = jnp.concatenate(blocks, axis=0).astype(jnp.bfloat16)
    motion = seen_ref[...].reshape(128, 128).astype(jnp.bfloat16)
    modal = lax.dot_general(filters, motion, (((0,), (1,)), ((), ())), preferred_element_type=F32)
    modes = lax.broadcasted_iota(jnp.int32, (MODES, 128), 0)
    count_ref[...] = jnp.zeros((8, 128), jnp.int32)
    count_ref[0:1, 0:CLASSES] = count_in[...]
    counts = jnp.where(modes == lane, jnp.broadcast_to(count_ref[0:1, :], (8, 128)), 0)
    counts = jnp.sum(counts, axis=1, keepdims=True)
    energies = []
    for kind in range(CLASSES):
        part = modal[MODES * kind : MODES * (kind + 1), :]
        part = jnp.where(modes < counts[kind : kind + 1, :], part * part, 0.0)
        energies.append(jnp.sum(part, axis=0, keepdims=True))
    demand = 0.5 * jnp.log1p(jnp.concatenate(energies, axis=0))
    for owner in range(table_out.shape[0]):
        cells = jnp.broadcast_to(cells_in[owner : owner + 1, :], (CLASSES, 128))
        chosen = jnp.take_along_axis(demand, cells, axis=1)
        for level in range(table_out.shape[1]):
            table_out[owner, level] = chosen


def fragility_kernel(
    table_ref, slot_ref, kind_ref, city_ref, amplify_ref, median_ref, spread_ref, out_ref, gain_ref, tables_ref
):
    sources = table_ref.shape[0]
    slot, kind, city = slot_ref[...], kind_ref[...], city_ref[...]
    column = slot % 128
    key = (slot // 128) * CLASSES + kind
    demand = jnp.zeros((8, 128), F32)
    for source in range(sources):
        for each in range(CLASSES):
            row = jnp.broadcast_to(table_ref[source, 0, each : each + 1, :], (8, 128))
            found = jnp.take_along_axis(row, column, axis=1)
            demand = jnp.where(key == source * CLASSES + each, found, demand)
    gain_ref[...] = jnp.ones((8, 128), F32)
    gain_ref[0:1, 0:CITIES] = amplify_ref[...]
    gain = jnp.log(jnp.broadcast_to(gain_ref[0:1, :], (8, 128)))
    demand = demand + jnp.take_along_axis(gain, city, axis=1)
    tables_ref[...] = jnp.ones((128, 128), F32)
    batches = median_ref.shape[1]
    tables_ref[0:CLASSES, 0:batches] = median_ref[...]
    medians = tables_ref[...].T
    tables_ref[0:CLASSES, 0:batches] = spread_ref[...]
    spreads = tables_ref[...].T
    for group in range(8):
        level = jnp.broadcast_to(demand[group : group + 1, :], (8, 128))
        index = jnp.broadcast_to(kind[group : group + 1, :], (8, 128))
        for half in range(0, batches, 8):
            middle = jnp.take_along_axis(medians[half : half + 8, :], index, axis=1)
            width = jnp.take_along_axis(spreads[half : half + 8, :], index, axis=1)
            out_ref[half : half + 8, 128 * group : 128 * group + 128] = jax.nn.sigmoid((level - middle) / width)


VM = pl.BlockSpec(memory_space=pltpu.VMEM)


TIMES = {"start": 1.4, "steps_first": 6.7, "steps_second": 6.5, "surface": 4.5, "fragility": 1.0}
FLOPS_A_US = 1.15e10


def call(kernel, name, shapes, args, specs=None, scratch=()):
    out = [s if isinstance(s, jax.ShapeDtypeStruct) else jax.ShapeDtypeStruct(s, F32) for s in shapes]
    return pl.pallas_call(
        kernel,
        out_shape=out,
        in_specs=specs or [VM] * len(args),
        out_specs=[VM] * len(out),
        scratch_shapes=list(scratch),
        compiler_params=pltpu.CompilerParams(vmem_limit_bytes=VMEM_LIMIT),
        cost_estimate=pl.CostEstimate(flops=int(TIMES.get(name, 0.3) * FLOPS_A_US), bytes_accessed=0, transcendentals=0),
        name=name,
    )(*args)


def both_ways(to_up, to_down, axis):
    count = lax.axis_size(axis)
    forward = [(i, i + 1) for i in range(count - 1)]
    backward = [(i + 1, i) for i in range(count - 1)]
    return lax.ppermute(to_up, axis, forward), lax.ppermute(to_down, axis, backward)


def exchange_x(u, p, faces, coefficients):
    extra = list(coefficients)
    z_low, z_high = both_ways(faces, faces, "gz")
    planes = 3 * XU + (3 + len(extra)) * XP + XH + 1
    message = jax.ShapeDtypeStruct((planes, 16, 128), jnp.int16)
    halo, up, down, powers = call(
        functools.partial(x_message_kernel, bool(extra)),
        "x_message",
        [(8, 16, 128), message, message, (16, 128)],
        [z_low, z_high, u, p] + extra,
    )
    return halo, powers, *both_ways(up, down, "gx")


def y_messages(u, p, coefficients, halo, powers, x_low, x_high):
    extra = list(coefficients)
    planes = (3 * YU + (3 + len(extra)) * YP + YH) // 2 + 1
    message = jax.ShapeDtypeStruct((planes, 16, 128), jnp.int16)
    return call(
        functools.partial(y_message_kernel, bool(extra)),
        "y_message",
        [message, message],
        [u, p] + extra + [halo, powers, x_low, x_high],
    )


def body(
    displacement,
    previous,
    courant,
    damping,
    send_cells,
    building_slot,
    building_class,
    city,
    mode_count,
    modal_filter,
    amplify,
    median,
    spread,
):
    own = (3, 8, 16, 128)
    plane = (8, 16, 128)
    wide = pltpu.VMEM((2, 4, 24, 48, 128), F32)
    samples = pltpu.VMEM((HALF, 24, 16, 128), F32)

    u, p, a, e, faces = call(
        start_kernel,
        "start",
        [own, own, plane, plane, plane],
        [displacement, previous, courant, damping],
        specs=[pl.BlockSpec(memory_space=pltpu.HBM)] * 4,
        scratch=[pltpu.VMEM(plane, F32)] * 2 + [pltpu.SemaphoreType.DMA((8,))],
    )
    halo, powers, x_low, x_high = exchange_x(u, p, faces, (a, e))
    messages = y_messages(u, p, (a, e), halo, powers, x_low, x_high)
    received = (halo, x_low, x_high, *both_ways(*messages, "gy"))
    weights = jnp.asarray(depth_weights(), jnp.bfloat16)
    u, p, faces, slab, seen, rates = call(
        functools.partial(steps_kernel, True),
        "steps_first",
        [own, own, plane, plane, plane, (4, 24, 32, 128)],
        [u, p, a, e, *received, weights],
        scratch=[wide, samples],
    )

    near_low, near_high = both_ways(slab, slab, "gx")
    halo, powers, x_low, x_high = exchange_x(u, p, faces, ())
    slab_messages = call(slab_message_kernel, "slab_message", [(24, 8, 128)] * 2, [slab, near_low, near_high, powers])
    side_low, side_high = both_ways(*slab_messages, "gy")
    messages = y_messages(u, p, (), halo, powers, x_low, x_high)
    received = (halo, x_low, x_high, *both_ways(*messages, "gy"))
    owners, levels = lax.axis_size("gx"), lax.axis_size("gz")
    (table,) = call(
        surface_kernel,
        "surface",
        [(owners, levels, CLASSES, 128)],
        [slab, near_low, near_high, side_low, side_high, jnp.asarray(slab_weights(), jnp.bfloat16), rates, seen]
        + [send_cells.reshape(owners, 128), modal_filter.T, mode_count.reshape(1, CLASSES), messages[0]],
        specs=[VM] * 11 + [pl.BlockSpec(memory_space=pl.ANY)],
        scratch=[
            pltpu.VMEM((2, 24, 48, 128), F32),
            pltpu.VMEM((2, 24, 32, 128), F32),
            samples,
            pltpu.VMEM(plane, F32),
            pltpu.VMEM((3 * STEPS, CLASSES * MODES), F32),
            pltpu.VMEM((8, 128), jnp.int32),
        ],
    )
    table = table.reshape(owners * levels, CLASSES, 128)
    table = lax.all_to_all(table, ("gx", "gz"), split_axis=0, concat_axis=0, tiled=True)
    (field,) = call(
        functools.partial(steps_kernel, False), "steps_second", [own], [u, p, *received, weights, rates], scratch=[wide]
    )
    (probability,) = call(
        fragility_kernel,
        "fragility",
        [(16, 1024)],
        [
            table.reshape(owners, levels, CLASSES, 128),
            building_slot.reshape(8, 128),
            building_class.reshape(8, 128),
            city.reshape(8, 128),
            amplify.reshape(1, CITIES),
            median.T,
            spread.T,
        ],
        scratch=[pltpu.VMEM((8, 128), F32), pltpu.VMEM((128, 128), F32)],
    )
    return (field, probability)


def solution(mesh):
    placed = (
        P(None, "gx", "gy", "gz"),
        P(None, "gx", "gy", "gz"),
        P("gx", "gy", "gz"),
        P("gx", "gy", "gz"),
        P("gx", "gy", None),
        P(("gx", "gy", "gz")),
        P(("gx", "gy", "gz")),
        P(("gx", "gy", "gz")),
        P(),
        P(),
        P(),
        P(),
        P(),
    )
    return jax.shard_map(
        body,
        mesh=mesh,
        in_specs=placed,
        out_specs=(P(None, "gx", "gy", "gz"), P(None, ("gx", "gy", "gz"))),
        check_vma=False,
    )
```

```python
import functools

import jax
import jax.numpy as jnp
import numpy as np
from jax import lax
from jax.experimental import pallas as pl
from jax.experimental.pallas import tpu as pltpu
from jax.sharding import PartitionSpec as P

STEPS = 8
HALF = 4
DEEP = 2 * HALF
CLASSES = 8
MODES = 8
CITIES = 16
F32 = jnp.float32
VMEM_LIMIT = 24 * 1024 * 1024
START_LIMIT = int(53.8 * 1024 * 1024)

XU, XP, XH = 8, 6, 7
YU, YP, YH = 24, 20, 20

FULL = 32000.0
BIAS = 200
UNIT_A = 2.0 / FULL
UNIT_E = 0.2 / 12.0 / FULL


PLANES = 4


def depth_weights():
    lanes = np.arange(256)
    result = np.zeros((3, 256, 256), np.float32)
    for k in range(3):
        at = lanes - 128 - 16 * k
        depth = np.where(lanes < 128, lanes, np.where(at < 8, at - 8, at + 120))
        used = (lanes < 128) | ((at >= 0) & (at < 16))
        apart = np.abs(depth[:, None] - depth[None, :])
        band = np.where(apart == 0, -90.0, np.where(apart == 1, 16.0, np.where(apart == 2, -1.0, 0.0)))
        result[k] = np.where(used[:, None] & used[None, :], band, 0.0)
        result[k, 0, 128 + 64 + 16 * k + 8] = 1.0
    return result


def slab_weights():
    lanes = np.arange(128)
    apart = np.abs(lanes[:, None] - lanes[None, :])
    band = np.where(apart == 0, -90.0, np.where(apart == 1, 16.0, np.where(apart == 2, -1.0, 0.0)))
    same = (lanes[:, None] // 16 == lanes[None, :] // 16) & (lanes[:, None] < 48)
    band = np.where(same, band, 0.0)
    return np.concatenate([band, band], axis=0)


def split(v):
    high = v.astype(jnp.bfloat16)
    return high, (v - high.astype(F32)).astype(jnp.bfloat16)


def lane_of():
    return lax.broadcasted_iota(jnp.int32, (8, 128), 1)


def pack_faces(values, lane):
    packed = pltpu.roll(values[0], 8, 1)
    for at in range(1, len(values)):
        packed = jnp.where(lane // 16 == at, pltpu.roll(values[at], (16 * at + 8) % 128, 1), packed)
    return packed


def start_kernel(u_in, p_in, c_in, d_in, a_ref, e_ref, face_ref, u_ref, p_ref, c_ref, d_ref, sems):
    copies = [pltpu.make_async_copy(c_in, c_ref, sems.at[0]), pltpu.make_async_copy(d_in, d_ref, sems.at[1])]
    for k in range(3):
        copies.append(pltpu.make_async_copy(u_in.at[k], u_ref.at[k], sems.at[2 + k]))
        copies.append(pltpu.make_async_copy(p_in.at[k], p_ref.at[k], sems.at[5 + k]))
    for copy in copies:
        copy.start()
    for copy in copies:
        copy.wait()
    lane = lane_of()

    def plane(x, carry):
        for row in (0, 8):
            rows = pl.ds(row, 8)
            share = 1.0 / (1.0 + d_ref[x, rows, :])
            values = [u_ref[k, x, rows, :] for k in range(3)] + [p_ref[k, x, rows, :] for k in range(3)]
            values += [2.0 * share, c_ref[x, rows, :] * share * (1.0 / 12.0)]
            a_ref[x, rows, :] = values[6]
            e_ref[x, rows, :] = values[7]
            face_ref[x, rows, :] = pack_faces(values, lane)
        return carry

    lax.fori_loop(0, 8, plane, 0)


def exponent_of(peak):
    peak = jnp.maximum(jnp.max(peak, axis=0, keepdims=True), 1e-30)
    return jnp.broadcast_to(jnp.ceil(jnp.log2(peak)), (8, 128))


def coded(values):
    return jnp.round(values).astype(jnp.int32).astype(jnp.int16)


def decoded(values):
    return values.astype(jnp.int32).astype(F32)


def twice(rows):
    return jnp.concatenate([rows, rows], axis=0)


def sent_exponents(message):
    both = decoded(message[message.shape[0] - 1]) - BIAS
    return both[0:8], both[8:16]


def x_message_kernel(coefficients, *refs):
    if coefficients:
        z_low_ref, z_high_ref, u_ref, p_ref, a_ref, e_ref, halo_ref, up_ref, down_ref, power_ref = refs
    else:
        z_low_ref, z_high_ref, u_ref, p_ref, halo_ref, up_ref, down_ref, power_ref = refs
    inner = lax.broadcasted_iota(jnp.int32, (16, 128), 1) % 16

    def largest(x, carry):
        field, face = carry
        for k in range(3):
            both = jnp.maximum(jnp.abs(u_ref[k, x]), jnp.abs(p_ref[k, x]))
            field = jnp.maximum(field, jnp.maximum(both[0:8], both[8:16]))
        halo = jnp.where(inner < 8, z_low_ref[x], z_high_ref[x])
        halo_ref[x] = halo
        halo = jnp.abs(halo)
        return field, jnp.maximum(face, jnp.maximum(halo[0:8], halo[8:16]))

    zero = jnp.zeros((8, 128), F32)
    field, face = lax.fori_loop(0, 8, largest, (zero, zero))
    powers = jnp.concatenate([exponent_of(field), exponent_of(face)], axis=0)
    power_ref[...] = powers
    up_ref[up_ref.shape[0] - 1] = coded(powers + BIAS)
    down_ref[down_ref.shape[0] - 1] = coded(powers + BIAS)
    scale = FULL * jnp.exp2(-powers)
    field, face = twice(scale[0:8]), twice(scale[8:16])

    def whole(x, carry):
        for k in range(3):
            code = coded(u_ref[k, x] * field)
            up_ref[XU * k + x] = code
            down_ref[XU * k + x] = code
        return carry

    def part(i, carry):
        parts = [(p_ref.at[k], field) for k in range(3)]
        if coefficients:
            parts += [(a_ref, 1.0 / UNIT_A), (e_ref, 1.0 / UNIT_E)]
        for at, (source, unit) in enumerate(parts):
            up_ref[3 * XU + XP * at + i] = coded(source[8 - XP + i] * unit)
            down_ref[3 * XU + XP * at + i] = coded(source[i] * unit)
        return carry

    at = 3 * XU + (5 if coefficients else 3) * XP

    def side(i, carry):
        up_ref[at + i] = coded(halo_ref[8 - XH + i] * face)
        down_ref[at + i] = coded(halo_ref[i] * face)
        return carry

    lax.fori_loop(0, 8, whole, 0)
    lax.fori_loop(0, XP, part, 0)
    lax.fori_loop(0, XH, side, 0)


def y_message_kernel(coefficients, *refs):
    if coefficients:
        u_ref, p_ref, a_ref, e_ref, halo_ref, power_ref, low_ref, high_ref, up_ref, down_ref = refs
    else:
        u_ref, p_ref, halo_ref, power_ref, low_ref, high_ref, up_ref, down_ref = refs
    powers = power_ref[...]
    low_powers = jnp.concatenate(sent_exponents(low_ref), axis=0)
    high_powers = jnp.concatenate(sent_exponents(high_ref), axis=0)
    most = jnp.maximum(powers, jnp.maximum(low_powers, high_powers))
    for out_ref in (up_ref, down_ref):
        out_ref[out_ref.shape[0] - 1] = coded(most + BIAS)
    own_scale = FULL * jnp.exp2(-most)
    low_scale = jnp.exp2(low_powers - most)
    high_scale = jnp.exp2(high_powers - most)
    field = [twice(scale[0:8]) for scale in (own_scale, low_scale, high_scale)]
    face = [twice(scale[8:16]) for scale in (own_scale, low_scale, high_scale)]

    def put(at, pair):
        up_ref[at] = coded(jnp.concatenate([pair[0][8:16], pair[1][8:16]], axis=0))
        down_ref[at] = coded(jnp.concatenate([pair[0][0:8], pair[1][0:8]], axis=0))

    def group(parts, x_planes, y_planes, x_at, y_at):
        side = (y_planes - 8) // 4

        def own(i, carry):
            for at, (source, units) in enumerate(parts):
                put(y_at + at * y_planes // 2 + side + i, [source[2 * i + j] * units[0] for j in (0, 1)])
            return carry

        def sides(i, carry):
            for at, (_, units) in enumerate(parts):
                start = x_at + at * x_planes
                first = start + x_planes - 2 * side + 2 * i
                put(y_at + at * y_planes // 2 + i, [decoded(low_ref[first + j]) * units[1] for j in (0, 1)])
                first = start + 2 * i
                pair = [decoded(high_ref[first + j]) * units[2] for j in (0, 1)]
                put(y_at + at * y_planes // 2 + side + 4 + i, pair)
            return carry

        lax.fori_loop(0, 4, own, 0)
        lax.fori_loop(0, side, sides, 0)
        return x_at + len(parts) * x_planes, y_at + len(parts) * y_planes // 2

    x_at, y_at = group([(u_ref.at[k], field) for k in range(3)], XU, YU, 0, 0)
    parts = [(p_ref.at[k], field) for k in range(3)]
    if coefficients:
        parts += [(a_ref, (1.0 / UNIT_A, 1.0, 1.0)), (e_ref, (1.0 / UNIT_E, 1.0, 1.0))]
    x_at, y_at = group(parts, XP, YP, x_at, y_at)
    group([(halo_ref, face)], XH, YH, x_at, y_at)


def fill(parts, x_low, x_high, y_low, y_high, x_at, x_planes, y_at, y_planes):
    count = len(parts)
    side = (y_planes - 8) // 2

    def own(i, carry):
        for target, row, block, _ in parts:
            target[8 + i, row + 8 : row + 24, :] = block[i]
        return carry

    def x_side(i, carry):
        for at, (target, row, _, units) in enumerate(parts):
            here = x_at + at * x_planes + i
            target[8 - x_planes + i, row + 8 : row + 24, :] = decoded(x_low[here]) * units[0]
            target[16 + i, row + 8 : row + 24, :] = decoded(x_high[here]) * units[1]
        return carry

    def y_side(i, carry):
        for at, (target, row, _, units) in enumerate(parts):
            here = y_at + at * y_planes // 2 + i
            low = decoded(y_low[here]) * units[2]
            high = decoded(y_high[here]) * units[3]
            for j in (0, 1):
                target[8 - side + 2 * i + j, row : row + 8, :] = low[8 * j : 8 * j + 8]
                target[8 - side + 2 * i + j, row + 24 : row + 32, :] = high[8 * j : 8 * j + 8]
        return carry

    lax.fori_loop(0, 8, own, 0, unroll=2)
    lax.fori_loop(0, x_planes, x_side, 0)
    lax.fori_loop(0, y_planes // 2, y_side, 0, unroll=2)
    return x_at + count * x_planes, y_at + count * y_planes // 2


def steps_kernel(first, *refs):
    if first:
        (u_in, p_in, a_in, e_in, halo_in, x_low, x_high, y_low, y_high, weight_in) = refs[:10]
        (u_out, p_out, face_out, slab_out, seen_out, code_ref) = refs[10:16]
        state_ref, rate_ref, edge_ref = refs[16:]
    else:
        (u_in, p_in, halo_in, x_low, x_high, y_low, y_high, weight_in, code_ref) = refs[:9]
        u_out, state_ref, rate_ref = refs[9:]
    a_ref, e_ref, ha_ref, he_ref = (rate_ref.at[at] for at in range(4))
    lane = lane_of()
    inner = lane % 16

    sides = (x_low, x_high, y_low, y_high)
    powers = [sent_exponents(message) for message in sides]
    field = [twice(jnp.exp2(power[0]) * (1.0 / FULL)) for power in powers]
    face = [twice(jnp.exp2(power[1]) * (1.0 / FULL)) for power in powers]
    x_at, y_at = fill([(state_ref.at[0, k], 8, u_in.at[k], field) for k in range(3)], *sides, 0, XU, 0, YU)
    parts = [(state_ref.at[1, k], 8, p_in.at[k], field) for k in range(3)]
    if first:
        parts += [(a_ref, 0, a_in, (UNIT_A,) * 4), (e_ref, 0, e_in, (UNIT_E,) * 4)]
    x_at, y_at = fill(parts, *sides, x_at, XP, y_at, YP)
    fill([(state_ref.at[0, 3], 8, halo_in, face)], *sides, x_at, XH, y_at, YH)

    unit = jnp.where(lane < 112, UNIT_A, UNIT_E)

    def prepare(x, carry):
        for half in (0, 16):
            held = pl.ds(half, 16)
            if first:
                code_ref[0, x - 2, held, :] = coded(a_ref[x, held, :] * (1.0 / UNIT_A))
                code_ref[1, x - 2, held, :] = coded(e_ref[x, held, :] * (1.0 / UNIT_E))
                sides = state_ref[0, 3, x, pl.ds(8 + half, 16), :]
                scale = twice(jnp.where(lane < 96, 0.0, 1.0 / unit))
                code_ref[2, x - 2, held, :] = coded(jnp.where(scale > 0.0, sides * scale, 0.0))
            else:
                a_ref[x, held, :] = decoded(code_ref[0, x - 2, held, :]) * UNIT_A
                e_ref[x, held, :] = decoded(code_ref[1, x - 2, held, :]) * UNIT_E
                sides = decoded(code_ref[2, x - 2, held, :]) * twice(unit)
            for tile in (0, 8):
                rows = pl.ds(8 + half + tile, 8)
                halo = state_ref[0, 3, x, rows, :]
                state_ref[0, 3, x, rows, :] = jnp.where(lane < 48, halo, 0.0)
                state_ref[1, 3, x, rows, :] = jnp.where(lane < 48, pltpu.roll(halo, 128 - 48, 1), 0.0)
                side = sides[tile : tile + 8]
                for target, at in ((ha_ref, 96), (he_ref, 112)):
                    spread = jnp.where(lane < 16, pltpu.roll(side, 128 - at, 1), pltpu.roll(side, 144 - at, 1))
                    spread = jnp.where(lane < 32, spread, pltpu.roll(side, 160 - at, 1))
                    target[x, pl.ds(half + tile, 8), :] = jnp.where(lane < 48, spread, 0.0)
        return carry

    lax.fori_loop(2, 22, prepare, 0, unroll=4)

    def advance(src, dst, x):
        rows = pl.ds(8, 32)
        fields = [[src[k, 2 + j, rows, :] for j in range(PLANES)] for k in range(4)]
        parts = [[split(v) for v in field] for field in fields]
        depth = []
        for k in range(3):
            pieces = [jnp.concatenate([parts[k][j][part], parts[3][j][part]], axis=1) for part in (0, 1) for j in range(PLANES)]
            both = jnp.dot(jnp.concatenate(pieces, axis=0), weight_in[k], preferred_element_type=F32)
            depth.append(both[0 : 32 * PLANES] + both[32 * PLANES :])
        side = depth[0][:, 128:] + depth[1][:, 128:] + depth[2][:, 128:]
        fresh = []
        for j in range(PLANES):
            for k in range(4):
                v = fields[k][j]
                near = (src[k, 1 + j, rows, :] + src[k, 3 + j, rows, :]) + (
                    src[k, 2 + j, pl.ds(7, 32), :] + src[k, 2 + j, pl.ds(9, 32), :]
                )
                far = (src[k, j, rows, :] + src[k, 4 + j, rows, :]) + (
                    src[k, 2 + j, pl.ds(6, 32), :] + src[k, 2 + j, pl.ds(10, 32), :]
                )
                along = side if k == 3 else depth[k][:, :128]
                laplace = along[32 * j : 32 * j + 32] + (16.0 * near - far)
                old = dst[k, x + j, rows, :]
                a_each, e_each = (ha_ref, he_ref) if k == 3 else (a_ref, e_ref)
                fresh.append((k, j, old + a_each[x + j] * (v - old) + e_each[x + j] * laplace))
        return fresh, side

    def one_step(step, carry):
        dst = state_ref.at[(step + 1) % 2]

        def planes(at, inside):
            x = 2 * step + 2 + PLANES * at
            fresh, side = advance(state_ref.at[step % 2, :, pl.ds(x - 2, 4 + PLANES)], dst, x)
            for k, j, value in fresh:
                dst[k, x + j, 8:40, :] = value
            if first:
                for j in range(PLANES):
                    edge_ref[step, x + j, :, :] = side[32 * j + 8 : 32 * j + 24]
            return inside

        lax.fori_loop(0, (20 - 4 * step) // PLANES, planes, 0)
        return carry

    lax.fori_loop(0, HALF, one_step, 0)

    block = pl.ds(16, 16)

    def finish(x, carry):
        for k in range(3):
            u_out[k, x, :, :] = state_ref[0, k, 8 + x, block, :]
            if first:
                p_out[k, x, :, :] = state_ref[1, k, 8 + x, block, :]
        if first:
            for row in (0, 8):
                rows = pl.ds(row, 8)
                values = [state_ref[slot, k, 8 + x, pl.ds(16 + row, 8), :] for slot in (0, 1) for k in range(3)]
                last = pack_faces(values, lane)
                face_out[x, rows, :] = last
                slab = values[0]
                for at in range(1, 6):
                    slab = jnp.where(lane // 16 == at, pltpu.roll(values[at], 16 * at, 1), slab)
                slab_out[x, rows, :] = slab
                seen = jnp.zeros((8, 128), F32)
                for step in range(HALF):
                    if step < HALF - 1:
                        sample = pltpu.roll(edge_ref[step + 1, 8 + x, rows, :], 56 + step, 1)
                    else:
                        sample = pltpu.roll(last, 120 + step, 1)
                    seen = jnp.where((inner == step) & (lane < 48), sample, seen)
                seen_out[x, rows, :] = seen
        return carry

    lax.fori_loop(0, 8, finish, 0, unroll=4)


def slab_message_kernel(own_ref, low_ref, high_ref, after_ref, up_ref, down_ref):
    def plane(i, carry):
        for at, source in ((0, low_ref), (8, own_ref), (16, high_ref)):
            up_ref[at + i] = source[i, 8:16, :]
            down_ref[at + i] = source[i, 0:8, :]
        return carry

    lax.fori_loop(0, 8, plane, 0, unroll=2)


def surface_kernel(
    own_in, x_low, x_high, y_low, y_high, weight_in, code_in, seen_in, filter_in, count_in,
    demand_out, state_ref, rate_ref, sample_ref, seen_ref, filter_ref, count_ref,
):
    lane = lane_of()
    inner = lane % 16

    def near_side(i, carry):
        state_ref[0, i, 16:32, :] = x_low[i]
        state_ref[0, 8 + i, 16:32, :] = own_in[i]
        state_ref[0, 16 + i, 16:32, :] = x_high[i]
        for part in range(3):
            state_ref[0, 8 * part + i, 8:16, :] = y_low[8 * part + i]
            state_ref[0, 8 * part + i, 32:40, :] = y_high[8 * part + i]
        return carry

    lax.fori_loop(0, 8, near_side, 0, unroll=2)

    def prepare(x, carry):
        for tile in range(4):
            rows = pl.ds(8 + 8 * tile, 8)
            value = state_ref[0, x, rows, :]
            state_ref[0, x, rows, :] = jnp.where(lane < 48, value, 0.0)
            state_ref[1, x, rows, :] = jnp.where(lane < 48, pltpu.roll(value, 128 - 48, 1), 0.0)
        return carry

    def rates(x, carry):
        for at, unit in ((0, UNIT_A), (1, UNIT_E)):
            for half in (0, 16):
                both = decoded(code_in[at, x - 2, half : half + 16, :]) * unit
                for tile in (0, 8):
                    rate = both[tile : tile + 8]
                    spread = jnp.where(lane < 32, pltpu.roll(rate, 16, 1), pltpu.roll(rate, 32, 1))
                    spread = jnp.where(lane < 16, rate, spread)
                    rate_ref[at, x, pl.ds(half + tile, 8), :] = jnp.where(lane < 48, spread, 0.0)
        return carry

    lax.fori_loop(0, 24, prepare, 0, unroll=4)
    lax.fori_loop(2, 22, rates, 0, unroll=4)

    def one_step(step, carry):
        dst = state_ref.at[(step + 1) % 2]

        def planes(at, inside):
            x = 2 * step + 2 + PLANES * at
            src = state_ref.at[step % 2, pl.ds(x - 2, 4 + PLANES)]
            rows = pl.ds(8, 32)
            fields = [src[2 + j, rows, :] for j in range(PLANES)]
            halves = jnp.concatenate([jnp.concatenate(split(v), axis=1) for v in fields], axis=0)
            depth = jnp.dot(halves, weight_in[...], preferred_element_type=F32)
            fresh = []
            for j, v in enumerate(fields):
                near = (src[1 + j, rows, :] + src[3 + j, rows, :]) + (src[2 + j, pl.ds(7, 32), :] + src[2 + j, pl.ds(9, 32), :])
                far = (src[j, rows, :] + src[4 + j, rows, :]) + (src[2 + j, pl.ds(6, 32), :] + src[2 + j, pl.ds(10, 32), :])
                laplace = depth[32 * j : 32 * j + 32] + (16.0 * near - far)
                old = dst[x + j, rows, :]
                fresh.append(old + rate_ref[0, x + j] * (v - old) + rate_ref[1, x + j] * laplace)
            for j, value in enumerate(fresh):
                dst[x + j, 8:40, :] = value
                sample_ref[step, x + j, :, :] = value[8:24]
            return inside

        lax.fori_loop(0, (20 - 4 * step) // PLANES, planes, 0)
        return carry

    lax.fori_loop(0, HALF, one_step, 0)

    def finish(x, carry):
        for row in (0, 8):
            rows = pl.ds(row, 8)
            seen = seen_in[x, rows, :]
            for step in range(HALF):
                at = HALF + step
                sample = pltpu.roll(sample_ref[step, 8 + x, rows, :], at, 1)
                seen = jnp.where((inner == at) & (lane < 48), sample, seen)
            seen_ref[x, rows, :] = seen
        return carry

    lax.fori_loop(0, 8, finish, 0, unroll=4)

    filter_ref[...] = filter_in[...].astype(F32)
    blocks = [jnp.zeros((8, CLASSES * MODES), F32)] * 16
    for k in range(3):
        blocks[2 * k] = filter_ref[pl.ds(k, STEPS, stride=3), :]
    filters = jnp.concatenate(blocks, axis=0).astype(jnp.bfloat16)
    motion = seen_ref[...].reshape(128, 128).astype(jnp.bfloat16)
    modal = lax.dot_general(filters, motion, (((0,), (1,)), ((), ())), preferred_element_type=F32)
    modes = lax.broadcasted_iota(jnp.int32, (MODES, 128), 0)
    count_ref[...] = jnp.zeros((8, 128), jnp.int32)
    count_ref[0:1, 0:CLASSES] = count_in[...]
    counts = jnp.where(modes == lane, jnp.broadcast_to(count_ref[0:1, :], (8, 128)), 0)
    counts = jnp.sum(counts, axis=1, keepdims=True)
    energies = []
    for kind in range(CLASSES):
        part = modal[MODES * kind : MODES * (kind + 1), :]
        part = jnp.where(modes < counts[kind : kind + 1, :], part * part, 0.0)
        energies.append(jnp.sum(part, axis=0, keepdims=True))
    demand_out[...] = 0.5 * jnp.log1p(jnp.concatenate(energies, axis=0))


def table_kernel(demand_ref, cells_ref, after_ref, table_out):
    demand = demand_ref[...]
    for owner in range(table_out.shape[0]):
        cells = jnp.broadcast_to(cells_ref[owner : owner + 1, :], (CLASSES, 128))
        chosen = jnp.take_along_axis(demand, cells, axis=1)
        for level in range(table_out.shape[1]):
            table_out[owner, level] = chosen


def fragility_kernel(
    table_ref, slot_ref, kind_ref, city_ref, amplify_ref, median_ref, spread_ref, out_ref, gain_ref, tables_ref
):
    sources = table_ref.shape[0]
    slot, kind, city = slot_ref[...], kind_ref[...], city_ref[...]
    column = slot % 128
    key = (slot // 128) * CLASSES + kind
    demand = jnp.zeros((8, 128), F32)
    for source in range(sources):
        for each in range(CLASSES):
            row = jnp.broadcast_to(table_ref[source, 0, each : each + 1, :], (8, 128))
            found = jnp.take_along_axis(row, column, axis=1)
            demand = jnp.where(key == source * CLASSES + each, found, demand)
    gain_ref[...] = jnp.ones((8, 128), F32)
    gain_ref[0:1, 0:CITIES] = amplify_ref[...]
    gain = jnp.log(jnp.broadcast_to(gain_ref[0:1, :], (8, 128)))
    demand = demand + jnp.take_along_axis(gain, city, axis=1)
    tables_ref[...] = jnp.ones((128, 128), F32)
    batches = median_ref.shape[1]
    tables_ref[0:CLASSES, 0:batches] = median_ref[...]
    medians = tables_ref[...].T
    tables_ref[0:CLASSES, 0:batches] = spread_ref[...]
    spreads = tables_ref[...].T
    for group in range(8):
        level = jnp.broadcast_to(demand[group : group + 1, :], (8, 128))
        index = jnp.broadcast_to(kind[group : group + 1, :], (8, 128))
        for half in range(0, batches, 8):
            middle = jnp.take_along_axis(medians[half : half + 8, :], index, axis=1)
            width = jnp.take_along_axis(spreads[half : half + 8, :], index, axis=1)
            out_ref[half : half + 8, 128 * group : 128 * group + 128] = jax.nn.sigmoid((level - middle) / width)


VM = pl.BlockSpec(memory_space=pltpu.VMEM)


WEIGHTS = {"start": 1.4, "steps_first": 6.7, "steps_second": 6.5, "slab_message": 4.0, "surface": 0.02, "table": 4.0, "fragility": 1.0}
UNIT_FLOPS = 1.15e10


def call(kernel, name, shapes, args, specs=None, scratch=(), limit=VMEM_LIMIT):
    out = [s if isinstance(s, jax.ShapeDtypeStruct) else jax.ShapeDtypeStruct(s, F32) for s in shapes]
    return pl.pallas_call(
        kernel,
        out_shape=out,
        in_specs=specs or [VM] * len(args),
        out_specs=[VM] * len(out),
        scratch_shapes=list(scratch),
        compiler_params=pltpu.CompilerParams(vmem_limit_bytes=limit),
        cost_estimate=pl.CostEstimate(flops=int(WEIGHTS.get(name, 0.3) * UNIT_FLOPS), bytes_accessed=0, transcendentals=0),
        name=name,
    )(*args)


def both_ways(to_up, to_down, axis):
    count = lax.axis_size(axis)
    forward = [(i, i + 1) for i in range(count - 1)]
    backward = [(i + 1, i) for i in range(count - 1)]
    return lax.ppermute(to_up, axis, forward), lax.ppermute(to_down, axis, backward)


def exchange_x(u, p, faces, coefficients):
    extra = list(coefficients)
    z_low, z_high = both_ways(faces, faces, "gz")
    planes = 3 * XU + (3 + len(extra)) * XP + XH + 1
    message = jax.ShapeDtypeStruct((planes, 16, 128), jnp.int16)
    halo, up, down, powers = call(
        functools.partial(x_message_kernel, bool(extra)),
        "x_message",
        [(8, 16, 128), message, message, (16, 128)],
        [z_low, z_high, u, p] + extra,
    )
    return halo, powers, *both_ways(up, down, "gx")


def y_messages(u, p, coefficients, halo, powers, x_low, x_high):
    extra = list(coefficients)
    planes = (3 * YU + (3 + len(extra)) * YP + YH) // 2 + 1
    message = jax.ShapeDtypeStruct((planes, 16, 128), jnp.int16)
    return call(
        functools.partial(y_message_kernel, bool(extra)),
        "y_message",
        [message, message],
        [u, p] + extra + [halo, powers, x_low, x_high],
    )


def body(
    displacement,
    previous,
    courant,
    damping,
    send_cells,
    building_slot,
    building_class,
    city,
    mode_count,
    modal_filter,
    amplify,
    median,
    spread,
):
    own = (3, 8, 16, 128)
    plane = (8, 16, 128)
    wide = pltpu.VMEM((2, 4, 24, 48, 128), F32)
    rates = pltpu.VMEM((4, 24, 32, 128), F32)
    samples = pltpu.VMEM((HALF, 24, 16, 128), F32)

    u, p = displacement, previous
    a, e, faces = call(
        start_kernel,
        "start",
        [plane, plane, plane],
        [u, p, courant, damping],
        specs=[pl.BlockSpec(memory_space=pltpu.HBM)] * 4,
        scratch=[pltpu.VMEM(own, F32)] * 2 + [pltpu.VMEM(plane, F32)] * 2 + [pltpu.SemaphoreType.DMA((8,))],
        limit=START_LIMIT,
    )
    halo, powers, x_low, x_high = exchange_x(u, p, faces, (a, e))
    messages = y_messages(u, p, (a, e), halo, powers, x_low, x_high)
    received = (halo, x_low, x_high, *both_ways(*messages, "gy"))
    weights = jnp.asarray(depth_weights(), jnp.bfloat16)
    u, p, faces, slab, seen, codes = call(
        functools.partial(steps_kernel, True),
        "steps_first",
        [own, own, plane, plane, plane, jax.ShapeDtypeStruct((3, 20, 32, 128), jnp.int16)],
        [u, p, a, e, *received, weights],
        scratch=[wide, rates, samples],
    )

    near_low, near_high = both_ways(slab, slab, "gx")
    halo, powers, x_low, x_high = exchange_x(u, p, faces, ())
    slab_messages = call(slab_message_kernel, "slab_message", [(24, 8, 128)] * 2, [slab, near_low, near_high, powers])
    side_low, side_high = both_ways(*slab_messages, "gy")
    (demand,) = call(
        surface_kernel,
        "surface",
        [(CLASSES, 128)],
        [slab, near_low, near_high, side_low, side_high, jnp.asarray(slab_weights(), jnp.bfloat16), codes, seen]
        + [modal_filter.T, mode_count.reshape(1, CLASSES)],
        scratch=[
            pltpu.VMEM((2, 24, 48, 128), F32),
            pltpu.VMEM((2, 24, 32, 128), F32),
            samples,
            pltpu.VMEM(plane, F32),
            pltpu.VMEM((3 * STEPS, CLASSES * MODES), F32),
            pltpu.VMEM((8, 128), jnp.int32),
        ],
    )
    messages = y_messages(u, p, (), halo, powers, x_low, x_high)
    received = (halo, x_low, x_high, *both_ways(*messages, "gy"))
    owners, levels = lax.axis_size("gx"), lax.axis_size("gz")
    (table,) = call(
        table_kernel,
        "table",
        [(owners, levels, CLASSES, 128)],
        [demand, send_cells.reshape(owners, 128), messages[0]],
        specs=[VM, VM, pl.BlockSpec(memory_space=pl.ANY)],
    )
    table = table.reshape(owners * levels, CLASSES, 128)
    table = lax.all_to_all(table, ("gx", "gz"), split_axis=0, concat_axis=0, tiled=True)
    (field,) = call(
        functools.partial(steps_kernel, False), "steps_second", [own], [u, p, *received, weights, codes], scratch=[wide, rates]
    )
    (probability,) = call(
        fragility_kernel,
        "fragility",
        [(16, 1024)],
        [
            table.reshape(owners, levels, CLASSES, 128),
            building_slot.reshape(8, 128),
            building_class.reshape(8, 128),
            city.reshape(8, 128),
            amplify.reshape(1, CITIES),
            median.T,
            spread.T,
        ],
        scratch=[pltpu.VMEM((8, 128), F32), pltpu.VMEM((128, 128), F32)],
    )
    return (field, probability)


def solution(mesh):
    placed = (
        P(None, "gx", "gy", "gz"),
        P(None, "gx", "gy", "gz"),
        P("gx", "gy", "gz"),
        P("gx", "gy", "gz"),
        P("gx", "gy", None),
        P(("gx", "gy", "gz")),
        P(("gx", "gy", "gz")),
        P(("gx", "gy", "gz")),
        P(),
        P(),
        P(),
        P(),
        P(),
    )
    return jax.shard_map(
        body,
        mesh=mesh,
        in_specs=placed,
        out_specs=(P(None, "gx", "gy", "gz"), P(None, ("gx", "gy", "gz"))),
        check_vma=False,
    )
```

```python
import functools

import jax
import jax.numpy as jnp
import numpy as np
from jax import lax
from jax.experimental import pallas as pl
from jax.experimental.pallas import tpu as pltpu
from jax.sharding import PartitionSpec as P

STEPS = 8
HALF = 4
DEEP = 2 * HALF
CLASSES = 8
MODES = 8
CITIES = 16
F32 = jnp.float32
VMEM_LIMIT = 24 * 1024 * 1024
START_LIMIT = int(53.8 * 1024 * 1024)

XU, XP, XH = 8, 6, 7
YU, YP, YH = 24, 20, 20

FULL = 32000.0
BIAS = 200
UNIT_A = 2.0 / FULL
UNIT_E = 0.2 / 12.0 / FULL


PLANES = 4


def depth_weights():
    lanes = np.arange(256)
    result = np.zeros((3, 256, 256), np.float32)
    for k in range(3):
        at = lanes - 128 - 16 * k
        depth = np.where(lanes < 128, lanes, np.where(at < 8, at - 8, at + 120))
        used = (lanes < 128) | ((at >= 0) & (at < 16))
        apart = np.abs(depth[:, None] - depth[None, :])
        band = np.where(apart == 0, -90.0, np.where(apart == 1, 16.0, np.where(apart == 2, -1.0, 0.0)))
        result[k] = np.where(used[:, None] & used[None, :], band, 0.0)
        result[k, 0, 128 + 64 + 16 * k + 8] = 1.0
    return result


def slab_weights():
    lanes = np.arange(128)
    apart = np.abs(lanes[:, None] - lanes[None, :])
    band = np.where(apart == 0, -90.0, np.where(apart == 1, 16.0, np.where(apart == 2, -1.0, 0.0)))
    same = (lanes[:, None] // 16 == lanes[None, :] // 16) & (lanes[:, None] < 48)
    band = np.where(same, band, 0.0)
    return np.concatenate([band, band], axis=0)


def split(v):
    high = v.astype(jnp.bfloat16)
    return high, (v - high.astype(F32)).astype(jnp.bfloat16)


def lane_of():
    return lax.broadcasted_iota(jnp.int32, (8, 128), 1)


def pack_faces(values, lane):
    packed = pltpu.roll(values[0], 8, 1)
    for at in range(1, len(values)):
        packed = jnp.where(lane // 16 == at, pltpu.roll(values[at], (16 * at + 8) % 128, 1), packed)
    return packed


def start_kernel(u_in, p_in, c_in, d_in, a_ref, e_ref, face_ref, u_ref, p_ref, c_ref, d_ref, sems):
    copies = [pltpu.make_async_copy(c_in, c_ref, sems.at[0]), pltpu.make_async_copy(d_in, d_ref, sems.at[1])]
    for k in range(3):
        copies.append(pltpu.make_async_copy(u_in.at[k], u_ref.at[k], sems.at[2 + k]))
        copies.append(pltpu.make_async_copy(p_in.at[k], p_ref.at[k], sems.at[5 + k]))
    for copy in copies:
        copy.start()
    for copy in copies:
        copy.wait()
    lane = lane_of()

    def plane(x, carry):
        for row in (0, 8):
            rows = pl.ds(row, 8)
            share = 1.0 / (1.0 + d_ref[x, rows, :])
            values = [u_ref[k, x, rows, :] for k in range(3)] + [p_ref[k, x, rows, :] for k in range(3)]
            values += [2.0 * share, c_ref[x, rows, :] * share * (1.0 / 12.0)]
            a_ref[x, rows, :] = values[6]
            e_ref[x, rows, :] = values[7]
            face_ref[x, rows, :] = pack_faces(values, lane)
        return carry

    lax.fori_loop(0, 8, plane, 0)


def exponent_of(peak):
    peak = jnp.maximum(jnp.max(peak, axis=0, keepdims=True), 1e-30)
    return jnp.broadcast_to(jnp.ceil(jnp.log2(peak)), (8, 128))


def coded(values):
    return jnp.round(values).astype(jnp.int32).astype(jnp.int16)


def decoded(values):
    return values.astype(jnp.int32).astype(F32)


def twice(rows):
    return jnp.concatenate([rows, rows], axis=0)


def sent_exponents(message):
    both = decoded(message[message.shape[0] - 1]) - BIAS
    return both[0:8], both[8:16]


def x_message_kernel(coefficients, *refs):
    if coefficients:
        z_low_ref, z_high_ref, u_ref, p_ref, a_ref, e_ref, halo_ref, up_ref, down_ref, power_ref = refs
    else:
        z_low_ref, z_high_ref, u_ref, p_ref, halo_ref, up_ref, down_ref, power_ref = refs
    inner = lax.broadcasted_iota(jnp.int32, (16, 128), 1) % 16

    def largest(x, carry):
        field, face = carry
        for k in range(3):
            both = jnp.maximum(jnp.abs(u_ref[k, x]), jnp.abs(p_ref[k, x]))
            field = jnp.maximum(field, jnp.maximum(both[0:8], both[8:16]))
        halo = jnp.where(inner < 8, z_low_ref[x], z_high_ref[x])
        halo_ref[x] = halo
        halo = jnp.abs(halo)
        return field, jnp.maximum(face, jnp.maximum(halo[0:8], halo[8:16]))

    zero = jnp.zeros((8, 128), F32)
    field, face = lax.fori_loop(0, 8, largest, (zero, zero))
    powers = jnp.concatenate([exponent_of(field), exponent_of(face)], axis=0)
    power_ref[...] = powers
    up_ref[up_ref.shape[0] - 1] = coded(powers + BIAS)
    down_ref[down_ref.shape[0] - 1] = coded(powers + BIAS)
    scale = FULL * jnp.exp2(-powers)
    field, face = twice(scale[0:8]), twice(scale[8:16])

    def whole(x, carry):
        for k in range(3):
            code = coded(u_ref[k, x] * field)
            up_ref[XU * k + x] = code
            down_ref[XU * k + x] = code
        return carry

    def part(i, carry):
        parts = [(p_ref.at[k], field) for k in range(3)]
        if coefficients:
            parts += [(a_ref, 1.0 / UNIT_A), (e_ref, 1.0 / UNIT_E)]
        for at, (source, unit) in enumerate(parts):
            up_ref[3 * XU + XP * at + i] = coded(source[8 - XP + i] * unit)
            down_ref[3 * XU + XP * at + i] = coded(source[i] * unit)
        return carry

    at = 3 * XU + (5 if coefficients else 3) * XP

    def side(i, carry):
        up_ref[at + i] = coded(halo_ref[8 - XH + i] * face)
        down_ref[at + i] = coded(halo_ref[i] * face)
        return carry

    lax.fori_loop(0, 8, whole, 0)
    lax.fori_loop(0, XP, part, 0)
    lax.fori_loop(0, XH, side, 0)


def y_message_kernel(coefficients, *refs):
    if coefficients:
        u_ref, p_ref, a_ref, e_ref, halo_ref, power_ref, low_ref, high_ref, up_ref, down_ref = refs
    else:
        u_ref, p_ref, halo_ref, power_ref, low_ref, high_ref, up_ref, down_ref = refs
    powers = power_ref[...]
    low_powers = jnp.concatenate(sent_exponents(low_ref), axis=0)
    high_powers = jnp.concatenate(sent_exponents(high_ref), axis=0)
    most = jnp.maximum(powers, jnp.maximum(low_powers, high_powers))
    for out_ref in (up_ref, down_ref):
        out_ref[out_ref.shape[0] - 1] = coded(most + BIAS)
    own_scale = FULL * jnp.exp2(-most)
    low_scale = jnp.exp2(low_powers - most)
    high_scale = jnp.exp2(high_powers - most)
    field = [twice(scale[0:8]) for scale in (own_scale, low_scale, high_scale)]
    face = [twice(scale[8:16]) for scale in (own_scale, low_scale, high_scale)]

    def put(at, pair):
        up_ref[at] = coded(jnp.concatenate([pair[0][8:16], pair[1][8:16]], axis=0))
        down_ref[at] = coded(jnp.concatenate([pair[0][0:8], pair[1][0:8]], axis=0))

    def group(parts, x_planes, y_planes, x_at, y_at):
        side = (y_planes - 8) // 4

        def own(i, carry):
            for at, (source, units) in enumerate(parts):
                put(y_at + at * y_planes // 2 + side + i, [source[2 * i + j] * units[0] for j in (0, 1)])
            return carry

        def sides(i, carry):
            for at, (_, units) in enumerate(parts):
                start = x_at + at * x_planes
                first = start + x_planes - 2 * side + 2 * i
                put(y_at + at * y_planes // 2 + i, [decoded(low_ref[first + j]) * units[1] for j in (0, 1)])
                first = start + 2 * i
                pair = [decoded(high_ref[first + j]) * units[2] for j in (0, 1)]
                put(y_at + at * y_planes // 2 + side + 4 + i, pair)
            return carry

        lax.fori_loop(0, 4, own, 0)
        lax.fori_loop(0, side, sides, 0)
        return x_at + len(parts) * x_planes, y_at + len(parts) * y_planes // 2

    x_at, y_at = group([(u_ref.at[k], field) for k in range(3)], XU, YU, 0, 0)
    parts = [(p_ref.at[k], field) for k in range(3)]
    if coefficients:
        parts += [(a_ref, (1.0 / UNIT_A, 1.0, 1.0)), (e_ref, (1.0 / UNIT_E, 1.0, 1.0))]
    x_at, y_at = group(parts, XP, YP, x_at, y_at)
    group([(halo_ref, face)], XH, YH, x_at, y_at)


def fill(parts, x_low, x_high, y_low, y_high, x_at, x_planes, y_at, y_planes):
    count = len(parts)
    side = (y_planes - 8) // 2

    def own(i, carry):
        for target, row, block, _ in parts:
            target[8 + i, row + 8 : row + 24, :] = block[i]
        return carry

    def x_side(i, carry):
        for at, (target, row, _, units) in enumerate(parts):
            here = x_at + at * x_planes + i
            target[8 - x_planes + i, row + 8 : row + 24, :] = decoded(x_low[here]) * units[0]
            target[16 + i, row + 8 : row + 24, :] = decoded(x_high[here]) * units[1]
        return carry

    def y_side(i, carry):
        for at, (target, row, _, units) in enumerate(parts):
            here = y_at + at * y_planes // 2 + i
            low = decoded(y_low[here]) * units[2]
            high = decoded(y_high[here]) * units[3]
            for j in (0, 1):
                target[8 - side + 2 * i + j, row : row + 8, :] = low[8 * j : 8 * j + 8]
                target[8 - side + 2 * i + j, row + 24 : row + 32, :] = high[8 * j : 8 * j + 8]
        return carry

    lax.fori_loop(0, 8, own, 0, unroll=2)
    lax.fori_loop(0, x_planes, x_side, 0)
    lax.fori_loop(0, y_planes // 2, y_side, 0, unroll=2)
    return x_at + count * x_planes, y_at + count * y_planes // 2


def steps_kernel(first, *refs):
    if first:
        (u_in, p_in, a_in, e_in, halo_in, x_low, x_high, y_low, y_high, weight_in) = refs[:10]
        (u_out, p_out, face_out, slab_out, seen_out, code_ref) = refs[10:16]
        state_ref, rate_ref, edge_ref = refs[16:]
    else:
        (u_in, p_in, halo_in, x_low, x_high, y_low, y_high, weight_in, code_ref) = refs[:9]
        u_out, state_ref, rate_ref = refs[9:]
    a_ref, e_ref, ha_ref, he_ref = (rate_ref.at[at] for at in range(4))
    lane = lane_of()
    inner = lane % 16

    sides = (x_low, x_high, y_low, y_high)
    powers = [sent_exponents(message) for message in sides]
    field = [twice(jnp.exp2(power[0]) * (1.0 / FULL)) for power in powers]
    face = [twice(jnp.exp2(power[1]) * (1.0 / FULL)) for power in powers]
    x_at, y_at = fill([(state_ref.at[0, k], 8, u_in.at[k], field) for k in range(3)], *sides, 0, XU, 0, YU)
    parts = [(state_ref.at[1, k], 8, p_in.at[k], field) for k in range(3)]
    if first:
        parts += [(a_ref, 0, a_in, (UNIT_A,) * 4), (e_ref, 0, e_in, (UNIT_E,) * 4)]
    x_at, y_at = fill(parts, *sides, x_at, XP, y_at, YP)
    fill([(state_ref.at[0, 3], 8, halo_in, face)], *sides, x_at, XH, y_at, YH)

    unit = jnp.where(lane < 112, UNIT_A, UNIT_E)

    def prepare(x, carry):
        for half in (0, 16):
            held = pl.ds(half, 16)
            if first:
                code_ref[0, x - 2, held, :] = coded(a_ref[x, held, :] * (1.0 / UNIT_A))
                code_ref[1, x - 2, held, :] = coded(e_ref[x, held, :] * (1.0 / UNIT_E))
                sides = state_ref[0, 3, x, pl.ds(8 + half, 16), :]
                scale = twice(jnp.where(lane < 96, 0.0, 1.0 / unit))
                code_ref[2, x - 2, held, :] = coded(jnp.where(scale > 0.0, sides * scale, 0.0))
            else:
                a_ref[x, held, :] = decoded(code_ref[0, x - 2, held, :]) * UNIT_A
                e_ref[x, held, :] = decoded(code_ref[1, x - 2, held, :]) * UNIT_E
                sides = decoded(code_ref[2, x - 2, held, :]) * twice(unit)
            for tile in (0, 8):
                rows = pl.ds(8 + half + tile, 8)
                halo = state_ref[0, 3, x, rows, :]
                state_ref[0, 3, x, rows, :] = jnp.where(lane < 48, halo, 0.0)
                state_ref[1, 3, x, rows, :] = jnp.where(lane < 48, pltpu.roll(halo, 128 - 48, 1), 0.0)
                side = sides[tile : tile + 8]
                for target, at in ((ha_ref, 96), (he_ref, 112)):
                    spread = jnp.where(lane < 16, pltpu.roll(side, 128 - at, 1), pltpu.roll(side, 144 - at, 1))
                    spread = jnp.where(lane < 32, spread, pltpu.roll(side, 160 - at, 1))
                    target[x, pl.ds(half + tile, 8), :] = jnp.where(lane < 48, spread, 0.0)
        return carry

    lax.fori_loop(2, 22, prepare, 0, unroll=4)

    def advance(src, dst, x):
        rows = pl.ds(8, 32)
        fields = [[src[k, 2 + j, rows, :] for j in range(PLANES)] for k in range(4)]
        parts = [[split(v) for v in field] for field in fields]
        depth = []
        for k in range(3):
            pieces = [jnp.concatenate([parts[k][j][part], parts[3][j][part]], axis=1) for part in (0, 1) for j in range(PLANES)]
            both = jnp.dot(jnp.concatenate(pieces, axis=0), weight_in[k], preferred_element_type=F32)
            depth.append(both[0 : 32 * PLANES] + both[32 * PLANES :])
        side = depth[0][:, 128:] + depth[1][:, 128:] + depth[2][:, 128:]
        fresh = []
        for j in range(PLANES):
            for k in range(4):
                v = fields[k][j]
                near = (src[k, 1 + j, rows, :] + src[k, 3 + j, rows, :]) + (
                    src[k, 2 + j, pl.ds(7, 32), :] + src[k, 2 + j, pl.ds(9, 32), :]
                )
                far = (src[k, j, rows, :] + src[k, 4 + j, rows, :]) + (
                    src[k, 2 + j, pl.ds(6, 32), :] + src[k, 2 + j, pl.ds(10, 32), :]
                )
                along = side if k == 3 else depth[k][:, :128]
                laplace = along[32 * j : 32 * j + 32] + (16.0 * near - far)
                old = dst[k, x + j, rows, :]
                a_each, e_each = (ha_ref, he_ref) if k == 3 else (a_ref, e_ref)
                fresh.append((k, j, old + a_each[x + j] * (v - old) + e_each[x + j] * laplace))
        return fresh, side

    def one_step(step, carry):
        dst = state_ref.at[(step + 1) % 2]

        def planes(at, inside):
            x = 2 * step + 2 + PLANES * at
            fresh, side = advance(state_ref.at[step % 2, :, pl.ds(x - 2, 4 + PLANES)], dst, x)
            for k, j, value in fresh:
                dst[k, x + j, 8:40, :] = value
            if first:
                for j in range(PLANES):
                    edge_ref[step, x + j, :, :] = side[32 * j + 8 : 32 * j + 24]
            return inside

        lax.fori_loop(0, (20 - 4 * step) // PLANES, planes, 0)
        return carry

    lax.fori_loop(0, HALF, one_step, 0)

    block = pl.ds(16, 16)

    def finish(x, carry):
        for k in range(3):
            u_out[k, x, :, :] = state_ref[0, k, 8 + x, block, :]
            if first:
                p_out[k, x, :, :] = state_ref[1, k, 8 + x, block, :]
        if first:
            for row in (0, 8):
                rows = pl.ds(row, 8)
                values = [state_ref[slot, k, 8 + x, pl.ds(16 + row, 8), :] for slot in (0, 1) for k in range(3)]
                last = pack_faces(values, lane)
                face_out[x, rows, :] = last
                slab = values[0]
                for at in range(1, 6):
                    slab = jnp.where(lane // 16 == at, pltpu.roll(values[at], 16 * at, 1), slab)
                slab_out[x, rows, :] = slab
                seen = jnp.zeros((8, 128), F32)
                for step in range(HALF):
                    if step < HALF - 1:
                        sample = pltpu.roll(edge_ref[step + 1, 8 + x, rows, :], 56 + step, 1)
                    else:
                        sample = pltpu.roll(last, 120 + step, 1)
                    seen = jnp.where((inner == step) & (lane < 48), sample, seen)
                seen_out[x, rows, :] = seen
        return carry

    lax.fori_loop(0, 8, finish, 0, unroll=4)


def slab_message_kernel(own_ref, low_ref, high_ref, after_ref, up_ref, down_ref):
    def plane(i, carry):
        for at, source in ((0, low_ref), (8, own_ref), (16, high_ref)):
            up_ref[at + i] = source[i, 8:16, :]
            down_ref[at + i] = source[i, 0:8, :]
        return carry

    lax.fori_loop(0, 8, plane, 0, unroll=2)


def surface_kernel(
    own_in, x_low, x_high, y_low, y_high, weight_in, code_in, seen_in, filter_in, count_in, after_in,
    demand_out, state_ref, rate_ref, sample_ref, seen_ref, filter_ref, count_ref,
):
    lane = lane_of()
    inner = lane % 16

    def near_side(i, carry):
        state_ref[0, i, 16:32, :] = x_low[i]
        state_ref[0, 8 + i, 16:32, :] = own_in[i]
        state_ref[0, 16 + i, 16:32, :] = x_high[i]
        for part in range(3):
            state_ref[0, 8 * part + i, 8:16, :] = y_low[8 * part + i]
            state_ref[0, 8 * part + i, 32:40, :] = y_high[8 * part + i]
        return carry

    lax.fori_loop(0, 8, near_side, 0, unroll=2)

    def prepare(x, carry):
        for tile in range(4):
            rows = pl.ds(8 + 8 * tile, 8)
            value = state_ref[0, x, rows, :]
            state_ref[0, x, rows, :] = jnp.where(lane < 48, value, 0.0)
            state_ref[1, x, rows, :] = jnp.where(lane < 48, pltpu.roll(value, 128 - 48, 1), 0.0)
        return carry

    def rates(x, carry):
        for at, unit in ((0, UNIT_A), (1, UNIT_E)):
            for half in (0, 16):
                both = decoded(code_in[at, x - 2, half : half + 16, :]) * unit
                for tile in (0, 8):
                    rate = both[tile : tile + 8]
                    spread = jnp.where(lane < 32, pltpu.roll(rate, 16, 1), pltpu.roll(rate, 32, 1))
                    spread = jnp.where(lane < 16, rate, spread)
                    rate_ref[at, x, pl.ds(half + tile, 8), :] = jnp.where(lane < 48, spread, 0.0)
        return carry

    lax.fori_loop(0, 24, prepare, 0, unroll=4)
    lax.fori_loop(2, 22, rates, 0, unroll=4)

    def one_step(step, carry):
        dst = state_ref.at[(step + 1) % 2]

        def planes(at, inside):
            x = 2 * step + 2 + PLANES * at
            src = state_ref.at[step % 2, pl.ds(x - 2, 4 + PLANES)]
            rows = pl.ds(8, 32)
            fields = [src[2 + j, rows, :] for j in range(PLANES)]
            halves = jnp.concatenate([jnp.concatenate(split(v), axis=1) for v in fields], axis=0)
            depth = jnp.dot(halves, weight_in[...], preferred_element_type=F32)
            fresh = []
            for j, v in enumerate(fields):
                near = (src[1 + j, rows, :] + src[3 + j, rows, :]) + (src[2 + j, pl.ds(7, 32), :] + src[2 + j, pl.ds(9, 32), :])
                far = (src[j, rows, :] + src[4 + j, rows, :]) + (src[2 + j, pl.ds(6, 32), :] + src[2 + j, pl.ds(10, 32), :])
                laplace = depth[32 * j : 32 * j + 32] + (16.0 * near - far)
                old = dst[x + j, rows, :]
                fresh.append(old + rate_ref[0, x + j] * (v - old) + rate_ref[1, x + j] * laplace)
            for j, value in enumerate(fresh):
                dst[x + j, 8:40, :] = value
                sample_ref[step, x + j, :, :] = value[8:24]
            return inside

        lax.fori_loop(0, (20 - 4 * step) // PLANES, planes, 0)
        return carry

    lax.fori_loop(0, HALF, one_step, 0)

    def finish(x, carry):
        for row in (0, 8):
            rows = pl.ds(row, 8)
            seen = seen_in[x, rows, :]
            for step in range(HALF):
                at = HALF + step
                sample = pltpu.roll(sample_ref[step, 8 + x, rows, :], at, 1)
                seen = jnp.where((inner == at) & (lane < 48), sample, seen)
            seen_ref[x, rows, :] = seen
        return carry

    lax.fori_loop(0, 8, finish, 0, unroll=4)

    filter_ref[...] = filter_in[...].astype(F32)
    blocks = [jnp.zeros((8, CLASSES * MODES), F32)] * 16
    for k in range(3):
        blocks[2 * k] = filter_ref[pl.ds(k, STEPS, stride=3), :]
    filters = jnp.concatenate(blocks, axis=0).astype(jnp.bfloat16)
    motion = seen_ref[...].reshape(128, 128).astype(jnp.bfloat16)
    modal = lax.dot_general(filters, motion, (((0,), (1,)), ((), ())), preferred_element_type=F32)
    modes = lax.broadcasted_iota(jnp.int32, (MODES, 128), 0)
    count_ref[...] = jnp.zeros((8, 128), jnp.int32)
    count_ref[0:1, 0:CLASSES] = count_in[...]
    counts = jnp.where(modes == lane, jnp.broadcast_to(count_ref[0:1, :], (8, 128)), 0)
    counts = jnp.sum(counts, axis=1, keepdims=True)
    energies = []
    for kind in range(CLASSES):
        part = modal[MODES * kind : MODES * (kind + 1), :]
        part = jnp.where(modes < counts[kind : kind + 1, :], part * part, 0.0)
        energies.append(jnp.sum(part, axis=0, keepdims=True))
    demand_out[...] = 0.5 * jnp.log1p(jnp.concatenate(energies, axis=0))


def table_kernel(demand_ref, cells_ref, table_out):
    demand = demand_ref[...]
    for owner in range(table_out.shape[0]):
        cells = jnp.broadcast_to(cells_ref[owner : owner + 1, :], (CLASSES, 128))
        chosen = jnp.take_along_axis(demand, cells, axis=1)
        for level in range(table_out.shape[1]):
            table_out[owner, level] = chosen


def fragility_kernel(
    table_ref, slot_ref, kind_ref, city_ref, amplify_ref, median_ref, spread_ref, out_ref, gain_ref, tables_ref
):
    sources = table_ref.shape[0]
    slot, kind, city = slot_ref[...], kind_ref[...], city_ref[...]
    column = slot % 128
    key = (slot // 128) * CLASSES + kind
    demand = jnp.zeros((8, 128), F32)
    for source in range(sources):
        for each in range(CLASSES):
            row = jnp.broadcast_to(table_ref[source, 0, each : each + 1, :], (8, 128))
            found = jnp.take_along_axis(row, column, axis=1)
            demand = jnp.where(key == source * CLASSES + each, found, demand)
    gain_ref[...] = jnp.ones((8, 128), F32)
    gain_ref[0:1, 0:CITIES] = amplify_ref[...]
    gain = jnp.log(jnp.broadcast_to(gain_ref[0:1, :], (8, 128)))
    demand = demand + jnp.take_along_axis(gain, city, axis=1)
    tables_ref[...] = jnp.ones((128, 128), F32)
    batches = median_ref.shape[1]
    tables_ref[0:CLASSES, 0:batches] = median_ref[...]
    medians = tables_ref[...].T
    tables_ref[0:CLASSES, 0:batches] = spread_ref[...]
    spreads = tables_ref[...].T
    for group in range(8):
        level = jnp.broadcast_to(demand[group : group + 1, :], (8, 128))
        index = jnp.broadcast_to(kind[group : group + 1, :], (8, 128))
        for half in range(0, batches, 8):
            middle = jnp.take_along_axis(medians[half : half + 8, :], index, axis=1)
            width = jnp.take_along_axis(spreads[half : half + 8, :], index, axis=1)
            out_ref[half : half + 8, 128 * group : 128 * group + 128] = jax.nn.sigmoid((level - middle) / width)


VM = pl.BlockSpec(memory_space=pltpu.VMEM)


WEIGHTS = {"start": 1.4, "steps_first": 6.7, "steps_second": 6.5, "surface": 4.0, "fragility": 1.0}
UNIT_FLOPS = 1.15e10


def call(kernel, name, shapes, args, specs=None, scratch=(), limit=VMEM_LIMIT):
    out = [s if isinstance(s, jax.ShapeDtypeStruct) else jax.ShapeDtypeStruct(s, F32) for s in shapes]
    return pl.pallas_call(
        kernel,
        out_shape=out,
        in_specs=specs or [VM] * len(args),
        out_specs=[VM] * len(out),
        scratch_shapes=list(scratch),
        compiler_params=pltpu.CompilerParams(vmem_limit_bytes=limit),
        cost_estimate=pl.CostEstimate(flops=int(WEIGHTS.get(name, 0.3) * UNIT_FLOPS), bytes_accessed=0, transcendentals=0),
        name=name,
    )(*args)


def both_ways(to_up, to_down, axis):
    count = lax.axis_size(axis)
    forward = [(i, i + 1) for i in range(count - 1)]
    backward = [(i + 1, i) for i in range(count - 1)]
    return lax.ppermute(to_up, axis, forward), lax.ppermute(to_down, axis, backward)


def exchange_x(u, p, faces, coefficients):
    extra = list(coefficients)
    z_low, z_high = both_ways(faces, faces, "gz")
    planes = 3 * XU + (3 + len(extra)) * XP + XH + 1
    message = jax.ShapeDtypeStruct((planes, 16, 128), jnp.int16)
    halo, up, down, powers = call(
        functools.partial(x_message_kernel, bool(extra)),
        "x_message",
        [(8, 16, 128), message, message, (16, 128)],
        [z_low, z_high, u, p] + extra,
    )
    return halo, powers, *both_ways(up, down, "gx")


def y_messages(u, p, coefficients, halo, powers, x_low, x_high):
    extra = list(coefficients)
    planes = (3 * YU + (3 + len(extra)) * YP + YH) // 2 + 1
    message = jax.ShapeDtypeStruct((planes, 16, 128), jnp.int16)
    return call(
        functools.partial(y_message_kernel, bool(extra)),
        "y_message",
        [message, message],
        [u, p] + extra + [halo, powers, x_low, x_high],
    )


def body(
    displacement,
    previous,
    courant,
    damping,
    send_cells,
    building_slot,
    building_class,
    city,
    mode_count,
    modal_filter,
    amplify,
    median,
    spread,
):
    own = (3, 8, 16, 128)
    plane = (8, 16, 128)
    wide = pltpu.VMEM((2, 4, 24, 48, 128), F32)
    rates = pltpu.VMEM((4, 24, 32, 128), F32)
    samples = pltpu.VMEM((HALF, 24, 16, 128), F32)

    u, p = displacement, previous
    a, e, faces = call(
        start_kernel,
        "start",
        [plane, plane, plane],
        [u, p, courant, damping],
        specs=[pl.BlockSpec(memory_space=pltpu.HBM)] * 4,
        scratch=[pltpu.VMEM(own, F32)] * 2 + [pltpu.VMEM(plane, F32)] * 2 + [pltpu.SemaphoreType.DMA((8,))],
        limit=START_LIMIT,
    )
    halo, powers, x_low, x_high = exchange_x(u, p, faces, (a, e))
    messages = y_messages(u, p, (a, e), halo, powers, x_low, x_high)
    received = (halo, x_low, x_high, *both_ways(*messages, "gy"))
    weights = jnp.asarray(depth_weights(), jnp.bfloat16)
    u, p, faces, slab, seen, codes = call(
        functools.partial(steps_kernel, True),
        "steps_first",
        [own, own, plane, plane, plane, jax.ShapeDtypeStruct((3, 20, 32, 128), jnp.int16)],
        [u, p, a, e, *received, weights],
        scratch=[wide, rates, samples],
    )

    near_low, near_high = both_ways(slab, slab, "gx")
    halo, powers, x_low, x_high = exchange_x(u, p, faces, ())
    slab_messages = call(slab_message_kernel, "slab_message", [(24, 8, 128)] * 2, [slab, near_low, near_high, powers])
    side_low, side_high = both_ways(*slab_messages, "gy")
    messages = y_messages(u, p, (), halo, powers, x_low, x_high)
    received = (halo, x_low, x_high, *both_ways(*messages, "gy"))
    (demand,) = call(
        surface_kernel,
        "surface",
        [(CLASSES, 128)],
        [slab, near_low, near_high, side_low, side_high, jnp.asarray(slab_weights(), jnp.bfloat16), codes, seen]
        + [modal_filter.T, mode_count.reshape(1, CLASSES), messages[0]],
        specs=[VM] * 10 + [pl.BlockSpec(memory_space=pl.ANY)],
        scratch=[
            pltpu.VMEM((2, 24, 48, 128), F32),
            pltpu.VMEM((2, 24, 32, 128), F32),
            samples,
            pltpu.VMEM(plane, F32),
            pltpu.VMEM((3 * STEPS, CLASSES * MODES), F32),
            pltpu.VMEM((8, 128), jnp.int32),
        ],
    )
    owners, levels = lax.axis_size("gx"), lax.axis_size("gz")
    (table,) = call(
        table_kernel,
        "table",
        [(owners, levels, CLASSES, 128)],
        [demand, send_cells.reshape(owners, 128)],
    )
    table = table.reshape(owners * levels, CLASSES, 128)
    table = lax.all_to_all(table, ("gx", "gz"), split_axis=0, concat_axis=0, tiled=True)
    (field,) = call(
        functools.partial(steps_kernel, False), "steps_second", [own], [u, p, *received, weights, codes], scratch=[wide, rates]
    )
    (probability,) = call(
        fragility_kernel,
        "fragility",
        [(16, 1024)],
        [
            table.reshape(owners, levels, CLASSES, 128),
            building_slot.reshape(8, 128),
            building_class.reshape(8, 128),
            city.reshape(8, 128),
            amplify.reshape(1, CITIES),
            median.T,
            spread.T,
        ],
        scratch=[pltpu.VMEM((8, 128), F32), pltpu.VMEM((128, 128), F32)],
    )
    return (field, probability)


def solution(mesh):
    placed = (
        P(None, "gx", "gy", "gz"),
        P(None, "gx", "gy", "gz"),
        P("gx", "gy", "gz"),
        P("gx", "gy", "gz"),
        P("gx", "gy", None),
        P(("gx", "gy", "gz")),
        P(("gx", "gy", "gz")),
        P(("gx", "gy", "gz")),
        P(),
        P(),
        P(),
        P(),
        P(),
    )
    return jax.shard_map(
        body,
        mesh=mesh,
        in_specs=placed,
        out_specs=(P(None, "gx", "gy", "gz"), P(None, ("gx", "gy", "gz"))),
        check_vma=False,
    )
```

```python
import functools

import jax
import jax.numpy as jnp
import numpy as np
from jax import lax
from jax.experimental import pallas as pl
from jax.experimental.pallas import tpu as pltpu
from jax.sharding import PartitionSpec as P

STEPS = 8
HALF = 4
DEEP = 2 * HALF
CLASSES = 8
MODES = 8
CITIES = 16
F32 = jnp.float32
VMEM_LIMIT = 24 * 1024 * 1024
START_LIMIT = int(53.8 * 1024 * 1024)

XU, XP, XH = 8, 6, 7
YU, YP, YH = 24, 20, 20

FULL = 32000.0
BIAS = 200
UNIT_A = 2.0 / FULL
UNIT_E = 0.2 / 12.0 / FULL


PLANES = 4


def depth_weights():
    lanes = np.arange(256)
    result = np.zeros((3, 256, 256), np.float32)
    for k in range(3):
        at = lanes - 128 - 16 * k
        depth = np.where(lanes < 128, lanes, np.where(at < 8, at - 8, at + 120))
        used = (lanes < 128) | ((at >= 0) & (at < 16))
        apart = np.abs(depth[:, None] - depth[None, :])
        band = np.where(apart == 0, -90.0, np.where(apart == 1, 16.0, np.where(apart == 2, -1.0, 0.0)))
        result[k] = np.where(used[:, None] & used[None, :], band, 0.0)
        result[k, 0, 128 + 64 + 16 * k + 8] = 1.0
    return result


def slab_weights():
    lanes = np.arange(128)
    apart = np.abs(lanes[:, None] - lanes[None, :])
    band = np.where(apart == 0, -90.0, np.where(apart == 1, 16.0, np.where(apart == 2, -1.0, 0.0)))
    same = (lanes[:, None] // 16 == lanes[None, :] // 16) & (lanes[:, None] < 48)
    band = np.where(same, band, 0.0)
    return np.concatenate([band, band], axis=0)


def split(v):
    high = v.astype(jnp.bfloat16)
    return high, (v - high.astype(F32)).astype(jnp.bfloat16)


def lane_of():
    return lax.broadcasted_iota(jnp.int32, (8, 128), 1)


def pack_faces(values, lane):
    packed = pltpu.roll(values[0], 8, 1)
    for at in range(1, len(values)):
        packed = jnp.where(lane // 16 == at, pltpu.roll(values[at], (16 * at + 8) % 128, 1), packed)
    return packed


def start_kernel(u_in, p_in, c_in, d_in, a_ref, e_ref, face_ref, u_ref, p_ref, c_ref, d_ref, sems):
    copies = [pltpu.make_async_copy(c_in, c_ref, sems.at[0]), pltpu.make_async_copy(d_in, d_ref, sems.at[1])]
    for k in range(3):
        copies.append(pltpu.make_async_copy(u_in.at[k], u_ref.at[k], sems.at[2 + k]))
        copies.append(pltpu.make_async_copy(p_in.at[k], p_ref.at[k], sems.at[5 + k]))
    for copy in copies:
        copy.start()
    for copy in copies:
        copy.wait()
    lane = lane_of()

    def plane(x, carry):
        for row in (0, 8):
            rows = pl.ds(row, 8)
            share = 1.0 / (1.0 + d_ref[x, rows, :])
            values = [u_ref[k, x, rows, :] for k in range(3)] + [p_ref[k, x, rows, :] for k in range(3)]
            values += [2.0 * share, c_ref[x, rows, :] * share * (1.0 / 12.0)]
            a_ref[x, rows, :] = values[6]
            e_ref[x, rows, :] = values[7]
            face_ref[x, rows, :] = pack_faces(values, lane)
        return carry

    lax.fori_loop(0, 8, plane, 0)


def exponent_of(peak):
    peak = jnp.maximum(jnp.max(peak, axis=0, keepdims=True), 1e-30)
    return jnp.broadcast_to(jnp.ceil(jnp.log2(peak)), (8, 128))


def coded(values):
    return jnp.round(values).astype(jnp.int32).astype(jnp.int16)


def decoded(values):
    return values.astype(jnp.int32).astype(F32)


def twice(rows):
    return jnp.concatenate([rows, rows], axis=0)


def sent_exponents(message):
    both = decoded(message[message.shape[0] - 1]) - BIAS
    return both[0:8], both[8:16]


def x_message_kernel(coefficients, *refs):
    if coefficients:
        z_second_ref, z_first_ref, u_ref, p_ref, a_ref, e_ref, halo_ref, up_ref, down_ref, power_ref = refs
    else:
        z_second_ref, z_first_ref, u_ref, p_ref, halo_ref, up_ref, down_ref, power_ref = refs
    inner = lax.broadcasted_iota(jnp.int32, (16, 128), 1) % 16
    from_first = (inner < 8) == is_odd("gz")

    def largest(x, carry):
        field, face = carry
        for k in range(3):
            both = jnp.maximum(jnp.abs(u_ref[k, x]), jnp.abs(p_ref[k, x]))
            field = jnp.maximum(field, jnp.maximum(both[0:8], both[8:16]))
        halo = jnp.where(from_first, z_first_ref[x], z_second_ref[x])
        halo_ref[x] = halo
        halo = jnp.abs(halo)
        return field, jnp.maximum(face, jnp.maximum(halo[0:8], halo[8:16]))

    zero = jnp.zeros((8, 128), F32)
    field, face = lax.fori_loop(0, 8, largest, (zero, zero))
    powers = jnp.concatenate([exponent_of(field), exponent_of(face)], axis=0)
    power_ref[...] = powers
    up_ref[up_ref.shape[0] - 1] = coded(powers + BIAS)
    down_ref[down_ref.shape[0] - 1] = coded(powers + BIAS)
    scale = FULL * jnp.exp2(-powers)
    field, face = twice(scale[0:8]), twice(scale[8:16])

    def whole(x, carry):
        for k in range(3):
            code = coded(u_ref[k, x] * field)
            up_ref[XU * k + x] = code
            down_ref[XU * k + x] = code
        return carry

    def part(i, carry):
        parts = [(p_ref.at[k], field) for k in range(3)]
        if coefficients:
            parts += [(a_ref, 1.0 / UNIT_A), (e_ref, 1.0 / UNIT_E)]
        for at, (source, unit) in enumerate(parts):
            up_ref[3 * XU + XP * at + i] = coded(source[8 - XP + i] * unit)
            down_ref[3 * XU + XP * at + i] = coded(source[i] * unit)
        return carry

    at = 3 * XU + (5 if coefficients else 3) * XP

    def side(i, carry):
        up_ref[at + i] = coded(halo_ref[8 - XH + i] * face)
        down_ref[at + i] = coded(halo_ref[i] * face)
        return carry

    lax.fori_loop(0, 8, whole, 0)
    lax.fori_loop(0, XP, part, 0)
    lax.fori_loop(0, XH, side, 0)


def y_message_kernel(coefficients, *refs):
    if coefficients:
        u_ref, p_ref, a_ref, e_ref, halo_ref, power_ref, low_ref, high_ref, first_ref, second_ref = refs
    else:
        u_ref, p_ref, halo_ref, power_ref, low_ref, high_ref, first_ref, second_ref = refs
    odd = is_odd("gy")
    powers = power_ref[...]
    low_powers = jnp.concatenate(sent_exponents(low_ref), axis=0)
    high_powers = jnp.concatenate(sent_exponents(high_ref), axis=0)
    most = jnp.maximum(powers, jnp.maximum(low_powers, high_powers))
    for out_ref in (first_ref, second_ref):
        out_ref[out_ref.shape[0] - 1] = coded(most + BIAS)
    own_scale = FULL * jnp.exp2(-most)
    low_scale = jnp.exp2(low_powers - most)
    high_scale = jnp.exp2(high_powers - most)
    field = [twice(scale[0:8]) for scale in (own_scale, low_scale, high_scale)]
    face = [twice(scale[8:16]) for scale in (own_scale, low_scale, high_scale)]

    def put(at, pair):
        up = jnp.concatenate([pair[0][8:16], pair[1][8:16]], axis=0)
        down = jnp.concatenate([pair[0][0:8], pair[1][0:8]], axis=0)
        first_ref[at] = coded(jnp.where(odd, down, up))
        second_ref[at] = coded(jnp.where(odd, up, down))

    def group(parts, x_planes, y_planes, x_at, y_at):
        side = (y_planes - 8) // 4

        def own(i, carry):
            for at, (source, units) in enumerate(parts):
                put(y_at + at * y_planes // 2 + side + i, [source[2 * i + j] * units[0] for j in (0, 1)])
            return carry

        def sides(i, carry):
            for at, (_, units) in enumerate(parts):
                start = x_at + at * x_planes
                first = start + x_planes - 2 * side + 2 * i
                put(y_at + at * y_planes // 2 + i, [decoded(low_ref[first + j]) * units[1] for j in (0, 1)])
                first = start + 2 * i
                pair = [decoded(high_ref[first + j]) * units[2] for j in (0, 1)]
                put(y_at + at * y_planes // 2 + side + 4 + i, pair)
            return carry

        lax.fori_loop(0, 4, own, 0)
        lax.fori_loop(0, side, sides, 0)
        return x_at + len(parts) * x_planes, y_at + len(parts) * y_planes // 2

    x_at, y_at = group([(u_ref.at[k], field) for k in range(3)], XU, YU, 0, 0)
    parts = [(p_ref.at[k], field) for k in range(3)]
    if coefficients:
        parts += [(a_ref, (1.0 / UNIT_A, 1.0, 1.0)), (e_ref, (1.0 / UNIT_E, 1.0, 1.0))]
    x_at, y_at = group(parts, XP, YP, x_at, y_at)
    group([(halo_ref, face)], XH, YH, x_at, y_at)


def fill(parts, x_low, x_high, y_first, y_second, x_at, x_planes, y_at, y_planes):
    count = len(parts)
    side = (y_planes - 8) // 2
    odd = is_odd("gy")

    def own(i, carry):
        for target, row, block, _ in parts:
            target[8 + i, row + 8 : row + 24, :] = block[i]
        return carry

    def x_side(i, carry):
        for at, (target, row, _, units) in enumerate(parts):
            here = x_at + at * x_planes + i
            target[8 - x_planes + i, row + 8 : row + 24, :] = decoded(x_low[here]) * units[0]
            target[16 + i, row + 8 : row + 24, :] = decoded(x_high[here]) * units[1]
        return carry

    def y_side(i, carry):
        for at, (target, row, _, units) in enumerate(parts):
            here = y_at + at * y_planes // 2 + i
            first, second = decoded(y_first[here]), decoded(y_second[here])
            low = jnp.where(odd, first, second) * units[2]
            high = jnp.where(odd, second, first) * units[3]
            for j in (0, 1):
                target[8 - side + 2 * i + j, row : row + 8, :] = low[8 * j : 8 * j + 8]
                target[8 - side + 2 * i + j, row + 24 : row + 32, :] = high[8 * j : 8 * j + 8]
        return carry

    lax.fori_loop(0, 8, own, 0, unroll=2)
    lax.fori_loop(0, x_planes, x_side, 0)
    lax.fori_loop(0, y_planes // 2, y_side, 0, unroll=2)
    return x_at + count * x_planes, y_at + count * y_planes // 2


def steps_kernel(first, *refs):
    if first:
        (u_in, p_in, a_in, e_in, halo_in, x_low, x_high, y_first, y_second, weight_in) = refs[:10]
        (u_out, p_out, face_out, slab_out, seen_out, code_ref) = refs[10:16]
        state_ref, rate_ref, edge_ref = refs[16:]
    else:
        (u_in, p_in, halo_in, x_low, x_high, y_second, y_first, weight_in, code_ref) = refs[:9]
        u_out, state_ref, rate_ref = refs[9:]
    a_ref, e_ref, ha_ref, he_ref = (rate_ref.at[at] for at in range(4))
    lane = lane_of()
    inner = lane % 16

    sides = (x_low, x_high, y_first, y_second)
    powers = [sent_exponents(message) for message in sides]
    odd = is_odd("gy")
    swapped = list(zip(powers[2], powers[3]))
    powers[2] = [jnp.where(odd, one, other) for one, other in swapped]
    powers[3] = [jnp.where(odd, other, one) for one, other in swapped]
    field = [twice(jnp.exp2(power[0]) * (1.0 / FULL)) for power in powers]
    face = [twice(jnp.exp2(power[1]) * (1.0 / FULL)) for power in powers]
    x_at, y_at = fill([(state_ref.at[0, k], 8, u_in.at[k], field) for k in range(3)], *sides, 0, XU, 0, YU)
    parts = [(state_ref.at[1, k], 8, p_in.at[k], field) for k in range(3)]
    if first:
        parts += [(a_ref, 0, a_in, (UNIT_A,) * 4), (e_ref, 0, e_in, (UNIT_E,) * 4)]
    x_at, y_at = fill(parts, *sides, x_at, XP, y_at, YP)
    fill([(state_ref.at[0, 3], 8, halo_in, face)], *sides, x_at, XH, y_at, YH)

    unit = jnp.where(lane < 112, UNIT_A, UNIT_E)

    def prepare(x, carry):
        for half in (0, 16):
            held = pl.ds(half, 16)
            if first:
                code_ref[0, x - 2, held, :] = coded(a_ref[x, held, :] * (1.0 / UNIT_A))
                code_ref[1, x - 2, held, :] = coded(e_ref[x, held, :] * (1.0 / UNIT_E))
                sides = state_ref[0, 3, x, pl.ds(8 + half, 16), :]
                scale = twice(jnp.where(lane < 96, 0.0, 1.0 / unit))
                code_ref[2, x - 2, held, :] = coded(jnp.where(scale > 0.0, sides * scale, 0.0))
            else:
                a_ref[x, held, :] = decoded(code_ref[0, x - 2, held, :]) * UNIT_A
                e_ref[x, held, :] = decoded(code_ref[1, x - 2, held, :]) * UNIT_E
                sides = decoded(code_ref[2, x - 2, held, :]) * twice(unit)
            for tile in (0, 8):
                rows = pl.ds(8 + half + tile, 8)
                halo = state_ref[0, 3, x, rows, :]
                state_ref[0, 3, x, rows, :] = jnp.where(lane < 48, halo, 0.0)
                state_ref[1, 3, x, rows, :] = jnp.where(lane < 48, pltpu.roll(halo, 128 - 48, 1), 0.0)
                side = sides[tile : tile + 8]
                for target, at in ((ha_ref, 96), (he_ref, 112)):
                    spread = jnp.where(lane < 16, pltpu.roll(side, 128 - at, 1), pltpu.roll(side, 144 - at, 1))
                    spread = jnp.where(lane < 32, spread, pltpu.roll(side, 160 - at, 1))
                    target[x, pl.ds(half + tile, 8), :] = jnp.where(lane < 48, spread, 0.0)
        return carry

    lax.fori_loop(2, 22, prepare, 0, unroll=4)

    def advance(src, dst, x):
        rows = pl.ds(8, 32)
        fields = [[src[k, 2 + j, rows, :] for j in range(PLANES)] for k in range(4)]
        parts = [[split(v) for v in field] for field in fields]
        depth = []
        for k in range(3):
            pieces = [jnp.concatenate([parts[k][j][part], parts[3][j][part]], axis=1) for part in (0, 1) for j in range(PLANES)]
            both = jnp.dot(jnp.concatenate(pieces, axis=0), weight_in[k], preferred_element_type=F32)
            depth.append(both[0 : 32 * PLANES] + both[32 * PLANES :])
        side = depth[0][:, 128:] + depth[1][:, 128:] + depth[2][:, 128:]
        fresh = []
        for j in range(PLANES):
            for k in range(4):
                v = fields[k][j]
                near = (src[k, 1 + j, rows, :] + src[k, 3 + j, rows, :]) + (
                    src[k, 2 + j, pl.ds(7, 32), :] + src[k, 2 + j, pl.ds(9, 32), :]
                )
                far = (src[k, j, rows, :] + src[k, 4 + j, rows, :]) + (
                    src[k, 2 + j, pl.ds(6, 32), :] + src[k, 2 + j, pl.ds(10, 32), :]
                )
                along = side if k == 3 else depth[k][:, :128]
                laplace = along[32 * j : 32 * j + 32] + (16.0 * near - far)
                old = dst[k, x + j, rows, :]
                a_each, e_each = (ha_ref, he_ref) if k == 3 else (a_ref, e_ref)
                fresh.append((k, j, old + a_each[x + j] * (v - old) + e_each[x + j] * laplace))
        return fresh, side

    def one_step(step, carry):
        dst = state_ref.at[(step + 1) % 2]

        def planes(at, inside):
            x = 2 * step + 2 + PLANES * at
            fresh, side = advance(state_ref.at[step % 2, :, pl.ds(x - 2, 4 + PLANES)], dst, x)
            for k, j, value in fresh:
                dst[k, x + j, 8:40, :] = value
            if first:
                for j in range(PLANES):
                    edge_ref[step, x + j, :, :] = side[32 * j + 8 : 32 * j + 24]
            return inside

        lax.fori_loop(0, (20 - 4 * step) // PLANES, planes, 0)
        return carry

    lax.fori_loop(0, HALF, one_step, 0)

    block = pl.ds(16, 16)

    def finish(x, carry):
        for k in range(3):
            u_out[k, x, :, :] = state_ref[0, k, 8 + x, block, :]
            if first:
                p_out[k, x, :, :] = state_ref[1, k, 8 + x, block, :]
        if first:
            for row in (0, 8):
                rows = pl.ds(row, 8)
                values = [state_ref[slot, k, 8 + x, pl.ds(16 + row, 8), :] for slot in (0, 1) for k in range(3)]
                last = pack_faces(values, lane)
                face_out[x, rows, :] = last
                slab = values[0]
                for at in range(1, 6):
                    slab = jnp.where(lane // 16 == at, pltpu.roll(values[at], 16 * at, 1), slab)
                slab_out[x, rows, :] = slab
                seen = jnp.zeros((8, 128), F32)
                for step in range(HALF):
                    if step < HALF - 1:
                        sample = pltpu.roll(edge_ref[step + 1, 8 + x, rows, :], 56 + step, 1)
                    else:
                        sample = pltpu.roll(last, 120 + step, 1)
                    seen = jnp.where((inner == step) & (lane < 48), sample, seen)
                seen_out[x, rows, :] = seen
        return carry

    lax.fori_loop(0, 8, finish, 0, unroll=4)


def slab_message_kernel(own_ref, low_ref, high_ref, after_ref, up_ref, down_ref):
    def plane(i, carry):
        for at, source in ((0, low_ref), (8, own_ref), (16, high_ref)):
            up_ref[at + i] = source[i, 8:16, :]
            down_ref[at + i] = source[i, 0:8, :]
        return carry

    lax.fori_loop(0, 8, plane, 0, unroll=2)


def surface_kernel(
    own_in, x_low, x_high, y_low, y_high, weight_in, code_in, seen_in, filter_in, count_in, after_in,
    demand_out, state_ref, rate_ref, sample_ref, seen_ref, filter_ref, count_ref,
):
    lane = lane_of()
    inner = lane % 16

    def near_side(i, carry):
        state_ref[0, i, 16:32, :] = x_low[i]
        state_ref[0, 8 + i, 16:32, :] = own_in[i]
        state_ref[0, 16 + i, 16:32, :] = x_high[i]
        for part in range(3):
            state_ref[0, 8 * part + i, 8:16, :] = y_low[8 * part + i]
            state_ref[0, 8 * part + i, 32:40, :] = y_high[8 * part + i]
        return carry

    lax.fori_loop(0, 8, near_side, 0, unroll=2)

    def prepare(x, carry):
        for tile in range(4):
            rows = pl.ds(8 + 8 * tile, 8)
            value = state_ref[0, x, rows, :]
            state_ref[0, x, rows, :] = jnp.where(lane < 48, value, 0.0)
            state_ref[1, x, rows, :] = jnp.where(lane < 48, pltpu.roll(value, 128 - 48, 1), 0.0)
        return carry

    def rates(x, carry):
        for at, unit in ((0, UNIT_A), (1, UNIT_E)):
            for half in (0, 16):
                both = decoded(code_in[at, x - 2, half : half + 16, :]) * unit
                for tile in (0, 8):
                    rate = both[tile : tile + 8]
                    spread = jnp.where(lane < 32, pltpu.roll(rate, 16, 1), pltpu.roll(rate, 32, 1))
                    spread = jnp.where(lane < 16, rate, spread)
                    rate_ref[at, x, pl.ds(half + tile, 8), :] = jnp.where(lane < 48, spread, 0.0)
        return carry

    lax.fori_loop(0, 24, prepare, 0, unroll=4)
    lax.fori_loop(2, 22, rates, 0, unroll=4)

    def one_step(step, carry):
        dst = state_ref.at[(step + 1) % 2]

        def planes(at, inside):
            x = 2 * step + 2 + PLANES * at
            src = state_ref.at[step % 2, pl.ds(x - 2, 4 + PLANES)]
            rows = pl.ds(8, 32)
            fields = [src[2 + j, rows, :] for j in range(PLANES)]
            halves = jnp.concatenate([jnp.concatenate(split(v), axis=1) for v in fields], axis=0)
            depth = jnp.dot(halves, weight_in[...], preferred_element_type=F32)
            fresh = []
            for j, v in enumerate(fields):
                near = (src[1 + j, rows, :] + src[3 + j, rows, :]) + (src[2 + j, pl.ds(7, 32), :] + src[2 + j, pl.ds(9, 32), :])
                far = (src[j, rows, :] + src[4 + j, rows, :]) + (src[2 + j, pl.ds(6, 32), :] + src[2 + j, pl.ds(10, 32), :])
                laplace = depth[32 * j : 32 * j + 32] + (16.0 * near - far)
                old = dst[x + j, rows, :]
                fresh.append(old + rate_ref[0, x + j] * (v - old) + rate_ref[1, x + j] * laplace)
            for j, value in enumerate(fresh):
                dst[x + j, 8:40, :] = value
                sample_ref[step, x + j, :, :] = value[8:24]
            return inside

        lax.fori_loop(0, (20 - 4 * step) // PLANES, planes, 0)
        return carry

    lax.fori_loop(0, HALF, one_step, 0)

    def finish(x, carry):
        for row in (0, 8):
            rows = pl.ds(row, 8)
            seen = seen_in[x, rows, :]
            for step in range(HALF):
                at = HALF + step
                sample = pltpu.roll(sample_ref[step, 8 + x, rows, :], at, 1)
                seen = jnp.where((inner == at) & (lane < 48), sample, seen)
            seen_ref[x, rows, :] = seen
        return carry

    lax.fori_loop(0, 8, finish, 0, unroll=4)

    filter_ref[...] = filter_in[...].astype(F32)
    blocks = [jnp.zeros((8, CLASSES * MODES), F32)] * 16
    for k in range(3):
        blocks[2 * k] = filter_ref[pl.ds(k, STEPS, stride=3), :]
    filters = jnp.concatenate(blocks, axis=0).astype(jnp.bfloat16)
    motion = seen_ref[...].reshape(128, 128).astype(jnp.bfloat16)
    modal = lax.dot_general(filters, motion, (((0,), (1,)), ((), ())), preferred_element_type=F32)
    modes = lax.broadcasted_iota(jnp.int32, (MODES, 128), 0)
    count_ref[...] = jnp.zeros((8, 128), jnp.int32)
    count_ref[0:1, 0:CLASSES] = count_in[...]
    counts = jnp.where(modes == lane, jnp.broadcast_to(count_ref[0:1, :], (8, 128)), 0)
    counts = jnp.sum(counts, axis=1, keepdims=True)
    energies = []
    for kind in range(CLASSES):
        part = modal[MODES * kind : MODES * (kind + 1), :]
        part = jnp.where(modes < counts[kind : kind + 1, :], part * part, 0.0)
        energies.append(jnp.sum(part, axis=0, keepdims=True))
    demand_out[...] = 0.5 * jnp.log1p(jnp.concatenate(energies, axis=0))


def table_kernel(demand_ref, cells_ref, table_out):
    demand = demand_ref[...]
    for owner in range(table_out.shape[0]):
        cells = jnp.broadcast_to(cells_ref[owner : owner + 1, :], (CLASSES, 128))
        chosen = jnp.take_along_axis(demand, cells, axis=1)
        for level in range(table_out.shape[1]):
            table_out[owner, level] = chosen


def fragility_kernel(
    table_ref, slot_ref, kind_ref, city_ref, amplify_ref, median_ref, spread_ref, out_ref, gain_ref, tables_ref
):
    sources = table_ref.shape[0]
    slot, kind, city = slot_ref[...], kind_ref[...], city_ref[...]
    column = slot % 128
    key = (slot // 128) * CLASSES + kind
    demand = jnp.zeros((8, 128), F32)
    for source in range(sources):
        for each in range(CLASSES):
            row = jnp.broadcast_to(table_ref[source, 0, each : each + 1, :], (8, 128))
            found = jnp.take_along_axis(row, column, axis=1)
            demand = jnp.where(key == source * CLASSES + each, found, demand)
    gain_ref[...] = jnp.ones((8, 128), F32)
    gain_ref[0:1, 0:CITIES] = amplify_ref[...]
    gain = jnp.log(jnp.broadcast_to(gain_ref[0:1, :], (8, 128)))
    demand = demand + jnp.take_along_axis(gain, city, axis=1)
    tables_ref[...] = jnp.ones((128, 128), F32)
    batches = median_ref.shape[1]
    tables_ref[0:CLASSES, 0:batches] = median_ref[...]
    medians = tables_ref[...].T
    tables_ref[0:CLASSES, 0:batches] = spread_ref[...]
    spreads = tables_ref[...].T
    for group in range(8):
        level = jnp.broadcast_to(demand[group : group + 1, :], (8, 128))
        index = jnp.broadcast_to(kind[group : group + 1, :], (8, 128))
        for half in range(0, batches, 8):
            middle = jnp.take_along_axis(medians[half : half + 8, :], index, axis=1)
            width = jnp.take_along_axis(spreads[half : half + 8, :], index, axis=1)
            out_ref[half : half + 8, 128 * group : 128 * group + 128] = jax.nn.sigmoid((level - middle) / width)


VM = pl.BlockSpec(memory_space=pltpu.VMEM)


WEIGHTS = {"start": 1.4, "steps_first": 6.7, "steps_second": 6.5, "surface": 4.0, "fragility": 1.0}
UNIT_FLOPS = 1.15e10


def call(kernel, name, shapes, args, specs=None, scratch=(), limit=VMEM_LIMIT):
    out = [s if isinstance(s, jax.ShapeDtypeStruct) else jax.ShapeDtypeStruct(s, F32) for s in shapes]
    return pl.pallas_call(
        kernel,
        out_shape=out,
        in_specs=specs or [VM] * len(args),
        out_specs=[VM] * len(out),
        scratch_shapes=list(scratch),
        compiler_params=pltpu.CompilerParams(vmem_limit_bytes=limit),
        cost_estimate=pl.CostEstimate(flops=int(WEIGHTS.get(name, 0.3) * UNIT_FLOPS), bytes_accessed=0, transcendentals=0),
        name=name,
    )(*args)


def both_ways(to_up, to_down, axis):
    count = lax.axis_size(axis)
    forward = [(i, i + 1) for i in range(count - 1)]
    backward = [(i + 1, i) for i in range(count - 1)]
    return lax.ppermute(to_up, axis, forward), lax.ppermute(to_down, axis, backward)


def swaps(first, second, axis):
    count = lax.axis_size(axis)
    pairs = [[(i, i + 1) for i in range(begin, count - 1, 2)] for begin in (0, 1)]
    pairs = [ways + [(b, a) for a, b in ways] for ways in pairs]
    return lax.ppermute(first, axis, pairs[0]), lax.ppermute(second, axis, pairs[1])


def is_odd(axis):
    return lax.rem(lax.axis_index(axis), 2) == 1


def exchange_x(u, p, faces, coefficients):
    extra = list(coefficients)
    z_first, z_second = swaps(faces, faces, "gz")
    planes = 3 * XU + (3 + len(extra)) * XP + XH + 1
    message = jax.ShapeDtypeStruct((planes, 16, 128), jnp.int16)
    halo, up, down, powers = call(
        functools.partial(x_message_kernel, bool(extra)),
        "x_message",
        [(8, 16, 128), message, message, (16, 128)],
        [z_second, z_first, u, p] + extra,
    )
    return halo, powers, *both_ways(up, down, "gx")


def y_messages(u, p, coefficients, halo, powers, x_low, x_high):
    extra = list(coefficients)
    planes = (3 * YU + (3 + len(extra)) * YP + YH) // 2 + 1
    message = jax.ShapeDtypeStruct((planes, 16, 128), jnp.int16)
    return call(
        functools.partial(y_message_kernel, bool(extra)),
        "y_message",
        [message, message],
        [u, p] + extra + [halo, powers, x_low, x_high],
    )


def body(
    displacement,
    previous,
    courant,
    damping,
    send_cells,
    building_slot,
    building_class,
    city,
    mode_count,
    modal_filter,
    amplify,
    median,
    spread,
):
    own = (3, 8, 16, 128)
    plane = (8, 16, 128)
    wide = pltpu.VMEM((2, 4, 24, 48, 128), F32)
    rates = pltpu.VMEM((4, 24, 32, 128), F32)
    samples = pltpu.VMEM((HALF, 24, 16, 128), F32)

    u, p = displacement, previous
    a, e, faces = call(
        start_kernel,
        "start",
        [plane, plane, plane],
        [u, p, courant, damping],
        specs=[pl.BlockSpec(memory_space=pltpu.HBM)] * 4,
        scratch=[pltpu.VMEM(own, F32)] * 2 + [pltpu.VMEM(plane, F32)] * 2 + [pltpu.SemaphoreType.DMA((8,))],
        limit=START_LIMIT,
    )
    halo, powers, x_low, x_high = exchange_x(u, p, faces, (a, e))
    messages = y_messages(u, p, (a, e), halo, powers, x_low, x_high)
    received = (halo, x_low, x_high, *swaps(*messages, "gy"))
    weights = jnp.asarray(depth_weights(), jnp.bfloat16)
    u, p, faces, slab, seen, codes = call(
        functools.partial(steps_kernel, True),
        "steps_first",
        [own, own, plane, plane, plane, jax.ShapeDtypeStruct((3, 20, 32, 128), jnp.int16)],
        [u, p, a, e, *received, weights],
        scratch=[wide, rates, samples],
    )

    near_low, near_high = both_ways(slab, slab, "gx")
    halo, powers, x_low, x_high = exchange_x(u, p, faces, ())
    slab_messages = call(slab_message_kernel, "slab_message", [(24, 8, 128)] * 2, [slab, near_low, near_high, powers])
    side_low, side_high = both_ways(*slab_messages, "gy")
    messages = y_messages(u, p, (), halo, powers, x_low, x_high)
    received = (halo, x_low, x_high, *reversed(swaps(*messages, "gy")))
    (demand,) = call(
        surface_kernel,
        "surface",
        [(CLASSES, 128)],
        [slab, near_low, near_high, side_low, side_high, jnp.asarray(slab_weights(), jnp.bfloat16), codes, seen]
        + [modal_filter.T, mode_count.reshape(1, CLASSES), messages[0]],
        specs=[VM] * 10 + [pl.BlockSpec(memory_space=pl.ANY)],
        scratch=[
            pltpu.VMEM((2, 24, 48, 128), F32),
            pltpu.VMEM((2, 24, 32, 128), F32),
            samples,
            pltpu.VMEM(plane, F32),
            pltpu.VMEM((3 * STEPS, CLASSES * MODES), F32),
            pltpu.VMEM((8, 128), jnp.int32),
        ],
    )
    owners, levels = lax.axis_size("gx"), lax.axis_size("gz")
    (table,) = call(
        table_kernel,
        "table",
        [(owners, levels, CLASSES, 128)],
        [demand, send_cells.reshape(owners, 128)],
    )
    table = table.reshape(owners * levels, CLASSES, 128)
    table = lax.all_to_all(table, ("gx", "gz"), split_axis=0, concat_axis=0, tiled=True)
    (field,) = call(
        functools.partial(steps_kernel, False), "steps_second", [own], [u, p, *received, weights, codes], scratch=[wide, rates]
    )
    (probability,) = call(
        fragility_kernel,
        "fragility",
        [(16, 1024)],
        [
            table.reshape(owners, levels, CLASSES, 128),
            building_slot.reshape(8, 128),
            building_class.reshape(8, 128),
            city.reshape(8, 128),
            amplify.reshape(1, CITIES),
            median.T,
            spread.T,
        ],
        scratch=[pltpu.VMEM((8, 128), F32), pltpu.VMEM((128, 128), F32)],
    )
    return (field, probability)


def solution(mesh):
    placed = (
        P(None, "gx", "gy", "gz"),
        P(None, "gx", "gy", "gz"),
        P("gx", "gy", "gz"),
        P("gx", "gy", "gz"),
        P("gx", "gy", None),
        P(("gx", "gy", "gz")),
        P(("gx", "gy", "gz")),
        P(("gx", "gy", "gz")),
        P(),
        P(),
        P(),
        P(),
        P(),
    )
    return jax.shard_map(
        body,
        mesh=mesh,
        in_specs=placed,
        out_specs=(P(None, "gx", "gy", "gz"), P(None, ("gx", "gy", "gz"))),
        check_vma=False,
    )
```

```python
import functools

import jax
import jax.numpy as jnp
import numpy as np
from jax import lax
from jax.experimental import pallas as pl
from jax.experimental.pallas import tpu as pltpu
from jax.sharding import PartitionSpec as P

STEPS = 8
HALF = 4
DEEP = 2 * HALF
CLASSES = 8
MODES = 8
CITIES = 16
F32 = jnp.float32
VMEM_LIMIT = 24 * 1024 * 1024
START_LIMIT = int(53.8 * 1024 * 1024)

XU, XP, XH = 8, 6, 7
YU, YP, YH = 24, 20, 20

FULL = 32000.0
BIAS = 200
UNIT_A = 2.0 / FULL
UNIT_E = 0.2 / 12.0 / FULL


PLANES = 4


def depth_weights():
    lanes = np.arange(256)
    result = np.zeros((3, 256, 256), np.float32)
    for k in range(3):
        at = lanes - 128 - 16 * k
        depth = np.where(lanes < 128, lanes, np.where(at < 8, at - 8, at + 120))
        used = (lanes < 128) | ((at >= 0) & (at < 16))
        apart = np.abs(depth[:, None] - depth[None, :])
        band = np.where(apart == 0, -90.0, np.where(apart == 1, 16.0, np.where(apart == 2, -1.0, 0.0)))
        result[k] = np.where(used[:, None] & used[None, :], band, 0.0)
        result[k, 0, 128 + 64 + 16 * k + 8] = 1.0
    return result


def slab_weights():
    lanes = np.arange(128)
    apart = np.abs(lanes[:, None] - lanes[None, :])
    band = np.where(apart == 0, -90.0, np.where(apart == 1, 16.0, np.where(apart == 2, -1.0, 0.0)))
    same = (lanes[:, None] // 16 == lanes[None, :] // 16) & (lanes[:, None] < 48)
    band = np.where(same, band, 0.0)
    return np.concatenate([band, band], axis=0)


def split(v):
    high = v.astype(jnp.bfloat16)
    return high, (v - high.astype(F32)).astype(jnp.bfloat16)


def lane_of():
    return lax.broadcasted_iota(jnp.int32, (8, 128), 1)


def pack_faces(values, lane):
    packed = pltpu.roll(values[0], 8, 1)
    for at in range(1, len(values)):
        packed = jnp.where(lane // 16 == at, pltpu.roll(values[at], (16 * at + 8) % 128, 1), packed)
    return packed


def start_kernel(u_in, p_in, c_in, d_in, a_ref, e_ref, face_ref, u_ref, p_ref, c_ref, d_ref, sems):
    copies = [pltpu.make_async_copy(c_in, c_ref, sems.at[0]), pltpu.make_async_copy(d_in, d_ref, sems.at[1])]
    for k in range(3):
        copies.append(pltpu.make_async_copy(u_in.at[k], u_ref.at[k], sems.at[2 + k]))
        copies.append(pltpu.make_async_copy(p_in.at[k], p_ref.at[k], sems.at[5 + k]))
    for copy in copies:
        copy.start()
    for copy in copies:
        copy.wait()
    lane = lane_of()

    def plane(x, carry):
        for row in (0, 8):
            rows = pl.ds(row, 8)
            share = 1.0 / (1.0 + d_ref[x, rows, :])
            values = [u_ref[k, x, rows, :] for k in range(3)] + [p_ref[k, x, rows, :] for k in range(3)]
            values += [2.0 * share, c_ref[x, rows, :] * share * (1.0 / 12.0)]
            a_ref[x, rows, :] = values[6]
            e_ref[x, rows, :] = values[7]
            face_ref[x, rows, :] = pack_faces(values, lane)
        return carry

    lax.fori_loop(0, 8, plane, 0)


def exponent_of(peak):
    peak = jnp.maximum(jnp.max(peak, axis=0, keepdims=True), 1e-30)
    return jnp.broadcast_to(jnp.ceil(jnp.log2(peak)), (8, 128))


def coded(values):
    return jnp.round(values).astype(jnp.int32).astype(jnp.int16)


def decoded(values):
    return values.astype(jnp.int32).astype(F32)


def twice(rows):
    return jnp.concatenate([rows, rows], axis=0)


def sent_exponents(message):
    both = decoded(message[message.shape[0] - 1]) - BIAS
    return both[0:8], both[8:16]


def x_message_kernel(coefficients, *refs):
    if coefficients:
        z_second_ref, z_first_ref, u_ref, p_ref, a_ref, e_ref, halo_ref, up_ref, down_ref, power_ref = refs
    else:
        z_second_ref, z_first_ref, u_ref, p_ref, halo_ref, up_ref, down_ref, power_ref = refs
    inner = lax.broadcasted_iota(jnp.int32, (16, 128), 1) % 16
    from_first = (inner < 8) == is_odd("gz")

    def largest(x, carry):
        field, face = carry
        for k in range(3):
            both = jnp.maximum(jnp.abs(u_ref[k, x]), jnp.abs(p_ref[k, x]))
            field = jnp.maximum(field, jnp.maximum(both[0:8], both[8:16]))
        halo = jnp.where(from_first, z_first_ref[x], z_second_ref[x])
        halo_ref[x] = halo
        halo = jnp.abs(halo)
        return field, jnp.maximum(face, jnp.maximum(halo[0:8], halo[8:16]))

    zero = jnp.zeros((8, 128), F32)
    field, face = lax.fori_loop(0, 8, largest, (zero, zero))
    powers = jnp.concatenate([exponent_of(field), exponent_of(face)], axis=0)
    power_ref[...] = powers
    up_ref[up_ref.shape[0] - 1] = coded(powers + BIAS)
    down_ref[down_ref.shape[0] - 1] = coded(powers + BIAS)
    scale = FULL * jnp.exp2(-powers)
    field, face = twice(scale[0:8]), twice(scale[8:16])

    def whole(x, carry):
        for k in range(3):
            code = coded(u_ref[k, x] * field)
            up_ref[XU * k + x] = code
            down_ref[XU * k + x] = code
        return carry

    def part(i, carry):
        parts = [(p_ref.at[k], field) for k in range(3)]
        if coefficients:
            parts += [(a_ref, 1.0 / UNIT_A), (e_ref, 1.0 / UNIT_E)]
        for at, (source, unit) in enumerate(parts):
            up_ref[3 * XU + XP * at + i] = coded(source[8 - XP + i] * unit)
            down_ref[3 * XU + XP * at + i] = coded(source[i] * unit)
        return carry

    at = 3 * XU + (5 if coefficients else 3) * XP

    def side(i, carry):
        up_ref[at + i] = coded(halo_ref[8 - XH + i] * face)
        down_ref[at + i] = coded(halo_ref[i] * face)
        return carry

    lax.fori_loop(0, 8, whole, 0)
    lax.fori_loop(0, XP, part, 0)
    lax.fori_loop(0, XH, side, 0)


def y_message_kernel(coefficients, *refs):
    if coefficients:
        u_ref, p_ref, a_ref, e_ref, halo_ref, power_ref, low_ref, high_ref, first_ref, second_ref = refs
    else:
        u_ref, p_ref, halo_ref, power_ref, low_ref, high_ref, second_ref, first_ref = refs
    odd = is_odd("gy")
    powers = power_ref[...]
    low_powers = jnp.concatenate(sent_exponents(low_ref), axis=0)
    high_powers = jnp.concatenate(sent_exponents(high_ref), axis=0)
    most = jnp.maximum(powers, jnp.maximum(low_powers, high_powers))
    for out_ref in (first_ref, second_ref):
        out_ref[out_ref.shape[0] - 1] = coded(most + BIAS)
    own_scale = FULL * jnp.exp2(-most)
    low_scale = jnp.exp2(low_powers - most)
    high_scale = jnp.exp2(high_powers - most)
    field = [twice(scale[0:8]) for scale in (own_scale, low_scale, high_scale)]
    face = [twice(scale[8:16]) for scale in (own_scale, low_scale, high_scale)]

    def put(at, pair):
        up = jnp.concatenate([pair[0][8:16], pair[1][8:16]], axis=0)
        down = jnp.concatenate([pair[0][0:8], pair[1][0:8]], axis=0)
        first_ref[at] = coded(jnp.where(odd, down, up))
        second_ref[at] = coded(jnp.where(odd, up, down))

    def group(parts, x_planes, y_planes, x_at, y_at):
        side = (y_planes - 8) // 4

        def own(i, carry):
            for at, (source, units) in enumerate(parts):
                put(y_at + at * y_planes // 2 + side + i, [source[2 * i + j] * units[0] for j in (0, 1)])
            return carry

        def sides(i, carry):
            for at, (_, units) in enumerate(parts):
                start = x_at + at * x_planes
                first = start + x_planes - 2 * side + 2 * i
                put(y_at + at * y_planes // 2 + i, [decoded(low_ref[first + j]) * units[1] for j in (0, 1)])
                first = start + 2 * i
                pair = [decoded(high_ref[first + j]) * units[2] for j in (0, 1)]
                put(y_at + at * y_planes // 2 + side + 4 + i, pair)
            return carry

        lax.fori_loop(0, 4, own, 0)
        lax.fori_loop(0, side, sides, 0)
        return x_at + len(parts) * x_planes, y_at + len(parts) * y_planes // 2

    x_at, y_at = group([(u_ref.at[k], field) for k in range(3)], XU, YU, 0, 0)
    parts = [(p_ref.at[k], field) for k in range(3)]
    if coefficients:
        parts += [(a_ref, (1.0 / UNIT_A, 1.0, 1.0)), (e_ref, (1.0 / UNIT_E, 1.0, 1.0))]
    x_at, y_at = group(parts, XP, YP, x_at, y_at)
    group([(halo_ref, face)], XH, YH, x_at, y_at)


def fill(parts, x_low, x_high, y_first, y_second, x_at, x_planes, y_at, y_planes):
    count = len(parts)
    side = (y_planes - 8) // 2
    odd = is_odd("gy")

    def own(i, carry):
        for target, row, block, _ in parts:
            target[8 + i, row + 8 : row + 24, :] = block[i]
        return carry

    def x_side(i, carry):
        for at, (target, row, _, units) in enumerate(parts):
            here = x_at + at * x_planes + i
            target[8 - x_planes + i, row + 8 : row + 24, :] = decoded(x_low[here]) * units[0]
            target[16 + i, row + 8 : row + 24, :] = decoded(x_high[here]) * units[1]
        return carry

    def y_side(i, carry):
        for at, (target, row, _, units) in enumerate(parts):
            here = y_at + at * y_planes // 2 + i
            first, second = decoded(y_first[here]), decoded(y_second[here])
            low = jnp.where(odd, first, second) * units[2]
            high = jnp.where(odd, second, first) * units[3]
            for j in (0, 1):
                target[8 - side + 2 * i + j, row : row + 8, :] = low[8 * j : 8 * j + 8]
                target[8 - side + 2 * i + j, row + 24 : row + 32, :] = high[8 * j : 8 * j + 8]
        return carry

    lax.fori_loop(0, 8, own, 0, unroll=2)
    lax.fori_loop(0, x_planes, x_side, 0)
    lax.fori_loop(0, y_planes // 2, y_side, 0, unroll=2)
    return x_at + count * x_planes, y_at + count * y_planes // 2


def steps_kernel(first, *refs):
    if first:
        (u_in, p_in, a_in, e_in, halo_in, x_low, x_high, y_first, y_second, weight_in) = refs[:10]
        (u_out, p_out, face_out, slab_out, seen_out, code_ref) = refs[10:16]
        state_ref, rate_ref, edge_ref = refs[16:]
    else:
        (u_in, p_in, halo_in, x_low, x_high, y_first, y_second, weight_in, code_ref) = refs[:9]
        u_out, state_ref, rate_ref = refs[9:]
    a_ref, e_ref, ha_ref, he_ref = (rate_ref.at[at] for at in range(4))
    lane = lane_of()
    inner = lane % 16

    sides = (x_low, x_high, y_first, y_second)
    powers = [sent_exponents(message) for message in sides]
    odd = is_odd("gy")
    swapped = list(zip(powers[2], powers[3]))
    powers[2] = [jnp.where(odd, one, other) for one, other in swapped]
    powers[3] = [jnp.where(odd, other, one) for one, other in swapped]
    field = [twice(jnp.exp2(power[0]) * (1.0 / FULL)) for power in powers]
    face = [twice(jnp.exp2(power[1]) * (1.0 / FULL)) for power in powers]
    x_at, y_at = fill([(state_ref.at[0, k], 8, u_in.at[k], field) for k in range(3)], *sides, 0, XU, 0, YU)
    parts = [(state_ref.at[1, k], 8, p_in.at[k], field) for k in range(3)]
    if first:
        parts += [(a_ref, 0, a_in, (UNIT_A,) * 4), (e_ref, 0, e_in, (UNIT_E,) * 4)]
    x_at, y_at = fill(parts, *sides, x_at, XP, y_at, YP)
    fill([(state_ref.at[0, 3], 8, halo_in, face)], *sides, x_at, XH, y_at, YH)

    unit = jnp.where(lane < 112, UNIT_A, UNIT_E)

    def prepare(x, carry):
        for half in (0, 16):
            held = pl.ds(half, 16)
            if first:
                code_ref[0, x - 2, held, :] = coded(a_ref[x, held, :] * (1.0 / UNIT_A))
                code_ref[1, x - 2, held, :] = coded(e_ref[x, held, :] * (1.0 / UNIT_E))
                sides = state_ref[0, 3, x, pl.ds(8 + half, 16), :]
                scale = twice(jnp.where(lane < 96, 0.0, 1.0 / unit))
                code_ref[2, x - 2, held, :] = coded(jnp.where(scale > 0.0, sides * scale, 0.0))
            else:
                a_ref[x, held, :] = decoded(code_ref[0, x - 2, held, :]) * UNIT_A
                e_ref[x, held, :] = decoded(code_ref[1, x - 2, held, :]) * UNIT_E
                sides = decoded(code_ref[2, x - 2, held, :]) * twice(unit)
            for tile in (0, 8):
                rows = pl.ds(8 + half + tile, 8)
                halo = state_ref[0, 3, x, rows, :]
                state_ref[0, 3, x, rows, :] = jnp.where(lane < 48, halo, 0.0)
                state_ref[1, 3, x, rows, :] = jnp.where(lane < 48, pltpu.roll(halo, 128 - 48, 1), 0.0)
                side = sides[tile : tile + 8]
                for target, at in ((ha_ref, 96), (he_ref, 112)):
                    spread = jnp.where(lane < 16, pltpu.roll(side, 128 - at, 1), pltpu.roll(side, 144 - at, 1))
                    spread = jnp.where(lane < 32, spread, pltpu.roll(side, 160 - at, 1))
                    target[x, pl.ds(half + tile, 8), :] = jnp.where(lane < 48, spread, 0.0)
        return carry

    lax.fori_loop(2, 22, prepare, 0, unroll=4)

    def advance(src, dst, x):
        rows = pl.ds(8, 32)
        fields = [[src[k, 2 + j, rows, :] for j in range(PLANES)] for k in range(4)]
        parts = [[split(v) for v in field] for field in fields]
        depth = []
        for k in range(3):
            pieces = [jnp.concatenate([parts[k][j][part], parts[3][j][part]], axis=1) for part in (0, 1) for j in range(PLANES)]
            both = jnp.dot(jnp.concatenate(pieces, axis=0), weight_in[k], preferred_element_type=F32)
            depth.append(both[0 : 32 * PLANES] + both[32 * PLANES :])
        side = depth[0][:, 128:] + depth[1][:, 128:] + depth[2][:, 128:]
        fresh = []
        for j in range(PLANES):
            for k in range(4):
                v = fields[k][j]
                near = (src[k, 1 + j, rows, :] + src[k, 3 + j, rows, :]) + (
                    src[k, 2 + j, pl.ds(7, 32), :] + src[k, 2 + j, pl.ds(9, 32), :]
                )
                far = (src[k, j, rows, :] + src[k, 4 + j, rows, :]) + (
                    src[k, 2 + j, pl.ds(6, 32), :] + src[k, 2 + j, pl.ds(10, 32), :]
                )
                along = side if k == 3 else depth[k][:, :128]
                laplace = along[32 * j : 32 * j + 32] + (16.0 * near - far)
                old = dst[k, x + j, rows, :]
                a_each, e_each = (ha_ref, he_ref) if k == 3 else (a_ref, e_ref)
                fresh.append((k, j, old + a_each[x + j] * (v - old) + e_each[x + j] * laplace))
        return fresh, side

    def one_step(step, carry):
        dst = state_ref.at[(step + 1) % 2]

        def planes(at, inside):
            x = 2 * step + 2 + PLANES * at
            fresh, side = advance(state_ref.at[step % 2, :, pl.ds(x - 2, 4 + PLANES)], dst, x)
            for k, j, value in fresh:
                dst[k, x + j, 8:40, :] = value
            if first:
                for j in range(PLANES):
                    edge_ref[step, x + j, :, :] = side[32 * j + 8 : 32 * j + 24]
            return inside

        lax.fori_loop(0, (20 - 4 * step) // PLANES, planes, 0)
        return carry

    lax.fori_loop(0, HALF, one_step, 0)

    block = pl.ds(16, 16)

    def finish(x, carry):
        for k in range(3):
            u_out[k, x, :, :] = state_ref[0, k, 8 + x, block, :]
            if first:
                p_out[k, x, :, :] = state_ref[1, k, 8 + x, block, :]
        if first:
            for row in (0, 8):
                rows = pl.ds(row, 8)
                values = [state_ref[slot, k, 8 + x, pl.ds(16 + row, 8), :] for slot in (0, 1) for k in range(3)]
                last = pack_faces(values, lane)
                face_out[x, rows, :] = last
                slab = values[0]
                for at in range(1, 6):
                    slab = jnp.where(lane // 16 == at, pltpu.roll(values[at], 16 * at, 1), slab)
                slab_out[x, rows, :] = slab
                seen = jnp.zeros((8, 128), F32)
                for step in range(HALF):
                    if step < HALF - 1:
                        sample = pltpu.roll(edge_ref[step + 1, 8 + x, rows, :], 56 + step, 1)
                    else:
                        sample = pltpu.roll(last, 120 + step, 1)
                    seen = jnp.where((inner == step) & (lane < 48), sample, seen)
                seen_out[x, rows, :] = seen
        return carry

    lax.fori_loop(0, 8, finish, 0, unroll=4)


def slab_message_kernel(own_ref, low_ref, high_ref, after_ref, first_ref, second_ref):
    odd = is_odd("gy")

    def plane(i, carry):
        for at, source in ((0, low_ref), (8, own_ref), (16, high_ref)):
            up, down = source[i, 8:16, :], source[i, 0:8, :]
            first_ref[at + i] = jnp.where(odd, down, up)
            second_ref[at + i] = jnp.where(odd, up, down)
        return carry

    lax.fori_loop(0, 8, plane, 0, unroll=2)


def surface_kernel(
    own_in, x_low, x_high, y_first, y_second, weight_in, code_in, seen_in, filter_in, count_in, after_in,
    demand_out, state_ref, rate_ref, sample_ref, seen_ref, filter_ref, count_ref,
):
    lane = lane_of()
    inner = lane % 16

    odd = is_odd("gy")

    def near_side(i, carry):
        state_ref[0, i, 16:32, :] = x_low[i]
        state_ref[0, 8 + i, 16:32, :] = own_in[i]
        state_ref[0, 16 + i, 16:32, :] = x_high[i]
        for part in range(3):
            one, other = y_first[8 * part + i], y_second[8 * part + i]
            state_ref[0, 8 * part + i, 8:16, :] = jnp.where(odd, one, other)
            state_ref[0, 8 * part + i, 32:40, :] = jnp.where(odd, other, one)
        return carry

    lax.fori_loop(0, 8, near_side, 0, unroll=2)

    def prepare(x, carry):
        for tile in range(4):
            rows = pl.ds(8 + 8 * tile, 8)
            value = state_ref[0, x, rows, :]
            state_ref[0, x, rows, :] = jnp.where(lane < 48, value, 0.0)
            state_ref[1, x, rows, :] = jnp.where(lane < 48, pltpu.roll(value, 128 - 48, 1), 0.0)
        return carry

    def rates(x, carry):
        for at, unit in ((0, UNIT_A), (1, UNIT_E)):
            for half in (0, 16):
                both = decoded(code_in[at, x - 2, half : half + 16, :]) * unit
                for tile in (0, 8):
                    rate = both[tile : tile + 8]
                    spread = jnp.where(lane < 32, pltpu.roll(rate, 16, 1), pltpu.roll(rate, 32, 1))
                    spread = jnp.where(lane < 16, rate, spread)
                    rate_ref[at, x, pl.ds(half + tile, 8), :] = jnp.where(lane < 48, spread, 0.0)
        return carry

    lax.fori_loop(0, 24, prepare, 0, unroll=4)
    lax.fori_loop(2, 22, rates, 0, unroll=4)

    def one_step(step, carry):
        dst = state_ref.at[(step + 1) % 2]

        def planes(at, inside):
            x = 2 * step + 2 + PLANES * at
            src = state_ref.at[step % 2, pl.ds(x - 2, 4 + PLANES)]
            rows = pl.ds(8, 32)
            fields = [src[2 + j, rows, :] for j in range(PLANES)]
            halves = jnp.concatenate([jnp.concatenate(split(v), axis=1) for v in fields], axis=0)
            depth = jnp.dot(halves, weight_in[...], preferred_element_type=F32)
            fresh = []
            for j, v in enumerate(fields):
                near = (src[1 + j, rows, :] + src[3 + j, rows, :]) + (src[2 + j, pl.ds(7, 32), :] + src[2 + j, pl.ds(9, 32), :])
                far = (src[j, rows, :] + src[4 + j, rows, :]) + (src[2 + j, pl.ds(6, 32), :] + src[2 + j, pl.ds(10, 32), :])
                laplace = depth[32 * j : 32 * j + 32] + (16.0 * near - far)
                old = dst[x + j, rows, :]
                fresh.append(old + rate_ref[0, x + j] * (v - old) + rate_ref[1, x + j] * laplace)
            for j, value in enumerate(fresh):
                dst[x + j, 8:40, :] = value
                sample_ref[step, x + j, :, :] = value[8:24]
            return inside

        lax.fori_loop(0, (20 - 4 * step) // PLANES, planes, 0)
        return carry

    lax.fori_loop(0, HALF, one_step, 0)

    def finish(x, carry):
        for row in (0, 8):
            rows = pl.ds(row, 8)
            seen = seen_in[x, rows, :]
            for step in range(HALF):
                at = HALF + step
                sample = pltpu.roll(sample_ref[step, 8 + x, rows, :], at, 1)
                seen = jnp.where((inner == at) & (lane < 48), sample, seen)
            seen_ref[x, rows, :] = seen
        return carry

    lax.fori_loop(0, 8, finish, 0, unroll=4)

    filter_ref[...] = filter_in[...].astype(F32)
    blocks = [jnp.zeros((8, CLASSES * MODES), F32)] * 16
    for k in range(3):
        blocks[2 * k] = filter_ref[pl.ds(k, STEPS, stride=3), :]
    filters = jnp.concatenate(blocks, axis=0).astype(jnp.bfloat16)
    motion = seen_ref[...].reshape(128, 128).astype(jnp.bfloat16)
    modal = lax.dot_general(filters, motion, (((0,), (1,)), ((), ())), preferred_element_type=F32)
    modes = lax.broadcasted_iota(jnp.int32, (MODES, 128), 0)
    count_ref[...] = jnp.zeros((8, 128), jnp.int32)
    count_ref[0:1, 0:CLASSES] = count_in[...]
    counts = jnp.where(modes == lane, jnp.broadcast_to(count_ref[0:1, :], (8, 128)), 0)
    counts = jnp.sum(counts, axis=1, keepdims=True)
    energies = []
    for kind in range(CLASSES):
        part = modal[MODES * kind : MODES * (kind + 1), :]
        part = jnp.where(modes < counts[kind : kind + 1, :], part * part, 0.0)
        energies.append(jnp.sum(part, axis=0, keepdims=True))
    demand_out[...] = 0.5 * jnp.log1p(jnp.concatenate(energies, axis=0))


def table_kernel(demand_ref, cells_ref, table_out):
    demand = demand_ref[...]
    for owner in range(table_out.shape[0]):
        cells = jnp.broadcast_to(cells_ref[owner : owner + 1, :], (CLASSES, 128))
        chosen = jnp.take_along_axis(demand, cells, axis=1)
        for level in range(table_out.shape[1]):
            table_out[owner, level] = chosen


def fragility_kernel(
    table_ref, slot_ref, kind_ref, city_ref, amplify_ref, median_ref, spread_ref, out_ref, gain_ref, tables_ref
):
    sources = table_ref.shape[0]
    slot, kind, city = slot_ref[...], kind_ref[...], city_ref[...]
    column = slot % 128
    key = (slot // 128) * CLASSES + kind
    demand = jnp.zeros((8, 128), F32)
    for source in range(sources):
        for each in range(CLASSES):
            row = jnp.broadcast_to(table_ref[source, 0, each : each + 1, :], (8, 128))
            found = jnp.take_along_axis(row, column, axis=1)
            demand = jnp.where(key == source * CLASSES + each, found, demand)
    gain_ref[...] = jnp.ones((8, 128), F32)
    gain_ref[0:1, 0:CITIES] = amplify_ref[...]
    gain = jnp.log(jnp.broadcast_to(gain_ref[0:1, :], (8, 128)))
    demand = demand + jnp.take_along_axis(gain, city, axis=1)
    tables_ref[...] = jnp.ones((128, 128), F32)
    batches = median_ref.shape[1]
    tables_ref[0:CLASSES, 0:batches] = median_ref[...]
    medians = tables_ref[...].T
    tables_ref[0:CLASSES, 0:batches] = spread_ref[...]
    spreads = tables_ref[...].T
    for group in range(8):
        level = jnp.broadcast_to(demand[group : group + 1, :], (8, 128))
        index = jnp.broadcast_to(kind[group : group + 1, :], (8, 128))
        for half in range(0, batches, 8):
            middle = jnp.take_along_axis(medians[half : half + 8, :], index, axis=1)
            width = jnp.take_along_axis(spreads[half : half + 8, :], index, axis=1)
            out_ref[half : half + 8, 128 * group : 128 * group + 128] = jax.nn.sigmoid((level - middle) / width)


VM = pl.BlockSpec(memory_space=pltpu.VMEM)


WEIGHTS = {"start": 1.4, "steps_first": 6.7, "steps_second": 6.5, "surface": 4.0, "fragility": 1.0}
UNIT_FLOPS = 1.15e10


def call(kernel, name, shapes, args, specs=None, scratch=(), limit=VMEM_LIMIT):
    out = [s if isinstance(s, jax.ShapeDtypeStruct) else jax.ShapeDtypeStruct(s, F32) for s in shapes]
    return pl.pallas_call(
        kernel,
        out_shape=out,
        in_specs=specs or [VM] * len(args),
        out_specs=[VM] * len(out),
        scratch_shapes=list(scratch),
        compiler_params=pltpu.CompilerParams(vmem_limit_bytes=limit),
        cost_estimate=pl.CostEstimate(flops=int(WEIGHTS.get(name, 0.3) * UNIT_FLOPS), bytes_accessed=0, transcendentals=0),
        name=name,
    )(*args)


def both_ways(to_up, to_down, axis):
    count = lax.axis_size(axis)
    forward = [(i, i + 1) for i in range(count - 1)]
    backward = [(i + 1, i) for i in range(count - 1)]
    return lax.ppermute(to_up, axis, forward), lax.ppermute(to_down, axis, backward)


def swaps(first, second, axis):
    count = lax.axis_size(axis)
    pairs = [[(i, i + 1) for i in range(begin, count - 1, 2)] for begin in (0, 1)]
    pairs = [ways + [(b, a) for a, b in ways] for ways in pairs]
    return lax.ppermute(first, axis, pairs[0]), lax.ppermute(second, axis, pairs[1])


def is_odd(axis):
    return lax.rem(lax.axis_index(axis), 2) == 1


def exchange_x(u, p, faces, coefficients):
    extra = list(coefficients)
    z_first, z_second = swaps(faces, faces, "gz")
    planes = 3 * XU + (3 + len(extra)) * XP + XH + 1
    message = jax.ShapeDtypeStruct((planes, 16, 128), jnp.int16)
    halo, up, down, powers = call(
        functools.partial(x_message_kernel, bool(extra)),
        "x_message",
        [(8, 16, 128), message, message, (16, 128)],
        [z_second, z_first, u, p] + extra,
    )
    return halo, powers, *both_ways(up, down, "gx")


def y_messages(u, p, coefficients, halo, powers, x_low, x_high):
    extra = list(coefficients)
    planes = (3 * YU + (3 + len(extra)) * YP + YH) // 2 + 1
    message = jax.ShapeDtypeStruct((planes, 16, 128), jnp.int16)
    messages = call(
        functools.partial(y_message_kernel, bool(extra)),
        "y_message",
        [message, message],
        [u, p] + extra + [halo, powers, x_low, x_high],
    )
    return messages if extra else messages[::-1]


def body(
    displacement,
    previous,
    courant,
    damping,
    send_cells,
    building_slot,
    building_class,
    city,
    mode_count,
    modal_filter,
    amplify,
    median,
    spread,
):
    own = (3, 8, 16, 128)
    plane = (8, 16, 128)
    wide = pltpu.VMEM((2, 4, 24, 48, 128), F32)
    rates = pltpu.VMEM((4, 24, 32, 128), F32)
    samples = pltpu.VMEM((HALF, 24, 16, 128), F32)

    u, p = displacement, previous
    a, e, faces = call(
        start_kernel,
        "start",
        [plane, plane, plane],
        [u, p, courant, damping],
        specs=[pl.BlockSpec(memory_space=pltpu.HBM)] * 4,
        scratch=[pltpu.VMEM(own, F32)] * 2 + [pltpu.VMEM(plane, F32)] * 2 + [pltpu.SemaphoreType.DMA((8,))],
        limit=START_LIMIT,
    )
    halo, powers, x_low, x_high = exchange_x(u, p, faces, (a, e))
    messages = y_messages(u, p, (a, e), halo, powers, x_low, x_high)
    received = (halo, x_low, x_high, *swaps(*messages, "gy"))
    weights = jnp.asarray(depth_weights(), jnp.bfloat16)
    u, p, faces, slab, seen, codes = call(
        functools.partial(steps_kernel, True),
        "steps_first",
        [own, own, plane, plane, plane, jax.ShapeDtypeStruct((3, 20, 32, 128), jnp.int16)],
        [u, p, a, e, *received, weights],
        scratch=[wide, rates, samples],
    )

    near_low, near_high = both_ways(slab, slab, "gx")
    halo, powers, x_low, x_high = exchange_x(u, p, faces, ())
    slab_messages = call(slab_message_kernel, "slab_message", [(24, 8, 128)] * 2, [slab, near_low, near_high, powers])
    side_first, side_second = swaps(*slab_messages, "gy")
    messages = y_messages(u, p, (), halo, powers, x_low, x_high)
    received = (halo, x_low, x_high, *swaps(*messages, "gy"))
    (demand,) = call(
        surface_kernel,
        "surface",
        [(CLASSES, 128)],
        [slab, near_low, near_high, side_first, side_second, jnp.asarray(slab_weights(), jnp.bfloat16), codes, seen]
        + [modal_filter.T, mode_count.reshape(1, CLASSES), messages[0]],
        specs=[VM] * 10 + [pl.BlockSpec(memory_space=pl.ANY)],
        scratch=[
            pltpu.VMEM((2, 24, 48, 128), F32),
            pltpu.VMEM((2, 24, 32, 128), F32),
            samples,
            pltpu.VMEM(plane, F32),
            pltpu.VMEM((3 * STEPS, CLASSES * MODES), F32),
            pltpu.VMEM((8, 128), jnp.int32),
        ],
    )
    owners, levels = lax.axis_size("gx"), lax.axis_size("gz")
    (table,) = call(
        table_kernel,
        "table",
        [(owners, levels, CLASSES, 128)],
        [demand, send_cells.reshape(owners, 128)],
    )
    table = table.reshape(owners * levels, CLASSES, 128)
    table = lax.all_to_all(table, ("gx", "gz"), split_axis=0, concat_axis=0, tiled=True)
    (field,) = call(
        functools.partial(steps_kernel, False), "steps_second", [own], [u, p, *received, weights, codes], scratch=[wide, rates]
    )
    (probability,) = call(
        fragility_kernel,
        "fragility",
        [(16, 1024)],
        [
            table.reshape(owners, levels, CLASSES, 128),
            building_slot.reshape(8, 128),
            building_class.reshape(8, 128),
            city.reshape(8, 128),
            amplify.reshape(1, CITIES),
            median.T,
            spread.T,
        ],
        scratch=[pltpu.VMEM((8, 128), F32), pltpu.VMEM((128, 128), F32)],
    )
    return (field, probability)


def solution(mesh):
    placed = (
        P(None, "gx", "gy", "gz"),
        P(None, "gx", "gy", "gz"),
        P("gx", "gy", "gz"),
        P("gx", "gy", "gz"),
        P("gx", "gy", None),
        P(("gx", "gy", "gz")),
        P(("gx", "gy", "gz")),
        P(("gx", "gy", "gz")),
        P(),
        P(),
        P(),
        P(),
        P(),
    )
    return jax.shard_map(
        body,
        mesh=mesh,
        in_specs=placed,
        out_specs=(P(None, "gx", "gy", "gz"), P(None, ("gx", "gy", "gz"))),
        check_vma=False,
    )
```

```python
import functools

import jax
import jax.numpy as jnp
import numpy as np
from jax import lax
from jax.experimental import pallas as pl
from jax.experimental.pallas import tpu as pltpu
from jax.sharding import PartitionSpec as P

STEPS = 8
HALF = 4
DEEP = 2 * HALF
CLASSES = 8
MODES = 8
CITIES = 16
F32 = jnp.float32
VMEM_LIMIT = 24 * 1024 * 1024
START_LIMIT = int(53.8 * 1024 * 1024)

XU, XP, XH = 8, 6, 7
YU, YP, YH = 24, 20, 20

FULL = 32000.0
BIAS = 200
UNIT_A = 2.0 / FULL
UNIT_E = 0.2 / 12.0 / FULL


PLANES = 4


def depth_weights():
    lanes = np.arange(256)
    result = np.zeros((3, 256, 256), np.float32)
    for k in range(3):
        at = lanes - 128 - 16 * k
        depth = np.where(lanes < 128, lanes, np.where(at < 8, at - 8, at + 120))
        used = (lanes < 128) | ((at >= 0) & (at < 16))
        apart = np.abs(depth[:, None] - depth[None, :])
        band = np.where(apart == 0, -90.0, np.where(apart == 1, 16.0, np.where(apart == 2, -1.0, 0.0)))
        result[k] = np.where(used[:, None] & used[None, :], band, 0.0)
        result[k, 0, 128 + 64 + 16 * k + 8] = 1.0
    return result


def slab_weights():
    lanes = np.arange(128)
    apart = np.abs(lanes[:, None] - lanes[None, :])
    band = np.where(apart == 0, -90.0, np.where(apart == 1, 16.0, np.where(apart == 2, -1.0, 0.0)))
    same = (lanes[:, None] // 16 == lanes[None, :] // 16) & (lanes[:, None] < 48)
    band = np.where(same, band, 0.0)
    return np.concatenate([band, band], axis=0)


def split(v):
    high = v.astype(jnp.bfloat16)
    return high, (v - high.astype(F32)).astype(jnp.bfloat16)


def lane_of():
    return lax.broadcasted_iota(jnp.int32, (8, 128), 1)


def pack_faces(values, lane):
    packed = pltpu.roll(values[0], 8, 1)
    for at in range(1, len(values)):
        packed = jnp.where(lane // 16 == at, pltpu.roll(values[at], (16 * at + 8) % 128, 1), packed)
    return packed


def start_kernel(u_in, p_in, c_in, d_in, a_ref, e_ref, face_ref, u_ref, p_ref, c_ref, d_ref, sems):
    copies = [pltpu.make_async_copy(c_in, c_ref, sems.at[0]), pltpu.make_async_copy(d_in, d_ref, sems.at[1])]
    for k in range(3):
        copies.append(pltpu.make_async_copy(u_in.at[k], u_ref.at[k], sems.at[2 + k]))
        copies.append(pltpu.make_async_copy(p_in.at[k], p_ref.at[k], sems.at[5 + k]))
    for copy in copies:
        copy.start()
    for copy in copies:
        copy.wait()
    lane = lane_of()

    def plane(x, carry):
        for row in (0, 8):
            rows = pl.ds(row, 8)
            share = 1.0 / (1.0 + d_ref[x, rows, :])
            values = [u_ref[k, x, rows, :] for k in range(3)] + [p_ref[k, x, rows, :] for k in range(3)]
            values += [2.0 * share, c_ref[x, rows, :] * share * (1.0 / 12.0)]
            a_ref[x, rows, :] = values[6]
            e_ref[x, rows, :] = values[7]
            face_ref[x, rows, :] = pack_faces(values, lane)
        return carry

    lax.fori_loop(0, 8, plane, 0)


def exponent_of(peak):
    peak = jnp.maximum(jnp.max(peak, axis=0, keepdims=True), 1e-30)
    return jnp.broadcast_to(jnp.ceil(jnp.log2(peak)), (8, 128))


def coded(values):
    return jnp.round(values).astype(jnp.int32).astype(jnp.int16)


def decoded(values):
    return values.astype(jnp.int32).astype(F32)


def twice(rows):
    return jnp.concatenate([rows, rows], axis=0)


def sent_exponents(message):
    both = decoded(message[message.shape[0] - 1]) - BIAS
    return both[0:8], both[8:16]


def x_message_kernel(coefficients, *refs):
    if coefficients:
        z_second_ref, z_first_ref, u_ref, p_ref, a_ref, e_ref, halo_ref, up_ref, down_ref, power_ref = refs
    else:
        z_second_ref, z_first_ref, u_ref, p_ref, halo_ref, up_ref, down_ref, power_ref = refs
    inner = lax.broadcasted_iota(jnp.int32, (16, 128), 1) % 16
    from_first = (inner < 8) == is_odd("gz")

    def largest(x, carry):
        field, face = carry
        for k in range(3):
            both = jnp.maximum(jnp.abs(u_ref[k, x]), jnp.abs(p_ref[k, x]))
            field = jnp.maximum(field, jnp.maximum(both[0:8], both[8:16]))
        halo = jnp.where(from_first, z_first_ref[x], z_second_ref[x])
        halo_ref[x] = halo
        halo = jnp.abs(halo)
        return field, jnp.maximum(face, jnp.maximum(halo[0:8], halo[8:16]))

    zero = jnp.zeros((8, 128), F32)
    field, face = lax.fori_loop(0, 8, largest, (zero, zero))
    powers = jnp.concatenate([exponent_of(field), exponent_of(face)], axis=0)
    power_ref[...] = powers
    up_ref[up_ref.shape[0] - 1] = coded(powers + BIAS)
    down_ref[down_ref.shape[0] - 1] = coded(powers + BIAS)
    scale = FULL * jnp.exp2(-powers)
    field, face = twice(scale[0:8]), twice(scale[8:16])

    def whole(x, carry):
        for k in range(3):
            code = coded(u_ref[k, x] * field)
            up_ref[XU * k + x] = code
            down_ref[XU * k + x] = code
        return carry

    def part(i, carry):
        parts = [(p_ref.at[k], field) for k in range(3)]
        if coefficients:
            parts += [(a_ref, 1.0 / UNIT_A), (e_ref, 1.0 / UNIT_E)]
        for at, (source, unit) in enumerate(parts):
            up_ref[3 * XU + XP * at + i] = coded(source[8 - XP + i] * unit)
            down_ref[3 * XU + XP * at + i] = coded(source[i] * unit)
        return carry

    at = 3 * XU + (5 if coefficients else 3) * XP

    def side(i, carry):
        up_ref[at + i] = coded(halo_ref[8 - XH + i] * face)
        down_ref[at + i] = coded(halo_ref[i] * face)
        return carry

    lax.fori_loop(0, 8, whole, 0)
    lax.fori_loop(0, XP, part, 0)
    lax.fori_loop(0, XH, side, 0)


def y_message_kernel(coefficients, *refs):
    if coefficients:
        u_ref, p_ref, a_ref, e_ref, halo_ref, power_ref, low_ref, high_ref, first_ref, second_ref = refs
    else:
        u_ref, p_ref, halo_ref, power_ref, low_ref, high_ref, second_ref, first_ref = refs
    odd = is_odd("gy")
    powers = power_ref[...]
    low_powers = jnp.concatenate(sent_exponents(low_ref), axis=0)
    high_powers = jnp.concatenate(sent_exponents(high_ref), axis=0)
    most = jnp.maximum(powers, jnp.maximum(low_powers, high_powers))
    for out_ref in (first_ref, second_ref):
        out_ref[out_ref.shape[0] - 1] = coded(most + BIAS)
    own_scale = FULL * jnp.exp2(-most)
    low_scale = jnp.exp2(low_powers - most)
    high_scale = jnp.exp2(high_powers - most)
    field = [twice(scale[0:8]) for scale in (own_scale, low_scale, high_scale)]
    face = [twice(scale[8:16]) for scale in (own_scale, low_scale, high_scale)]

    def put(at, pair):
        up = jnp.concatenate([pair[0][8:16], pair[1][8:16]], axis=0)
        down = jnp.concatenate([pair[0][0:8], pair[1][0:8]], axis=0)
        first_ref[at] = coded(jnp.where(odd, down, up))
        second_ref[at] = coded(jnp.where(odd, up, down))

    def group(parts, x_planes, y_planes, x_at, y_at):
        side = (y_planes - 8) // 4

        def own(i, carry):
            for at, (source, units) in enumerate(parts):
                put(y_at + at * y_planes // 2 + side + i, [source[2 * i + j] * units[0] for j in (0, 1)])
            return carry

        def sides(i, carry):
            for at, (_, units) in enumerate(parts):
                start = x_at + at * x_planes
                first = start + x_planes - 2 * side + 2 * i
                put(y_at + at * y_planes // 2 + i, [decoded(low_ref[first + j]) * units[1] for j in (0, 1)])
                first = start + 2 * i
                pair = [decoded(high_ref[first + j]) * units[2] for j in (0, 1)]
                put(y_at + at * y_planes // 2 + side + 4 + i, pair)
            return carry

        lax.fori_loop(0, 4, own, 0)
        lax.fori_loop(0, side, sides, 0)
        return x_at + len(parts) * x_planes, y_at + len(parts) * y_planes // 2

    x_at, y_at = group([(u_ref.at[k], field) for k in range(3)], XU, YU, 0, 0)
    parts = [(p_ref.at[k], field) for k in range(3)]
    if coefficients:
        parts += [(a_ref, (1.0 / UNIT_A, 1.0, 1.0)), (e_ref, (1.0 / UNIT_E, 1.0, 1.0))]
    x_at, y_at = group(parts, XP, YP, x_at, y_at)
    group([(halo_ref, face)], XH, YH, x_at, y_at)


def fill(parts, x_low, x_high, y_first, y_second, x_at, x_planes, y_at, y_planes):
    count = len(parts)
    side = (y_planes - 8) // 2
    odd = is_odd("gy")

    def own(i, carry):
        for target, row, block, _ in parts:
            target[8 + i, row + 8 : row + 24, :] = block[i]
        return carry

    def x_side(i, carry):
        for at, (target, row, _, units) in enumerate(parts):
            here = x_at + at * x_planes + i
            target[8 - x_planes + i, row + 8 : row + 24, :] = decoded(x_low[here]) * units[0]
            target[16 + i, row + 8 : row + 24, :] = decoded(x_high[here]) * units[1]
        return carry

    def y_side(i, carry):
        for at, (target, row, _, units) in enumerate(parts):
            here = y_at + at * y_planes // 2 + i
            first, second = decoded(y_first[here]), decoded(y_second[here])
            low = jnp.where(odd, first, second) * units[2]
            high = jnp.where(odd, second, first) * units[3]
            for j in (0, 1):
                target[8 - side + 2 * i + j, row : row + 8, :] = low[8 * j : 8 * j + 8]
                target[8 - side + 2 * i + j, row + 24 : row + 32, :] = high[8 * j : 8 * j + 8]
        return carry

    lax.fori_loop(0, 8, own, 0, unroll=2)
    lax.fori_loop(0, x_planes, x_side, 0)
    lax.fori_loop(0, y_planes // 2, y_side, 0, unroll=2)
    return x_at + count * x_planes, y_at + count * y_planes // 2


def steps_kernel(first, *refs):
    if first:
        (u_in, p_in, a_in, e_in, halo_in, x_low, x_high, y_first, y_second, weight_in) = refs[:10]
        (u_out, p_out, face_out, slab_out, seen_out, code_ref) = refs[10:16]
        state_ref, rate_ref, edge_ref = refs[16:]
    else:
        (u_in, p_in, halo_in, x_low, x_high, y_first, y_second, weight_in, code_ref) = refs[:9]
        u_out, state_ref, rate_ref = refs[9:]
    a_ref, e_ref, ha_ref, he_ref = (rate_ref.at[at] for at in range(4))
    lane = lane_of()
    inner = lane % 16

    sides = (x_low, x_high, y_first, y_second)
    powers = [sent_exponents(message) for message in sides]
    odd = is_odd("gy")
    swapped = list(zip(powers[2], powers[3]))
    powers[2] = [jnp.where(odd, one, other) for one, other in swapped]
    powers[3] = [jnp.where(odd, other, one) for one, other in swapped]
    field = [twice(jnp.exp2(power[0]) * (1.0 / FULL)) for power in powers]
    face = [twice(jnp.exp2(power[1]) * (1.0 / FULL)) for power in powers]
    x_at, y_at = fill([(state_ref.at[0, k], 8, u_in.at[k], field) for k in range(3)], *sides, 0, XU, 0, YU)
    parts = [(state_ref.at[1, k], 8, p_in.at[k], field) for k in range(3)]
    if first:
        parts += [(a_ref, 0, a_in, (UNIT_A,) * 4), (e_ref, 0, e_in, (UNIT_E,) * 4)]
    x_at, y_at = fill(parts, *sides, x_at, XP, y_at, YP)
    fill([(state_ref.at[0, 3], 8, halo_in, face)], *sides, x_at, XH, y_at, YH)

    unit = jnp.where(lane < 112, UNIT_A, UNIT_E)

    def prepare(x, carry):
        for half in (0, 16):
            held = pl.ds(half, 16)
            if first:
                code_ref[0, x - 2, held, :] = coded(a_ref[x, held, :] * (1.0 / UNIT_A))
                code_ref[1, x - 2, held, :] = coded(e_ref[x, held, :] * (1.0 / UNIT_E))
                sides = state_ref[0, 3, x, pl.ds(8 + half, 16), :]
                scale = twice(jnp.where(lane < 96, 0.0, 1.0 / unit))
                code_ref[2, x - 2, held, :] = coded(jnp.where(scale > 0.0, sides * scale, 0.0))
            else:
                a_ref[x, held, :] = decoded(code_ref[0, x - 2, held, :]) * UNIT_A
                e_ref[x, held, :] = decoded(code_ref[1, x - 2, held, :]) * UNIT_E
                sides = decoded(code_ref[2, x - 2, held, :]) * twice(unit)
            for tile in (0, 8):
                rows = pl.ds(8 + half + tile, 8)
                halo = state_ref[0, 3, x, rows, :]
                state_ref[0, 3, x, rows, :] = jnp.where(lane < 48, halo, 0.0)
                state_ref[1, 3, x, rows, :] = jnp.where(lane < 48, pltpu.roll(halo, 128 - 48, 1), 0.0)
                side = sides[tile : tile + 8]
                for target, at in ((ha_ref, 96), (he_ref, 112)):
                    spread = jnp.where(lane < 16, pltpu.roll(side, 128 - at, 1), pltpu.roll(side, 144 - at, 1))
                    spread = jnp.where(lane < 32, spread, pltpu.roll(side, 160 - at, 1))
                    target[x, pl.ds(half + tile, 8), :] = jnp.where(lane < 48, spread, 0.0)
        return carry

    lax.fori_loop(2, 22, prepare, 0, unroll=4)

    def advance(src, dst, x):
        rows = pl.ds(8, 32)
        fields = [[src[k, 2 + j, rows, :] for j in range(PLANES)] for k in range(4)]
        parts = [[split(v) for v in field] for field in fields]
        depth = []
        for k in range(3):
            pieces = [jnp.concatenate([parts[k][j][part], parts[3][j][part]], axis=1) for part in (0, 1) for j in range(PLANES)]
            both = jnp.dot(jnp.concatenate(pieces, axis=0), weight_in[k], preferred_element_type=F32)
            depth.append(both[0 : 32 * PLANES] + both[32 * PLANES :])
        side = depth[0][:, 128:] + depth[1][:, 128:] + depth[2][:, 128:]
        fresh = []
        for j in range(PLANES):
            for k in range(4):
                v = fields[k][j]
                near = (src[k, 1 + j, rows, :] + src[k, 3 + j, rows, :]) + (
                    src[k, 2 + j, pl.ds(7, 32), :] + src[k, 2 + j, pl.ds(9, 32), :]
                )
                far = (src[k, j, rows, :] + src[k, 4 + j, rows, :]) + (
                    src[k, 2 + j, pl.ds(6, 32), :] + src[k, 2 + j, pl.ds(10, 32), :]
                )
                along = side if k == 3 else depth[k][:, :128]
                laplace = along[32 * j : 32 * j + 32] + (16.0 * near - far)
                old = dst[k, x + j, rows, :]
                a_each, e_each = (ha_ref, he_ref) if k == 3 else (a_ref, e_ref)
                fresh.append((k, j, old + a_each[x + j] * (v - old) + e_each[x + j] * laplace))
        return fresh, side

    def one_step(step, carry):
        dst = state_ref.at[(step + 1) % 2]

        def planes(at, inside):
            x = 2 * step + 2 + PLANES * at
            fresh, side = advance(state_ref.at[step % 2, :, pl.ds(x - 2, 4 + PLANES)], dst, x)
            for k, j, value in fresh:
                dst[k, x + j, 8:40, :] = value
            if first:
                for j in range(PLANES):
                    edge_ref[step, x + j, :, :] = side[32 * j + 8 : 32 * j + 24]
            return inside

        lax.fori_loop(0, (20 - 4 * step) // PLANES, planes, 0)
        return carry

    lax.fori_loop(0, HALF, one_step, 0)

    block = pl.ds(16, 16)

    def finish(x, carry):
        for k in range(3):
            u_out[k, x, :, :] = state_ref[0, k, 8 + x, block, :]
            if first:
                p_out[k, x, :, :] = state_ref[1, k, 8 + x, block, :]
        if first:
            for row in (0, 8):
                rows = pl.ds(row, 8)
                values = [state_ref[slot, k, 8 + x, pl.ds(16 + row, 8), :] for slot in (0, 1) for k in range(3)]
                last = pack_faces(values, lane)
                face_out[x, rows, :] = last
                slab = values[0]
                for at in range(1, 6):
                    slab = jnp.where(lane // 16 == at, pltpu.roll(values[at], 16 * at, 1), slab)
                slab_out[x, rows, :] = slab
                seen = jnp.zeros((8, 128), F32)
                for step in range(HALF):
                    if step < HALF - 1:
                        sample = pltpu.roll(edge_ref[step + 1, 8 + x, rows, :], 56 + step, 1)
                    else:
                        sample = pltpu.roll(last, 120 + step, 1)
                    seen = jnp.where((inner == step) & (lane < 48), sample, seen)
                seen_out[x, rows, :] = seen
        return carry

    lax.fori_loop(0, 8, finish, 0, unroll=4)


def slab_message_kernel(own_ref, low_ref, high_ref, after_ref, first_ref, second_ref):
    odd = is_odd("gy")

    def plane(i, carry):
        for at, source in ((0, low_ref), (8, own_ref), (16, high_ref)):
            up, down = source[i, 8:16, :], source[i, 0:8, :]
            first_ref[at + i] = jnp.where(odd, down, up)
            second_ref[at + i] = jnp.where(odd, up, down)
        return carry

    lax.fori_loop(0, 8, plane, 0, unroll=2)


def surface_kernel(
    own_in, x_low, x_high, y_first, y_second, weight_in, code_in, seen_in, filter_in, count_in,
    demand_out, state_ref, rate_ref, sample_ref, seen_ref, filter_ref, count_ref,
):
    lane = lane_of()
    inner = lane % 16

    odd = is_odd("gy")

    def near_side(i, carry):
        state_ref[0, i, 16:32, :] = x_low[i]
        state_ref[0, 8 + i, 16:32, :] = own_in[i]
        state_ref[0, 16 + i, 16:32, :] = x_high[i]
        for part in range(3):
            one, other = y_first[8 * part + i], y_second[8 * part + i]
            state_ref[0, 8 * part + i, 8:16, :] = jnp.where(odd, one, other)
            state_ref[0, 8 * part + i, 32:40, :] = jnp.where(odd, other, one)
        return carry

    lax.fori_loop(0, 8, near_side, 0, unroll=2)

    def prepare(x, carry):
        for tile in range(4):
            rows = pl.ds(8 + 8 * tile, 8)
            value = state_ref[0, x, rows, :]
            state_ref[0, x, rows, :] = jnp.where(lane < 48, value, 0.0)
            state_ref[1, x, rows, :] = jnp.where(lane < 48, pltpu.roll(value, 128 - 48, 1), 0.0)
        return carry

    def rates(x, carry):
        for at, unit in ((0, UNIT_A), (1, UNIT_E)):
            for half in (0, 16):
                both = decoded(code_in[at, x - 2, half : half + 16, :]) * unit
                for tile in (0, 8):
                    rate = both[tile : tile + 8]
                    spread = jnp.where(lane < 32, pltpu.roll(rate, 16, 1), pltpu.roll(rate, 32, 1))
                    spread = jnp.where(lane < 16, rate, spread)
                    rate_ref[at, x, pl.ds(half + tile, 8), :] = jnp.where(lane < 48, spread, 0.0)
        return carry

    lax.fori_loop(0, 24, prepare, 0, unroll=4)
    lax.fori_loop(2, 22, rates, 0, unroll=4)

    def one_step(step, carry):
        dst = state_ref.at[(step + 1) % 2]

        def planes(at, inside):
            x = 2 * step + 2 + PLANES * at
            src = state_ref.at[step % 2, pl.ds(x - 2, 4 + PLANES)]
            rows = pl.ds(8, 32)
            fields = [src[2 + j, rows, :] for j in range(PLANES)]
            halves = jnp.concatenate([jnp.concatenate(split(v), axis=1) for v in fields], axis=0)
            depth = jnp.dot(halves, weight_in[...], preferred_element_type=F32)
            fresh = []
            for j, v in enumerate(fields):
                near = (src[1 + j, rows, :] + src[3 + j, rows, :]) + (src[2 + j, pl.ds(7, 32), :] + src[2 + j, pl.ds(9, 32), :])
                far = (src[j, rows, :] + src[4 + j, rows, :]) + (src[2 + j, pl.ds(6, 32), :] + src[2 + j, pl.ds(10, 32), :])
                laplace = depth[32 * j : 32 * j + 32] + (16.0 * near - far)
                old = dst[x + j, rows, :]
                fresh.append(old + rate_ref[0, x + j] * (v - old) + rate_ref[1, x + j] * laplace)
            for j, value in enumerate(fresh):
                dst[x + j, 8:40, :] = value
                sample_ref[step, x + j, :, :] = value[8:24]
            return inside

        lax.fori_loop(0, (20 - 4 * step) // PLANES, planes, 0)
        return carry

    lax.fori_loop(0, HALF, one_step, 0)

    def finish(x, carry):
        for row in (0, 8):
            rows = pl.ds(row, 8)
            seen = seen_in[x, rows, :]
            for step in range(HALF):
                at = HALF + step
                sample = pltpu.roll(sample_ref[step, 8 + x, rows, :], at, 1)
                seen = jnp.where((inner == at) & (lane < 48), sample, seen)
            seen_ref[x, rows, :] = seen
        return carry

    lax.fori_loop(0, 8, finish, 0, unroll=4)

    filter_ref[...] = filter_in[...].astype(F32)
    blocks = [jnp.zeros((8, CLASSES * MODES), F32)] * 16
    for k in range(3):
        blocks[2 * k] = filter_ref[pl.ds(k, STEPS, stride=3), :]
    filters = jnp.concatenate(blocks, axis=0).astype(jnp.bfloat16)
    motion = seen_ref[...].reshape(128, 128).astype(jnp.bfloat16)
    modal = lax.dot_general(filters, motion, (((0,), (1,)), ((), ())), preferred_element_type=F32)
    modes = lax.broadcasted_iota(jnp.int32, (MODES, 128), 0)
    count_ref[...] = jnp.zeros((8, 128), jnp.int32)
    count_ref[0:1, 0:CLASSES] = count_in[...]
    counts = jnp.where(modes == lane, jnp.broadcast_to(count_ref[0:1, :], (8, 128)), 0)
    counts = jnp.sum(counts, axis=1, keepdims=True)
    energies = []
    for kind in range(CLASSES):
        part = modal[MODES * kind : MODES * (kind + 1), :]
        part = jnp.where(modes < counts[kind : kind + 1, :], part * part, 0.0)
        energies.append(jnp.sum(part, axis=0, keepdims=True))
    demand_out[...] = 0.5 * jnp.log1p(jnp.concatenate(energies, axis=0))


def table_kernel(demand_ref, cells_ref, after_ref, table_out):
    demand = demand_ref[...]
    for owner in range(table_out.shape[0]):
        cells = jnp.broadcast_to(cells_ref[owner : owner + 1, :], (CLASSES, 128))
        chosen = jnp.take_along_axis(demand, cells, axis=1)
        for level in range(table_out.shape[1]):
            table_out[owner, level] = chosen


def fragility_kernel(
    table_ref, slot_ref, kind_ref, city_ref, amplify_ref, median_ref, spread_ref, out_ref, gain_ref, tables_ref
):
    sources = table_ref.shape[0]
    slot, kind, city = slot_ref[...], kind_ref[...], city_ref[...]
    column = slot % 128
    key = (slot // 128) * CLASSES + kind
    demand = jnp.zeros((8, 128), F32)
    for source in range(sources):
        for each in range(CLASSES):
            row = jnp.broadcast_to(table_ref[source, 0, each : each + 1, :], (8, 128))
            found = jnp.take_along_axis(row, column, axis=1)
            demand = jnp.where(key == source * CLASSES + each, found, demand)
    gain_ref[...] = jnp.ones((8, 128), F32)
    gain_ref[0:1, 0:CITIES] = amplify_ref[...]
    gain = jnp.log(jnp.broadcast_to(gain_ref[0:1, :], (8, 128)))
    demand = demand + jnp.take_along_axis(gain, city, axis=1)
    tables_ref[...] = jnp.ones((128, 128), F32)
    batches = median_ref.shape[1]
    tables_ref[0:CLASSES, 0:batches] = median_ref[...]
    medians = tables_ref[...].T
    tables_ref[0:CLASSES, 0:batches] = spread_ref[...]
    spreads = tables_ref[...].T
    for group in range(8):
        level = jnp.broadcast_to(demand[group : group + 1, :], (8, 128))
        index = jnp.broadcast_to(kind[group : group + 1, :], (8, 128))
        for half in range(0, batches, 8):
            middle = jnp.take_along_axis(medians[half : half + 8, :], index, axis=1)
            width = jnp.take_along_axis(spreads[half : half + 8, :], index, axis=1)
            out_ref[half : half + 8, 128 * group : 128 * group + 128] = jax.nn.sigmoid((level - middle) / width)


VM = pl.BlockSpec(memory_space=pltpu.VMEM)


WEIGHTS = {"start": 1.4, "steps_first": 6.7, "steps_second": 6.5, "slab_message": 4.0, "surface": 0.02, "table": 4.0, "fragility": 1.0}
UNIT_FLOPS = 1.15e10


def call(kernel, name, shapes, args, specs=None, scratch=(), limit=VMEM_LIMIT):
    out = [s if isinstance(s, jax.ShapeDtypeStruct) else jax.ShapeDtypeStruct(s, F32) for s in shapes]
    return pl.pallas_call(
        kernel,
        out_shape=out,
        in_specs=specs or [VM] * len(args),
        out_specs=[VM] * len(out),
        scratch_shapes=list(scratch),
        compiler_params=pltpu.CompilerParams(vmem_limit_bytes=limit),
        cost_estimate=pl.CostEstimate(flops=int(WEIGHTS.get(name, 0.3) * UNIT_FLOPS), bytes_accessed=0, transcendentals=0),
        name=name,
    )(*args)


def both_ways(to_up, to_down, axis):
    count = lax.axis_size(axis)
    forward = [(i, i + 1) for i in range(count - 1)]
    backward = [(i + 1, i) for i in range(count - 1)]
    return lax.ppermute(to_up, axis, forward), lax.ppermute(to_down, axis, backward)


def swaps(first, second, axis):
    count = lax.axis_size(axis)
    pairs = [[(i, i + 1) for i in range(begin, count - 1, 2)] for begin in (0, 1)]
    pairs = [ways + [(b, a) for a, b in ways] for ways in pairs]
    return lax.ppermute(first, axis, pairs[0]), lax.ppermute(second, axis, pairs[1])


def is_odd(axis):
    return lax.rem(lax.axis_index(axis), 2) == 1


def exchange_x(u, p, faces, coefficients):
    extra = list(coefficients)
    z_first, z_second = swaps(faces, faces, "gz")
    planes = 3 * XU + (3 + len(extra)) * XP + XH + 1
    message = jax.ShapeDtypeStruct((planes, 16, 128), jnp.int16)
    halo, up, down, powers = call(
        functools.partial(x_message_kernel, bool(extra)),
        "x_message",
        [(8, 16, 128), message, message, (16, 128)],
        [z_second, z_first, u, p] + extra,
    )
    return halo, powers, *both_ways(up, down, "gx")


def y_messages(u, p, coefficients, halo, powers, x_low, x_high):
    extra = list(coefficients)
    planes = (3 * YU + (3 + len(extra)) * YP + YH) // 2 + 1
    message = jax.ShapeDtypeStruct((planes, 16, 128), jnp.int16)
    messages = call(
        functools.partial(y_message_kernel, bool(extra)),
        "y_message",
        [message, message],
        [u, p] + extra + [halo, powers, x_low, x_high],
    )
    return messages if extra else messages[::-1]


def body(
    displacement,
    previous,
    courant,
    damping,
    send_cells,
    building_slot,
    building_class,
    city,
    mode_count,
    modal_filter,
    amplify,
    median,
    spread,
):
    own = (3, 8, 16, 128)
    plane = (8, 16, 128)
    wide = pltpu.VMEM((2, 4, 24, 48, 128), F32)
    rates = pltpu.VMEM((4, 24, 32, 128), F32)
    samples = pltpu.VMEM((HALF, 24, 16, 128), F32)

    u, p = displacement, previous
    a, e, faces = call(
        start_kernel,
        "start",
        [plane, plane, plane],
        [u, p, courant, damping],
        specs=[pl.BlockSpec(memory_space=pltpu.HBM)] * 4,
        scratch=[pltpu.VMEM(own, F32)] * 2 + [pltpu.VMEM(plane, F32)] * 2 + [pltpu.SemaphoreType.DMA((8,))],
        limit=START_LIMIT,
    )
    halo, powers, x_low, x_high = exchange_x(u, p, faces, (a, e))
    messages = y_messages(u, p, (a, e), halo, powers, x_low, x_high)
    received = (halo, x_low, x_high, *swaps(*messages, "gy"))
    weights = jnp.asarray(depth_weights(), jnp.bfloat16)
    u, p, faces, slab, seen, codes = call(
        functools.partial(steps_kernel, True),
        "steps_first",
        [own, own, plane, plane, plane, jax.ShapeDtypeStruct((3, 20, 32, 128), jnp.int16)],
        [u, p, a, e, *received, weights],
        scratch=[wide, rates, samples],
    )

    near_low, near_high = both_ways(slab, slab, "gx")
    halo, powers, x_low, x_high = exchange_x(u, p, faces, ())
    slab_messages = call(slab_message_kernel, "slab_message", [(24, 8, 128)] * 2, [slab, near_low, near_high, powers])
    side_first, side_second = swaps(*slab_messages, "gy")
    (demand,) = call(
        surface_kernel,
        "surface",
        [(CLASSES, 128)],
        [slab, near_low, near_high, side_first, side_second, jnp.asarray(slab_weights(), jnp.bfloat16), codes, seen]
        + [modal_filter.T, mode_count.reshape(1, CLASSES)],
        scratch=[
            pltpu.VMEM((2, 24, 48, 128), F32),
            pltpu.VMEM((2, 24, 32, 128), F32),
            samples,
            pltpu.VMEM(plane, F32),
            pltpu.VMEM((3 * STEPS, CLASSES * MODES), F32),
            pltpu.VMEM((8, 128), jnp.int32),
        ],
    )
    messages = y_messages(u, p, (), halo, powers, x_low, x_high)
    received = (halo, x_low, x_high, *swaps(*messages, "gy"))
    owners, levels = lax.axis_size("gx"), lax.axis_size("gz")
    (table,) = call(
        table_kernel,
        "table",
        [(owners, levels, CLASSES, 128)],
        [demand, send_cells.reshape(owners, 128), messages[0]],
        specs=[VM, VM, pl.BlockSpec(memory_space=pl.ANY)],
    )
    table = table.reshape(owners * levels, CLASSES, 128)
    table = lax.all_to_all(table, ("gx", "gz"), split_axis=0, concat_axis=0, tiled=True)
    (field,) = call(
        functools.partial(steps_kernel, False), "steps_second", [own], [u, p, *received, weights, codes], scratch=[wide, rates]
    )
    (probability,) = call(
        fragility_kernel,
        "fragility",
        [(16, 1024)],
        [
            table.reshape(owners, levels, CLASSES, 128),
            building_slot.reshape(8, 128),
            building_class.reshape(8, 128),
            city.reshape(8, 128),
            amplify.reshape(1, CITIES),
            median.T,
            spread.T,
        ],
        scratch=[pltpu.VMEM((8, 128), F32), pltpu.VMEM((128, 128), F32)],
    )
    return (field, probability)


def solution(mesh):
    placed = (
        P(None, "gx", "gy", "gz"),
        P(None, "gx", "gy", "gz"),
        P("gx", "gy", "gz"),
        P("gx", "gy", "gz"),
        P("gx", "gy", None),
        P(("gx", "gy", "gz")),
        P(("gx", "gy", "gz")),
        P(("gx", "gy", "gz")),
        P(),
        P(),
        P(),
        P(),
        P(),
    )
    return jax.shard_map(
        body,
        mesh=mesh,
        in_specs=placed,
        out_specs=(P(None, "gx", "gy", "gz"), P(None, ("gx", "gy", "gz"))),
        check_vma=False,
    )
```

```python
import functools

import jax
import jax.numpy as jnp
import numpy as np
from jax import lax
from jax.experimental import pallas as pl
from jax.experimental.pallas import tpu as pltpu
from jax.sharding import PartitionSpec as P

STEPS = 8
HALF = 4
DEEP = 2 * HALF
CLASSES = 8
MODES = 8
CITIES = 16
F32 = jnp.float32
VMEM_LIMIT = 24 * 1024 * 1024
START_LIMIT = int(53.8 * 1024 * 1024)

XU, XP, XH = 8, 6, 7
YU, YP, YH = 24, 20, 20

FULL = 32000.0
BIAS = 200
UNIT_A = 2.0 / FULL
UNIT_E = 0.2 / 12.0 / FULL


def depth_weights():
    lanes = np.arange(256)
    result = np.zeros((3, 256, 256), np.float32)
    for k in range(3):
        at = lanes - 128 - 16 * k
        depth = np.where(lanes < 128, lanes, np.where(at < 8, at - 8, at + 120))
        used = (lanes < 128) | ((at >= 0) & (at < 16))
        apart = np.abs(depth[:, None] - depth[None, :])
        band = np.where(apart == 0, -90.0, np.where(apart == 1, 16.0, np.where(apart == 2, -1.0, 0.0)))
        result[k] = np.where(used[:, None] & used[None, :], band, 0.0)
        result[k, 0, 128 + 64 + 16 * k + 8] = 1.0
    return result


def slab_weights():
    lanes = np.arange(128)
    apart = np.abs(lanes[:, None] - lanes[None, :])
    band = np.where(apart == 0, -90.0, np.where(apart == 1, 16.0, np.where(apart == 2, -1.0, 0.0)))
    same = (lanes[:, None] // 16 == lanes[None, :] // 16) & (lanes[:, None] < 48)
    band = np.where(same, band, 0.0)
    return np.concatenate([band, band], axis=0)


def split(v):
    high = v.astype(jnp.bfloat16)
    return high, (v - high.astype(F32)).astype(jnp.bfloat16)


def lane_of():
    return lax.broadcasted_iota(jnp.int32, (8, 128), 1)


def pack_faces(values, lane):
    packed = pltpu.roll(values[0], 8, 1)
    for at in range(1, len(values)):
        packed = jnp.where(lane // 16 == at, pltpu.roll(values[at], (16 * at + 8) % 128, 1), packed)
    return packed


def start_kernel(u_in, p_in, c_in, d_in, a_ref, e_ref, face_ref, u_ref, p_ref, c_ref, d_ref, sems):
    copies = [pltpu.make_async_copy(c_in, c_ref, sems.at[0]), pltpu.make_async_copy(d_in, d_ref, sems.at[1])]
    for k in range(3):
        copies.append(pltpu.make_async_copy(u_in.at[k], u_ref.at[k], sems.at[2 + k]))
        copies.append(pltpu.make_async_copy(p_in.at[k], p_ref.at[k], sems.at[5 + k]))
    for copy in copies:
        copy.start()
    for copy in copies:
        copy.wait()
    lane = lane_of()

    def plane(x, carry):
        for row in (0, 8):
            rows = pl.ds(row, 8)
            share = 1.0 / (1.0 + d_ref[x, rows, :])
            values = [u_ref[k, x, rows, :] for k in range(3)] + [p_ref[k, x, rows, :] for k in range(3)]
            values += [2.0 * share, c_ref[x, rows, :] * share * (1.0 / 12.0)]
            a_ref[x, rows, :] = values[6]
            e_ref[x, rows, :] = values[7]
            face_ref[x, rows, :] = pack_faces(values, lane)
        return carry

    lax.fori_loop(0, 8, plane, 0)


def exponent_of(peak):
    peak = jnp.maximum(jnp.max(peak, axis=0, keepdims=True), 1e-30)
    return jnp.broadcast_to(jnp.ceil(jnp.log2(peak)), (8, 128))


def coded(values):
    return jnp.round(values).astype(jnp.int32).astype(jnp.int16)


def decoded(values):
    return values.astype(jnp.int32).astype(F32)


def twice(rows):
    return jnp.concatenate([rows, rows], axis=0)


def sent_exponents(message):
    both = decoded(message[message.shape[0] - 1]) - BIAS
    return both[0:8], both[8:16]


def x_message_kernel(coefficients, *refs):
    if coefficients:
        z_second_ref, z_first_ref, u_ref, p_ref, a_ref, e_ref, halo_ref, up_ref, down_ref, power_ref = refs
    else:
        z_second_ref, z_first_ref, u_ref, p_ref, halo_ref, up_ref, down_ref, power_ref = refs
    inner = lax.broadcasted_iota(jnp.int32, (16, 128), 1) % 16
    from_first = (inner < 8) == is_odd("gz")

    def largest(x, carry):
        field, face = carry
        for k in range(3):
            both = jnp.maximum(jnp.abs(u_ref[k, x]), jnp.abs(p_ref[k, x]))
            field = jnp.maximum(field, jnp.maximum(both[0:8], both[8:16]))
        halo = jnp.where(from_first, z_first_ref[x], z_second_ref[x])
        halo_ref[x] = halo
        halo = jnp.abs(halo)
        return field, jnp.maximum(face, jnp.maximum(halo[0:8], halo[8:16]))

    zero = jnp.zeros((8, 128), F32)
    field, face = lax.fori_loop(0, 8, largest, (zero, zero))
    powers = jnp.concatenate([exponent_of(field), exponent_of(face)], axis=0)
    power_ref[...] = powers
    up_ref[up_ref.shape[0] - 1] = coded(powers + BIAS)
    down_ref[down_ref.shape[0] - 1] = coded(powers + BIAS)
    scale = FULL * jnp.exp2(-powers)
    field, face = twice(scale[0:8]), twice(scale[8:16])

    def whole(x, carry):
        for k in range(3):
            code = coded(u_ref[k, x] * field)
            up_ref[XU * k + x] = code
            down_ref[XU * k + x] = code
        return carry

    def part(i, carry):
        parts = [(p_ref.at[k], field) for k in range(3)]
        if coefficients:
            parts += [(a_ref, 1.0 / UNIT_A), (e_ref, 1.0 / UNIT_E)]
        for at, (source, unit) in enumerate(parts):
            up_ref[3 * XU + XP * at + i] = coded(source[8 - XP + i] * unit)
            down_ref[3 * XU + XP * at + i] = coded(source[i] * unit)
        return carry

    at = 3 * XU + (5 if coefficients else 3) * XP

    def side(i, carry):
        up_ref[at + i] = coded(halo_ref[8 - XH + i] * face)
        down_ref[at + i] = coded(halo_ref[i] * face)
        return carry

    lax.fori_loop(0, 8, whole, 0)
    lax.fori_loop(0, XP, part, 0)
    lax.fori_loop(0, XH, side, 0)


def y_message_kernel(coefficients, *refs):
    if coefficients:
        u_ref, p_ref, a_ref, e_ref, halo_ref, power_ref, low_ref, high_ref, first_ref, second_ref = refs
    else:
        u_ref, p_ref, halo_ref, power_ref, low_ref, high_ref, second_ref, first_ref = refs
    odd = is_odd("gy")
    powers = power_ref[...]
    low_powers = jnp.concatenate(sent_exponents(low_ref), axis=0)
    high_powers = jnp.concatenate(sent_exponents(high_ref), axis=0)
    most = jnp.maximum(powers, jnp.maximum(low_powers, high_powers))
    for out_ref in (first_ref, second_ref):
        out_ref[out_ref.shape[0] - 1] = coded(most + BIAS)
    own_scale = FULL * jnp.exp2(-most)
    low_scale = jnp.exp2(low_powers - most)
    high_scale = jnp.exp2(high_powers - most)
    field = [twice(scale[0:8]) for scale in (own_scale, low_scale, high_scale)]
    face = [twice(scale[8:16]) for scale in (own_scale, low_scale, high_scale)]

    def put(at, pair):
        up = jnp.concatenate([pair[0][8:16], pair[1][8:16]], axis=0)
        down = jnp.concatenate([pair[0][0:8], pair[1][0:8]], axis=0)
        first_ref[at] = coded(jnp.where(odd, down, up))
        second_ref[at] = coded(jnp.where(odd, up, down))

    def group(parts, x_planes, y_planes, x_at, y_at):
        side = (y_planes - 8) // 4

        def own(i, carry):
            for at, (source, units) in enumerate(parts):
                put(y_at + at * y_planes // 2 + side + i, [source[2 * i + j] * units[0] for j in (0, 1)])
            return carry

        def sides(i, carry):
            for at, (_, units) in enumerate(parts):
                start = x_at + at * x_planes
                first = start + x_planes - 2 * side + 2 * i
                put(y_at + at * y_planes // 2 + i, [decoded(low_ref[first + j]) * units[1] for j in (0, 1)])
                first = start + 2 * i
                pair = [decoded(high_ref[first + j]) * units[2] for j in (0, 1)]
                put(y_at + at * y_planes // 2 + side + 4 + i, pair)
            return carry

        lax.fori_loop(0, 4, own, 0)
        lax.fori_loop(0, side, sides, 0)
        return x_at + len(parts) * x_planes, y_at + len(parts) * y_planes // 2

    x_at, y_at = group([(u_ref.at[k], field) for k in range(3)], XU, YU, 0, 0)
    parts = [(p_ref.at[k], field) for k in range(3)]
    if coefficients:
        parts += [(a_ref, (1.0 / UNIT_A, 1.0, 1.0)), (e_ref, (1.0 / UNIT_E, 1.0, 1.0))]
    x_at, y_at = group(parts, XP, YP, x_at, y_at)
    group([(halo_ref, face)], XH, YH, x_at, y_at)


def fill(parts, x_low, x_high, y_first, y_second, x_at, x_planes, y_at, y_planes):
    count = len(parts)
    side = (y_planes - 8) // 2
    odd = is_odd("gy")

    def own(i, carry):
        for target, row, block, _ in parts:
            target[8 + i, row + 8 : row + 24, :] = block[i]
        return carry

    def x_side(i, carry):
        for at, (target, row, _, units) in enumerate(parts):
            here = x_at + at * x_planes + i
            target[8 - x_planes + i, row + 8 : row + 24, :] = decoded(x_low[here]) * units[0]
            target[16 + i, row + 8 : row + 24, :] = decoded(x_high[here]) * units[1]
        return carry

    def y_side(i, carry):
        for at, (target, row, _, units) in enumerate(parts):
            here = y_at + at * y_planes // 2 + i
            first, second = decoded(y_first[here]), decoded(y_second[here])
            low = jnp.where(odd, first, second) * units[2]
            high = jnp.where(odd, second, first) * units[3]
            for j in (0, 1):
                target[8 - side + 2 * i + j, row : row + 8, :] = low[8 * j : 8 * j + 8]
                target[8 - side + 2 * i + j, row + 24 : row + 32, :] = high[8 * j : 8 * j + 8]
        return carry

    lax.fori_loop(0, 8, own, 0, unroll=2)
    lax.fori_loop(0, x_planes, x_side, 0)
    lax.fori_loop(0, y_planes // 2, y_side, 0, unroll=2)
    return x_at + count * x_planes, y_at + count * y_planes // 2


def steps_kernel(first, *refs):
    if first:
        (u_in, p_in, a_in, e_in, halo_in, x_low, x_high, y_first, y_second, weight_in) = refs[:10]
        (u_out, p_out, face_out, slab_out, seen_out, code_ref) = refs[10:16]
        state_ref, rate_ref, edge_ref = refs[16:]
    else:
        (u_in, p_in, halo_in, x_low, x_high, y_first, y_second, weight_in, code_ref) = refs[:9]
        u_out, state_ref, rate_ref = refs[9:]
    a_ref, e_ref, ha_ref, he_ref = (rate_ref.at[at] for at in range(4))
    lane = lane_of()
    inner = lane % 16

    sides = (x_low, x_high, y_first, y_second)
    powers = [sent_exponents(message) for message in sides]
    odd = is_odd("gy")
    swapped = list(zip(powers[2], powers[3]))
    powers[2] = [jnp.where(odd, one, other) for one, other in swapped]
    powers[3] = [jnp.where(odd, other, one) for one, other in swapped]
    field = [twice(jnp.exp2(power[0]) * (1.0 / FULL)) for power in powers]
    face = [twice(jnp.exp2(power[1]) * (1.0 / FULL)) for power in powers]
    x_at, y_at = fill([(state_ref.at[0, k], 8, u_in.at[k], field) for k in range(3)], *sides, 0, XU, 0, YU)
    parts = [(state_ref.at[1, k], 8, p_in.at[k], field) for k in range(3)]
    if first:
        parts += [(a_ref, 0, a_in, (UNIT_A,) * 4), (e_ref, 0, e_in, (UNIT_E,) * 4)]
    x_at, y_at = fill(parts, *sides, x_at, XP, y_at, YP)
    fill([(state_ref.at[0, 3], 8, halo_in, face)], *sides, x_at, XH, y_at, YH)

    unit = jnp.where(lane < 112, UNIT_A, UNIT_E)

    def prepare(x, carry):
        for half in (0, 16):
            held = pl.ds(half, 16)
            if first:
                code_ref[0, x - 2, held, :] = coded(a_ref[x, held, :] * (1.0 / UNIT_A))
                code_ref[1, x - 2, held, :] = coded(e_ref[x, held, :] * (1.0 / UNIT_E))
                sides = state_ref[0, 3, x, pl.ds(8 + half, 16), :]
                scale = twice(jnp.where(lane < 96, 0.0, 1.0 / unit))
                code_ref[2, x - 2, held, :] = coded(jnp.where(scale > 0.0, sides * scale, 0.0))
            else:
                a_ref[x, held, :] = decoded(code_ref[0, x - 2, held, :]) * UNIT_A
                e_ref[x, held, :] = decoded(code_ref[1, x - 2, held, :]) * UNIT_E
                sides = decoded(code_ref[2, x - 2, held, :]) * twice(unit)
            for tile in (0, 8):
                rows = pl.ds(8 + half + tile, 8)
                halo = state_ref[0, 3, x, rows, :]
                state_ref[0, 3, x, rows, :] = jnp.where(lane < 48, halo, 0.0)
                state_ref[1, 3, x, rows, :] = jnp.where(lane < 48, pltpu.roll(halo, 128 - 48, 1), 0.0)
                side = sides[tile : tile + 8]
                for target, at in ((ha_ref, 96), (he_ref, 112)):
                    spread = jnp.where(lane < 16, pltpu.roll(side, 128 - at, 1), pltpu.roll(side, 144 - at, 1))
                    spread = jnp.where(lane < 32, spread, pltpu.roll(side, 160 - at, 1))
                    target[x, pl.ds(half + tile, 8), :] = jnp.where(lane < 48, spread, 0.0)
        return carry

    lax.fori_loop(2, 22, prepare, 0, unroll=4)

    def advance(src, dst, x, count):
        rows = pl.ds(8, 32)
        fields = [[src[k, 2 + j, rows, :] for j in range(count)] for k in range(4)]
        parts = [[split(v) for v in field] for field in fields]
        depth = []
        for k in range(3):
            pieces = [jnp.concatenate([parts[k][j][part], parts[3][j][part]], axis=1) for part in (0, 1) for j in range(count)]
            both = jnp.dot(jnp.concatenate(pieces, axis=0), weight_in[k], preferred_element_type=F32)
            depth.append(both[0 : 32 * count] + both[32 * count :])
        side = depth[0][:, 128:] + depth[1][:, 128:] + depth[2][:, 128:]
        fresh = []
        for j in range(count):
            for k in range(4):
                v = fields[k][j]
                near = (src[k, 1 + j, rows, :] + src[k, 3 + j, rows, :]) + (
                    src[k, 2 + j, pl.ds(7, 32), :] + src[k, 2 + j, pl.ds(9, 32), :]
                )
                far = (src[k, j, rows, :] + src[k, 4 + j, rows, :]) + (
                    src[k, 2 + j, pl.ds(6, 32), :] + src[k, 2 + j, pl.ds(10, 32), :]
                )
                along = side if k == 3 else depth[k][:, :128]
                laplace = along[32 * j : 32 * j + 32] + (16.0 * near - far)
                old = dst[k, x + j, rows, :]
                a_each, e_each = (ha_ref, he_ref) if k == 3 else (a_ref, e_ref)
                fresh.append((k, j, old + a_each[x + j] * (v - old) + e_each[x + j] * laplace))
        return fresh, side

    def block_of(step, x, count):
        dst = state_ref.at[(step + 1) % 2]
        fresh, side = advance(state_ref.at[step % 2, :, pl.ds(x - 2, 4 + count)], dst, x, count)
        for k, j, value in fresh:
            dst[k, x + j, 8:40, :] = value
        if first:
            for j in range(count):
                edge_ref[step, x + j, :, :] = side[32 * j + 8 : 32 * j + 24]

    for step in range(HALF):
        count = (20 - 4 * step) // 2
        block_of(step, 2 * step + 2, count)
        block_of(step, 2 * step + 2 + count, count)

    block = pl.ds(16, 16)

    def finish(x, carry):
        for k in range(3):
            u_out[k, x, :, :] = state_ref[0, k, 8 + x, block, :]
            if first:
                p_out[k, x, :, :] = state_ref[1, k, 8 + x, block, :]
        if first:
            for row in (0, 8):
                rows = pl.ds(row, 8)
                values = [state_ref[slot, k, 8 + x, pl.ds(16 + row, 8), :] for slot in (0, 1) for k in range(3)]
                last = pack_faces(values, lane)
                face_out[x, rows, :] = last
                slab = values[0]
                for at in range(1, 6):
                    slab = jnp.where(lane // 16 == at, pltpu.roll(values[at], 16 * at, 1), slab)
                slab_out[x, rows, :] = slab
                seen = jnp.zeros((8, 128), F32)
                for step in range(HALF):
                    if step < HALF - 1:
                        sample = pltpu.roll(edge_ref[step + 1, 8 + x, rows, :], 56 + step, 1)
                    else:
                        sample = pltpu.roll(last, 120 + step, 1)
                    seen = jnp.where((inner == step) & (lane < 48), sample, seen)
                seen_out[x, rows, :] = seen
        return carry

    lax.fori_loop(0, 8, finish, 0, unroll=4)


def slab_message_kernel(own_ref, low_ref, high_ref, after_ref, first_ref, second_ref):
    odd = is_odd("gy")

    def plane(i, carry):
        for at, source in ((0, low_ref), (8, own_ref), (16, high_ref)):
            up, down = source[i, 8:16, :], source[i, 0:8, :]
            first_ref[at + i] = jnp.where(odd, down, up)
            second_ref[at + i] = jnp.where(odd, up, down)
        return carry

    lax.fori_loop(0, 8, plane, 0, unroll=2)


def surface_kernel(
    own_in, x_low, x_high, y_first, y_second, weight_in, code_in, seen_in, filter_in, count_in, after_in,
    demand_out, state_ref, rate_ref, sample_ref, seen_ref, filter_ref, count_ref,
):
    lane = lane_of()
    inner = lane % 16

    odd = is_odd("gy")

    def near_side(i, carry):
        state_ref[0, i, 16:32, :] = x_low[i]
        state_ref[0, 8 + i, 16:32, :] = own_in[i]
        state_ref[0, 16 + i, 16:32, :] = x_high[i]
        for part in range(3):
            one, other = y_first[8 * part + i], y_second[8 * part + i]
            state_ref[0, 8 * part + i, 8:16, :] = jnp.where(odd, one, other)
            state_ref[0, 8 * part + i, 32:40, :] = jnp.where(odd, other, one)
        return carry

    lax.fori_loop(0, 8, near_side, 0, unroll=2)

    def prepare(x, carry):
        for tile in range(4):
            rows = pl.ds(8 + 8 * tile, 8)
            value = state_ref[0, x, rows, :]
            state_ref[0, x, rows, :] = jnp.where(lane < 48, value, 0.0)
            state_ref[1, x, rows, :] = jnp.where(lane < 48, pltpu.roll(value, 128 - 48, 1), 0.0)
        return carry

    def rates(x, carry):
        for at, unit in ((0, UNIT_A), (1, UNIT_E)):
            for half in (0, 16):
                both = decoded(code_in[at, x - 2, half : half + 16, :]) * unit
                for tile in (0, 8):
                    rate = both[tile : tile + 8]
                    spread = jnp.where(lane < 32, pltpu.roll(rate, 16, 1), pltpu.roll(rate, 32, 1))
                    spread = jnp.where(lane < 16, rate, spread)
                    rate_ref[at, x, pl.ds(half + tile, 8), :] = jnp.where(lane < 48, spread, 0.0)
        return carry

    lax.fori_loop(0, 24, prepare, 0, unroll=4)
    lax.fori_loop(2, 22, rates, 0, unroll=4)

    def advance(step, x, count):
        src, dst = state_ref.at[step % 2, pl.ds(x - 2, 4 + count)], state_ref.at[(step + 1) % 2]
        rows = pl.ds(8, 32)
        fields = [src[2 + j, rows, :] for j in range(count)]
        halves = jnp.concatenate([jnp.concatenate(split(v), axis=1) for v in fields], axis=0)
        depth = jnp.dot(halves, weight_in[...], preferred_element_type=F32)
        fresh = []
        for j, v in enumerate(fields):
            near = (src[1 + j, rows, :] + src[3 + j, rows, :]) + (src[2 + j, pl.ds(7, 32), :] + src[2 + j, pl.ds(9, 32), :])
            far = (src[j, rows, :] + src[4 + j, rows, :]) + (src[2 + j, pl.ds(6, 32), :] + src[2 + j, pl.ds(10, 32), :])
            laplace = depth[32 * j : 32 * j + 32] + (16.0 * near - far)
            old = dst[x + j, rows, :]
            fresh.append(old + rate_ref[0, x + j] * (v - old) + rate_ref[1, x + j] * laplace)
        for j, value in enumerate(fresh):
            dst[x + j, 8:40, :] = value
            sample_ref[step, x + j, :, :] = value[8:24]

    for step in range(HALF):
        count = (20 - 4 * step) // 2
        advance(step, 2 * step + 2, count)
        advance(step, 2 * step + 2 + count, count)

    def finish(x, carry):
        for row in (0, 8):
            rows = pl.ds(row, 8)
            seen = seen_in[x, rows, :]
            for step in range(HALF):
                at = HALF + step
                sample = pltpu.roll(sample_ref[step, 8 + x, rows, :], at, 1)
                seen = jnp.where((inner == at) & (lane < 48), sample, seen)
            seen_ref[x, rows, :] = seen
        return carry

    lax.fori_loop(0, 8, finish, 0, unroll=4)

    filter_ref[...] = filter_in[...].astype(F32)
    blocks = [jnp.zeros((8, CLASSES * MODES), F32)] * 16
    for k in range(3):
        blocks[2 * k] = filter_ref[pl.ds(k, STEPS, stride=3), :]
    filters = jnp.concatenate(blocks, axis=0).astype(jnp.bfloat16)
    motion = seen_ref[...].reshape(128, 128).astype(jnp.bfloat16)
    modal = lax.dot_general(filters, motion, (((0,), (1,)), ((), ())), preferred_element_type=F32)
    modes = lax.broadcasted_iota(jnp.int32, (MODES, 128), 0)
    count_ref[...] = jnp.zeros((8, 128), jnp.int32)
    count_ref[0:1, 0:CLASSES] = count_in[...]
    counts = jnp.where(modes == lane, jnp.broadcast_to(count_ref[0:1, :], (8, 128)), 0)
    counts = jnp.sum(counts, axis=1, keepdims=True)
    energies = []
    for kind in range(CLASSES):
        part = modal[MODES * kind : MODES * (kind + 1), :]
        part = jnp.where(modes < counts[kind : kind + 1, :], part * part, 0.0)
        energies.append(jnp.sum(part, axis=0, keepdims=True))
    demand_out[...] = 0.5 * jnp.log1p(jnp.concatenate(energies, axis=0))


def table_kernel(demand_ref, cells_ref, table_out):
    demand = demand_ref[...]
    for owner in range(table_out.shape[0]):
        cells = jnp.broadcast_to(cells_ref[owner : owner + 1, :], (CLASSES, 128))
        chosen = jnp.take_along_axis(demand, cells, axis=1)
        for level in range(table_out.shape[1]):
            table_out[owner, level] = chosen


def fragility_kernel(
    table_ref, slot_ref, kind_ref, city_ref, amplify_ref, median_ref, spread_ref, out_ref, gain_ref, tables_ref
):
    sources = table_ref.shape[0]
    slot, kind, city = slot_ref[...], kind_ref[...], city_ref[...]
    column = slot % 128
    key = (slot // 128) * CLASSES + kind
    demand = jnp.zeros((8, 128), F32)
    for source in range(sources):
        for each in range(CLASSES):
            row = jnp.broadcast_to(table_ref[source, 0, each : each + 1, :], (8, 128))
            found = jnp.take_along_axis(row, column, axis=1)
            demand = jnp.where(key == source * CLASSES + each, found, demand)
    gain_ref[...] = jnp.ones((8, 128), F32)
    gain_ref[0:1, 0:CITIES] = amplify_ref[...]
    gain = jnp.log(jnp.broadcast_to(gain_ref[0:1, :], (8, 128)))
    demand = demand + jnp.take_along_axis(gain, city, axis=1)
    tables_ref[...] = jnp.ones((128, 128), F32)
    batches = median_ref.shape[1]
    tables_ref[0:CLASSES, 0:batches] = median_ref[...]
    medians = tables_ref[...].T
    tables_ref[0:CLASSES, 0:batches] = spread_ref[...]
    spreads = tables_ref[...].T
    for group in range(8):
        level = jnp.broadcast_to(demand[group : group + 1, :], (8, 128))
        index = jnp.broadcast_to(kind[group : group + 1, :], (8, 128))
        for half in range(0, batches, 8):
            middle = jnp.take_along_axis(medians[half : half + 8, :], index, axis=1)
            width = jnp.take_along_axis(spreads[half : half + 8, :], index, axis=1)
            out_ref[half : half + 8, 128 * group : 128 * group + 128] = jax.nn.sigmoid((level - middle) / width)


VM = pl.BlockSpec(memory_space=pltpu.VMEM)


WEIGHTS = {"start": 1.4, "steps_first": 6.7, "steps_second": 6.5, "surface": 4.0, "fragility": 1.0}
UNIT_FLOPS = 1.15e10


def call(kernel, name, shapes, args, specs=None, scratch=(), limit=VMEM_LIMIT):
    out = [s if isinstance(s, jax.ShapeDtypeStruct) else jax.ShapeDtypeStruct(s, F32) for s in shapes]
    return pl.pallas_call(
        kernel,
        out_shape=out,
        in_specs=specs or [VM] * len(args),
        out_specs=[VM] * len(out),
        scratch_shapes=list(scratch),
        compiler_params=pltpu.CompilerParams(vmem_limit_bytes=limit),
        cost_estimate=pl.CostEstimate(flops=int(WEIGHTS.get(name, 0.3) * UNIT_FLOPS), bytes_accessed=0, transcendentals=0),
        name=name,
    )(*args)


def both_ways(to_up, to_down, axis):
    count = lax.axis_size(axis)
    forward = [(i, i + 1) for i in range(count - 1)]
    backward = [(i + 1, i) for i in range(count - 1)]
    return lax.ppermute(to_up, axis, forward), lax.ppermute(to_down, axis, backward)


def swaps(first, second, axis):
    count = lax.axis_size(axis)
    pairs = [[(i, i + 1) for i in range(begin, count - 1, 2)] for begin in (0, 1)]
    pairs = [ways + [(b, a) for a, b in ways] for ways in pairs]
    return lax.ppermute(first, axis, pairs[0]), lax.ppermute(second, axis, pairs[1])


def is_odd(axis):
    return lax.rem(lax.axis_index(axis), 2) == 1


def exchange_x(u, p, faces, coefficients):
    extra = list(coefficients)
    z_first, z_second = swaps(faces, faces, "gz")
    planes = 3 * XU + (3 + len(extra)) * XP + XH + 1
    message = jax.ShapeDtypeStruct((planes, 16, 128), jnp.int16)
    halo, up, down, powers = call(
        functools.partial(x_message_kernel, bool(extra)),
        "x_message",
        [(8, 16, 128), message, message, (16, 128)],
        [z_second, z_first, u, p] + extra,
    )
    return halo, powers, *both_ways(up, down, "gx")


def y_messages(u, p, coefficients, halo, powers, x_low, x_high):
    extra = list(coefficients)
    planes = (3 * YU + (3 + len(extra)) * YP + YH) // 2 + 1
    message = jax.ShapeDtypeStruct((planes, 16, 128), jnp.int16)
    messages = call(
        functools.partial(y_message_kernel, bool(extra)),
        "y_message",
        [message, message],
        [u, p] + extra + [halo, powers, x_low, x_high],
    )
    return messages if extra else messages[::-1]


def body(
    displacement,
    previous,
    courant,
    damping,
    send_cells,
    building_slot,
    building_class,
    city,
    mode_count,
    modal_filter,
    amplify,
    median,
    spread,
):
    own = (3, 8, 16, 128)
    plane = (8, 16, 128)
    wide = pltpu.VMEM((2, 4, 24, 48, 128), F32)
    rates = pltpu.VMEM((4, 24, 32, 128), F32)
    samples = pltpu.VMEM((HALF, 24, 16, 128), F32)

    u, p = displacement, previous
    a, e, faces = call(
        start_kernel,
        "start",
        [plane, plane, plane],
        [u, p, courant, damping],
        specs=[pl.BlockSpec(memory_space=pltpu.HBM)] * 4,
        scratch=[pltpu.VMEM(own, F32)] * 2 + [pltpu.VMEM(plane, F32)] * 2 + [pltpu.SemaphoreType.DMA((8,))],
        limit=START_LIMIT,
    )
    halo, powers, x_low, x_high = exchange_x(u, p, faces, (a, e))
    messages = y_messages(u, p, (a, e), halo, powers, x_low, x_high)
    received = (halo, x_low, x_high, *swaps(*messages, "gy"))
    weights = jnp.asarray(depth_weights(), jnp.bfloat16)
    u, p, faces, slab, seen, codes = call(
        functools.partial(steps_kernel, True),
        "steps_first",
        [own, own, plane, plane, plane, jax.ShapeDtypeStruct((3, 20, 32, 128), jnp.int16)],
        [u, p, a, e, *received, weights],
        scratch=[wide, rates, samples],
    )

    near_low, near_high = both_ways(slab, slab, "gx")
    halo, powers, x_low, x_high = exchange_x(u, p, faces, ())
    slab_messages = call(slab_message_kernel, "slab_message", [(24, 8, 128)] * 2, [slab, near_low, near_high, powers])
    side_first, side_second = swaps(*slab_messages, "gy")
    messages = y_messages(u, p, (), halo, powers, x_low, x_high)
    received = (halo, x_low, x_high, *swaps(*messages, "gy"))
    (demand,) = call(
        surface_kernel,
        "surface",
        [(CLASSES, 128)],
        [slab, near_low, near_high, side_first, side_second, jnp.asarray(slab_weights(), jnp.bfloat16), codes, seen]
        + [modal_filter.T, mode_count.reshape(1, CLASSES), messages[0]],
        specs=[VM] * 10 + [pl.BlockSpec(memory_space=pl.ANY)],
        scratch=[
            pltpu.VMEM((2, 24, 48, 128), F32),
            pltpu.VMEM((2, 24, 32, 128), F32),
            samples,
            pltpu.VMEM(plane, F32),
            pltpu.VMEM((3 * STEPS, CLASSES * MODES), F32),
            pltpu.VMEM((8, 128), jnp.int32),
        ],
    )
    owners, levels = lax.axis_size("gx"), lax.axis_size("gz")
    (table,) = call(
        table_kernel,
        "table",
        [(owners, levels, CLASSES, 128)],
        [demand, send_cells.reshape(owners, 128)],
    )
    table = table.reshape(owners * levels, CLASSES, 128)
    table = lax.all_to_all(table, ("gx", "gz"), split_axis=0, concat_axis=0, tiled=True)
    (field,) = call(
        functools.partial(steps_kernel, False), "steps_second", [own], [u, p, *received, weights, codes], scratch=[wide, rates]
    )
    (probability,) = call(
        fragility_kernel,
        "fragility",
        [(16, 1024)],
        [
            table.reshape(owners, levels, CLASSES, 128),
            building_slot.reshape(8, 128),
            building_class.reshape(8, 128),
            city.reshape(8, 128),
            amplify.reshape(1, CITIES),
            median.T,
            spread.T,
        ],
        scratch=[pltpu.VMEM((8, 128), F32), pltpu.VMEM((128, 128), F32)],
    )
    return (field, probability)


def solution(mesh):
    placed = (
        P(None, "gx", "gy", "gz"),
        P(None, "gx", "gy", "gz"),
        P("gx", "gy", "gz"),
        P("gx", "gy", "gz"),
        P("gx", "gy", None),
        P(("gx", "gy", "gz")),
        P(("gx", "gy", "gz")),
        P(("gx", "gy", "gz")),
        P(),
        P(),
        P(),
        P(),
        P(),
    )
    return jax.shard_map(
        body,
        mesh=mesh,
        in_specs=placed,
        out_specs=(P(None, "gx", "gy", "gz"), P(None, ("gx", "gy", "gz"))),
        check_vma=False,
    )
```

```python
import functools

import jax
import jax.numpy as jnp
import numpy as np
from jax import lax
from jax.experimental import pallas as pl
from jax.experimental.pallas import tpu as pltpu
from jax.sharding import PartitionSpec as P

STEPS = 8
HALF = 4
DEEP = 2 * HALF
CLASSES = 8
MODES = 8
CITIES = 16
F32 = jnp.float32
VMEM_LIMIT = 24 * 1024 * 1024
START_LIMIT = int(53.8 * 1024 * 1024)

XU, XP, XH = 8, 6, 7
YU, YP, YH = 24, 20, 20

FULL = 32000.0
BIAS = 200
UNIT_A = 2.0 / FULL
UNIT_E = 0.2 / 12.0 / FULL


def depth_weights():
    lanes = np.arange(256)
    result = np.zeros((3, 256, 256), np.float32)
    for k in range(3):
        at = lanes - 128 - 16 * k
        depth = np.where(lanes < 128, lanes, np.where(at < 8, at - 8, at + 120))
        used = (lanes < 128) | ((at >= 0) & (at < 16))
        apart = np.abs(depth[:, None] - depth[None, :])
        band = np.where(apart == 0, -90.0, np.where(apart == 1, 16.0, np.where(apart == 2, -1.0, 0.0)))
        result[k] = np.where(used[:, None] & used[None, :], band, 0.0)
        result[k, 0, 128 + 64 + 16 * k + 8] = 1.0
    return result


def slab_weights():
    lanes = np.arange(128)
    apart = np.abs(lanes[:, None] - lanes[None, :])
    band = np.where(apart == 0, -90.0, np.where(apart == 1, 16.0, np.where(apart == 2, -1.0, 0.0)))
    same = (lanes[:, None] // 16 == lanes[None, :] // 16) & (lanes[:, None] < 48)
    band = np.where(same, band, 0.0)
    return np.concatenate([band, band], axis=0)


def split(v):
    high = v.astype(jnp.bfloat16)
    return high, (v - high.astype(F32)).astype(jnp.bfloat16)


def lane_of():
    return lax.broadcasted_iota(jnp.int32, (8, 128), 1)


def pack_faces(values, lane):
    packed = pltpu.roll(values[0], 8, 1)
    for at in range(1, len(values)):
        packed = jnp.where(lane // 16 == at, pltpu.roll(values[at], (16 * at + 8) % 128, 1), packed)
    return packed


def start_kernel(u_in, p_in, c_in, d_in, a_ref, e_ref, face_ref, u_ref, p_ref, c_ref, d_ref, sems):
    copies = [pltpu.make_async_copy(c_in, c_ref, sems.at[0]), pltpu.make_async_copy(d_in, d_ref, sems.at[1])]
    for k in range(3):
        copies.append(pltpu.make_async_copy(u_in.at[k], u_ref.at[k], sems.at[2 + k]))
        copies.append(pltpu.make_async_copy(p_in.at[k], p_ref.at[k], sems.at[5 + k]))
    for copy in copies:
        copy.start()
    for copy in copies:
        copy.wait()
    lane = lane_of()

    def plane(x, carry):
        for row in (0, 8):
            rows = pl.ds(row, 8)
            share = 1.0 / (1.0 + d_ref[x, rows, :])
            values = [u_ref[k, x, rows, :] for k in range(3)] + [p_ref[k, x, rows, :] for k in range(3)]
            values += [2.0 * share, c_ref[x, rows, :] * share * (1.0 / 12.0)]
            a_ref[x, rows, :] = values[6]
            e_ref[x, rows, :] = values[7]
            face_ref[x, rows, :] = pack_faces(values, lane)
        return carry

    lax.fori_loop(0, 8, plane, 0)


def exponent_of(peak):
    peak = jnp.maximum(jnp.max(peak, axis=0, keepdims=True), 1e-30)
    return jnp.broadcast_to(jnp.ceil(jnp.log2(peak)), (8, 128))


def coded(values):
    return jnp.round(values).astype(jnp.int32).astype(jnp.int16)


def decoded(values):
    return values.astype(jnp.int32).astype(F32)


def twice(rows):
    return jnp.concatenate([rows, rows], axis=0)


def sent_exponents(message):
    both = decoded(message[message.shape[0] - 1]) - BIAS
    return both[0:8], both[8:16]


def x_message_kernel(coefficients, *refs):
    if coefficients:
        z_second_ref, z_first_ref, u_ref, p_ref, a_ref, e_ref, halo_ref, up_ref, down_ref, power_ref = refs
    else:
        z_second_ref, z_first_ref, u_ref, p_ref, halo_ref, up_ref, down_ref, power_ref = refs
    inner = lax.broadcasted_iota(jnp.int32, (16, 128), 1) % 16
    from_first = (inner < 8) == is_odd("gz")

    def largest(x, carry):
        field, face = carry
        for k in range(3):
            both = jnp.maximum(jnp.abs(u_ref[k, x]), jnp.abs(p_ref[k, x]))
            field = jnp.maximum(field, jnp.maximum(both[0:8], both[8:16]))
        halo = jnp.where(from_first, z_first_ref[x], z_second_ref[x])
        halo_ref[x] = halo
        halo = jnp.abs(halo)
        return field, jnp.maximum(face, jnp.maximum(halo[0:8], halo[8:16]))

    zero = jnp.zeros((8, 128), F32)
    field, face = lax.fori_loop(0, 8, largest, (zero, zero))
    powers = jnp.concatenate([exponent_of(field), exponent_of(face)], axis=0)
    power_ref[...] = powers
    up_ref[up_ref.shape[0] - 1] = coded(powers + BIAS)
    down_ref[down_ref.shape[0] - 1] = coded(powers + BIAS)
    scale = FULL * jnp.exp2(-powers)
    field, face = twice(scale[0:8]), twice(scale[8:16])

    def whole(x, carry):
        for k in range(3):
            code = coded(u_ref[k, x] * field)
            up_ref[XU * k + x] = code
            down_ref[XU * k + x] = code
        return carry

    def part(i, carry):
        parts = [(p_ref.at[k], field) for k in range(3)]
        if coefficients:
            parts += [(a_ref, 1.0 / UNIT_A), (e_ref, 1.0 / UNIT_E)]
        for at, (source, unit) in enumerate(parts):
            up_ref[3 * XU + XP * at + i] = coded(source[8 - XP + i] * unit)
            down_ref[3 * XU + XP * at + i] = coded(source[i] * unit)
        return carry

    at = 3 * XU + (5 if coefficients else 3) * XP

    def side(i, carry):
        up_ref[at + i] = coded(halo_ref[8 - XH + i] * face)
        down_ref[at + i] = coded(halo_ref[i] * face)
        return carry

    lax.fori_loop(0, 8, whole, 0)
    lax.fori_loop(0, XP, part, 0)
    lax.fori_loop(0, XH, side, 0)


def y_message_kernel(coefficients, *refs):
    if coefficients:
        u_ref, p_ref, a_ref, e_ref, halo_ref, power_ref, low_ref, high_ref, first_ref, second_ref = refs
    else:
        u_ref, p_ref, halo_ref, power_ref, low_ref, high_ref, second_ref, first_ref = refs
    odd = is_odd("gy")
    powers = power_ref[...]
    low_powers = jnp.concatenate(sent_exponents(low_ref), axis=0)
    high_powers = jnp.concatenate(sent_exponents(high_ref), axis=0)
    most = jnp.maximum(powers, jnp.maximum(low_powers, high_powers))
    for out_ref in (first_ref, second_ref):
        out_ref[out_ref.shape[0] - 1] = coded(most + BIAS)
    own_scale = FULL * jnp.exp2(-most)
    low_scale = jnp.exp2(low_powers - most)
    high_scale = jnp.exp2(high_powers - most)
    field = [twice(scale[0:8]) for scale in (own_scale, low_scale, high_scale)]
    face = [twice(scale[8:16]) for scale in (own_scale, low_scale, high_scale)]

    def put(at, pair):
        up = jnp.concatenate([pair[0][8:16], pair[1][8:16]], axis=0)
        down = jnp.concatenate([pair[0][0:8], pair[1][0:8]], axis=0)
        first_ref[at] = coded(jnp.where(odd, down, up))
        second_ref[at] = coded(jnp.where(odd, up, down))

    def group(parts, x_planes, y_planes, x_at, y_at):
        side = (y_planes - 8) // 4

        def own(i, carry):
            for at, (source, units) in enumerate(parts):
                put(y_at + at * y_planes // 2 + side + i, [source[2 * i + j] * units[0] for j in (0, 1)])
            return carry

        def sides(i, carry):
            for at, (_, units) in enumerate(parts):
                start = x_at + at * x_planes
                first = start + x_planes - 2 * side + 2 * i
                put(y_at + at * y_planes // 2 + i, [decoded(low_ref[first + j]) * units[1] for j in (0, 1)])
                first = start + 2 * i
                pair = [decoded(high_ref[first + j]) * units[2] for j in (0, 1)]
                put(y_at + at * y_planes // 2 + side + 4 + i, pair)
            return carry

        lax.fori_loop(0, 4, own, 0)
        lax.fori_loop(0, side, sides, 0)
        return x_at + len(parts) * x_planes, y_at + len(parts) * y_planes // 2

    x_at, y_at = group([(u_ref.at[k], field) for k in range(3)], XU, YU, 0, 0)
    parts = [(p_ref.at[k], field) for k in range(3)]
    if coefficients:
        parts += [(a_ref, (1.0 / UNIT_A, 1.0, 1.0)), (e_ref, (1.0 / UNIT_E, 1.0, 1.0))]
    x_at, y_at = group(parts, XP, YP, x_at, y_at)
    group([(halo_ref, face)], XH, YH, x_at, y_at)


def fill(parts, x_low, x_high, y_first, y_second, x_at, x_planes, y_at, y_planes):
    count = len(parts)
    side = (y_planes - 8) // 2
    odd = is_odd("gy")

    def own(i, carry):
        for target, row, block, _ in parts:
            target[8 + i, row + 8 : row + 24, :] = block[i]
        return carry

    def x_side(i, carry):
        for at, (target, row, _, units) in enumerate(parts):
            here = x_at + at * x_planes + i
            target[8 - x_planes + i, row + 8 : row + 24, :] = decoded(x_low[here]) * units[0]
            target[16 + i, row + 8 : row + 24, :] = decoded(x_high[here]) * units[1]
        return carry

    def y_side(i, carry):
        for at, (target, row, _, units) in enumerate(parts):
            here = y_at + at * y_planes // 2 + i
            first, second = decoded(y_first[here]), decoded(y_second[here])
            low = jnp.where(odd, first, second) * units[2]
            high = jnp.where(odd, second, first) * units[3]
            for j in (0, 1):
                target[8 - side + 2 * i + j, row : row + 8, :] = low[8 * j : 8 * j + 8]
                target[8 - side + 2 * i + j, row + 24 : row + 32, :] = high[8 * j : 8 * j + 8]
        return carry

    lax.fori_loop(0, 8, own, 0, unroll=2)
    lax.fori_loop(0, x_planes, x_side, 0)
    lax.fori_loop(0, y_planes // 2, y_side, 0, unroll=2)
    return x_at + count * x_planes, y_at + count * y_planes // 2


def steps_kernel(first, *refs):
    if first:
        (u_in, p_in, a_in, e_in, halo_in, x_low, x_high, y_first, y_second, weight_in) = refs[:10]
        (u_out, p_out, face_out, slab_out, seen_out, code_ref) = refs[10:16]
        state_ref, rate_ref, edge_ref = refs[16:]
    else:
        (u_in, p_in, halo_in, x_low, x_high, y_first, y_second, weight_in, code_ref) = refs[:9]
        u_out, state_ref, rate_ref = refs[-3:]
    a_ref, e_ref, ha_ref, he_ref = (rate_ref.at[at] for at in range(4))
    lane = lane_of()
    inner = lane % 16

    sides = (x_low, x_high, y_first, y_second)
    powers = [sent_exponents(message) for message in sides]
    odd = is_odd("gy")
    swapped = list(zip(powers[2], powers[3]))
    powers[2] = [jnp.where(odd, one, other) for one, other in swapped]
    powers[3] = [jnp.where(odd, other, one) for one, other in swapped]
    field = [twice(jnp.exp2(power[0]) * (1.0 / FULL)) for power in powers]
    face = [twice(jnp.exp2(power[1]) * (1.0 / FULL)) for power in powers]
    x_at, y_at = fill([(state_ref.at[0, k], 8, u_in.at[k], field) for k in range(3)], *sides, 0, XU, 0, YU)
    parts = [(state_ref.at[1, k], 8, p_in.at[k], field) for k in range(3)]
    if first:
        parts += [(a_ref, 0, a_in, (UNIT_A,) * 4), (e_ref, 0, e_in, (UNIT_E,) * 4)]
    x_at, y_at = fill(parts, *sides, x_at, XP, y_at, YP)
    fill([(state_ref.at[0, 3], 8, halo_in, face)], *sides, x_at, XH, y_at, YH)

    unit = jnp.where(lane < 112, UNIT_A, UNIT_E)

    def prepare(x, carry):
        for half in (0, 16):
            held = pl.ds(half, 16)
            if first:
                code_ref[0, x - 2, held, :] = coded(a_ref[x, held, :] * (1.0 / UNIT_A))
                code_ref[1, x - 2, held, :] = coded(e_ref[x, held, :] * (1.0 / UNIT_E))
                sides = state_ref[0, 3, x, pl.ds(8 + half, 16), :]
                scale = twice(jnp.where(lane < 96, 0.0, 1.0 / unit))
                code_ref[2, x - 2, held, :] = coded(jnp.where(scale > 0.0, sides * scale, 0.0))
            else:
                a_ref[x, held, :] = decoded(code_ref[0, x - 2, held, :]) * UNIT_A
                e_ref[x, held, :] = decoded(code_ref[1, x - 2, held, :]) * UNIT_E
                sides = decoded(code_ref[2, x - 2, held, :]) * twice(unit)
            for tile in (0, 8):
                rows = pl.ds(8 + half + tile, 8)
                halo = state_ref[0, 3, x, rows, :]
                state_ref[0, 3, x, rows, :] = jnp.where(lane < 48, halo, 0.0)
                state_ref[1, 3, x, rows, :] = jnp.where(lane < 48, pltpu.roll(halo, 128 - 48, 1), 0.0)
                side = sides[tile : tile + 8]
                for target, at in ((ha_ref, 96), (he_ref, 112)):
                    spread = jnp.where(lane < 16, pltpu.roll(side, 128 - at, 1), pltpu.roll(side, 144 - at, 1))
                    spread = jnp.where(lane < 32, spread, pltpu.roll(side, 160 - at, 1))
                    target[x, pl.ds(half + tile, 8), :] = jnp.where(lane < 48, spread, 0.0)
        return carry

    lax.fori_loop(2, 22, prepare, 0, unroll=4)

    def advance(src, dst, x, count):
        rows = pl.ds(8, 32)
        fields = [[src[k, 2 + j, rows, :] for j in range(count)] for k in range(4)]
        parts = [[split(v) for v in field] for field in fields]
        depth = []
        for k in range(3):
            pieces = [jnp.concatenate([parts[k][j][part], parts[3][j][part]], axis=1) for part in (0, 1) for j in range(count)]
            both = jnp.dot(jnp.concatenate(pieces, axis=0), weight_in[k], preferred_element_type=F32)
            depth.append(both[0 : 32 * count] + both[32 * count :])
        side = depth[0][:, 128:] + depth[1][:, 128:] + depth[2][:, 128:]
        fresh = []
        for j in range(count):
            for k in range(4):
                v = fields[k][j]
                near = (src[k, 1 + j, rows, :] + src[k, 3 + j, rows, :]) + (
                    src[k, 2 + j, pl.ds(7, 32), :] + src[k, 2 + j, pl.ds(9, 32), :]
                )
                far = (src[k, j, rows, :] + src[k, 4 + j, rows, :]) + (
                    src[k, 2 + j, pl.ds(6, 32), :] + src[k, 2 + j, pl.ds(10, 32), :]
                )
                along = side if k == 3 else depth[k][:, :128]
                laplace = along[32 * j : 32 * j + 32] + (16.0 * near - far)
                old = dst[k, x + j, rows, :]
                a_each, e_each = (ha_ref, he_ref) if k == 3 else (a_ref, e_ref)
                fresh.append((k, j, old + a_each[x + j] * (v - old) + e_each[x + j] * laplace))
        return fresh, side

    def block_of(step, x, count):
        dst = state_ref.at[(step + 1) % 2]
        fresh, side = advance(state_ref.at[step % 2, :, pl.ds(x - 2, 4 + count)], dst, x, count)
        for k, j, value in fresh:
            dst[k, x + j, 8:40, :] = value
        if first:
            for j in range(count):
                edge_ref[step, x + j, :, :] = side[32 * j + 8 : 32 * j + 24]

    for step in range(HALF):
        count = (20 - 4 * step) // 2
        block_of(step, 2 * step + 2, count)
        block_of(step, 2 * step + 2 + count, count)

    block = pl.ds(16, 16)

    def finish(x, carry):
        for k in range(3):
            u_out[k, x, :, :] = state_ref[0, k, 8 + x, block, :]
            if first:
                p_out[k, x, :, :] = state_ref[1, k, 8 + x, block, :]
        if first:
            for row in (0, 8):
                rows = pl.ds(row, 8)
                values = [state_ref[slot, k, 8 + x, pl.ds(16 + row, 8), :] for slot in (0, 1) for k in range(3)]
                last = pack_faces(values, lane)
                face_out[x, rows, :] = last
                slab = values[0]
                for at in range(1, 6):
                    slab = jnp.where(lane // 16 == at, pltpu.roll(values[at], 16 * at, 1), slab)
                slab_out[x, rows, :] = slab
                seen = jnp.zeros((8, 128), F32)
                for step in range(HALF):
                    if step < HALF - 1:
                        sample = pltpu.roll(edge_ref[step + 1, 8 + x, rows, :], 56 + step, 1)
                    else:
                        sample = pltpu.roll(last, 120 + step, 1)
                    seen = jnp.where((inner == step) & (lane < 48), sample, seen)
                seen_out[x, rows, :] = seen
        return carry

    lax.fori_loop(0, 8, finish, 0, unroll=4)


def slab_message_kernel(own_ref, low_ref, high_ref, *refs):
    first_ref, second_ref = refs[-2:]
    odd = is_odd("gy")

    def plane(i, carry):
        for at, source in ((0, low_ref), (8, own_ref), (16, high_ref)):
            up, down = source[i, 8:16, :], source[i, 0:8, :]
            first_ref[at + i] = jnp.where(odd, down, up)
            second_ref[at + i] = jnp.where(odd, up, down)
        return carry

    lax.fori_loop(0, 8, plane, 0, unroll=2)


def surface_kernel(
    own_in, x_low, x_high, y_first, y_second, weight_in, code_in, seen_in, filter_in, count_in, after_in,
    demand_out, state_ref, rate_ref, sample_ref, seen_ref, filter_ref, count_ref,
):
    lane = lane_of()
    inner = lane % 16

    odd = is_odd("gy")

    def near_side(i, carry):
        state_ref[0, i, 16:32, :] = x_low[i]
        state_ref[0, 8 + i, 16:32, :] = own_in[i]
        state_ref[0, 16 + i, 16:32, :] = x_high[i]
        for part in range(3):
            one, other = y_first[8 * part + i], y_second[8 * part + i]
            state_ref[0, 8 * part + i, 8:16, :] = jnp.where(odd, one, other)
            state_ref[0, 8 * part + i, 32:40, :] = jnp.where(odd, other, one)
        return carry

    lax.fori_loop(0, 8, near_side, 0, unroll=2)

    def prepare(x, carry):
        for tile in range(4):
            rows = pl.ds(8 + 8 * tile, 8)
            value = state_ref[0, x, rows, :]
            state_ref[0, x, rows, :] = jnp.where(lane < 48, value, 0.0)
            state_ref[1, x, rows, :] = jnp.where(lane < 48, pltpu.roll(value, 128 - 48, 1), 0.0)
        return carry

    def rates(x, carry):
        for at, unit in ((0, UNIT_A), (1, UNIT_E)):
            for half in (0, 16):
                both = decoded(code_in[at, x - 2, half : half + 16, :]) * unit
                for tile in (0, 8):
                    rate = both[tile : tile + 8]
                    spread = jnp.where(lane < 32, pltpu.roll(rate, 16, 1), pltpu.roll(rate, 32, 1))
                    spread = jnp.where(lane < 16, rate, spread)
                    rate_ref[at, x, pl.ds(half + tile, 8), :] = jnp.where(lane < 48, spread, 0.0)
        return carry

    lax.fori_loop(0, 24, prepare, 0, unroll=4)
    lax.fori_loop(2, 22, rates, 0, unroll=4)

    def advance(step, x, count):
        src, dst = state_ref.at[step % 2, pl.ds(x - 2, 4 + count)], state_ref.at[(step + 1) % 2]
        rows = pl.ds(8, 32)
        fields = [src[2 + j, rows, :] for j in range(count)]
        halves = jnp.concatenate([jnp.concatenate(split(v), axis=1) for v in fields], axis=0)
        depth = jnp.dot(halves, weight_in[...], preferred_element_type=F32)
        fresh = []
        for j, v in enumerate(fields):
            near = (src[1 + j, rows, :] + src[3 + j, rows, :]) + (src[2 + j, pl.ds(7, 32), :] + src[2 + j, pl.ds(9, 32), :])
            far = (src[j, rows, :] + src[4 + j, rows, :]) + (src[2 + j, pl.ds(6, 32), :] + src[2 + j, pl.ds(10, 32), :])
            laplace = depth[32 * j : 32 * j + 32] + (16.0 * near - far)
            old = dst[x + j, rows, :]
            fresh.append(old + rate_ref[0, x + j] * (v - old) + rate_ref[1, x + j] * laplace)
        for j, value in enumerate(fresh):
            dst[x + j, 8:40, :] = value
            sample_ref[step, x + j, :, :] = value[8:24]

    for step in range(HALF):
        count = (20 - 4 * step) // 2
        advance(step, 2 * step + 2, count)
        advance(step, 2 * step + 2 + count, count)

    def finish(x, carry):
        for row in (0, 8):
            rows = pl.ds(row, 8)
            seen = seen_in[x, rows, :]
            for step in range(HALF):
                at = HALF + step
                sample = pltpu.roll(sample_ref[step, 8 + x, rows, :], at, 1)
                seen = jnp.where((inner == at) & (lane < 48), sample, seen)
            seen_ref[x, rows, :] = seen
        return carry

    lax.fori_loop(0, 8, finish, 0, unroll=4)

    filter_ref[...] = filter_in[...].astype(F32)
    blocks = [jnp.zeros((8, CLASSES * MODES), F32)] * 16
    for k in range(3):
        blocks[2 * k] = filter_ref[pl.ds(k, STEPS, stride=3), :]
    filters = jnp.concatenate(blocks, axis=0).astype(jnp.bfloat16)
    motion = seen_ref[...].reshape(128, 128).astype(jnp.bfloat16)
    modal = lax.dot_general(filters, motion, (((0,), (1,)), ((), ())), preferred_element_type=F32)
    modes = lax.broadcasted_iota(jnp.int32, (MODES, 128), 0)
    count_ref[...] = jnp.zeros((8, 128), jnp.int32)
    count_ref[0:1, 0:CLASSES] = count_in[...]
    counts = jnp.where(modes == lane, jnp.broadcast_to(count_ref[0:1, :], (8, 128)), 0)
    counts = jnp.sum(counts, axis=1, keepdims=True)
    energies = []
    for kind in range(CLASSES):
        part = modal[MODES * kind : MODES * (kind + 1), :]
        part = jnp.where(modes < counts[kind : kind + 1, :], part * part, 0.0)
        energies.append(jnp.sum(part, axis=0, keepdims=True))
    demand_out[...] = 0.5 * jnp.log1p(jnp.concatenate(energies, axis=0))


def table_kernel(demand_ref, cells_ref, table_out):
    demand = demand_ref[...]
    for owner in range(table_out.shape[0]):
        cells = jnp.broadcast_to(cells_ref[owner : owner + 1, :], (CLASSES, 128))
        chosen = jnp.take_along_axis(demand, cells, axis=1)
        for level in range(table_out.shape[1]):
            table_out[owner, level] = chosen


def fragility_kernel(
    table_ref, slot_ref, kind_ref, city_ref, amplify_ref, median_ref, spread_ref, out_ref, gain_ref, tables_ref
):
    sources = table_ref.shape[0]
    slot, kind, city = slot_ref[...], kind_ref[...], city_ref[...]
    column = slot % 128
    key = (slot // 128) * CLASSES + kind
    demand = jnp.zeros((8, 128), F32)
    for source in range(sources):
        for each in range(CLASSES):
            row = jnp.broadcast_to(table_ref[source, 0, each : each + 1, :], (8, 128))
            found = jnp.take_along_axis(row, column, axis=1)
            demand = jnp.where(key == source * CLASSES + each, found, demand)
    gain_ref[...] = jnp.ones((8, 128), F32)
    gain_ref[0:1, 0:CITIES] = amplify_ref[...]
    gain = jnp.log(jnp.broadcast_to(gain_ref[0:1, :], (8, 128)))
    demand = demand + jnp.take_along_axis(gain, city, axis=1)
    tables_ref[...] = jnp.ones((128, 128), F32)
    batches = median_ref.shape[1]
    tables_ref[0:CLASSES, 0:batches] = median_ref[...]
    medians = tables_ref[...].T
    tables_ref[0:CLASSES, 0:batches] = spread_ref[...]
    spreads = tables_ref[...].T
    for group in range(8):
        level = jnp.broadcast_to(demand[group : group + 1, :], (8, 128))
        index = jnp.broadcast_to(kind[group : group + 1, :], (8, 128))
        for half in range(0, batches, 8):
            middle = jnp.take_along_axis(medians[half : half + 8, :], index, axis=1)
            width = jnp.take_along_axis(spreads[half : half + 8, :], index, axis=1)
            out_ref[half : half + 8, 128 * group : 128 * group + 128] = jax.nn.sigmoid((level - middle) / width)


VM = pl.BlockSpec(memory_space=pltpu.VMEM)


WEIGHTS = {"start": 1.4, "steps_first": 6.7, "steps_second": 6.5, "surface": 4.0, "fragility": 1.0}
UNIT_FLOPS = 1.15e10


def call(kernel, name, shapes, args, specs=None, scratch=(), limit=VMEM_LIMIT):
    out = [s if isinstance(s, jax.ShapeDtypeStruct) else jax.ShapeDtypeStruct(s, F32) for s in shapes]
    return pl.pallas_call(
        kernel,
        out_shape=out,
        in_specs=specs or [VM] * len(args),
        out_specs=[VM] * len(out),
        scratch_shapes=list(scratch),
        compiler_params=pltpu.CompilerParams(vmem_limit_bytes=limit),
        cost_estimate=pl.CostEstimate(flops=int(WEIGHTS.get(name, 0.3) * UNIT_FLOPS), bytes_accessed=0, transcendentals=0),
        name=name,
    )(*args)


def both_ways(to_up, to_down, axis):
    count = lax.axis_size(axis)
    forward = [(i, i + 1) for i in range(count - 1)]
    backward = [(i + 1, i) for i in range(count - 1)]
    return lax.ppermute(to_up, axis, forward), lax.ppermute(to_down, axis, backward)


def swaps(first, second, axis):
    count = lax.axis_size(axis)
    pairs = [[(i, i + 1) for i in range(begin, count - 1, 2)] for begin in (0, 1)]
    pairs = [ways + [(b, a) for a, b in ways] for ways in pairs]
    return lax.ppermute(first, axis, pairs[0]), lax.ppermute(second, axis, pairs[1])


def is_odd(axis):
    return lax.rem(lax.axis_index(axis), 2) == 1


def exchange_x(u, p, faces, coefficients):
    extra = list(coefficients)
    z_first, z_second = swaps(faces, faces, "gz")
    planes = 3 * XU + (3 + len(extra)) * XP + XH + 1
    message = jax.ShapeDtypeStruct((planes, 16, 128), jnp.int16)
    halo, up, down, powers = call(
        functools.partial(x_message_kernel, bool(extra)),
        "x_message",
        [(8, 16, 128), message, message, (16, 128)],
        [z_second, z_first, u, p] + extra,
    )
    return halo, powers, *both_ways(up, down, "gx")


def y_messages(u, p, coefficients, halo, powers, x_low, x_high):
    extra = list(coefficients)
    planes = (3 * YU + (3 + len(extra)) * YP + YH) // 2 + 1
    message = jax.ShapeDtypeStruct((planes, 16, 128), jnp.int16)
    messages = call(
        functools.partial(y_message_kernel, bool(extra)),
        "y_message",
        [message, message],
        [u, p] + extra + [halo, powers, x_low, x_high],
    )
    return messages if extra else messages[::-1]


def body(
    displacement,
    previous,
    courant,
    damping,
    send_cells,
    building_slot,
    building_class,
    city,
    mode_count,
    modal_filter,
    amplify,
    median,
    spread,
):
    own = (3, 8, 16, 128)
    plane = (8, 16, 128)
    wide = pltpu.VMEM((2, 4, 24, 48, 128), F32)
    rates = pltpu.VMEM((4, 24, 32, 128), F32)
    samples = pltpu.VMEM((HALF, 24, 16, 128), F32)

    u, p = displacement, previous
    a, e, faces = call(
        start_kernel,
        "start",
        [plane, plane, plane],
        [u, p, courant, damping],
        specs=[pl.BlockSpec(memory_space=pltpu.HBM)] * 4,
        scratch=[pltpu.VMEM(own, F32)] * 2 + [pltpu.VMEM(plane, F32)] * 2 + [pltpu.SemaphoreType.DMA((8,))],
        limit=START_LIMIT,
    )
    halo, powers, x_low, x_high = exchange_x(u, p, faces, (a, e))
    messages = y_messages(u, p, (a, e), halo, powers, x_low, x_high)
    received = (halo, x_low, x_high, *swaps(*messages, "gy"))
    weights = jnp.asarray(depth_weights(), jnp.bfloat16)
    u, p, faces, slab, seen, codes = call(
        functools.partial(steps_kernel, True),
        "steps_first",
        [own, own, plane, plane, plane, jax.ShapeDtypeStruct((3, 20, 32, 128), jnp.int16)],
        [u, p, a, e, *received, weights],
        scratch=[wide, rates, samples],
    )

    near_low, near_high = both_ways(slab, slab, "gx")
    halo, powers, x_low, x_high = exchange_x(u, p, faces, ())
    owners, levels = lax.axis_size("gx"), lax.axis_size("gz")
    slab_inputs = [jnp.asarray(slab_weights(), jnp.bfloat16), modal_filter.T, mode_count.reshape(1, CLASSES)]
    cells = send_cells.reshape(owners, 128)
    slab_messages = call(
        slab_message_kernel,
        "slab_message",
        [(24, 8, 128)] * 2,
        [slab, near_low, near_high, powers, cells] + slab_inputs,
    )
    side_first, side_second = swaps(*slab_messages, "gy")
    messages = y_messages(u, p, (), halo, powers, x_low, x_high)
    received = (halo, x_low, x_high, *swaps(*messages, "gy"))
    (demand,) = call(
        surface_kernel,
        "surface",
        [(CLASSES, 128)],
        [slab, near_low, near_high, side_first, side_second, slab_inputs[0], codes, seen] + slab_inputs[1:] + [messages[0]],
        specs=[VM] * 10 + [pl.BlockSpec(memory_space=pl.ANY)],
        scratch=[
            pltpu.VMEM((2, 24, 48, 128), F32),
            pltpu.VMEM((2, 24, 32, 128), F32),
            samples,
            pltpu.VMEM(plane, F32),
            pltpu.VMEM((3 * STEPS, CLASSES * MODES), F32),
            pltpu.VMEM((8, 128), jnp.int32),
        ],
    )
    (table,) = call(
        table_kernel,
        "table",
        [(owners, levels, CLASSES, 128)],
        [demand, cells],
    )
    table = table.reshape(owners * levels, CLASSES, 128)
    table = lax.all_to_all(table, ("gx", "gz"), split_axis=0, concat_axis=0, tiled=True)
    building_inputs = [
        building_slot.reshape(8, 128),
        building_class.reshape(8, 128),
        city.reshape(8, 128),
        amplify.reshape(1, CITIES),
        median.T,
        spread.T,
    ]
    (field,) = call(
        functools.partial(steps_kernel, False),
        "steps_second",
        [own],
        [u, p, *received, weights, codes] + building_inputs,
        scratch=[wide, rates],
    )
    (probability,) = call(
        fragility_kernel,
        "fragility",
        [(16, 1024)],
        [table.reshape(owners, levels, CLASSES, 128)] + building_inputs,
        scratch=[pltpu.VMEM((8, 128), F32), pltpu.VMEM((128, 128), F32)],
    )
    return (field, probability)


def solution(mesh):
    placed = (
        P(None, "gx", "gy", "gz"),
        P(None, "gx", "gy", "gz"),
        P("gx", "gy", "gz"),
        P("gx", "gy", "gz"),
        P("gx", "gy", None),
        P(("gx", "gy", "gz")),
        P(("gx", "gy", "gz")),
        P(("gx", "gy", "gz")),
        P(),
        P(),
        P(),
        P(),
        P(),
    )
    return jax.shard_map(
        body,
        mesh=mesh,
        in_specs=placed,
        out_specs=(P(None, "gx", "gy", "gz"), P(None, ("gx", "gy", "gz"))),
        check_vma=False,
    )
```

```python
import functools

import jax
import jax.numpy as jnp
import numpy as np
from jax import lax
from jax.experimental import pallas as pl
from jax.experimental.pallas import tpu as pltpu
from jax.sharding import PartitionSpec as P

STEPS = 8
HALF = 4
DEEP = 2 * HALF
CLASSES = 8
MODES = 8
CITIES = 16
F32 = jnp.float32
VMEM_LIMIT = 24 * 1024 * 1024
START_LIMIT = int(53.8 * 1024 * 1024)

XU, XP, XH = 8, 6, 7
YU, YP, YH = 24, 20, 20

FULL = 32000.0
BIAS = 200
UNIT_A = 2.0 / FULL
UNIT_E = 0.2 / 12.0 / FULL


def depth_weights():
    lanes = np.arange(256)
    result = np.zeros((3, 256, 256), np.float32)
    for k in range(3):
        at = lanes - 128 - 16 * k
        depth = np.where(lanes < 128, lanes, np.where(at < 8, at - 8, at + 120))
        used = (lanes < 128) | ((at >= 0) & (at < 16))
        apart = np.abs(depth[:, None] - depth[None, :])
        band = np.where(apart == 0, -90.0, np.where(apart == 1, 16.0, np.where(apart == 2, -1.0, 0.0)))
        result[k] = np.where(used[:, None] & used[None, :], band, 0.0)
        result[k, 0, 128 + 64 + 16 * k + 8] = 1.0
    return result


def slab_weights():
    lanes = np.arange(128)
    apart = np.abs(lanes[:, None] - lanes[None, :])
    band = np.where(apart == 0, -90.0, np.where(apart == 1, 16.0, np.where(apart == 2, -1.0, 0.0)))
    same = (lanes[:, None] // 16 == lanes[None, :] // 16) & (lanes[:, None] < 48)
    band = np.where(same, band, 0.0)
    return np.concatenate([band, band], axis=0)


def split(v):
    high = v.astype(jnp.bfloat16)
    return high, (v - high.astype(F32)).astype(jnp.bfloat16)


def lane_of():
    return lax.broadcasted_iota(jnp.int32, (8, 128), 1)


def pack_faces(values, lane):
    packed = pltpu.roll(values[0], 8, 1)
    for at in range(1, len(values)):
        packed = jnp.where(lane // 16 == at, pltpu.roll(values[at], (16 * at + 8) % 128, 1), packed)
    return packed


def start_kernel(u_in, p_in, c_in, d_in, a_ref, e_ref, face_ref, u_ref, p_ref, c_ref, d_ref, sems):
    copies = [pltpu.make_async_copy(c_in, c_ref, sems.at[0]), pltpu.make_async_copy(d_in, d_ref, sems.at[1])]
    for k in range(3):
        copies.append(pltpu.make_async_copy(u_in.at[k], u_ref.at[k], sems.at[2 + k]))
        copies.append(pltpu.make_async_copy(p_in.at[k], p_ref.at[k], sems.at[5 + k]))
    for copy in copies:
        copy.start()
    for copy in copies:
        copy.wait()
    lane = lane_of()

    def plane(x, carry):
        for row in (0, 8):
            rows = pl.ds(row, 8)
            share = 1.0 / (1.0 + d_ref[x, rows, :])
            values = [u_ref[k, x, rows, :] for k in range(3)] + [p_ref[k, x, rows, :] for k in range(3)]
            values += [2.0 * share, c_ref[x, rows, :] * share * (1.0 / 12.0)]
            a_ref[x, rows, :] = values[6]
            e_ref[x, rows, :] = values[7]
            face_ref[x, rows, :] = pack_faces(values, lane)
        return carry

    lax.fori_loop(0, 8, plane, 0)


def exponent_of(peak):
    peak = jnp.maximum(jnp.max(peak, axis=0, keepdims=True), 1e-30)
    return jnp.broadcast_to(jnp.ceil(jnp.log2(peak)), (8, 128))


def coded(values):
    return jnp.round(values).astype(jnp.int32).astype(jnp.int16)


def decoded(values):
    return values.astype(jnp.int32).astype(F32)


def twice(rows):
    return jnp.concatenate([rows, rows], axis=0)


def sent_exponents(message):
    both = decoded(message[message.shape[0] - 1]) - BIAS
    return both[0:8], both[8:16]


def x_message_kernel(coefficients, *refs):
    if coefficients:
        z_second_ref, z_first_ref, u_ref, p_ref, a_ref, e_ref, halo_ref, up_ref, down_ref, power_ref = refs
    else:
        z_second_ref, z_first_ref, u_ref, p_ref, halo_ref, up_ref, down_ref, power_ref = refs
    inner = lax.broadcasted_iota(jnp.int32, (16, 128), 1) % 16
    from_first = (inner < 8) == is_odd("gz")

    def largest(x, carry):
        field, face = carry
        for k in range(3):
            both = jnp.maximum(jnp.abs(u_ref[k, x]), jnp.abs(p_ref[k, x]))
            field = jnp.maximum(field, jnp.maximum(both[0:8], both[8:16]))
        halo = jnp.where(from_first, z_first_ref[x], z_second_ref[x])
        halo_ref[x] = halo
        halo = jnp.abs(halo)
        return field, jnp.maximum(face, jnp.maximum(halo[0:8], halo[8:16]))

    zero = jnp.zeros((8, 128), F32)
    field, face = lax.fori_loop(0, 8, largest, (zero, zero))
    powers = jnp.concatenate([exponent_of(field), exponent_of(face)], axis=0)
    power_ref[...] = powers
    up_ref[up_ref.shape[0] - 1] = coded(powers + BIAS)
    down_ref[down_ref.shape[0] - 1] = coded(powers + BIAS)
    scale = FULL * jnp.exp2(-powers)
    field, face = twice(scale[0:8]), twice(scale[8:16])

    def whole(x, carry):
        for k in range(3):
            code = coded(u_ref[k, x] * field)
            up_ref[XU * k + x] = code
            down_ref[XU * k + x] = code
        return carry

    def part(i, carry):
        parts = [(p_ref.at[k], field) for k in range(3)]
        if coefficients:
            parts += [(a_ref, 1.0 / UNIT_A), (e_ref, 1.0 / UNIT_E)]
        for at, (source, unit) in enumerate(parts):
            up_ref[3 * XU + XP * at + i] = coded(source[8 - XP + i] * unit)
            down_ref[3 * XU + XP * at + i] = coded(source[i] * unit)
        return carry

    at = 3 * XU + (5 if coefficients else 3) * XP

    def side(i, carry):
        up_ref[at + i] = coded(halo_ref[8 - XH + i] * face)
        down_ref[at + i] = coded(halo_ref[i] * face)
        return carry

    lax.fori_loop(0, 8, whole, 0)
    lax.fori_loop(0, XP, part, 0)
    lax.fori_loop(0, XH, side, 0)


def y_message_kernel(coefficients, *refs):
    if coefficients:
        u_ref, p_ref, a_ref, e_ref, halo_ref, power_ref, low_ref, high_ref, first_ref, second_ref = refs
    else:
        u_ref, p_ref, halo_ref, power_ref, low_ref, high_ref, second_ref, first_ref = refs
    odd = is_odd("gy")
    powers = power_ref[...]
    low_powers = jnp.concatenate(sent_exponents(low_ref), axis=0)
    high_powers = jnp.concatenate(sent_exponents(high_ref), axis=0)
    most = jnp.maximum(powers, jnp.maximum(low_powers, high_powers))
    for out_ref in (first_ref, second_ref):
        out_ref[out_ref.shape[0] - 1] = coded(most + BIAS)
    own_scale = FULL * jnp.exp2(-most)
    low_scale = jnp.exp2(low_powers - most)
    high_scale = jnp.exp2(high_powers - most)
    field = [twice(scale[0:8]) for scale in (own_scale, low_scale, high_scale)]
    face = [twice(scale[8:16]) for scale in (own_scale, low_scale, high_scale)]

    def put(at, pair):
        up = jnp.concatenate([pair[0][8:16], pair[1][8:16]], axis=0)
        down = jnp.concatenate([pair[0][0:8], pair[1][0:8]], axis=0)
        first_ref[at] = coded(jnp.where(odd, down, up))
        second_ref[at] = coded(jnp.where(odd, up, down))

    def group(parts, x_planes, y_planes, x_at, y_at):
        side = (y_planes - 8) // 4

        def own(i, carry):
            for at, (source, units) in enumerate(parts):
                put(y_at + at * y_planes // 2 + side + i, [source[2 * i + j] * units[0] for j in (0, 1)])
            return carry

        def sides(i, carry):
            for at, (_, units) in enumerate(parts):
                start = x_at + at * x_planes
                first = start + x_planes - 2 * side + 2 * i
                put(y_at + at * y_planes // 2 + i, [decoded(low_ref[first + j]) * units[1] for j in (0, 1)])
                first = start + 2 * i
                pair = [decoded(high_ref[first + j]) * units[2] for j in (0, 1)]
                put(y_at + at * y_planes // 2 + side + 4 + i, pair)
            return carry

        lax.fori_loop(0, 4, own, 0)
        lax.fori_loop(0, side, sides, 0)
        return x_at + len(parts) * x_planes, y_at + len(parts) * y_planes // 2

    x_at, y_at = group([(u_ref.at[k], field) for k in range(3)], XU, YU, 0, 0)
    parts = [(p_ref.at[k], field) for k in range(3)]
    if coefficients:
        parts += [(a_ref, (1.0 / UNIT_A, 1.0, 1.0)), (e_ref, (1.0 / UNIT_E, 1.0, 1.0))]
    x_at, y_at = group(parts, XP, YP, x_at, y_at)
    group([(halo_ref, face)], XH, YH, x_at, y_at)


def fill(parts, x_low, x_high, y_first, y_second, x_at, x_planes, y_at, y_planes):
    count = len(parts)
    side = (y_planes - 8) // 2
    odd = is_odd("gy")

    def own(i, carry):
        for target, row, block, _ in parts:
            target[8 + i, row + 8 : row + 24, :] = block[i]
        return carry

    def x_side(i, carry):
        for at, (target, row, _, units) in enumerate(parts):
            here = x_at + at * x_planes + i
            target[8 - x_planes + i, row + 8 : row + 24, :] = decoded(x_low[here]) * units[0]
            target[16 + i, row + 8 : row + 24, :] = decoded(x_high[here]) * units[1]
        return carry

    def y_side(i, carry):
        for at, (target, row, _, units) in enumerate(parts):
            here = y_at + at * y_planes // 2 + i
            first, second = decoded(y_first[here]), decoded(y_second[here])
            low = jnp.where(odd, first, second) * units[2]
            high = jnp.where(odd, second, first) * units[3]
            for j in (0, 1):
                target[8 - side + 2 * i + j, row : row + 8, :] = low[8 * j : 8 * j + 8]
                target[8 - side + 2 * i + j, row + 24 : row + 32, :] = high[8 * j : 8 * j + 8]
        return carry

    lax.fori_loop(0, 8, own, 0, unroll=2)
    lax.fori_loop(0, x_planes, x_side, 0)
    lax.fori_loop(0, y_planes // 2, y_side, 0, unroll=2)
    return x_at + count * x_planes, y_at + count * y_planes // 2


def steps_kernel(first, *refs):
    if first:
        (u_in, p_in, a_in, e_in, halo_in, x_low, x_high, y_first, y_second, weight_in) = refs[:10]
        (u_out, p_out, face_out, slab_out, seen_out, code_ref) = refs[10:16]
        state_ref, rate_ref, edge_ref = refs[16:]
    else:
        (u_in, p_in, halo_in, x_low, x_high, y_first, y_second, weight_in, code_ref) = refs[:9]
        u_out, state_ref, rate_ref = refs[-3:]
    a_ref, e_ref, ha_ref, he_ref = (rate_ref.at[at] for at in range(4))
    lane = lane_of()
    inner = lane % 16

    sides = (x_low, x_high, y_first, y_second)
    powers = [sent_exponents(message) for message in sides]
    odd = is_odd("gy")
    swapped = list(zip(powers[2], powers[3]))
    powers[2] = [jnp.where(odd, one, other) for one, other in swapped]
    powers[3] = [jnp.where(odd, other, one) for one, other in swapped]
    field = [twice(jnp.exp2(power[0]) * (1.0 / FULL)) for power in powers]
    face = [twice(jnp.exp2(power[1]) * (1.0 / FULL)) for power in powers]
    x_at, y_at = fill([(state_ref.at[0, k], 8, u_in.at[k], field) for k in range(3)], *sides, 0, XU, 0, YU)
    parts = [(state_ref.at[1, k], 8, p_in.at[k], field) for k in range(3)]
    if first:
        parts += [(a_ref, 0, a_in, (UNIT_A,) * 4), (e_ref, 0, e_in, (UNIT_E,) * 4)]
    x_at, y_at = fill(parts, *sides, x_at, XP, y_at, YP)
    fill([(state_ref.at[0, 3], 8, halo_in, face)], *sides, x_at, XH, y_at, YH)

    unit = jnp.where(lane < 112, UNIT_A, UNIT_E)

    def prepare(x, carry):
        for half in (0, 16):
            held = pl.ds(half, 16)
            if first:
                code_ref[0, x - 2, held, :] = coded(a_ref[x, held, :] * (1.0 / UNIT_A))
                code_ref[1, x - 2, held, :] = coded(e_ref[x, held, :] * (1.0 / UNIT_E))
                sides = state_ref[0, 3, x, pl.ds(8 + half, 16), :]
                scale = twice(jnp.where(lane < 96, 0.0, 1.0 / unit))
                code_ref[2, x - 2, held, :] = coded(jnp.where(scale > 0.0, sides * scale, 0.0))
            else:
                a_ref[x, held, :] = decoded(code_ref[0, x - 2, held, :]) * UNIT_A
                e_ref[x, held, :] = decoded(code_ref[1, x - 2, held, :]) * UNIT_E
                sides = decoded(code_ref[2, x - 2, held, :]) * twice(unit)
            for tile in (0, 8):
                rows = pl.ds(8 + half + tile, 8)
                halo = state_ref[0, 3, x, rows, :]
                state_ref[0, 3, x, rows, :] = jnp.where(lane < 48, halo, 0.0)
                state_ref[1, 3, x, rows, :] = jnp.where(lane < 48, pltpu.roll(halo, 128 - 48, 1), 0.0)
                side = sides[tile : tile + 8]
                for target, at in ((ha_ref, 96), (he_ref, 112)):
                    spread = jnp.where(lane < 16, pltpu.roll(side, 128 - at, 1), pltpu.roll(side, 144 - at, 1))
                    spread = jnp.where(lane < 32, spread, pltpu.roll(side, 160 - at, 1))
                    target[x, pl.ds(half + tile, 8), :] = jnp.where(lane < 48, spread, 0.0)
        return carry

    lax.fori_loop(2, 22, prepare, 0, unroll=4)

    def advance(src, dst, x, count):
        rows = pl.ds(8, 32)
        fields = [[src[k, 2 + j, rows, :] for j in range(count)] for k in range(4)]
        parts = [[split(v) for v in field] for field in fields]
        depth = []
        for k in range(3):
            pieces = [jnp.concatenate([parts[k][j][part], parts[3][j][part]], axis=1) for part in (0, 1) for j in range(count)]
            both = jnp.dot(jnp.concatenate(pieces, axis=0), weight_in[k], preferred_element_type=F32)
            depth.append(both[0 : 32 * count] + both[32 * count :])
        side = depth[0][:, 128:] + depth[1][:, 128:] + depth[2][:, 128:]
        fresh = []
        for j in range(count):
            for k in range(4):
                v = fields[k][j]
                near = (src[k, 1 + j, rows, :] + src[k, 3 + j, rows, :]) + (
                    src[k, 2 + j, pl.ds(7, 32), :] + src[k, 2 + j, pl.ds(9, 32), :]
                )
                far = (src[k, j, rows, :] + src[k, 4 + j, rows, :]) + (
                    src[k, 2 + j, pl.ds(6, 32), :] + src[k, 2 + j, pl.ds(10, 32), :]
                )
                along = side if k == 3 else depth[k][:, :128]
                laplace = along[32 * j : 32 * j + 32] + (16.0 * near - far)
                old = dst[k, x + j, rows, :]
                a_each, e_each = (ha_ref, he_ref) if k == 3 else (a_ref, e_ref)
                fresh.append((k, j, old + a_each[x + j] * (v - old) + e_each[x + j] * laplace))
        return fresh, side

    def block_of(step, x, count):
        dst = state_ref.at[(step + 1) % 2]
        fresh, side = advance(state_ref.at[step % 2, :, pl.ds(x - 2, 4 + count)], dst, x, count)
        for k, j, value in fresh:
            dst[k, x + j, 8:40, :] = value
        if first:
            for j in range(count):
                edge_ref[step, x + j, :, :] = side[32 * j + 8 : 32 * j + 24]

    for step in range(HALF):
        count = (20 - 4 * step) // 2
        block_of(step, 2 * step + 2, count)
        block_of(step, 2 * step + 2 + count, count)

    block = pl.ds(16, 16)

    def finish(x, carry):
        for k in range(3):
            u_out[k, x, :, :] = state_ref[0, k, 8 + x, block, :]
            if first:
                p_out[k, x, :, :] = state_ref[1, k, 8 + x, block, :]
        if first:
            for row in (0, 8):
                rows = pl.ds(row, 8)
                values = [state_ref[slot, k, 8 + x, pl.ds(16 + row, 8), :] for slot in (0, 1) for k in range(3)]
                last = pack_faces(values, lane)
                face_out[x, rows, :] = last
                slab = values[0]
                for at in range(1, 6):
                    slab = jnp.where(lane // 16 == at, pltpu.roll(values[at], 16 * at, 1), slab)
                slab_out[x, rows, :] = slab
                seen = jnp.zeros((8, 128), F32)
                for step in range(HALF):
                    if step < HALF - 1:
                        sample = pltpu.roll(edge_ref[step + 1, 8 + x, rows, :], 56 + step, 1)
                    else:
                        sample = pltpu.roll(last, 120 + step, 1)
                    seen = jnp.where((inner == step) & (lane < 48), sample, seen)
                seen_out[x, rows, :] = seen
        return carry

    lax.fori_loop(0, 8, finish, 0, unroll=4)


def slab_message_kernel(own_ref, low_ref, high_ref, *refs):
    first_ref, second_ref = refs[-2:]
    odd = is_odd("gy")

    def plane(i, carry):
        for at, source in ((0, low_ref), (8, own_ref), (16, high_ref)):
            up, down = source[i, 8:16, :], source[i, 0:8, :]
            first_ref[at + i] = jnp.where(odd, down, up)
            second_ref[at + i] = jnp.where(odd, up, down)
        return carry

    lax.fori_loop(0, 8, plane, 0, unroll=2)


def surface_kernel(
    own_in, x_low, x_high, y_first, y_second, weight_in, code_in, seen_in, filter_in, count_in, cells_in, after_in,
    table_out, state_ref, rate_ref, sample_ref, seen_ref, filter_ref, count_ref,
):
    lane = lane_of()
    inner = lane % 16

    odd = is_odd("gy")

    def near_side(i, carry):
        state_ref[0, i, 16:32, :] = x_low[i]
        state_ref[0, 8 + i, 16:32, :] = own_in[i]
        state_ref[0, 16 + i, 16:32, :] = x_high[i]
        for part in range(3):
            one, other = y_first[8 * part + i], y_second[8 * part + i]
            state_ref[0, 8 * part + i, 8:16, :] = jnp.where(odd, one, other)
            state_ref[0, 8 * part + i, 32:40, :] = jnp.where(odd, other, one)
        return carry

    lax.fori_loop(0, 8, near_side, 0, unroll=2)

    def prepare(x, carry):
        for tile in range(4):
            rows = pl.ds(8 + 8 * tile, 8)
            value = state_ref[0, x, rows, :]
            state_ref[0, x, rows, :] = jnp.where(lane < 48, value, 0.0)
            state_ref[1, x, rows, :] = jnp.where(lane < 48, pltpu.roll(value, 128 - 48, 1), 0.0)
        return carry

    def rates(x, carry):
        for at, unit in ((0, UNIT_A), (1, UNIT_E)):
            for half in (0, 16):
                both = decoded(code_in[at, x - 2, half : half + 16, :]) * unit
                for tile in (0, 8):
                    rate = both[tile : tile + 8]
                    spread = jnp.where(lane < 32, pltpu.roll(rate, 16, 1), pltpu.roll(rate, 32, 1))
                    spread = jnp.where(lane < 16, rate, spread)
                    rate_ref[at, x, pl.ds(half + tile, 8), :] = jnp.where(lane < 48, spread, 0.0)
        return carry

    lax.fori_loop(0, 24, prepare, 0, unroll=4)
    lax.fori_loop(2, 22, rates, 0, unroll=4)

    def advance(step, x, count):
        src, dst = state_ref.at[step % 2, pl.ds(x - 2, 4 + count)], state_ref.at[(step + 1) % 2]
        rows = pl.ds(8, 32)
        fields = [src[2 + j, rows, :] for j in range(count)]
        halves = jnp.concatenate([jnp.concatenate(split(v), axis=1) for v in fields], axis=0)
        depth = jnp.dot(halves, weight_in[...], preferred_element_type=F32)
        fresh = []
        for j, v in enumerate(fields):
            near = (src[1 + j, rows, :] + src[3 + j, rows, :]) + (src[2 + j, pl.ds(7, 32), :] + src[2 + j, pl.ds(9, 32), :])
            far = (src[j, rows, :] + src[4 + j, rows, :]) + (src[2 + j, pl.ds(6, 32), :] + src[2 + j, pl.ds(10, 32), :])
            laplace = depth[32 * j : 32 * j + 32] + (16.0 * near - far)
            old = dst[x + j, rows, :]
            fresh.append(old + rate_ref[0, x + j] * (v - old) + rate_ref[1, x + j] * laplace)
        for j, value in enumerate(fresh):
            dst[x + j, 8:40, :] = value
            sample_ref[step, x + j, :, :] = value[8:24]

    for step in range(HALF):
        count = (20 - 4 * step) // 2
        advance(step, 2 * step + 2, count)
        advance(step, 2 * step + 2 + count, count)

    def finish(x, carry):
        for row in (0, 8):
            rows = pl.ds(row, 8)
            seen = seen_in[x, rows, :]
            for step in range(HALF):
                at = HALF + step
                sample = pltpu.roll(sample_ref[step, 8 + x, rows, :], at, 1)
                seen = jnp.where((inner == at) & (lane < 48), sample, seen)
            seen_ref[x, rows, :] = seen
        return carry

    lax.fori_loop(0, 8, finish, 0, unroll=4)

    filter_ref[...] = filter_in[...].astype(F32)
    blocks = [jnp.zeros((8, CLASSES * MODES), F32)] * 16
    for k in range(3):
        blocks[2 * k] = filter_ref[pl.ds(k, STEPS, stride=3), :]
    filters = jnp.concatenate(blocks, axis=0).astype(jnp.bfloat16)
    motion = seen_ref[...].reshape(128, 128).astype(jnp.bfloat16)
    modal = lax.dot_general(filters, motion, (((0,), (1,)), ((), ())), preferred_element_type=F32)
    modes = lax.broadcasted_iota(jnp.int32, (MODES, 128), 0)
    count_ref[...] = jnp.zeros((8, 128), jnp.int32)
    count_ref[0:1, 0:CLASSES] = count_in[...]
    counts = jnp.where(modes == lane, jnp.broadcast_to(count_ref[0:1, :], (8, 128)), 0)
    counts = jnp.sum(counts, axis=1, keepdims=True)
    energies = []
    for kind in range(CLASSES):
        part = modal[MODES * kind : MODES * (kind + 1), :]
        part = jnp.where(modes < counts[kind : kind + 1, :], part * part, 0.0)
        energies.append(jnp.sum(part, axis=0, keepdims=True))
    demand = 0.5 * jnp.log1p(jnp.concatenate(energies, axis=0))
    for owner in range(table_out.shape[0]):
        cells = jnp.broadcast_to(cells_in[owner : owner + 1, :], (CLASSES, 128))
        chosen = jnp.take_along_axis(demand, cells, axis=1)
        for level in range(table_out.shape[1]):
            table_out[owner, level] = chosen


def fragility_kernel(
    table_ref, slot_ref, kind_ref, city_ref, amplify_ref, median_ref, spread_ref, out_ref, gain_ref, tables_ref
):
    sources = table_ref.shape[0]
    slot, kind, city = slot_ref[...], kind_ref[...], city_ref[...]
    column = slot % 128
    key = (slot // 128) * CLASSES + kind
    demand = jnp.zeros((8, 128), F32)
    for source in range(sources):
        for each in range(CLASSES):
            row = jnp.broadcast_to(table_ref[source, 0, each : each + 1, :], (8, 128))
            found = jnp.take_along_axis(row, column, axis=1)
            demand = jnp.where(key == source * CLASSES + each, found, demand)
    gain_ref[...] = jnp.ones((8, 128), F32)
    gain_ref[0:1, 0:CITIES] = amplify_ref[...]
    gain = jnp.log(jnp.broadcast_to(gain_ref[0:1, :], (8, 128)))
    demand = demand + jnp.take_along_axis(gain, city, axis=1)
    tables_ref[...] = jnp.ones((128, 128), F32)
    batches = median_ref.shape[1]
    tables_ref[0:CLASSES, 0:batches] = median_ref[...]
    medians = tables_ref[...].T
    tables_ref[0:CLASSES, 0:batches] = spread_ref[...]
    spreads = tables_ref[...].T
    for group in range(8):
        level = jnp.broadcast_to(demand[group : group + 1, :], (8, 128))
        index = jnp.broadcast_to(kind[group : group + 1, :], (8, 128))
        for half in range(0, batches, 8):
            middle = jnp.take_along_axis(medians[half : half + 8, :], index, axis=1)
            width = jnp.take_along_axis(spreads[half : half + 8, :], index, axis=1)
            out_ref[half : half + 8, 128 * group : 128 * group + 128] = jax.nn.sigmoid((level - middle) / width)


VM = pl.BlockSpec(memory_space=pltpu.VMEM)


WEIGHTS = {"start": 1.4, "steps_first": 6.7, "steps_second": 6.5, "surface": 4.0, "fragility": 1.0}
UNIT_FLOPS = 1.15e10


def call(kernel, name, shapes, args, specs=None, scratch=(), limit=VMEM_LIMIT):
    out = [s if isinstance(s, jax.ShapeDtypeStruct) else jax.ShapeDtypeStruct(s, F32) for s in shapes]
    return pl.pallas_call(
        kernel,
        out_shape=out,
        in_specs=specs or [VM] * len(args),
        out_specs=[VM] * len(out),
        scratch_shapes=list(scratch),
        compiler_params=pltpu.CompilerParams(vmem_limit_bytes=limit),
        cost_estimate=pl.CostEstimate(flops=int(WEIGHTS.get(name, 0.3) * UNIT_FLOPS), bytes_accessed=0, transcendentals=0),
        name=name,
    )(*args)


def both_ways(to_up, to_down, axis):
    count = lax.axis_size(axis)
    forward = [(i, i + 1) for i in range(count - 1)]
    backward = [(i + 1, i) for i in range(count - 1)]
    return lax.ppermute(to_up, axis, forward), lax.ppermute(to_down, axis, backward)


def swaps(first, second, axis):
    count = lax.axis_size(axis)
    pairs = [[(i, i + 1) for i in range(begin, count - 1, 2)] for begin in (0, 1)]
    pairs = [ways + [(b, a) for a, b in ways] for ways in pairs]
    return lax.ppermute(first, axis, pairs[0]), lax.ppermute(second, axis, pairs[1])


def is_odd(axis):
    return lax.rem(lax.axis_index(axis), 2) == 1


def exchange_x(u, p, faces, coefficients):
    extra = list(coefficients)
    z_first, z_second = swaps(faces, faces, "gz")
    planes = 3 * XU + (3 + len(extra)) * XP + XH + 1
    message = jax.ShapeDtypeStruct((planes, 16, 128), jnp.int16)
    halo, up, down, powers = call(
        functools.partial(x_message_kernel, bool(extra)),
        "x_message",
        [(8, 16, 128), message, message, (16, 128)],
        [z_second, z_first, u, p] + extra,
    )
    return halo, powers, *both_ways(up, down, "gx")


def y_messages(u, p, coefficients, halo, powers, x_low, x_high):
    extra = list(coefficients)
    planes = (3 * YU + (3 + len(extra)) * YP + YH) // 2 + 1
    message = jax.ShapeDtypeStruct((planes, 16, 128), jnp.int16)
    messages = call(
        functools.partial(y_message_kernel, bool(extra)),
        "y_message",
        [message, message],
        [u, p] + extra + [halo, powers, x_low, x_high],
    )
    return messages if extra else messages[::-1]


def body(
    displacement,
    previous,
    courant,
    damping,
    send_cells,
    building_slot,
    building_class,
    city,
    mode_count,
    modal_filter,
    amplify,
    median,
    spread,
):
    own = (3, 8, 16, 128)
    plane = (8, 16, 128)
    wide = pltpu.VMEM((2, 4, 24, 48, 128), F32)
    rates = pltpu.VMEM((4, 24, 32, 128), F32)
    samples = pltpu.VMEM((HALF, 24, 16, 128), F32)

    u, p = displacement, previous
    a, e, faces = call(
        start_kernel,
        "start",
        [plane, plane, plane],
        [u, p, courant, damping],
        specs=[pl.BlockSpec(memory_space=pltpu.HBM)] * 4,
        scratch=[pltpu.VMEM(own, F32)] * 2 + [pltpu.VMEM(plane, F32)] * 2 + [pltpu.SemaphoreType.DMA((8,))],
        limit=START_LIMIT,
    )
    halo, powers, x_low, x_high = exchange_x(u, p, faces, (a, e))
    messages = y_messages(u, p, (a, e), halo, powers, x_low, x_high)
    received = (halo, x_low, x_high, *swaps(*messages, "gy"))
    weights = jnp.asarray(depth_weights(), jnp.bfloat16)
    u, p, faces, slab, seen, codes = call(
        functools.partial(steps_kernel, True),
        "steps_first",
        [own, own, plane, plane, plane, jax.ShapeDtypeStruct((3, 20, 32, 128), jnp.int16)],
        [u, p, a, e, *received, weights],
        scratch=[wide, rates, samples],
    )

    near_low, near_high = both_ways(slab, slab, "gx")
    halo, powers, x_low, x_high = exchange_x(u, p, faces, ())
    owners, levels = lax.axis_size("gx"), lax.axis_size("gz")
    slab_inputs = [jnp.asarray(slab_weights(), jnp.bfloat16), modal_filter.T, mode_count.reshape(1, CLASSES)]
    cells = send_cells.reshape(owners, 128)
    slab_messages = call(
        slab_message_kernel,
        "slab_message",
        [(24, 8, 128)] * 2,
        [slab, near_low, near_high, powers, cells] + slab_inputs,
    )
    side_first, side_second = swaps(*slab_messages, "gy")
    messages = y_messages(u, p, (), halo, powers, x_low, x_high)
    received = (halo, x_low, x_high, *swaps(*messages, "gy"))
    (table,) = call(
        surface_kernel,
        "surface",
        [(owners, levels, CLASSES, 128)],
        [slab, near_low, near_high, side_first, side_second, slab_inputs[0], codes, seen] + slab_inputs[1:] + [cells, messages[0]],
        specs=[VM] * 11 + [pl.BlockSpec(memory_space=pl.ANY)],
        scratch=[
            pltpu.VMEM((2, 24, 48, 128), F32),
            pltpu.VMEM((2, 24, 32, 128), F32),
            samples,
            pltpu.VMEM(plane, F32),
            pltpu.VMEM((3 * STEPS, CLASSES * MODES), F32),
            pltpu.VMEM((8, 128), jnp.int32),
        ],
    )
    table = table.reshape(owners * levels, CLASSES, 128)
    table = lax.all_to_all(table, ("gx", "gz"), split_axis=0, concat_axis=0, tiled=True)
    building_inputs = [
        building_slot.reshape(8, 128),
        building_class.reshape(8, 128),
        city.reshape(8, 128),
        amplify.reshape(1, CITIES),
        median.T,
        spread.T,
    ]
    (field,) = call(
        functools.partial(steps_kernel, False),
        "steps_second",
        [own],
        [u, p, *received, weights, codes] + building_inputs,
        scratch=[wide, rates],
    )
    (probability,) = call(
        fragility_kernel,
        "fragility",
        [(16, 1024)],
        [table.reshape(owners, levels, CLASSES, 128)] + building_inputs,
        scratch=[pltpu.VMEM((8, 128), F32), pltpu.VMEM((128, 128), F32)],
    )
    return (field, probability)


def solution(mesh):
    placed = (
        P(None, "gx", "gy", "gz"),
        P(None, "gx", "gy", "gz"),
        P("gx", "gy", "gz"),
        P("gx", "gy", "gz"),
        P("gx", "gy", None),
        P(("gx", "gy", "gz")),
        P(("gx", "gy", "gz")),
        P(("gx", "gy", "gz")),
        P(),
        P(),
        P(),
        P(),
        P(),
    )
    return jax.shard_map(
        body,
        mesh=mesh,
        in_specs=placed,
        out_specs=(P(None, "gx", "gy", "gz"), P(None, ("gx", "gy", "gz"))),
        check_vma=False,
    )
```
